32 devices in a mesh: fsdp: 16 (over z, x, core), ctx: 2 (over y).
Axes of the slice: x: 2, y: 2, z: 4, core: 2. Of those that a mesh axis runs over, the one named last changes fastest.
Arguments:
- activations: bfloat16 [16, 1568, 1024], P('fsdp', 'ctx'), may hold values from -6 to 6
- cotangent: bfloat16 [16, 1568, 1024], P('fsdp', 'ctx'), may hold values from -6 to 6
- query_weight: bfloat16 [1024, 1024], P('fsdp'), may hold values from -0.1875 to 0.1875
- key_weight: bfloat16 [1024, 1024], P('fsdp'), may hold values from -0.1875 to 0.1875
- value_weight: bfloat16 [1024, 1024], P('fsdp'), may hold values from -0.1875 to 0.1875
- output_weight: bfloat16 [1024, 1024], P('fsdp'), may hold values from -1.5 to 1.5
- first_gain: bfloat16 [1024], P('fsdp'), may hold values from 0.25 to 1.75
- first_shift: bfloat16 [1024], P('fsdp'), may hold values from -2 to 2
- query_bias: bfloat16 [1024], P('fsdp'), may hold values from -2 to 2
- value_bias: bfloat16 [1024], P('fsdp'), may hold values from -2 to 2
- output_bias: bfloat16 [1024], P('fsdp'), may hold values from -2 to 2
- up_weight: bfloat16 [1024, 4096], P('fsdp'), may hold values from -0.1875 to 0.1875
- down_weight: bfloat16 [4096, 1024], P('fsdp'), may hold values from -0.09375 to 0.09375
- second_gain: bfloat16 [1024], P('fsdp'), may hold values from 0.25 to 1.75
- second_shift: bfloat16 [1024], P('fsdp'), may hold values from -2 to 2
- up_bias: bfloat16 [4096], P('fsdp'), may hold values from -2 to 2
- down_bias: bfloat16 [1024], P('fsdp'), may hold values from -2 to 2
Outputs:
- block_out: bfloat16 [16, 1568, 1024], P('fsdp', 'ctx')
- input_grad: float32 [16, 1568, 1024], P('fsdp', 'ctx')
- query_weight_grad: float32 [1024, 1024], P('fsdp')
- key_weight_grad: float32 [1024, 1024], P('fsdp')
- value_weight_grad: float32 [1024, 1024], P('fsdp')
- output_weight_grad: float32 [1024, 1024], P('fsdp')
- first_gain_grad: float32 [1024], P('fsdp')
- first_shift_grad: float32 [1024], P('fsdp')
- query_bias_grad: float32 [1024], P('fsdp')
- value_bias_grad: float32 [1024], P('fsdp')
- output_bias_grad: float32 [1024], P('fsdp')
- up_weight_grad: float32 [1024, 4096], P('fsdp')
- down_weight_grad: float32 [4096, 1024], P('fsdp')
- second_gain_grad: float32 [1024], P('fsdp')
- second_shift_grad: float32 [1024], P('fsdp')
- up_bias_grad: float32 [4096], P('fsdp')
- down_bias_grad: float32 [1024], P('fsdp')
The draws below stay inside these ranges and needn't reach their ends.
All inputs are finite; a program needn't handle non-finite values.
Results may differ from the reference program's by a relative error of at most 0.02.
Values may be sent and summed in bfloat16 or wider, within the bound.
A program may use at most 384 MiB of HBM per device.

```python
import jax
import jax.numpy as jnp
from jax import lax

D = 1024
HEADS = 16
FF = 4096
LENGTH = 1568
HDIM = 64
CLIPS_ALL = 16


def steps_of(own_key, shape, pieces, low, high):
    def one(axis_at, blocks):
        heights = jax.random.uniform(jax.random.fold_in(jax.random.fold_in(own_key, 6), axis_at), (blocks,), jnp.float32, low / len(pieces), high / len(pieces))
        return jnp.repeat(jnp.exp(heights), shape[axis_at] // blocks).reshape((-1,) + (1,) * (len(shape) - axis_at - 1))

    loudness = one(*pieces[0])
    for cut in pieces[1:]:
        loudness = loudness * one(*cut)
    return loudness


def scatter_about(own_key, shape, width, reach, pieces=(), dtype=jnp.bfloat16):
    loudness = steps_of(own_key, shape, pieces, -0.22, 0.18) if pieces else 1.0
    values = jax.random.normal(own_key, shape, jnp.float32) * width * loudness
    return jnp.minimum(jnp.maximum(values, -reach), reach).astype(dtype)


def setup_inputs(seed: int = 0) -> dict:
    key_of = jax.random.split(jax.random.key(seed), 18)
    return {
        "activations": scatter_about(key_of[0], (CLIPS_ALL, LENGTH, D), 1.0, 6.0, ((0, 16), (1, 2))),
        "cotangent": scatter_about(key_of[1], (CLIPS_ALL, LENGTH, D), 1.0, 6.0, ((0, 16), (1, 2))),
        "query_weight": scatter_about(key_of[2], (D, D), D ** -0.5, 0.1875, ((0, 16),)),
        "key_weight": scatter_about(key_of[3], (D, D), D ** -0.5, 0.1875, ((0, 16),)),
        "value_weight": scatter_about(key_of[4], (D, D), D ** -0.5, 0.1875, ((0, 16),)),
        "output_weight": scatter_about(key_of[5], (D, D), (D // 64) ** -0.5, 1.5, ((0, 16),)),
        "first_gain": jnp.clip(1.0 + 0.15 * jax.random.normal(key_of[6], (D,), jnp.float32), 0.25, 1.75).astype(jnp.bfloat16),
        "first_shift": scatter_about(key_of[7], (D,), 0.3, 2.0, ((0, 16),)),
        "query_bias": scatter_about(key_of[8], (D,), 0.3, 2.0, ((0, 16),)),
        "value_bias": scatter_about(key_of[9], (D,), 0.3, 2.0, ((0, 16),)),
        "output_bias": scatter_about(key_of[10], (D,), 0.3, 2.0, ((0, 16),)),
        "up_weight": scatter_about(key_of[11], (D, FF), D ** -0.5, 0.1875, ((0, 16),)),
        "down_weight": scatter_about(key_of[12], (FF, D), FF ** -0.5, 0.09375, ((0, 16),)),
        "second_gain": jnp.clip(1.0 + 0.15 * jax.random.normal(key_of[13], (D,), jnp.float32), 0.25, 1.75).astype(jnp.bfloat16),
        "second_shift": scatter_about(key_of[14], (D,), 0.3, 2.0, ((0, 16),)),
        "up_bias": scatter_about(key_of[15], (FF,), 0.3, 2.0, ((0, 16),)),
        "down_bias": scatter_about(key_of[16], (D,), 0.3, 2.0, ((0, 16),)),
    }


@jax.custom_vjp
def low(v):
    return lax.optimization_barrier(v.astype(jnp.bfloat16)).astype(jnp.float32)

@jax.custom_vjp
def low_back(v):
    return v

def low_keep(v):
    return (low(v), None)

def low_pass(kept, grad):
    return (grad,)

def back_keep(v):
    return (v, None)

def back_low(kept, grad):
    return (low(grad),)
low.defvjp(low_keep, low_pass)
low_back.defvjp(back_keep, back_low)
highest = lax.Precision.HIGHEST
epsilon = 1e-05

def layer_norm(token_rows, gain, shift):
    centered = token_rows - lax.optimization_barrier(jnp.mean(token_rows, axis=-1, keepdims=True))
    variance = lax.optimization_barrier(jnp.mean(centered * centered, axis=-1, keepdims=True))
    return centered * lax.rsqrt(variance + epsilon) * gain + shift

def forward_clip(params, clip_rows):
    query_w, key_w, value_w, output_w, gain_one, shift_one, query_b, value_b, output_b, up_w, down_w, gain_two, shift_two, up_b, down_b = params
    normed = low(layer_norm(clip_rows, gain_one, shift_one))
    queries = low(low_back(jnp.dot(normed, query_w, precision=highest) + query_b))
    keys_all = low(low_back(jnp.dot(normed, key_w, precision=highest)))
    values_all = low(low_back(jnp.dot(normed, value_w, precision=highest) + value_b))
    query_heads = queries.reshape(LENGTH, HEADS, HDIM)
    key_heads = keys_all.reshape(LENGTH, HEADS, HDIM)
    value_heads = values_all.reshape(LENGTH, HEADS, HDIM)
    scores = low_back(jnp.einsum('qhd,khd->hqk', query_heads, key_heads, precision=highest) * HDIM ** (-0.5))
    probs = low(jax.nn.softmax(scores, axis=-1))
    attended = jnp.einsum('hqk,khd->qhd', probs, value_heads, precision=highest).reshape(LENGTH, D)
    attended = low(low_back(attended))
    mid_rows = clip_rows + low_back(jnp.dot(attended, output_w, precision=highest) + output_b)
    normed_two = low(layer_norm(mid_rows, gain_two, shift_two))
    pre_act = low_back(jnp.dot(normed_two, up_w, precision=highest) + up_b)
    hidden = low(jax.nn.gelu(pre_act, approximate=True))
    return mid_rows + low_back(jnp.dot(hidden, down_w, precision=highest) + down_b)

def reference(activations, cotangent, query_weight, key_weight, value_weight, output_weight, first_gain, first_shift, query_bias, value_bias, output_bias, up_weight, down_weight, second_gain, second_shift, up_bias, down_bias):
    params = tuple((item.astype(jnp.float32) for item in (query_weight, key_weight, value_weight, output_weight, first_gain, first_shift, query_bias, value_bias, output_bias, up_weight, down_weight, second_gain, second_shift, up_bias, down_bias)))

    def one_clip(totals, clip_pair):
        clip_in, clip_cot = clip_pair
        result, backward = jax.vjp(forward_clip, params, clip_in)
        param_grads, clip_grad = backward(clip_cot)
        totals = jax.tree.map(lambda left, right: left + right, totals, param_grads)
        return (totals, (result.astype(jnp.bfloat16), clip_grad))
    initial = tuple((jnp.zeros_like(item) for item in params))
    totals, (outputs, in_grads) = lax.scan(one_clip, initial, (activations.astype(jnp.float32), cotangent.astype(jnp.float32)))
    return (outputs, in_grads, totals[0], totals[1], totals[2], totals[3], totals[4], totals[5], totals[6], totals[7], totals[8], totals[9], totals[10], totals[11], totals[12], totals[13], totals[14])
```

```python
import functools

import jax
import jax.numpy as jnp
from jax import lax
from jax.experimental import pallas as pl
from jax.experimental.pallas import tpu as pltpu
from jax.sharding import PartitionSpec as P

HEADS = 16
HDIM = 64
MESH = pl.DeviceIdType.MESH


epsilon = 1e-05


def layer_norm(token_rows, gain, shift):
    centered = token_rows - jnp.mean(token_rows, axis=-1, keepdims=True)
    variance = jnp.mean(centered * centered, axis=-1, keepdims=True)
    return centered * lax.rsqrt(variance + epsilon) * gain + shift


def gelu_act(values_in):
    return jax.nn.gelu(values_in, approximate=True)


def gather_attention(shards):
    return (
        lax.all_gather(shards[0], "fsdp", axis=0, tiled=True),
        lax.all_gather(shards[1], "fsdp", axis=0, tiled=True),
        lax.all_gather(shards[2], "fsdp", axis=0, tiled=True),
        lax.all_gather(shards[3], "fsdp", axis=0, tiled=True),
        lax.all_gather(shards[4], "fsdp", axis=0, tiled=True),
        lax.all_gather(shards[5], "fsdp", axis=0, tiled=True),
        lax.all_gather(shards[6], "fsdp", axis=0, tiled=True),
        lax.all_gather(shards[7], "fsdp", axis=0, tiled=True),
        lax.all_gather(shards[8], "fsdp", axis=0, tiled=True),
    )


def gather_feed(shards):
    return (
        lax.all_gather(shards[0], "fsdp", axis=0, tiled=True),
        lax.all_gather(shards[1], "fsdp", axis=0, tiled=True),
        lax.all_gather(shards[2], "fsdp", axis=0, tiled=True),
        lax.all_gather(shards[3], "fsdp", axis=0, tiled=True),
        lax.all_gather(shards[4], "fsdp", axis=0, tiled=True),
        lax.all_gather(shards[5], "fsdp", axis=0, tiled=True),
    )


def plain_device(
    activations,
    cotangent,
    query_weight,
    key_weight,
    value_weight,
    output_weight,
    first_gain,
    first_shift,
    query_bias,
    value_bias,
    output_bias,
    up_weight,
    down_weight,
    second_gain,
    second_shift,
    up_bias,
    down_bias,
):
    clip_count, local_len, width = activations.shape
    scaling = HDIM ** (-0.5)
    attend_shards = (
        query_weight,
        key_weight,
        value_weight,
        output_weight,
        first_gain,
        first_shift,
        query_bias,
        value_bias,
        output_bias,
    )
    feed_shards = (up_weight, down_weight, second_gain, second_shift, up_bias, down_bias)
    attend_full = gather_attention(attend_shards)
    (
        full_query,
        full_key,
        full_value,
        full_output,
        full_gain_one,
        full_shift_one,
        full_query_bias,
        full_value_bias,
        full_output_bias,
    ) = attend_full
    gain_one = full_gain_one.astype(jnp.float32)
    shift_one = full_shift_one.astype(jnp.float32)
    token_rows = activations.reshape(-1, width).astype(jnp.float32)
    normed_one = layer_norm(token_rows, gain_one, shift_one).astype(jnp.bfloat16)
    queries = (
        jnp.dot(normed_one, full_query, preferred_element_type=jnp.float32)
        + full_query_bias.astype(jnp.float32)
    ).astype(jnp.bfloat16)
    keys_local = jnp.dot(normed_one, full_key, preferred_element_type=jnp.float32).astype(
        jnp.bfloat16
    )
    values_local = (
        jnp.dot(normed_one, full_value, preferred_element_type=jnp.float32)
        + full_value_bias.astype(jnp.float32)
    ).astype(jnp.bfloat16)
    query_heads = queries.reshape(clip_count, local_len, HEADS, HDIM)
    keys_block = keys_local.reshape(clip_count, local_len, width)
    values_block = values_local.reshape(clip_count, local_len, width)
    run_max = jnp.full((clip_count, local_len, HEADS), -1e30, jnp.float32)
    key_piece = lax.all_gather(keys_block, "ctx", axis=1, tiled=True)
    value_piece = lax.all_gather(values_block, "ctx", axis=1, tiled=True)
    key_heads = key_piece.reshape(clip_count, -1, HEADS, HDIM)
    value_heads = value_piece.reshape(clip_count, -1, HEADS, HDIM)
    scores = (
        jnp.einsum("cqhd,ckhd->cqhk", query_heads, key_heads, preferred_element_type=jnp.float32)
        * scaling
    )
    new_max = jnp.maximum(run_max, jnp.max(scores, axis=-1))
    weights = jnp.exp(scores - new_max[..., None])
    run_sum = jnp.sum(weights, axis=-1)
    accum = jnp.einsum(
        "cqhk,ckhd->cqhd",
        weights.astype(jnp.bfloat16),
        value_heads,
        preferred_element_type=jnp.float32,
    )
    run_max, run_sum, accum = (new_max, run_sum, accum)
    attend_exact = accum / run_sum[..., None]
    log_total = run_max + jnp.log(run_sum)
    attended = attend_exact.reshape(-1, width).astype(jnp.bfloat16)
    mid_rows = (
        token_rows
        + jnp.dot(attended, full_output, preferred_element_type=jnp.float32)
        + full_output_bias.astype(jnp.float32)
    )
    feed_full = gather_feed(feed_shards)
    full_up, full_down, full_gain_two, full_shift_two, full_up_bias, full_down_bias = feed_full
    gain_two = full_gain_two.astype(jnp.float32)
    shift_two = full_shift_two.astype(jnp.float32)
    normed_two = layer_norm(mid_rows, gain_two, shift_two).astype(jnp.bfloat16)
    pre_act = jnp.dot(
        normed_two, full_up, preferred_element_type=jnp.float32
    ) + full_up_bias.astype(jnp.float32)
    hidden = gelu_act(pre_act).astype(jnp.bfloat16)
    block_rows = (
        mid_rows
        + jnp.dot(hidden, full_down, preferred_element_type=jnp.float32)
        + full_down_bias.astype(jnp.float32)
    )
    block_out = block_rows.astype(jnp.bfloat16).reshape(activations.shape)
    back_attend = gather_attention(attend_shards)
    back_feed = gather_feed(feed_shards)
    back_query, back_key, back_value, back_output = (
        back_attend[0],
        back_attend[1],
        back_attend[2],
        back_attend[3],
    )
    back_up, back_down = (back_feed[0], back_feed[1])
    cot_rows = cotangent.reshape(-1, width)
    outer_grad = cot_rows.astype(jnp.float32)
    down_wgrad = jnp.einsum("rf,rd->fd", hidden, cot_rows, preferred_element_type=jnp.float32)
    down_bgrad = jnp.sum(outer_grad, axis=0)
    hidden_grad = jnp.einsum("rd,fd->rf", cot_rows, back_down, preferred_element_type=jnp.float32)
    _, gelu_back = jax.vjp(gelu_act, pre_act)
    pre_grad = gelu_back(hidden_grad)[0].astype(jnp.bfloat16)
    up_wgrad = jnp.einsum("rd,rf->df", normed_two, pre_grad, preferred_element_type=jnp.float32)
    up_bgrad = jnp.sum(pre_grad.astype(jnp.float32), axis=0)
    normed_two_grad = jnp.einsum("rf,df->rd", pre_grad, back_up, preferred_element_type=jnp.float32)
    _, norm_two_back = jax.vjp(layer_norm, mid_rows, gain_two, shift_two)
    mid_part, gain_two_grad, shift_two_grad = norm_two_back(normed_two_grad)
    mid_grad = outer_grad + mid_part
    feed_owned = (
        lax.psum_scatter(
            up_wgrad.astype(jnp.bfloat16), "fsdp", scatter_dimension=0, tiled=True
        ).astype(jnp.float32),
        lax.psum_scatter(
            down_wgrad.astype(jnp.bfloat16), "fsdp", scatter_dimension=0, tiled=True
        ).astype(jnp.float32),
        lax.psum_scatter(
            gain_two_grad.astype(jnp.bfloat16), "fsdp", scatter_dimension=0, tiled=True
        ).astype(jnp.float32),
        lax.psum_scatter(
            shift_two_grad.astype(jnp.bfloat16), "fsdp", scatter_dimension=0, tiled=True
        ).astype(jnp.float32),
        lax.psum_scatter(
            up_bgrad.astype(jnp.bfloat16), "fsdp", scatter_dimension=0, tiled=True
        ).astype(jnp.float32),
        lax.psum_scatter(
            down_bgrad.astype(jnp.bfloat16), "fsdp", scatter_dimension=0, tiled=True
        ).astype(jnp.float32),
    )
    feed_done = (
        lax.psum(feed_owned[0].astype(jnp.bfloat16), "ctx").astype(jnp.float32),
        lax.psum(feed_owned[1].astype(jnp.bfloat16), "ctx").astype(jnp.float32),
        lax.psum(feed_owned[2].astype(jnp.bfloat16), "ctx").astype(jnp.float32),
        lax.psum(feed_owned[3].astype(jnp.bfloat16), "ctx").astype(jnp.float32),
        lax.psum(feed_owned[4].astype(jnp.bfloat16), "ctx").astype(jnp.float32),
        lax.psum(feed_owned[5].astype(jnp.bfloat16), "ctx").astype(jnp.float32),
    )
    branch_grad = mid_grad.astype(jnp.bfloat16)
    output_wgrad = jnp.einsum(
        "rd,re->de", attended, branch_grad, preferred_element_type=jnp.float32
    )
    output_bgrad = jnp.sum(branch_grad.astype(jnp.float32), axis=0)
    attended_grad = jnp.einsum(
        "re,de->rd", branch_grad, back_output, preferred_element_type=jnp.float32
    ).astype(jnp.bfloat16)
    grad_heads = attended_grad.reshape(clip_count, local_len, HEADS, HDIM)
    delta = jnp.sum(grad_heads.astype(jnp.float32) * attend_exact, axis=-1)
    keys_whole, values_whole = (
        lax.all_gather(keys_block, "ctx", axis=1, tiled=True),
        lax.all_gather(values_block, "ctx", axis=1, tiled=True),
    )
    key_heads_all = keys_whole.reshape(clip_count, -1, HEADS, HDIM)
    value_heads_all = values_whole.reshape(clip_count, -1, HEADS, HDIM)
    scores_all = (
        jnp.einsum(
            "cqhd,ckhd->cqhk", query_heads, key_heads_all, preferred_element_type=jnp.float32
        )
        * scaling
    )
    probs = jnp.exp(scores_all - log_total[..., None])
    prob_grad = jnp.einsum(
        "cqhd,ckhd->cqhk", grad_heads, value_heads_all, preferred_element_type=jnp.float32
    )
    score_grad = (probs * (prob_grad - delta[..., None])).astype(jnp.bfloat16)
    query_grad = (
        jnp.einsum("cqhk,ckhd->cqhd", score_grad, key_heads_all, preferred_element_type=jnp.float32)
        * scaling
    ).astype(jnp.bfloat16)
    query_grad = query_grad.reshape(-1, width)
    probs_low = probs.astype(jnp.bfloat16)
    key_part = (
        jnp.einsum("cqhk,cqhd->kchd", score_grad, query_heads, preferred_element_type=jnp.float32)
        * scaling
    )
    value_part = jnp.einsum(
        "cqhk,cqhd->kchd", probs_low, grad_heads, preferred_element_type=jnp.float32
    )
    summed = lax.psum_scatter(
        jnp.stack([key_part, value_part], axis=2)
        .reshape(lax.axis_size("ctx") * local_len, clip_count, 2, width)
        .astype(jnp.bfloat16),
        "ctx",
        scatter_dimension=0,
        tiled=True,
    ).astype(jnp.float32)
    key_grad = jnp.transpose(summed[:, :, 0], (1, 0, 2)).reshape(-1, width).astype(jnp.bfloat16)
    value_grad = jnp.transpose(summed[:, :, 1], (1, 0, 2)).reshape(-1, width).astype(jnp.bfloat16)
    query_wgrad = jnp.einsum(
        "rd,re->de", normed_one, query_grad, preferred_element_type=jnp.float32
    )
    key_wgrad = jnp.einsum("rd,re->de", normed_one, key_grad, preferred_element_type=jnp.float32)
    value_wgrad = jnp.einsum(
        "rd,re->de", normed_one, value_grad, preferred_element_type=jnp.float32
    )
    query_bgrad = jnp.sum(query_grad.astype(jnp.float32), axis=0)
    value_bgrad = jnp.sum(value_grad.astype(jnp.float32), axis=0)
    normed_one_grad = (
        jnp.einsum("re,de->rd", query_grad, back_query, preferred_element_type=jnp.float32)
        + jnp.einsum("re,de->rd", key_grad, back_key, preferred_element_type=jnp.float32)
        + jnp.einsum("re,de->rd", value_grad, back_value, preferred_element_type=jnp.float32)
    )
    _, norm_one_back = jax.vjp(layer_norm, token_rows, gain_one, shift_one)
    input_part, gain_one_grad, shift_one_grad = norm_one_back(normed_one_grad)
    input_grad = (mid_grad + input_part).reshape(activations.shape)
    attend_owned = (
        lax.psum_scatter(
            query_wgrad.astype(jnp.bfloat16), "fsdp", scatter_dimension=0, tiled=True
        ).astype(jnp.float32),
        lax.psum_scatter(
            key_wgrad.astype(jnp.bfloat16), "fsdp", scatter_dimension=0, tiled=True
        ).astype(jnp.float32),
        lax.psum_scatter(
            value_wgrad.astype(jnp.bfloat16), "fsdp", scatter_dimension=0, tiled=True
        ).astype(jnp.float32),
        lax.psum_scatter(
            output_wgrad.astype(jnp.bfloat16), "fsdp", scatter_dimension=0, tiled=True
        ).astype(jnp.float32),
        lax.psum_scatter(
            gain_one_grad.astype(jnp.bfloat16), "fsdp", scatter_dimension=0, tiled=True
        ).astype(jnp.float32),
        lax.psum_scatter(
            shift_one_grad.astype(jnp.bfloat16), "fsdp", scatter_dimension=0, tiled=True
        ).astype(jnp.float32),
        lax.psum_scatter(
            query_bgrad.astype(jnp.bfloat16), "fsdp", scatter_dimension=0, tiled=True
        ).astype(jnp.float32),
        lax.psum_scatter(
            value_bgrad.astype(jnp.bfloat16), "fsdp", scatter_dimension=0, tiled=True
        ).astype(jnp.float32),
        lax.psum_scatter(
            output_bgrad.astype(jnp.bfloat16), "fsdp", scatter_dimension=0, tiled=True
        ).astype(jnp.float32),
    )
    attend_done = (
        lax.psum(attend_owned[0].astype(jnp.bfloat16), "ctx").astype(jnp.float32),
        lax.psum(attend_owned[1].astype(jnp.bfloat16), "ctx").astype(jnp.float32),
        lax.psum(attend_owned[2].astype(jnp.bfloat16), "ctx").astype(jnp.float32),
        lax.psum(attend_owned[3].astype(jnp.bfloat16), "ctx").astype(jnp.float32),
        lax.psum(attend_owned[4].astype(jnp.bfloat16), "ctx").astype(jnp.float32),
        lax.psum(attend_owned[5].astype(jnp.bfloat16), "ctx").astype(jnp.float32),
        lax.psum(attend_owned[6].astype(jnp.bfloat16), "ctx").astype(jnp.float32),
        lax.psum(attend_owned[7].astype(jnp.bfloat16), "ctx").astype(jnp.float32),
        lax.psum(attend_owned[8].astype(jnp.bfloat16), "ctx").astype(jnp.float32),
    )
    return (
        block_out,
        input_grad,
        attend_done[0],
        attend_done[1],
        attend_done[2],
        attend_done[3],
        attend_done[4],
        attend_done[5],
        attend_done[6],
        attend_done[7],
        attend_done[8],
        feed_done[0],
        feed_done[1],
        feed_done[2],
        feed_done[3],
        feed_done[4],
        feed_done[5],
    )


def place():
    f = lax.axis_index("fsdp"); y = lax.axis_index("ctx")
    return f // 4, (f // 2) % 2, f % 2, y

def greet(z, x, c, y, depth):
    barrier = pltpu.get_barrier_semaphore()
    def one(dz, dx, dc, dy):
        pl.semaphore_signal(barrier, inc=1, device_id=(dz * 4 + dx * 2 + dc, dy), device_id_type=MESH)
    for k in range(1, depth):
        one((z + k) % depth, x, c, y)
    one(z, 1 - x, c, y); one(z, x, 1 - c, y); one(z, x, c, 1 - y)
    pl.semaphore_wait(barrier, depth + 2)

class Gather:
    def __init__(self, depth, chunks, ins, outs, sems, where):
        self.depth, self.chunks, self.ins, self.outs = depth, chunks, ins, outs
        self.zs, self.zr, self.xs, self.xr, self.ys, self.yr, self.cs, self.cr, self.loc = sems
        self.where = where
    def src(self, ch, half):
        t, r0, h, both = self.chunks[ch]
        if not both: return self.ins[t].at[pl.ds(r0, h)]
        h2 = h // 2
        return self.ins[t].at[pl.ds(pl.multiple_of(r0 + half * h2, 16), h2)]
    def dst(self, ch, dz, dx, dc, half):
        t, r0, h, both = self.chunks[ch]
        full = self.ins[t].shape[0]
        start = (dz * 4 + dx * 2 + dc) * full + r0
        if not both: return self.outs[t].at[pl.ds(pl.multiple_of(start, 16), h)]
        h2 = h // 2
        return self.outs[t].at[pl.ds(pl.multiple_of(start + half * h2, 16), h2)]
    def copy(self, src, dst, s, r, dz, dx, dc, dy):
        return pltpu.make_async_remote_copy(src_ref=src, dst_ref=dst, send_sem=s, recv_sem=r,
            device_id=(dz * 4 + dx * 2 + dc, dy), device_id_type=MESH)
    def zz(self, j):
        return (self.where[0] - j + self.depth) % self.depth
    def zmove(self, ch, k, recv=False):
        z, x, c, y = self.where
        if recv:
            d = self.dst(ch, self.zz(k), x, c, y)
            return self.copy(d, d, self.zs.at[ch, k], self.zr.at[ch, k], z, x, 1 - c, y)
        return self.copy(self.src(ch, y), self.dst(ch, z, x, c, y), self.zs.at[ch, k], self.zr.at[ch, k], (z + k) % self.depth, x, c, y)
    def xmove(self, ch, j, recv=False):
        z, x, c, y = self.where
        d = self.dst(ch, self.zz(j), 1 - x if recv else x, c, y)
        s = self.src(ch, y) if (j == 0 and not recv) else d
        return self.copy(s, d, self.xs.at[ch, j], self.xr.at[ch, j], z, 1 - x, c, y)
    def ymove(self, ch, i, j, recv=False):
        z, x, c, y = self.where
        d = self.dst(ch, self.zz(j), x if i == 0 else 1 - x, c, 1 - y if recv else y)
        n = i * self.depth + j
        return self.copy(d, d, self.ys.at[ch, n], self.yr.at[ch, n], z, x, c, 1 - y)
    def cmove(self, ch, i, j, other, recv=False):
        z, x, c, y = self.where
        half = 1 - y if other else y
        d = self.dst(ch, self.zz(j), x if i == 0 else 1 - x, 1 - c if recv else c, half)
        s = self.src(ch, half) if (i == 0 and j == 0 and not recv) else d
        n = (i * self.depth + j) + (2 * self.depth if other else 0)
        return self.copy(s, d, self.cs.at[ch, n], self.cr.at[ch, n], z, x, 1 - c, y)
    def own(self, ch):
        z, x, c, y = self.where
        t, r0, h, both = self.chunks[ch]
        full = self.ins[t].shape[0]
        return pltpu.make_async_copy(self.ins[t].at[pl.ds(r0, h)],
            self.outs[t].at[pl.ds(pl.multiple_of((z * 4 + x * 2 + c) * full + r0, 16), h)], self.loc.at[ch])
    def begin(self, ch):
        for k in range(1, self.depth): self.zmove(ch, k).start()
        self.xmove(ch, 0).start()
        self.cmove(ch, 0, 0, False).start()
        if self.chunks[ch][3]: self.cmove(ch, 0, 0, True).start()
        self.own(ch).start()
    def zstage(self, ch):
        for k in range(1, self.depth):
            self.zmove(ch, k, True).wait_recv()
            self.xmove(ch, k).start()
            if self.chunks[ch][3]: self.ymove(ch, 0, k).start()
            self.cmove(ch, 0, k, False).start()
    def xstage(self, ch):
        for j in range(self.depth):
            self.xmove(ch, j, True).wait_recv()
            if self.chunks[ch][3]: self.ymove(ch, 1, j).start()
            self.cmove(ch, 1, j, False).start()
    def ystage(self, ch):
        if not self.chunks[ch][3]: return
        for i in range(2):
            for j in range(1 - i, self.depth):
                self.ymove(ch, i, j, True).wait_recv()
                self.cmove(ch, i, j, True).start()
    def arrived(self, ch):
        for i in range(2):
            for j in range(self.depth):
                self.cmove(ch, i, j, False, True).wait_recv()
                if self.chunks[ch][3]: self.cmove(ch, i, j, True, True).wait_recv()
        self.own(ch).wait()
    def sent(self, ch):
        both = self.chunks[ch][3]
        for k in range(1, self.depth): self.zmove(ch, k).wait_send()
        for j in range(self.depth): self.xmove(ch, j).wait_send()
        for i in range(2):
            for j in range(self.depth):
                self.cmove(ch, i, j, False).wait_send()
                if both:
                    self.cmove(ch, i, j, True).wait_send()
                    if i or j: self.ymove(ch, i, j).wait_send()

def gather_sems(depth, n):
    S = pltpu.SemaphoreType.DMA
    return [S((n, depth)), S((n, depth)), S((n, depth)), S((n, depth)), S((n, 2 * depth)), S((n, 2 * depth)), S((n, 4 * depth)), S((n, 4 * depth)), S((n,))]

def ag_kernel(depth, n, chunks, ahead, lag, *refs):
    ins = refs[:n]; x_in = refs[n]
    outs = refs[n + 1:2 * n + 1]; x_out = refs[2 * n + 1]
    sems = refs[2 * n + 2:2 * n + 11]; ys, yr = refs[2 * n + 11:]
    z, x, c, y = place()
    g = Gather(depth, chunks, ins, outs, sems, (z, x, c, y))
    greet(z, x, c, y, depth)
    xw = g.copy(x_in, x_out, ys, yr, z, x, c, 1 - y)
    xw.start()
    N = len(chunks)
    for ch in range(min(ahead, N)): g.begin(ch)
    for s in range(N + 2 * lag):
        if s < N:
            g.zstage(s)
            if s + ahead < N: g.begin(s + ahead)
        if 0 <= s - lag < N: g.xstage(s - lag)
        if 0 <= s - 2 * lag < N: g.ystage(s - 2 * lag)
    xw.wait()
    for ch in range(N): g.arrived(ch)
    for ch in range(N): g.sent(ch)


def gather_all(shards, x, chunks, depth=4, ahead=2, lag=1, cid=1):
    n = len(shards)
    S = pltpu.SemaphoreType.DMA
    return pl.pallas_call(
        functools.partial(ag_kernel, depth, n, chunks, ahead, lag),
        out_shape=[jax.ShapeDtypeStruct((depth * 4 * s.shape[0],) + s.shape[1:], s.dtype) for s in shards] + [jax.ShapeDtypeStruct(x.shape, x.dtype)],
        in_specs=[pl.BlockSpec(memory_space=pl.ANY)] * (n + 1),
        out_specs=[pl.BlockSpec(memory_space=pl.ANY)] * (n + 1),
        scratch_shapes=gather_sems(depth, len(chunks)) + [S, S],
        compiler_params=pltpu.CompilerParams(collective_id=cid, has_side_effects=True),
        name="weights_gather")(*shards, x)


def rowwise(h, w, body):
    wide = min(w, 1024 if w % 1024 == 0 else 512)
    steps_w = w // wide
    total = (h // 16) * steps_w
    if total == 1:
        body(pl.ds(0, 16), pl.ds(0, wide)); return
    def one(i, _):
        body(pl.ds(pl.multiple_of((i // steps_w) * 16, 16), 16), pl.ds(pl.multiple_of((i % steps_w) * wide, 128), wide))
        return 0
    lax.fori_loop(0, total, one, 0)

class Scatter:
    def __init__(self, depth, chunks, grads, outs, bufs, sems, where):
        self.depth, self.chunks, self.grads, self.outs, self.bufs = depth, chunks, grads, outs, bufs
        self.ls, self.cs, self.cr, self.xs, self.xr, self.zs, self.zr, self.ys, self.yr = sems
        self.where = where
    def piece(self, ch, dz, dx, dc):
        t, k, r0, h = self.chunks[ch]
        full = self.grads[t].shape[0] // (4 * self.depth)
        return self.grads[t].at[pl.ds(pl.multiple_of((dz * 4 + dx * 2 + dc) * full + r0, 16), h)]
    def copy(self, src, dst, s, r, dz, dx, dc, dy):
        return pltpu.make_async_remote_copy(src_ref=src, dst_ref=dst, send_sem=s, recv_sem=r,
            device_id=(dz * 4 + dx * 2 + dc, dy), device_id_type=MESH)
    def zz(self, j): return (self.where[0] + j) % self.depth
    def load(self, ch, i, j):
        z, x, c, y = self.where; t, k = self.chunks[ch][:2]
        return pltpu.make_async_copy(self.piece(ch, self.zz(j), x if i == 0 else 1 - x, c), self.bufs[t][0].at[k, i, j], self.ls.at[ch, i * self.depth + j])
    def cmove(self, ch, i, j):
        z, x, c, y = self.where; t, k = self.chunks[ch][:2]; n = i * self.depth + j
        return self.copy(self.piece(ch, self.zz(j), x if i == 0 else 1 - x, 1 - c), self.bufs[t][1].at[k, i, j], self.cs.at[ch, n], self.cr.at[ch, n], z, x, 1 - c, y)
    def xmove(self, ch, j):
        z, x, c, y = self.where; t, k = self.chunks[ch][:2]
        return self.copy(self.bufs[t][0].at[k, 1, j], self.bufs[t][2].at[k, j], self.xs.at[ch, j], self.xr.at[ch, j], z, 1 - x, c, y)
    def zmove(self, ch, j):
        z, x, c, y = self.where; t, k = self.chunks[ch][:2]
        return self.copy(self.bufs[t][0].at[k, 0, j], self.bufs[t][3].at[k, j - 1], self.zs.at[ch, j], self.zr.at[ch, j], self.zz(j), x, c, y)
    def ymove(self, ch):
        z, x, c, y = self.where; t, k = self.chunks[ch][:2]
        return self.copy(self.bufs[t][4].at[k], self.bufs[t][5].at[k], self.ys.at[ch], self.yr.at[ch], z, x, c, 1 - y)
    def begin(self, ch):
        for i in (1, 0):
            for j in range(self.depth):
                self.load(ch, i, j).start()
                self.cmove(ch, i, j).start()
    def cstage(self, ch):
        t, k, r0, h = self.chunks[ch]; L, C = self.bufs[t][:2]; w = L.shape[-1]
        for i in (1, 0):
            for j in range(self.depth):
                self.load(ch, i, j).wait(); self.cmove(ch, i, j).wait_recv()
                def add(r, q):
                    L[k, i, j, r, q] = L[k, i, j, r, q] + C[k, i, j, r, q]
                rowwise(h, w, add)
                if i == 1: self.xmove(ch, j).start()
    def xstage(self, ch):
        t, k, r0, h = self.chunks[ch]; L, C, X = self.bufs[t][:3]; w = L.shape[-1]
        for j in list(range(1, self.depth)) + [0]:
            self.xmove(ch, j).wait_recv()
            def add(r, q):
                L[k, 0, j, r, q] = L[k, 0, j, r, q] + X[k, j, r, q]
            rowwise(h, w, add)
            if j: self.zmove(ch, j).start()
    def zstage(self, ch):
        t, k, r0, h = self.chunks[ch]; L, C, X, Z, F, Y = self.bufs[t]; w = L.shape[-1]
        for j in range(1, self.depth): self.zmove(ch, j).wait_recv()
        def add(r, q):
            tot = L[k, 0, 0, r, q].astype(jnp.float32)
            for j in range(1, self.depth): tot = tot + Z[k, j - 1, r, q].astype(jnp.float32)
            F[k, r, q] = tot.astype(jnp.bfloat16)
        rowwise(h, w, add)
        self.ymove(ch).start()
    def ystage(self, ch):
        t, k, r0, h = self.chunks[ch]; L, C, X, Z, F, Y = self.bufs[t]; w = L.shape[-1]
        z, x, c, y = self.where
        self.ymove(ch).wait_recv()
        out = self.outs[t]
        if out.shape[-1] == w:
            def add(r, q):
                out[pl.ds(pl.multiple_of(r0 + r.start, 16), 16), q] = F[k, r, q].astype(jnp.float32) + Y[k, r, q].astype(jnp.float32)
            rowwise(h, w, add)
        else:
            part = w // 3
            for n in range(3):
                def lay(r, q, n=n):
                    mine = F[k, r, n * part:(n + 1) * part].astype(jnp.float32)
                    other = Y[k, r, n * part:(n + 1) * part].astype(jnp.float32)
                    rr = pl.ds(pl.multiple_of(r0 + r.start, 16), 16)
                    out[rr, 2 * n * part:(2 * n + 1) * part] = jnp.where(y == 0, mine, other)
                    out[rr, (2 * n + 1) * part:(2 * n + 2) * part] = jnp.where(y == 0, other, mine)
                rowwise(h, 128, lay)
    def sent(self, ch):
        for i in range(2):
            for j in range(self.depth): self.cmove(ch, i, j).wait_send()
        for j in range(self.depth):
            self.xmove(ch, j).wait_send()
            if j: self.zmove(ch, j).wait_send()
        self.ymove(ch).wait_send()

def scatter_scratch(depth, chunks, widths):
    S = pltpu.SemaphoreType.DMA; n = len(chunks); out = []
    for t, w in enumerate(widths):
        mine = [c for c in chunks if c[0] == t]; m = len(mine); h = mine[0][3]
        B = lambda *lead: pltpu.VMEM(lead + (h, w), jnp.bfloat16)
        out += [B(m, 2, depth), B(m, 2, depth), B(m, depth), B(m, depth - 1), B(m), B(m)]
    return out + [S((n, 2 * depth)), S((n, 2 * depth)), S((n, 2 * depth)), S((n, depth)), S((n, depth)), S((n, depth)), S((n, depth)), S((n,)), S((n,))]

def rs_kernel(depth, n, chunks, lag, *refs):
    grads, outs = refs[:n], refs[n:2 * n]
    bufs = [refs[2 * n + 6 * t:2 * n + 6 * t + 6] for t in range(n)]
    sems = refs[8 * n:8 * n + 9]
    where = place()
    s = Scatter(depth, chunks, grads, outs, bufs, sems, where)
    greet(*where, depth)
    N = len(chunks)
    for ch in range(N): s.begin(ch)
    for st in range(N + 3 * lag):
        if st < N: s.cstage(st)
        if 0 <= st - lag < N: s.xstage(st - lag)
        if 0 <= st - 2 * lag < N: s.zstage(st - 2 * lag)
        if 0 <= st - 3 * lag < N: s.ystage(st - 3 * lag)
    for ch in range(N): s.sent(ch)

def scatter_all(grads, chunks, wide, depth=4, lag=1, cid=2):
    n = len(grads)
    return pl.pallas_call(
        functools.partial(rs_kernel, depth, n, chunks, lag),
        out_shape=[jax.ShapeDtypeStruct((g.shape[0] // (4 * depth), g.shape[1] * (2 if t == wide else 1)), jnp.float32) for t, g in enumerate(grads)],
        in_specs=[pl.BlockSpec(memory_space=pl.ANY)] * n,
        out_specs=[pl.BlockSpec(memory_space=pltpu.VMEM)] * n,
        scratch_shapes=scatter_scratch(depth, chunks, [g.shape[1] for g in grads]),
        compiler_params=pltpu.CompilerParams(collective_id=cid, has_side_effects=True, vmem_limit_bytes=60 * 2 ** 20),
        name="gradients_scatter")(*grads)


DEPTH, BOTH = 4, 2


def pack_small(vectors, up_bias, c):
    rows = jnp.stack(vectors)
    zero = jnp.zeros_like(rows)
    rows = jnp.concatenate([jnp.where(c == 0, rows, zero), jnp.where(c == 0, zero, rows)], axis=1)
    return jnp.concatenate([rows, up_bias.reshape(2, 128), jnp.zeros((6, 128), rows.dtype)], axis=0)


def unpack_small(gathered):
    blocks = gathered.astype(jnp.float32).reshape(-1, 2, 16, 128)
    vectors = (blocks[:, 0, :8] + blocks[:, 1, :8]).transpose(1, 0, 2).reshape(8, -1)
    return vectors, blocks[:, :, 8:10].reshape(-1)


def pack_small_grads(vectors, up_grad):
    parts = 4 * DEPTH
    rows = jnp.stack(vectors).reshape(8, parts, 64).transpose(1, 0, 2)
    rows = jnp.concatenate([rows, jnp.zeros_like(rows)], axis=2)
    rows = jnp.concatenate([rows, up_grad.reshape(parts, 2, 128), jnp.zeros((parts, 6, 128), jnp.float32)], axis=1)
    return rows.astype(jnp.bfloat16).reshape(parts * 16, 128)


def swap(value):
    return lax.ppermute(value, "ctx", [(0, 1), (1, 0)])


def gather_chunks():
    return (
        (0, 0, 16, False),
        (1, 0, 64, False),
    ) + tuple((4, 64 * i, 64, True) for i in range(4)) + ((2, 0, 64, False),) + tuple(
        (3, 16 * i, 16, False) for i in range(4)
    )


def scatter_chunks():
    return ((0, 0, 0, 16),) + tuple((4, i, 64 * i, 64) for i in range(4)) + tuple(
        (3, i, 16 * i, 16) for i in range(4)
    ) + ((2, 0, 0, 64), (1, 0, 0, 64))


def fast_device(
    activations, cotangent, query_weight, key_weight, value_weight, output_weight, first_gain, first_shift,
    query_bias, value_bias, output_bias, up_weight, down_weight, second_gain, second_shift, up_bias, down_bias,
):
    _, rows, width = activations.shape
    half = width // 2
    heads = half // HDIM
    scaling = HDIM ** (-0.5)
    y = lax.axis_index("ctx")
    c = lax.axis_index("fsdp") % 2
    f32, bf16 = jnp.float32, jnp.bfloat16

    def mine(value):
        return lax.dynamic_slice_in_dim(value, y * half, half, value.ndim - 1)

    def others(value):
        return lax.dynamic_slice_in_dim(value, (1 - y) * half, half, value.ndim - 1)

    def both(own, other):
        return jnp.where(y == 0, jnp.concatenate([own, other], -1), jnp.concatenate([other, own], -1))

    small = pack_small(
        (first_gain, first_shift, query_bias, value_bias, output_bias, second_gain, second_shift, down_bias), up_bias, c
    )
    own_qkv = jnp.concatenate([mine(query_weight), mine(key_weight), mine(value_weight)], axis=1)
    x_own = activations[0]
    all_small, all_qkv, all_out, all_up, all_down, x_other = gather_all(
        (small, own_qkv, output_weight, up_weight, down_weight), x_own, gather_chunks()
    )
    vectors, full_up_bias = unpack_small(all_small)
    gain_one, shift_one, full_query_bias, full_value_bias, full_output_bias, gain_two, shift_two, full_down_bias = vectors

    token_rows = jnp.concatenate([x_own, x_other], axis=0).astype(f32)
    normed_one = layer_norm(token_rows, gain_one, shift_one).astype(bf16)
    bias = jnp.concatenate([mine(full_query_bias), jnp.zeros((half,), f32), mine(full_value_bias)])
    qkv = (jnp.dot(normed_one, all_qkv, preferred_element_type=f32) + bias).astype(bf16)
    queries, keys, values = [v.reshape(2 * rows, heads, HDIM) for v in jnp.split(qkv, 3, axis=1)]
    scores = jnp.einsum("qhd,khd->hqk", queries, keys, preferred_element_type=f32) * scaling
    top = jnp.max(scores, axis=-1, keepdims=True)
    weights = jnp.exp(scores - top)
    total = jnp.sum(weights, axis=-1, keepdims=True)
    exact = jnp.einsum("hqk,khd->hqd", weights.astype(bf16), values, preferred_element_type=f32) / total
    log_total = top + jnp.log(total)
    attended_mine = exact.transpose(1, 0, 2).reshape(2 * rows, half).astype(bf16)
    attended = both(attended_mine[:rows], swap(attended_mine[rows:]))

    x_rows = x_own.astype(f32)
    mid_rows = x_rows + jnp.dot(attended, all_out, preferred_element_type=f32) + full_output_bias
    normed_two = layer_norm(mid_rows, gain_two, shift_two).astype(bf16)
    pre_act = jnp.dot(normed_two, all_up, preferred_element_type=f32) + full_up_bias
    hidden = gelu_act(pre_act).astype(bf16)
    block_rows = mid_rows + jnp.dot(hidden, all_down, preferred_element_type=f32) + full_down_bias
    block_out = block_rows.astype(bf16).reshape(activations.shape)

    cot_rows = cotangent[0]
    outer_grad = cot_rows.astype(f32)
    down_wgrad = jnp.einsum("rf,rd->fd", hidden, cot_rows, preferred_element_type=f32).astype(bf16)
    down_bgrad = jnp.sum(outer_grad, axis=0)
    hidden_grad = jnp.einsum("rd,fd->rf", cot_rows, all_down, preferred_element_type=f32)
    _, gelu_back = jax.vjp(gelu_act, pre_act)
    pre_grad = gelu_back(hidden_grad)[0].astype(bf16)
    up_wgrad = jnp.einsum("rd,rf->df", normed_two, pre_grad, preferred_element_type=f32).astype(bf16)
    up_bgrad = jnp.sum(pre_grad.astype(f32), axis=0)
    normed_two_grad = jnp.einsum("rf,df->rd", pre_grad, all_up, preferred_element_type=f32)
    _, norm_two_back = jax.vjp(layer_norm, mid_rows, gain_two, shift_two)
    mid_part, gain_two_grad, shift_two_grad = norm_two_back(normed_two_grad)
    mid_grad = outer_grad + mid_part
    branch_grad = mid_grad.astype(bf16)
    output_wgrad = jnp.einsum("rd,re->de", attended, branch_grad, preferred_element_type=f32).astype(bf16)
    output_bgrad = jnp.sum(branch_grad.astype(f32), axis=0)
    attended_grad = jnp.einsum("re,de->rd", branch_grad, all_out, preferred_element_type=f32).astype(bf16)
    grad_mine = jnp.concatenate([mine(attended_grad), swap(others(attended_grad))], axis=0)
    grad_heads = grad_mine.reshape(2 * rows, heads, HDIM)
    delta = jnp.einsum("qhd,hqd->hq", grad_heads.astype(f32), exact)[..., None]
    scores = jnp.einsum("qhd,khd->hqk", queries, keys, preferred_element_type=f32) * scaling
    probs = jnp.exp(scores - log_total)
    prob_grad = jnp.einsum("qhd,khd->hqk", grad_heads, values, preferred_element_type=f32)
    score_grad = (probs * (prob_grad - delta)).astype(bf16)
    probs_low = probs.astype(bf16)
    query_grad = jnp.einsum("hqk,khd->qhd", score_grad, keys, preferred_element_type=f32) * scaling
    key_grad = jnp.einsum("hqk,qhd->khd", score_grad, queries, preferred_element_type=f32) * scaling
    value_grad = jnp.einsum("hqk,qhd->khd", probs_low, grad_heads, preferred_element_type=f32)
    qkv_grad = jnp.concatenate(
        [v.astype(bf16).reshape(2 * rows, half) for v in (query_grad, key_grad, value_grad)], axis=1
    )
    qkv_wgrad = jnp.einsum("rd,re->de", normed_one, qkv_grad, preferred_element_type=f32).astype(bf16)
    qkv_bgrad = jnp.sum(qkv_grad.astype(f32), axis=0)
    nothing = jnp.zeros((half,), f32)
    query_bgrad = both(qkv_bgrad[:half], nothing)
    value_bgrad = both(qkv_bgrad[2 * half :], nothing)
    normed_grad = jnp.einsum("re,de->rd", qkv_grad, all_qkv, preferred_element_type=f32)
    normed_one_grad = normed_grad[:rows] + swap(normed_grad[rows:].astype(bf16)).astype(f32)
    _, norm_one_back = jax.vjp(layer_norm, x_rows, gain_one, shift_one)
    input_part, gain_one_grad, shift_one_grad = norm_one_back(normed_one_grad)
    input_grad = (mid_grad + input_part).reshape(activations.shape)
    small_grads = pack_small_grads(
        (gain_one_grad, shift_one_grad, query_bgrad, value_bgrad, output_bgrad, gain_two_grad, shift_two_grad, down_bgrad),
        up_bgrad,
    )
    own_small, own_qkv_grad, own_output, own_up, own_down = scatter_all(
        (small_grads, qkv_wgrad, output_wgrad, up_wgrad, down_wgrad), scatter_chunks(), 1
    )
    return (
        block_out,
        input_grad,
        own_qkv_grad[:, :width],
        own_qkv_grad[:, width : 2 * width],
        own_qkv_grad[:, 2 * width :],
        own_output,
        own_small[0, :64],
        own_small[1, :64],
        own_small[2, :64],
        own_small[3, :64],
        own_small[4, :64],
        own_up,
        own_down,
        own_small[5, :64],
        own_small[6, :64],
        own_small[8:10].reshape(-1),
        own_small[7, :64],
    )


def solution(mesh):
    fits = mesh.shape["fsdp"] == 4 * DEPTH and mesh.shape["ctx"] == BOTH
    return jax.shard_map(
        fast_device if fits else plain_device,
        mesh=mesh,
        in_specs=(
            P("fsdp", "ctx", None),
            P("fsdp", "ctx", None),
            P("fsdp", None),
            P("fsdp", None),
            P("fsdp", None),
            P("fsdp", None),
            P("fsdp"),
            P("fsdp"),
            P("fsdp"),
            P("fsdp"),
            P("fsdp"),
            P("fsdp", None),
            P("fsdp", None),
            P("fsdp"),
            P("fsdp"),
            P("fsdp"),
            P("fsdp"),
        ),
        out_specs=(
            P("fsdp", "ctx", None),
            P("fsdp", "ctx", None),
            P("fsdp", None),
            P("fsdp", None),
            P("fsdp", None),
            P("fsdp", None),
            P("fsdp"),
            P("fsdp"),
            P("fsdp"),
            P("fsdp"),
            P("fsdp"),
            P("fsdp", None),
            P("fsdp", None),
            P("fsdp"),
            P("fsdp"),
            P("fsdp"),
            P("fsdp"),
        ),
        check_vma=False,
    )
```

```python
import functools

import jax
import jax.numpy as jnp
from jax import lax
from jax.experimental import pallas as pl
from jax.experimental.pallas import tpu as pltpu
from jax.sharding import PartitionSpec as P

HEADS = 16
HDIM = 64
MESH = pl.DeviceIdType.MESH


epsilon = 1e-05


def layer_norm(token_rows, gain, shift):
    centered = token_rows - jnp.mean(token_rows, axis=-1, keepdims=True)
    variance = jnp.mean(centered * centered, axis=-1, keepdims=True)
    return centered * lax.rsqrt(variance + epsilon) * gain + shift


def gelu_act(values_in):
    return jax.nn.gelu(values_in, approximate=True)


def gather_attention(shards):
    return (
        lax.all_gather(shards[0], "fsdp", axis=0, tiled=True),
        lax.all_gather(shards[1], "fsdp", axis=0, tiled=True),
        lax.all_gather(shards[2], "fsdp", axis=0, tiled=True),
        lax.all_gather(shards[3], "fsdp", axis=0, tiled=True),
        lax.all_gather(shards[4], "fsdp", axis=0, tiled=True),
        lax.all_gather(shards[5], "fsdp", axis=0, tiled=True),
        lax.all_gather(shards[6], "fsdp", axis=0, tiled=True),
        lax.all_gather(shards[7], "fsdp", axis=0, tiled=True),
        lax.all_gather(shards[8], "fsdp", axis=0, tiled=True),
    )


def gather_feed(shards):
    return (
        lax.all_gather(shards[0], "fsdp", axis=0, tiled=True),
        lax.all_gather(shards[1], "fsdp", axis=0, tiled=True),
        lax.all_gather(shards[2], "fsdp", axis=0, tiled=True),
        lax.all_gather(shards[3], "fsdp", axis=0, tiled=True),
        lax.all_gather(shards[4], "fsdp", axis=0, tiled=True),
        lax.all_gather(shards[5], "fsdp", axis=0, tiled=True),
    )


def plain_device(
    activations,
    cotangent,
    query_weight,
    key_weight,
    value_weight,
    output_weight,
    first_gain,
    first_shift,
    query_bias,
    value_bias,
    output_bias,
    up_weight,
    down_weight,
    second_gain,
    second_shift,
    up_bias,
    down_bias,
):
    clip_count, local_len, width = activations.shape
    scaling = HDIM ** (-0.5)
    attend_shards = (
        query_weight,
        key_weight,
        value_weight,
        output_weight,
        first_gain,
        first_shift,
        query_bias,
        value_bias,
        output_bias,
    )
    feed_shards = (up_weight, down_weight, second_gain, second_shift, up_bias, down_bias)
    attend_full = gather_attention(attend_shards)
    (
        full_query,
        full_key,
        full_value,
        full_output,
        full_gain_one,
        full_shift_one,
        full_query_bias,
        full_value_bias,
        full_output_bias,
    ) = attend_full
    gain_one = full_gain_one.astype(jnp.float32)
    shift_one = full_shift_one.astype(jnp.float32)
    token_rows = activations.reshape(-1, width).astype(jnp.float32)
    normed_one = layer_norm(token_rows, gain_one, shift_one).astype(jnp.bfloat16)
    queries = (
        jnp.dot(normed_one, full_query, preferred_element_type=jnp.float32)
        + full_query_bias.astype(jnp.float32)
    ).astype(jnp.bfloat16)
    keys_local = jnp.dot(normed_one, full_key, preferred_element_type=jnp.float32).astype(
        jnp.bfloat16
    )
    values_local = (
        jnp.dot(normed_one, full_value, preferred_element_type=jnp.float32)
        + full_value_bias.astype(jnp.float32)
    ).astype(jnp.bfloat16)
    query_heads = queries.reshape(clip_count, local_len, HEADS, HDIM)
    keys_block = keys_local.reshape(clip_count, local_len, width)
    values_block = values_local.reshape(clip_count, local_len, width)
    run_max = jnp.full((clip_count, local_len, HEADS), -1e30, jnp.float32)
    key_piece = lax.all_gather(keys_block, "ctx", axis=1, tiled=True)
    value_piece = lax.all_gather(values_block, "ctx", axis=1, tiled=True)
    key_heads = key_piece.reshape(clip_count, -1, HEADS, HDIM)
    value_heads = value_piece.reshape(clip_count, -1, HEADS, HDIM)
    scores = (
        jnp.einsum("cqhd,ckhd->cqhk", query_heads, key_heads, preferred_element_type=jnp.float32)
        * scaling
    )
    new_max = jnp.maximum(run_max, jnp.max(scores, axis=-1))
    weights = jnp.exp(scores - new_max[..., None])
    run_sum = jnp.sum(weights, axis=-1)
    accum = jnp.einsum(
        "cqhk,ckhd->cqhd",
        weights.astype(jnp.bfloat16),
        value_heads,
        preferred_element_type=jnp.float32,
    )
    run_max, run_sum, accum = (new_max, run_sum, accum)
    attend_exact = accum / run_sum[..., None]
    log_total = run_max + jnp.log(run_sum)
    attended = attend_exact.reshape(-1, width).astype(jnp.bfloat16)
    mid_rows = (
        token_rows
        + jnp.dot(attended, full_output, preferred_element_type=jnp.float32)
        + full_output_bias.astype(jnp.float32)
    )
    feed_full = gather_feed(feed_shards)
    full_up, full_down, full_gain_two, full_shift_two, full_up_bias, full_down_bias = feed_full
    gain_two = full_gain_two.astype(jnp.float32)
    shift_two = full_shift_two.astype(jnp.float32)
    normed_two = layer_norm(mid_rows, gain_two, shift_two).astype(jnp.bfloat16)
    pre_act = jnp.dot(
        normed_two, full_up, preferred_element_type=jnp.float32
    ) + full_up_bias.astype(jnp.float32)
    hidden = gelu_act(pre_act).astype(jnp.bfloat16)
    block_rows = (
        mid_rows
        + jnp.dot(hidden, full_down, preferred_element_type=jnp.float32)
        + full_down_bias.astype(jnp.float32)
    )
    block_out = block_rows.astype(jnp.bfloat16).reshape(activations.shape)
    back_attend = gather_attention(attend_shards)
    back_feed = gather_feed(feed_shards)
    back_query, back_key, back_value, back_output = (
        back_attend[0],
        back_attend[1],
        back_attend[2],
        back_attend[3],
    )
    back_up, back_down = (back_feed[0], back_feed[1])
    cot_rows = cotangent.reshape(-1, width)
    outer_grad = cot_rows.astype(jnp.float32)
    down_wgrad = jnp.einsum("rf,rd->fd", hidden, cot_rows, preferred_element_type=jnp.float32)
    down_bgrad = jnp.sum(outer_grad, axis=0)
    hidden_grad = jnp.einsum("rd,fd->rf", cot_rows, back_down, preferred_element_type=jnp.float32)
    _, gelu_back = jax.vjp(gelu_act, pre_act)
    pre_grad = gelu_back(hidden_grad)[0].astype(jnp.bfloat16)
    up_wgrad = jnp.einsum("rd,rf->df", normed_two, pre_grad, preferred_element_type=jnp.float32)
    up_bgrad = jnp.sum(pre_grad.astype(jnp.float32), axis=0)
    normed_two_grad = jnp.einsum("rf,df->rd", pre_grad, back_up, preferred_element_type=jnp.float32)
    _, norm_two_back = jax.vjp(layer_norm, mid_rows, gain_two, shift_two)
    mid_part, gain_two_grad, shift_two_grad = norm_two_back(normed_two_grad)
    mid_grad = outer_grad + mid_part
    feed_owned = (
        lax.psum_scatter(
            up_wgrad.astype(jnp.bfloat16), "fsdp", scatter_dimension=0, tiled=True
        ).astype(jnp.float32),
        lax.psum_scatter(
            down_wgrad.astype(jnp.bfloat16), "fsdp", scatter_dimension=0, tiled=True
        ).astype(jnp.float32),
        lax.psum_scatter(
            gain_two_grad.astype(jnp.bfloat16), "fsdp", scatter_dimension=0, tiled=True
        ).astype(jnp.float32),
        lax.psum_scatter(
            shift_two_grad.astype(jnp.bfloat16), "fsdp", scatter_dimension=0, tiled=True
        ).astype(jnp.float32),
        lax.psum_scatter(
            up_bgrad.astype(jnp.bfloat16), "fsdp", scatter_dimension=0, tiled=True
        ).astype(jnp.float32),
        lax.psum_scatter(
            down_bgrad.astype(jnp.bfloat16), "fsdp", scatter_dimension=0, tiled=True
        ).astype(jnp.float32),
    )
    feed_done = (
        lax.psum(feed_owned[0].astype(jnp.bfloat16), "ctx").astype(jnp.float32),
        lax.psum(feed_owned[1].astype(jnp.bfloat16), "ctx").astype(jnp.float32),
        lax.psum(feed_owned[2].astype(jnp.bfloat16), "ctx").astype(jnp.float32),
        lax.psum(feed_owned[3].astype(jnp.bfloat16), "ctx").astype(jnp.float32),
        lax.psum(feed_owned[4].astype(jnp.bfloat16), "ctx").astype(jnp.float32),
        lax.psum(feed_owned[5].astype(jnp.bfloat16), "ctx").astype(jnp.float32),
    )
    branch_grad = mid_grad.astype(jnp.bfloat16)
    output_wgrad = jnp.einsum(
        "rd,re->de", attended, branch_grad, preferred_element_type=jnp.float32
    )
    output_bgrad = jnp.sum(branch_grad.astype(jnp.float32), axis=0)
    attended_grad = jnp.einsum(
        "re,de->rd", branch_grad, back_output, preferred_element_type=jnp.float32
    ).astype(jnp.bfloat16)
    grad_heads = attended_grad.reshape(clip_count, local_len, HEADS, HDIM)
    delta = jnp.sum(grad_heads.astype(jnp.float32) * attend_exact, axis=-1)
    keys_whole, values_whole = (
        lax.all_gather(keys_block, "ctx", axis=1, tiled=True),
        lax.all_gather(values_block, "ctx", axis=1, tiled=True),
    )
    key_heads_all = keys_whole.reshape(clip_count, -1, HEADS, HDIM)
    value_heads_all = values_whole.reshape(clip_count, -1, HEADS, HDIM)
    scores_all = (
        jnp.einsum(
            "cqhd,ckhd->cqhk", query_heads, key_heads_all, preferred_element_type=jnp.float32
        )
        * scaling
    )
    probs = jnp.exp(scores_all - log_total[..., None])
    prob_grad = jnp.einsum(
        "cqhd,ckhd->cqhk", grad_heads, value_heads_all, preferred_element_type=jnp.float32
    )
    score_grad = (probs * (prob_grad - delta[..., None])).astype(jnp.bfloat16)
    query_grad = (
        jnp.einsum("cqhk,ckhd->cqhd", score_grad, key_heads_all, preferred_element_type=jnp.float32)
        * scaling
    ).astype(jnp.bfloat16)
    query_grad = query_grad.reshape(-1, width)
    probs_low = probs.astype(jnp.bfloat16)
    key_part = (
        jnp.einsum("cqhk,cqhd->kchd", score_grad, query_heads, preferred_element_type=jnp.float32)
        * scaling
    )
    value_part = jnp.einsum(
        "cqhk,cqhd->kchd", probs_low, grad_heads, preferred_element_type=jnp.float32
    )
    summed = lax.psum_scatter(
        jnp.stack([key_part, value_part], axis=2)
        .reshape(lax.axis_size("ctx") * local_len, clip_count, 2, width)
        .astype(jnp.bfloat16),
        "ctx",
        scatter_dimension=0,
        tiled=True,
    ).astype(jnp.float32)
    key_grad = jnp.transpose(summed[:, :, 0], (1, 0, 2)).reshape(-1, width).astype(jnp.bfloat16)
    value_grad = jnp.transpose(summed[:, :, 1], (1, 0, 2)).reshape(-1, width).astype(jnp.bfloat16)
    query_wgrad = jnp.einsum(
        "rd,re->de", normed_one, query_grad, preferred_element_type=jnp.float32
    )
    key_wgrad = jnp.einsum("rd,re->de", normed_one, key_grad, preferred_element_type=jnp.float32)
    value_wgrad = jnp.einsum(
        "rd,re->de", normed_one, value_grad, preferred_element_type=jnp.float32
    )
    query_bgrad = jnp.sum(query_grad.astype(jnp.float32), axis=0)
    value_bgrad = jnp.sum(value_grad.astype(jnp.float32), axis=0)
    normed_one_grad = (
        jnp.einsum("re,de->rd", query_grad, back_query, preferred_element_type=jnp.float32)
        + jnp.einsum("re,de->rd", key_grad, back_key, preferred_element_type=jnp.float32)
        + jnp.einsum("re,de->rd", value_grad, back_value, preferred_element_type=jnp.float32)
    )
    _, norm_one_back = jax.vjp(layer_norm, token_rows, gain_one, shift_one)
    input_part, gain_one_grad, shift_one_grad = norm_one_back(normed_one_grad)
    input_grad = (mid_grad + input_part).reshape(activations.shape)
    attend_owned = (
        lax.psum_scatter(
            query_wgrad.astype(jnp.bfloat16), "fsdp", scatter_dimension=0, tiled=True
        ).astype(jnp.float32),
        lax.psum_scatter(
            key_wgrad.astype(jnp.bfloat16), "fsdp", scatter_dimension=0, tiled=True
        ).astype(jnp.float32),
        lax.psum_scatter(
            value_wgrad.astype(jnp.bfloat16), "fsdp", scatter_dimension=0, tiled=True
        ).astype(jnp.float32),
        lax.psum_scatter(
            output_wgrad.astype(jnp.bfloat16), "fsdp", scatter_dimension=0, tiled=True
        ).astype(jnp.float32),
        lax.psum_scatter(
            gain_one_grad.astype(jnp.bfloat16), "fsdp", scatter_dimension=0, tiled=True
        ).astype(jnp.float32),
        lax.psum_scatter(
            shift_one_grad.astype(jnp.bfloat16), "fsdp", scatter_dimension=0, tiled=True
        ).astype(jnp.float32),
        lax.psum_scatter(
            query_bgrad.astype(jnp.bfloat16), "fsdp", scatter_dimension=0, tiled=True
        ).astype(jnp.float32),
        lax.psum_scatter(
            value_bgrad.astype(jnp.bfloat16), "fsdp", scatter_dimension=0, tiled=True
        ).astype(jnp.float32),
        lax.psum_scatter(
            output_bgrad.astype(jnp.bfloat16), "fsdp", scatter_dimension=0, tiled=True
        ).astype(jnp.float32),
    )
    attend_done = (
        lax.psum(attend_owned[0].astype(jnp.bfloat16), "ctx").astype(jnp.float32),
        lax.psum(attend_owned[1].astype(jnp.bfloat16), "ctx").astype(jnp.float32),
        lax.psum(attend_owned[2].astype(jnp.bfloat16), "ctx").astype(jnp.float32),
        lax.psum(attend_owned[3].astype(jnp.bfloat16), "ctx").astype(jnp.float32),
        lax.psum(attend_owned[4].astype(jnp.bfloat16), "ctx").astype(jnp.float32),
        lax.psum(attend_owned[5].astype(jnp.bfloat16), "ctx").astype(jnp.float32),
        lax.psum(attend_owned[6].astype(jnp.bfloat16), "ctx").astype(jnp.float32),
        lax.psum(attend_owned[7].astype(jnp.bfloat16), "ctx").astype(jnp.float32),
        lax.psum(attend_owned[8].astype(jnp.bfloat16), "ctx").astype(jnp.float32),
    )
    return (
        block_out,
        input_grad,
        attend_done[0],
        attend_done[1],
        attend_done[2],
        attend_done[3],
        attend_done[4],
        attend_done[5],
        attend_done[6],
        attend_done[7],
        attend_done[8],
        feed_done[0],
        feed_done[1],
        feed_done[2],
        feed_done[3],
        feed_done[4],
        feed_done[5],
    )


def place():
    f = lax.axis_index("fsdp"); y = lax.axis_index("ctx")
    return f // 4, (f // 2) % 2, f % 2, y

def greet(z, x, c, y, depth):
    barrier = pltpu.get_barrier_semaphore()
    def one(dz, dx, dc, dy):
        pl.semaphore_signal(barrier, inc=1, device_id=(dz * 4 + dx * 2 + dc, dy), device_id_type=MESH)
    for k in range(1, depth):
        one((z + k) % depth, x, c, y)
    one(z, 1 - x, c, y); one(z, x, 1 - c, y); one(z, x, c, 1 - y)
    pl.semaphore_wait(barrier, depth + 2)

class Gather:
    def __init__(self, depth, chunks, ins, outs, sems, where):
        self.depth, self.chunks, self.ins, self.outs = depth, chunks, ins, outs
        self.zs, self.zr, self.xs, self.xr, self.ys, self.yr, self.cs, self.cr, self.loc = sems
        self.where = where
    def src(self, ch, half):
        t, r0, h, both = self.chunks[ch]
        if not both: return self.ins[t].at[pl.ds(r0, h)]
        h2 = h // 2
        return self.ins[t].at[pl.ds(pl.multiple_of(r0 + half * h2, 16), h2)]
    def dst(self, ch, dz, dx, dc, half):
        t, r0, h, both = self.chunks[ch]
        full = self.ins[t].shape[0]
        start = (dz * 4 + dx * 2 + dc) * full + r0
        if not both: return self.outs[t].at[pl.ds(pl.multiple_of(start, 16), h)]
        h2 = h // 2
        return self.outs[t].at[pl.ds(pl.multiple_of(start + half * h2, 16), h2)]
    def copy(self, src, dst, s, r, dz, dx, dc, dy):
        return pltpu.make_async_remote_copy(src_ref=src, dst_ref=dst, send_sem=s, recv_sem=r,
            device_id=(dz * 4 + dx * 2 + dc, dy), device_id_type=MESH)
    def zz(self, j):
        return (self.where[0] - j + self.depth) % self.depth
    def zmove(self, ch, k, recv=False):
        z, x, c, y = self.where
        if recv:
            d = self.dst(ch, self.zz(k), x, c, y)
            return self.copy(d, d, self.zs.at[ch, k], self.zr.at[ch, k], z, x, 1 - c, y)
        return self.copy(self.src(ch, y), self.dst(ch, z, x, c, y), self.zs.at[ch, k], self.zr.at[ch, k], (z + k) % self.depth, x, c, y)
    def xmove(self, ch, j, recv=False):
        z, x, c, y = self.where
        d = self.dst(ch, self.zz(j), 1 - x if recv else x, c, y)
        s = self.src(ch, y) if (j == 0 and not recv) else d
        return self.copy(s, d, self.xs.at[ch, j], self.xr.at[ch, j], z, 1 - x, c, y)
    def ymove(self, ch, i, j, recv=False):
        z, x, c, y = self.where
        d = self.dst(ch, self.zz(j), x if i == 0 else 1 - x, c, 1 - y if recv else y)
        n = i * self.depth + j
        return self.copy(d, d, self.ys.at[ch, n], self.yr.at[ch, n], z, x, c, 1 - y)
    def cmove(self, ch, i, j, other, recv=False):
        z, x, c, y = self.where
        half = 1 - y if other else y
        d = self.dst(ch, self.zz(j), x if i == 0 else 1 - x, 1 - c if recv else c, half)
        s = self.src(ch, half) if (i == 0 and j == 0 and not recv) else d
        n = (i * self.depth + j) + (2 * self.depth if other else 0)
        return self.copy(s, d, self.cs.at[ch, n], self.cr.at[ch, n], z, x, 1 - c, y)
    def own(self, ch):
        z, x, c, y = self.where
        t, r0, h, both = self.chunks[ch]
        full = self.ins[t].shape[0]
        return pltpu.make_async_copy(self.ins[t].at[pl.ds(r0, h)],
            self.outs[t].at[pl.ds(pl.multiple_of((z * 4 + x * 2 + c) * full + r0, 16), h)], self.loc.at[ch])
    def begin(self, ch):
        for k in range(1, self.depth): self.zmove(ch, k).start()
        self.xmove(ch, 0).start()
        self.cmove(ch, 0, 0, False).start()
        if self.chunks[ch][3]: self.cmove(ch, 0, 0, True).start()
        self.own(ch).start()
    def zstage(self, ch):
        for k in range(1, self.depth):
            self.zmove(ch, k, True).wait_recv()
            self.xmove(ch, k).start()
            if self.chunks[ch][3]: self.ymove(ch, 0, k).start()
            self.cmove(ch, 0, k, False).start()
    def xstage(self, ch):
        for j in range(self.depth):
            self.xmove(ch, j, True).wait_recv()
            if self.chunks[ch][3]: self.ymove(ch, 1, j).start()
            self.cmove(ch, 1, j, False).start()
    def ystage(self, ch):
        if not self.chunks[ch][3]: return
        for i in range(2):
            for j in range(1 - i, self.depth):
                self.ymove(ch, i, j, True).wait_recv()
                self.cmove(ch, i, j, True).start()
    def arrived(self, ch):
        for i in range(2):
            for j in range(self.depth):
                self.cmove(ch, i, j, False, True).wait_recv()
                if self.chunks[ch][3]: self.cmove(ch, i, j, True, True).wait_recv()
        self.own(ch).wait()
    def sent(self, ch):
        both = self.chunks[ch][3]
        for k in range(1, self.depth): self.zmove(ch, k).wait_send()
        for j in range(self.depth): self.xmove(ch, j).wait_send()
        for i in range(2):
            for j in range(self.depth):
                self.cmove(ch, i, j, False).wait_send()
                if both:
                    self.cmove(ch, i, j, True).wait_send()
                    if i or j: self.ymove(ch, i, j).wait_send()

def gather_sems(depth, n):
    S = pltpu.SemaphoreType.DMA
    return [S((n, depth)), S((n, depth)), S((n, depth)), S((n, depth)), S((n, 2 * depth)), S((n, 2 * depth)), S((n, 4 * depth)), S((n, 4 * depth)), S((n,))]

def ag_kernel(depth, n, chunks, ahead, lag, *refs):
    ins = refs[:n]; x_in = refs[n]
    outs = refs[n + 1:2 * n + 1]; x_out = refs[2 * n + 1]
    sems = refs[2 * n + 2:2 * n + 11]; ys, yr = refs[2 * n + 11:]
    z, x, c, y = place()
    g = Gather(depth, chunks, ins, outs, sems, (z, x, c, y))
    greet(z, x, c, y, depth)
    xw = g.copy(x_in, x_out, ys, yr, z, x, c, 1 - y)
    xw.start()
    N = len(chunks)
    for ch in range(min(ahead, N)): g.begin(ch)
    for s in range(N + 2 * lag):
        if s < N:
            g.zstage(s)
            if s + ahead < N: g.begin(s + ahead)
        if 0 <= s - lag < N: g.xstage(s - lag)
        if 0 <= s - 2 * lag < N: g.ystage(s - 2 * lag)
    xw.wait()
    for ch in range(N): g.arrived(ch)
    for ch in range(N): g.sent(ch)


def gather_all(shards, x, chunks, depth=4, ahead=2, lag=1, cid=1):
    n = len(shards)
    S = pltpu.SemaphoreType.DMA
    return pl.pallas_call(
        functools.partial(ag_kernel, depth, n, chunks, ahead, lag),
        out_shape=[jax.ShapeDtypeStruct((depth * 4 * s.shape[0],) + s.shape[1:], s.dtype) for s in shards] + [jax.ShapeDtypeStruct(x.shape, x.dtype)],
        in_specs=[pl.BlockSpec(memory_space=pl.ANY)] * (n + 1),
        out_specs=[pl.BlockSpec(memory_space=pl.ANY)] * (n + 1),
        scratch_shapes=gather_sems(depth, len(chunks)) + [S, S],
        compiler_params=pltpu.CompilerParams(collective_id=cid, has_side_effects=True),
        name="weights_gather")(*shards, x)


def rowwise(h, w, body):
    wide = min(w, 1024 if w % 1024 == 0 else 512)
    steps_w = w // wide
    total = (h // 16) * steps_w
    if total == 1:
        body(pl.ds(0, 16), pl.ds(0, wide)); return
    def one(i, _):
        body(pl.ds(pl.multiple_of((i // steps_w) * 16, 16), 16), pl.ds(pl.multiple_of((i % steps_w) * wide, 128), wide))
        return 0
    lax.fori_loop(0, total, one, 0)

class Scatter:
    def __init__(self, depth, chunks, grads, outs, bufs, sems, where):
        self.depth, self.chunks, self.grads, self.outs, self.bufs = depth, chunks, grads, outs, bufs
        self.ls, self.cs, self.cr, self.xs, self.xr, self.zs, self.zr, self.ys, self.yr = sems
        self.where = where
    def piece(self, ch, dz, dx, dc):
        t, k, r0, h = self.chunks[ch]
        full = self.grads[t].shape[0] // (4 * self.depth)
        return self.grads[t].at[pl.ds(pl.multiple_of((dz * 4 + dx * 2 + dc) * full + r0, 16), h)]
    def copy(self, src, dst, s, r, dz, dx, dc, dy):
        return pltpu.make_async_remote_copy(src_ref=src, dst_ref=dst, send_sem=s, recv_sem=r,
            device_id=(dz * 4 + dx * 2 + dc, dy), device_id_type=MESH)
    def zz(self, j): return (self.where[0] + j) % self.depth
    def load(self, ch, i, j):
        z, x, c, y = self.where; t, k = self.chunks[ch][:2]
        return pltpu.make_async_copy(self.piece(ch, self.zz(j), x if i == 0 else 1 - x, c), self.bufs[t][0].at[k, i, j], self.ls.at[ch, i * self.depth + j])
    def cmove(self, ch, i, j):
        z, x, c, y = self.where; t, k = self.chunks[ch][:2]; n = i * self.depth + j
        return self.copy(self.piece(ch, self.zz(j), x if i == 0 else 1 - x, 1 - c), self.bufs[t][1].at[k, i, j], self.cs.at[ch, n], self.cr.at[ch, n], z, x, 1 - c, y)
    def xmove(self, ch, j):
        z, x, c, y = self.where; t, k = self.chunks[ch][:2]
        return self.copy(self.bufs[t][0].at[k, 1, j], self.bufs[t][2].at[k, j], self.xs.at[ch, j], self.xr.at[ch, j], z, 1 - x, c, y)
    def zmove(self, ch, j):
        z, x, c, y = self.where; t, k = self.chunks[ch][:2]
        return self.copy(self.bufs[t][0].at[k, 0, j], self.bufs[t][3].at[k, j - 1], self.zs.at[ch, j], self.zr.at[ch, j], self.zz(j), x, c, y)
    def ymove(self, ch):
        z, x, c, y = self.where; t, k = self.chunks[ch][:2]
        return self.copy(self.bufs[t][4].at[k], self.bufs[t][5].at[k], self.ys.at[ch], self.yr.at[ch], z, x, c, 1 - y)
    def begin(self, ch):
        for i in (1, 0):
            for j in range(self.depth):
                self.load(ch, i, j).start()
                self.cmove(ch, i, j).start()
    def cstage(self, ch):
        t, k, r0, h = self.chunks[ch]; L, C = self.bufs[t][:2]; w = L.shape[-1]
        for i in (1, 0):
            for j in range(self.depth):
                self.load(ch, i, j).wait(); self.cmove(ch, i, j).wait_recv()
                def add(r, q):
                    L[k, i, j, r, q] = L[k, i, j, r, q] + C[k, i, j, r, q]
                rowwise(h, w, add)
                if i == 1: self.xmove(ch, j).start()
    def xstage(self, ch):
        t, k, r0, h = self.chunks[ch]; L, C, X = self.bufs[t][:3]; w = L.shape[-1]
        for j in list(range(1, self.depth)) + [0]:
            self.xmove(ch, j).wait_recv()
            def add(r, q):
                L[k, 0, j, r, q] = L[k, 0, j, r, q] + X[k, j, r, q]
            rowwise(h, w, add)
            if j: self.zmove(ch, j).start()
    def zstage(self, ch):
        t, k, r0, h = self.chunks[ch]; L, C, X, Z, F, Y = self.bufs[t]; w = L.shape[-1]
        for j in range(1, self.depth): self.zmove(ch, j).wait_recv()
        def add(r, q):
            tot = L[k, 0, 0, r, q].astype(jnp.float32)
            for j in range(1, self.depth): tot = tot + Z[k, j - 1, r, q].astype(jnp.float32)
            F[k, r, q] = tot.astype(jnp.bfloat16)
        rowwise(h, w, add)
        self.ymove(ch).start()
    def ystage(self, ch):
        t, k, r0, h = self.chunks[ch]; L, C, X, Z, F, Y = self.bufs[t]; w = L.shape[-1]
        z, x, c, y = self.where
        self.ymove(ch).wait_recv()
        out = self.outs[t]
        if out.shape[-1] == w:
            def add(r, q):
                out[pl.ds(pl.multiple_of(r0 + r.start, 16), 16), q] = F[k, r, q].astype(jnp.float32) + Y[k, r, q].astype(jnp.float32)
            rowwise(h, w, add)
        else:
            part = w // 3
            for n in range(3):
                def lay(r, q, n=n):
                    mine = F[k, r, n * part:(n + 1) * part].astype(jnp.float32)
                    other = Y[k, r, n * part:(n + 1) * part].astype(jnp.float32)
                    rr = pl.ds(pl.multiple_of(r0 + r.start, 16), 16)
                    out[rr, 2 * n * part:(2 * n + 1) * part] = jnp.where(y == 0, mine, other)
                    out[rr, (2 * n + 1) * part:(2 * n + 2) * part] = jnp.where(y == 0, other, mine)
                rowwise(h, 128, lay)
    def sent(self, ch):
        for i in range(2):
            for j in range(self.depth): self.cmove(ch, i, j).wait_send()
        for j in range(self.depth):
            self.xmove(ch, j).wait_send()
            if j: self.zmove(ch, j).wait_send()
        self.ymove(ch).wait_send()

def scatter_scratch(depth, chunks, widths):
    S = pltpu.SemaphoreType.DMA; n = len(chunks); out = []
    for t, w in enumerate(widths):
        mine = [c for c in chunks if c[0] == t]; m = len(mine); h = mine[0][3]
        B = lambda *lead: pltpu.VMEM(lead + (h, w), jnp.bfloat16)
        out += [B(m, 2, depth), B(m, 2, depth), B(m, depth), B(m, depth - 1), B(m), B(m)]
    return out + [S((n, 2 * depth)), S((n, 2 * depth)), S((n, 2 * depth)), S((n, depth)), S((n, depth)), S((n, depth)), S((n, depth)), S((n,)), S((n,))]

def rs_kernel(depth, n, chunks, lag, *refs):
    grads, outs = refs[:n], refs[n:2 * n]
    bufs = [refs[2 * n + 6 * t:2 * n + 6 * t + 6] for t in range(n)]
    sems = refs[8 * n:8 * n + 9]
    where = place()
    s = Scatter(depth, chunks, grads, outs, bufs, sems, where)
    greet(*where, depth)
    N = len(chunks)
    for ch in range(N): s.begin(ch)
    for st in range(N + 3 * lag):
        if st < N: s.cstage(st)
        if 0 <= st - lag < N: s.xstage(st - lag)
        if 0 <= st - 2 * lag < N: s.zstage(st - 2 * lag)
        if 0 <= st - 3 * lag < N: s.ystage(st - 3 * lag)
    for ch in range(N): s.sent(ch)

def scatter_all(grads, chunks, wide, depth=4, lag=1, cid=2):
    n = len(grads)
    return pl.pallas_call(
        functools.partial(rs_kernel, depth, n, chunks, lag),
        out_shape=[jax.ShapeDtypeStruct((g.shape[0] // (4 * depth), g.shape[1] * (2 if t == wide else 1)), jnp.float32) for t, g in enumerate(grads)],
        in_specs=[pl.BlockSpec(memory_space=pl.ANY)] * n,
        out_specs=[pl.BlockSpec(memory_space=pltpu.VMEM)] * n,
        scratch_shapes=scatter_scratch(depth, chunks, [g.shape[1] for g in grads]),
        compiler_params=pltpu.CompilerParams(collective_id=cid, has_side_effects=True, vmem_limit_bytes=60 * 2 ** 20),
        name="gradients_scatter")(*grads)


NT = (((1,), (1,)), ((), ()))
NN = (((1,), (0,)), ((), ()))


def attend_kernel(block_rows, qkv, attended, inverse, weights_out, values_ones, kept, sem):
    length = qkv.shape[0]
    half = qkv.shape[1] // 3
    blocks, pairs = length // block_rows, half // 128
    low_lanes = lax.broadcasted_iota(jnp.int32, (block_rows, 128), 1) < HDIM

    def out(pair, block, head, slot):
        rows = pl.ds(pl.multiple_of(block * block_rows, 16), block_rows)
        return pltpu.make_async_copy(kept.at[slot, head], weights_out.at[2 * pair + head, rows], sem.at[slot, head])

    values_ones[:, 128:] = jnp.ones((length, 128), jnp.bfloat16)

    def one_pair(pair, _):
        at = pl.multiple_of(pair * 128, 128)
        values_ones[:, :128] = qkv[:, pl.ds(2 * half + at, 128)]

        def one_block(block, _):
            turn = pair * blocks + block
            slot = turn % 2

            @pl.when(turn > 1)
            def _():
                for head in range(2):
                    out(0, 0, head, slot).wait()

            rows = pl.ds(pl.multiple_of(block * block_rows, 16), block_rows)
            queries = qkv[rows, pl.ds(at, 128)] * jnp.bfloat16(HDIM**-0.5)
            keys = qkv[:, pl.ds(half + at, 128)]
            values = values_ones[...]
            parts = []
            for head in range(2):
                masked = jnp.where(low_lanes == (head == 0), queries, jnp.zeros_like(queries))
                scores = lax.dot_general(masked, keys, NT, preferred_element_type=jnp.float32)
                top = jnp.max(scores, axis=1, keepdims=True)
                weights = jnp.exp(scores - top).astype(jnp.bfloat16)
                kept[slot, head] = weights
                summed = lax.dot_general(weights, values, NN, preferred_element_type=jnp.float32)
                parts.append((summed[:, :128], 1.0 / summed[:, 128:]))
            (low, low_inverse), (high, high_inverse) = parts
            scale = jnp.where(low_lanes, low_inverse, high_inverse)
            attended[rows, pl.ds(at, 128)] = (jnp.where(low_lanes, low, high) * scale).astype(jnp.bfloat16)
            inverse[rows, pl.ds(at, 128)] = scale
            for head in range(2):
                out(pair, block, head, slot).start()
            return 0

        lax.fori_loop(0, blocks, one_block, 0)
        return 0

    lax.fori_loop(0, pairs, one_pair, 0)
    for slot in range(2):
        for head in range(2):
            out(0, 0, head, slot).wait()


def attend(qkv, block_rows):
    length, wide = qkv.shape
    half = wide // 3
    whole = pl.BlockSpec(memory_space=pltpu.VMEM)
    return pl.pallas_call(
        functools.partial(attend_kernel, block_rows),
        out_shape=[
            jax.ShapeDtypeStruct((length, half), jnp.bfloat16),
            jax.ShapeDtypeStruct((length, half), jnp.float32),
            jax.ShapeDtypeStruct((half // HDIM, length, length), jnp.bfloat16),
        ],
        in_specs=[whole],
        out_specs=[whole, whole, pl.BlockSpec(memory_space=pl.ANY)],
        scratch_shapes=[
            pltpu.VMEM((length, 256), jnp.bfloat16),
            pltpu.VMEM((2, 2, block_rows, length), jnp.bfloat16),
            pltpu.SemaphoreType.DMA((2, 2)),
        ],
        compiler_params=pltpu.CompilerParams(vmem_limit_bytes=60 * 2**20),
        name="attend",
    )(qkv)


def attend_back_kernel(block_rows, qkv, attended, inverse, grads, weights_in, out, key_sum, value_sum, kept, sem):
    length = qkv.shape[0]
    half = qkv.shape[1] // 3
    blocks, pairs = length // block_rows, half // 128
    low_lanes = lax.broadcasted_iota(jnp.int32, (block_rows, 128), 1) < HDIM

    def load(turn, head, slot):
        rows = pl.ds(pl.multiple_of((turn % blocks) * block_rows, 16), block_rows)
        return pltpu.make_async_copy(weights_in.at[2 * (turn // blocks) + head, rows], kept.at[slot, head], sem.at[slot, head])

    for head in range(2):
        load(0, head, 0).start()

    def one_pair(pair, _):
        at = pl.multiple_of(pair * 128, 128)

        def one_block(block, _):
            turn = pair * blocks + block
            slot = turn % 2
            for head in range(2):
                load(turn, head, slot).wait()

            @pl.when(turn + 1 < blocks * pairs)
            def _():
                for head in range(2):
                    load(turn + 1, head, 1 - slot).start()

            rows = pl.ds(pl.multiple_of(block * block_rows, 16), block_rows)
            queries = qkv[rows, pl.ds(at, 128)] * jnp.bfloat16(HDIM**-0.5)
            keys = qkv[:, pl.ds(half + at, 128)]
            values = qkv[:, pl.ds(2 * half + at, 128)]
            scaled = grads[rows, pl.ds(at, 128)].astype(jnp.float32) * inverse[rows, pl.ds(at, 128)]
            product = scaled * attended[rows, pl.ds(at, 128)].astype(jnp.float32)
            low = scaled.astype(jnp.bfloat16)
            queries_t, low_t = queries.T, low.T
            query_parts, key_parts, value_parts = [], [], []
            for head in range(2):
                own = low_lanes == (head == 0)
                lanes = slice(HDIM * head, HDIM * head + HDIM)
                masked = jnp.where(own, low, jnp.zeros_like(low))
                prob_grad = lax.dot_general(masked, values, NT, preferred_element_type=jnp.float32)
                delta = jnp.sum(jnp.where(own, product, 0.0), axis=1, keepdims=True)
                weights = kept[slot, head]
                score_grad = (weights.astype(jnp.float32) * (prob_grad - delta)).astype(jnp.bfloat16)
                query_parts.append(lax.dot_general(score_grad, keys, NN, preferred_element_type=jnp.float32))
                key_parts.append(lax.dot_general(queries_t[lanes], score_grad, NN, preferred_element_type=jnp.float32))
                value_parts.append(lax.dot_general(low_t[lanes], weights, NN, preferred_element_type=jnp.float32))
            query_grad = jnp.where(low_lanes, query_parts[0], query_parts[1]) * HDIM**-0.5
            out[rows, pl.ds(at, 128)] = query_grad.astype(jnp.bfloat16)
            key_part = jnp.concatenate(key_parts, axis=0)
            value_part = jnp.concatenate(value_parts, axis=0)
            key_sum[...] = jnp.where(block == 0, key_part, key_sum[...] + key_part)
            value_sum[...] = jnp.where(block == 0, value_part, value_sum[...] + value_part)
            return 0

        lax.fori_loop(0, blocks, one_block, 0)
        out[:, pl.ds(half + at, 128)] = key_sum[...].T.astype(jnp.bfloat16)
        out[:, pl.ds(2 * half + at, 128)] = value_sum[...].T.astype(jnp.bfloat16)
        return 0

    lax.fori_loop(0, pairs, one_pair, 0)


def attend_back(qkv, attended, inverse, grads, weights, block_rows):
    length, wide = qkv.shape
    whole = pl.BlockSpec(memory_space=pltpu.VMEM)
    return pl.pallas_call(
        functools.partial(attend_back_kernel, block_rows),
        out_shape=jax.ShapeDtypeStruct((length, wide), jnp.bfloat16),
        in_specs=[whole] * 4 + [pl.BlockSpec(memory_space=pl.ANY)],
        out_specs=whole,
        scratch_shapes=[
            pltpu.VMEM((128, length), jnp.float32),
            pltpu.VMEM((128, length), jnp.float32),
            pltpu.VMEM((2, 2, block_rows, length), jnp.bfloat16),
            pltpu.SemaphoreType.DMA((2, 2)),
        ],
        compiler_params=pltpu.CompilerParams(vmem_limit_bytes=60 * 2**20),
        name="attend_back",
    )(qkv, attended, inverse, grads, weights)


DEPTH, BOTH = 4, 2


def pack_small(vectors, up_bias, c):
    rows = jnp.stack(vectors)
    zero = jnp.zeros_like(rows)
    rows = jnp.concatenate([jnp.where(c == 0, rows, zero), jnp.where(c == 0, zero, rows)], axis=1)
    return jnp.concatenate([rows, up_bias.reshape(2, 128), jnp.zeros((6, 128), rows.dtype)], axis=0)


def unpack_small(gathered):
    blocks = gathered.astype(jnp.float32).reshape(-1, 2, 16, 128)
    vectors = (blocks[:, 0, :8] + blocks[:, 1, :8]).transpose(1, 0, 2).reshape(8, -1)
    return vectors, blocks[:, :, 8:10].reshape(-1)


def pack_small_grads(vectors, up_grad):
    parts = 4 * DEPTH
    rows = jnp.stack(vectors).reshape(8, parts, 64).transpose(1, 0, 2)
    rows = jnp.concatenate([rows, jnp.zeros_like(rows)], axis=2)
    rows = jnp.concatenate([rows, up_grad.reshape(parts, 2, 128), jnp.zeros((parts, 6, 128), jnp.float32)], axis=1)
    return rows.astype(jnp.bfloat16).reshape(parts * 16, 128)


def swap(value):
    return lax.ppermute(value, "ctx", [(0, 1), (1, 0)])


def gather_chunks():
    return (
        (0, 0, 16, False),
        (1, 0, 64, False),
    ) + tuple((4, 64 * i, 64, True) for i in range(4)) + ((2, 0, 64, False),) + tuple(
        (3, 16 * i, 16, False) for i in range(4)
    )


def scatter_chunks():
    return ((0, 0, 0, 16),) + tuple((4, i, 64 * i, 64) for i in range(4)) + tuple(
        (3, i, 16 * i, 16) for i in range(4)
    ) + ((2, 0, 0, 64), (1, 0, 0, 64))


def fast_device(
    activations, cotangent, query_weight, key_weight, value_weight, output_weight, first_gain, first_shift,
    query_bias, value_bias, output_bias, up_weight, down_weight, second_gain, second_shift, up_bias, down_bias,
):
    _, rows, width = activations.shape
    half = width // 2
    y = lax.axis_index("ctx")
    c = lax.axis_index("fsdp") % 2
    f32, bf16 = jnp.float32, jnp.bfloat16

    def mine(value):
        return lax.dynamic_slice_in_dim(value, y * half, half, value.ndim - 1)

    def others(value):
        return lax.dynamic_slice_in_dim(value, (1 - y) * half, half, value.ndim - 1)

    def both(own, other):
        return jnp.where(y == 0, jnp.concatenate([own, other], -1), jnp.concatenate([other, own], -1))

    small = pack_small(
        (first_gain, first_shift, query_bias, value_bias, output_bias, second_gain, second_shift, down_bias), up_bias, c
    )
    own_qkv = jnp.concatenate([mine(query_weight), mine(key_weight), mine(value_weight)], axis=1)
    x_own = activations[0]
    all_small, all_qkv, all_out, all_up, all_down, x_other = gather_all(
        (small, own_qkv, output_weight, up_weight, down_weight), x_own, gather_chunks()
    )
    vectors, full_up_bias = unpack_small(all_small)
    gain_one, shift_one, full_query_bias, full_value_bias, full_output_bias, gain_two, shift_two, full_down_bias = vectors

    token_rows = jnp.concatenate([x_own, x_other], axis=0).astype(f32)
    normed_one = layer_norm(token_rows, gain_one, shift_one).astype(bf16)
    bias = jnp.concatenate([mine(full_query_bias), jnp.zeros((half,), f32), mine(full_value_bias)])
    qkv = (jnp.dot(normed_one, all_qkv, preferred_element_type=f32) + bias).astype(bf16)
    attended_mine, inverse, weights = attend(qkv, rows)
    attended = both(attended_mine[:rows], swap(attended_mine[rows:]))

    x_rows = x_own.astype(f32)
    mid_rows = x_rows + jnp.dot(attended, all_out, preferred_element_type=f32) + full_output_bias
    normed_two = layer_norm(mid_rows, gain_two, shift_two).astype(bf16)
    pre_act = jnp.dot(normed_two, all_up, preferred_element_type=f32) + full_up_bias
    hidden = gelu_act(pre_act).astype(bf16)
    block_rows = mid_rows + jnp.dot(hidden, all_down, preferred_element_type=f32) + full_down_bias
    block_out = block_rows.astype(bf16).reshape(activations.shape)

    cot_rows = cotangent[0]
    outer_grad = cot_rows.astype(f32)
    down_wgrad = jnp.einsum("rf,rd->fd", hidden, cot_rows, preferred_element_type=f32).astype(bf16)
    down_bgrad = jnp.sum(outer_grad, axis=0)
    hidden_grad = jnp.einsum("rd,fd->rf", cot_rows, all_down, preferred_element_type=f32)
    _, gelu_back = jax.vjp(gelu_act, pre_act)
    pre_grad = gelu_back(hidden_grad)[0].astype(bf16)
    up_wgrad = jnp.einsum("rd,rf->df", normed_two, pre_grad, preferred_element_type=f32).astype(bf16)
    up_bgrad = jnp.sum(pre_grad.astype(f32), axis=0)
    normed_two_grad = jnp.einsum("rf,df->rd", pre_grad, all_up, preferred_element_type=f32)
    _, norm_two_back = jax.vjp(layer_norm, mid_rows, gain_two, shift_two)
    mid_part, gain_two_grad, shift_two_grad = norm_two_back(normed_two_grad)
    mid_grad = outer_grad + mid_part
    branch_grad = mid_grad.astype(bf16)
    output_wgrad = jnp.einsum("rd,re->de", attended, branch_grad, preferred_element_type=f32).astype(bf16)
    output_bgrad = jnp.sum(branch_grad.astype(f32), axis=0)
    attended_grad = jnp.einsum("re,de->rd", branch_grad, all_out, preferred_element_type=f32).astype(bf16)
    grad_mine = jnp.concatenate([mine(attended_grad), swap(others(attended_grad))], axis=0)
    qkv_grad = attend_back(qkv, attended_mine, inverse, grad_mine, weights, 224)
    qkv_wgrad = jnp.einsum("rd,re->de", normed_one, qkv_grad, preferred_element_type=f32).astype(bf16)
    qkv_bgrad = jnp.sum(qkv_grad.astype(f32), axis=0)
    nothing = jnp.zeros((half,), f32)
    query_bgrad = both(qkv_bgrad[:half], nothing)
    value_bgrad = both(qkv_bgrad[2 * half :], nothing)
    normed_grad = jnp.einsum("re,de->rd", qkv_grad, all_qkv, preferred_element_type=f32)
    normed_one_grad = normed_grad[:rows] + swap(normed_grad[rows:].astype(bf16)).astype(f32)
    _, norm_one_back = jax.vjp(layer_norm, x_rows, gain_one, shift_one)
    input_part, gain_one_grad, shift_one_grad = norm_one_back(normed_one_grad)
    input_grad = (mid_grad + input_part).reshape(activations.shape)
    small_grads = pack_small_grads(
        (gain_one_grad, shift_one_grad, query_bgrad, value_bgrad, output_bgrad, gain_two_grad, shift_two_grad, down_bgrad),
        up_bgrad,
    )
    own_small, own_qkv_grad, own_output, own_up, own_down = scatter_all(
        (small_grads, qkv_wgrad, output_wgrad, up_wgrad, down_wgrad), scatter_chunks(), 1
    )
    return (
        block_out,
        input_grad,
        own_qkv_grad[:, :width],
        own_qkv_grad[:, width : 2 * width],
        own_qkv_grad[:, 2 * width :],
        own_output,
        own_small[0, :64],
        own_small[1, :64],
        own_small[2, :64],
        own_small[3, :64],
        own_small[4, :64],
        own_up,
        own_down,
        own_small[5, :64],
        own_small[6, :64],
        own_small[8:10].reshape(-1),
        own_small[7, :64],
    )


def solution(mesh):
    fits = mesh.shape["fsdp"] == 4 * DEPTH and mesh.shape["ctx"] == BOTH
    return jax.shard_map(
        fast_device if fits else plain_device,
        mesh=mesh,
        in_specs=(
            P("fsdp", "ctx", None),
            P("fsdp", "ctx", None),
            P("fsdp", None),
            P("fsdp", None),
            P("fsdp", None),
            P("fsdp", None),
            P("fsdp"),
            P("fsdp"),
            P("fsdp"),
            P("fsdp"),
            P("fsdp"),
            P("fsdp", None),
            P("fsdp", None),
            P("fsdp"),
            P("fsdp"),
            P("fsdp"),
            P("fsdp"),
        ),
        out_specs=(
            P("fsdp", "ctx", None),
            P("fsdp", "ctx", None),
            P("fsdp", None),
            P("fsdp", None),
            P("fsdp", None),
            P("fsdp", None),
            P("fsdp"),
            P("fsdp"),
            P("fsdp"),
            P("fsdp"),
            P("fsdp"),
            P("fsdp", None),
            P("fsdp", None),
            P("fsdp"),
            P("fsdp"),
            P("fsdp"),
            P("fsdp"),
        ),
        check_vma=False,
    )
```

```python
import functools

import jax
import jax.numpy as jnp
from jax import lax
from jax.experimental import pallas as pl
from jax.experimental.pallas import tpu as pltpu
from jax.sharding import PartitionSpec as P

HEADS = 16
HDIM = 64
MESH = pl.DeviceIdType.MESH


epsilon = 1e-05


def layer_norm(token_rows, gain, shift):
    centered = token_rows - jnp.mean(token_rows, axis=-1, keepdims=True)
    variance = jnp.mean(centered * centered, axis=-1, keepdims=True)
    return centered * lax.rsqrt(variance + epsilon) * gain + shift


def gelu_act(values_in):
    return jax.nn.gelu(values_in, approximate=True)


def gather_attention(shards):
    return (
        lax.all_gather(shards[0], "fsdp", axis=0, tiled=True),
        lax.all_gather(shards[1], "fsdp", axis=0, tiled=True),
        lax.all_gather(shards[2], "fsdp", axis=0, tiled=True),
        lax.all_gather(shards[3], "fsdp", axis=0, tiled=True),
        lax.all_gather(shards[4], "fsdp", axis=0, tiled=True),
        lax.all_gather(shards[5], "fsdp", axis=0, tiled=True),
        lax.all_gather(shards[6], "fsdp", axis=0, tiled=True),
        lax.all_gather(shards[7], "fsdp", axis=0, tiled=True),
        lax.all_gather(shards[8], "fsdp", axis=0, tiled=True),
    )


def gather_feed(shards):
    return (
        lax.all_gather(shards[0], "fsdp", axis=0, tiled=True),
        lax.all_gather(shards[1], "fsdp", axis=0, tiled=True),
        lax.all_gather(shards[2], "fsdp", axis=0, tiled=True),
        lax.all_gather(shards[3], "fsdp", axis=0, tiled=True),
        lax.all_gather(shards[4], "fsdp", axis=0, tiled=True),
        lax.all_gather(shards[5], "fsdp", axis=0, tiled=True),
    )


def plain_device(
    activations,
    cotangent,
    query_weight,
    key_weight,
    value_weight,
    output_weight,
    first_gain,
    first_shift,
    query_bias,
    value_bias,
    output_bias,
    up_weight,
    down_weight,
    second_gain,
    second_shift,
    up_bias,
    down_bias,
):
    clip_count, local_len, width = activations.shape
    scaling = HDIM ** (-0.5)
    attend_shards = (
        query_weight,
        key_weight,
        value_weight,
        output_weight,
        first_gain,
        first_shift,
        query_bias,
        value_bias,
        output_bias,
    )
    feed_shards = (up_weight, down_weight, second_gain, second_shift, up_bias, down_bias)
    attend_full = gather_attention(attend_shards)
    (
        full_query,
        full_key,
        full_value,
        full_output,
        full_gain_one,
        full_shift_one,
        full_query_bias,
        full_value_bias,
        full_output_bias,
    ) = attend_full
    gain_one = full_gain_one.astype(jnp.float32)
    shift_one = full_shift_one.astype(jnp.float32)
    token_rows = activations.reshape(-1, width).astype(jnp.float32)
    normed_one = layer_norm(token_rows, gain_one, shift_one).astype(jnp.bfloat16)
    queries = (
        jnp.dot(normed_one, full_query, preferred_element_type=jnp.float32)
        + full_query_bias.astype(jnp.float32)
    ).astype(jnp.bfloat16)
    keys_local = jnp.dot(normed_one, full_key, preferred_element_type=jnp.float32).astype(
        jnp.bfloat16
    )
    values_local = (
        jnp.dot(normed_one, full_value, preferred_element_type=jnp.float32)
        + full_value_bias.astype(jnp.float32)
    ).astype(jnp.bfloat16)
    query_heads = queries.reshape(clip_count, local_len, HEADS, HDIM)
    keys_block = keys_local.reshape(clip_count, local_len, width)
    values_block = values_local.reshape(clip_count, local_len, width)
    run_max = jnp.full((clip_count, local_len, HEADS), -1e30, jnp.float32)
    key_piece = lax.all_gather(keys_block, "ctx", axis=1, tiled=True)
    value_piece = lax.all_gather(values_block, "ctx", axis=1, tiled=True)
    key_heads = key_piece.reshape(clip_count, -1, HEADS, HDIM)
    value_heads = value_piece.reshape(clip_count, -1, HEADS, HDIM)
    scores = (
        jnp.einsum("cqhd,ckhd->cqhk", query_heads, key_heads, preferred_element_type=jnp.float32)
        * scaling
    )
    new_max = jnp.maximum(run_max, jnp.max(scores, axis=-1))
    weights = jnp.exp(scores - new_max[..., None])
    run_sum = jnp.sum(weights, axis=-1)
    accum = jnp.einsum(
        "cqhk,ckhd->cqhd",
        weights.astype(jnp.bfloat16),
        value_heads,
        preferred_element_type=jnp.float32,
    )
    run_max, run_sum, accum = (new_max, run_sum, accum)
    attend_exact = accum / run_sum[..., None]
    log_total = run_max + jnp.log(run_sum)
    attended = attend_exact.reshape(-1, width).astype(jnp.bfloat16)
    mid_rows = (
        token_rows
        + jnp.dot(attended, full_output, preferred_element_type=jnp.float32)
        + full_output_bias.astype(jnp.float32)
    )
    feed_full = gather_feed(feed_shards)
    full_up, full_down, full_gain_two, full_shift_two, full_up_bias, full_down_bias = feed_full
    gain_two = full_gain_two.astype(jnp.float32)
    shift_two = full_shift_two.astype(jnp.float32)
    normed_two = layer_norm(mid_rows, gain_two, shift_two).astype(jnp.bfloat16)
    pre_act = jnp.dot(
        normed_two, full_up, preferred_element_type=jnp.float32
    ) + full_up_bias.astype(jnp.float32)
    hidden = gelu_act(pre_act).astype(jnp.bfloat16)
    block_rows = (
        mid_rows
        + jnp.dot(hidden, full_down, preferred_element_type=jnp.float32)
        + full_down_bias.astype(jnp.float32)
    )
    block_out = block_rows.astype(jnp.bfloat16).reshape(activations.shape)
    back_attend = gather_attention(attend_shards)
    back_feed = gather_feed(feed_shards)
    back_query, back_key, back_value, back_output = (
        back_attend[0],
        back_attend[1],
        back_attend[2],
        back_attend[3],
    )
    back_up, back_down = (back_feed[0], back_feed[1])
    cot_rows = cotangent.reshape(-1, width)
    outer_grad = cot_rows.astype(jnp.float32)
    down_wgrad = jnp.einsum("rf,rd->fd", hidden, cot_rows, preferred_element_type=jnp.float32)
    down_bgrad = jnp.sum(outer_grad, axis=0)
    hidden_grad = jnp.einsum("rd,fd->rf", cot_rows, back_down, preferred_element_type=jnp.float32)
    _, gelu_back = jax.vjp(gelu_act, pre_act)
    pre_grad = gelu_back(hidden_grad)[0].astype(jnp.bfloat16)
    up_wgrad = jnp.einsum("rd,rf->df", normed_two, pre_grad, preferred_element_type=jnp.float32)
    up_bgrad = jnp.sum(pre_grad.astype(jnp.float32), axis=0)
    normed_two_grad = jnp.einsum("rf,df->rd", pre_grad, back_up, preferred_element_type=jnp.float32)
    _, norm_two_back = jax.vjp(layer_norm, mid_rows, gain_two, shift_two)
    mid_part, gain_two_grad, shift_two_grad = norm_two_back(normed_two_grad)
    mid_grad = outer_grad + mid_part
    feed_owned = (
        lax.psum_scatter(
            up_wgrad.astype(jnp.bfloat16), "fsdp", scatter_dimension=0, tiled=True
        ).astype(jnp.float32),
        lax.psum_scatter(
            down_wgrad.astype(jnp.bfloat16), "fsdp", scatter_dimension=0, tiled=True
        ).astype(jnp.float32),
        lax.psum_scatter(
            gain_two_grad.astype(jnp.bfloat16), "fsdp", scatter_dimension=0, tiled=True
        ).astype(jnp.float32),
        lax.psum_scatter(
            shift_two_grad.astype(jnp.bfloat16), "fsdp", scatter_dimension=0, tiled=True
        ).astype(jnp.float32),
        lax.psum_scatter(
            up_bgrad.astype(jnp.bfloat16), "fsdp", scatter_dimension=0, tiled=True
        ).astype(jnp.float32),
        lax.psum_scatter(
            down_bgrad.astype(jnp.bfloat16), "fsdp", scatter_dimension=0, tiled=True
        ).astype(jnp.float32),
    )
    feed_done = (
        lax.psum(feed_owned[0].astype(jnp.bfloat16), "ctx").astype(jnp.float32),
        lax.psum(feed_owned[1].astype(jnp.bfloat16), "ctx").astype(jnp.float32),
        lax.psum(feed_owned[2].astype(jnp.bfloat16), "ctx").astype(jnp.float32),
        lax.psum(feed_owned[3].astype(jnp.bfloat16), "ctx").astype(jnp.float32),
        lax.psum(feed_owned[4].astype(jnp.bfloat16), "ctx").astype(jnp.float32),
        lax.psum(feed_owned[5].astype(jnp.bfloat16), "ctx").astype(jnp.float32),
    )
    branch_grad = mid_grad.astype(jnp.bfloat16)
    output_wgrad = jnp.einsum(
        "rd,re->de", attended, branch_grad, preferred_element_type=jnp.float32
    )
    output_bgrad = jnp.sum(branch_grad.astype(jnp.float32), axis=0)
    attended_grad = jnp.einsum(
        "re,de->rd", branch_grad, back_output, preferred_element_type=jnp.float32
    ).astype(jnp.bfloat16)
    grad_heads = attended_grad.reshape(clip_count, local_len, HEADS, HDIM)
    delta = jnp.sum(grad_heads.astype(jnp.float32) * attend_exact, axis=-1)
    keys_whole, values_whole = (
        lax.all_gather(keys_block, "ctx", axis=1, tiled=True),
        lax.all_gather(values_block, "ctx", axis=1, tiled=True),
    )
    key_heads_all = keys_whole.reshape(clip_count, -1, HEADS, HDIM)
    value_heads_all = values_whole.reshape(clip_count, -1, HEADS, HDIM)
    scores_all = (
        jnp.einsum(
            "cqhd,ckhd->cqhk", query_heads, key_heads_all, preferred_element_type=jnp.float32
        )
        * scaling
    )
    probs = jnp.exp(scores_all - log_total[..., None])
    prob_grad = jnp.einsum(
        "cqhd,ckhd->cqhk", grad_heads, value_heads_all, preferred_element_type=jnp.float32
    )
    score_grad = (probs * (prob_grad - delta[..., None])).astype(jnp.bfloat16)
    query_grad = (
        jnp.einsum("cqhk,ckhd->cqhd", score_grad, key_heads_all, preferred_element_type=jnp.float32)
        * scaling
    ).astype(jnp.bfloat16)
    query_grad = query_grad.reshape(-1, width)
    probs_low = probs.astype(jnp.bfloat16)
    key_part = (
        jnp.einsum("cqhk,cqhd->kchd", score_grad, query_heads, preferred_element_type=jnp.float32)
        * scaling
    )
    value_part = jnp.einsum(
        "cqhk,cqhd->kchd", probs_low, grad_heads, preferred_element_type=jnp.float32
    )
    summed = lax.psum_scatter(
        jnp.stack([key_part, value_part], axis=2)
        .reshape(lax.axis_size("ctx") * local_len, clip_count, 2, width)
        .astype(jnp.bfloat16),
        "ctx",
        scatter_dimension=0,
        tiled=True,
    ).astype(jnp.float32)
    key_grad = jnp.transpose(summed[:, :, 0], (1, 0, 2)).reshape(-1, width).astype(jnp.bfloat16)
    value_grad = jnp.transpose(summed[:, :, 1], (1, 0, 2)).reshape(-1, width).astype(jnp.bfloat16)
    query_wgrad = jnp.einsum(
        "rd,re->de", normed_one, query_grad, preferred_element_type=jnp.float32
    )
    key_wgrad = jnp.einsum("rd,re->de", normed_one, key_grad, preferred_element_type=jnp.float32)
    value_wgrad = jnp.einsum(
        "rd,re->de", normed_one, value_grad, preferred_element_type=jnp.float32
    )
    query_bgrad = jnp.sum(query_grad.astype(jnp.float32), axis=0)
    value_bgrad = jnp.sum(value_grad.astype(jnp.float32), axis=0)
    normed_one_grad = (
        jnp.einsum("re,de->rd", query_grad, back_query, preferred_element_type=jnp.float32)
        + jnp.einsum("re,de->rd", key_grad, back_key, preferred_element_type=jnp.float32)
        + jnp.einsum("re,de->rd", value_grad, back_value, preferred_element_type=jnp.float32)
    )
    _, norm_one_back = jax.vjp(layer_norm, token_rows, gain_one, shift_one)
    input_part, gain_one_grad, shift_one_grad = norm_one_back(normed_one_grad)
    input_grad = (mid_grad + input_part).reshape(activations.shape)
    attend_owned = (
        lax.psum_scatter(
            query_wgrad.astype(jnp.bfloat16), "fsdp", scatter_dimension=0, tiled=True
        ).astype(jnp.float32),
        lax.psum_scatter(
            key_wgrad.astype(jnp.bfloat16), "fsdp", scatter_dimension=0, tiled=True
        ).astype(jnp.float32),
        lax.psum_scatter(
            value_wgrad.astype(jnp.bfloat16), "fsdp", scatter_dimension=0, tiled=True
        ).astype(jnp.float32),
        lax.psum_scatter(
            output_wgrad.astype(jnp.bfloat16), "fsdp", scatter_dimension=0, tiled=True
        ).astype(jnp.float32),
        lax.psum_scatter(
            gain_one_grad.astype(jnp.bfloat16), "fsdp", scatter_dimension=0, tiled=True
        ).astype(jnp.float32),
        lax.psum_scatter(
            shift_one_grad.astype(jnp.bfloat16), "fsdp", scatter_dimension=0, tiled=True
        ).astype(jnp.float32),
        lax.psum_scatter(
            query_bgrad.astype(jnp.bfloat16), "fsdp", scatter_dimension=0, tiled=True
        ).astype(jnp.float32),
        lax.psum_scatter(
            value_bgrad.astype(jnp.bfloat16), "fsdp", scatter_dimension=0, tiled=True
        ).astype(jnp.float32),
        lax.psum_scatter(
            output_bgrad.astype(jnp.bfloat16), "fsdp", scatter_dimension=0, tiled=True
        ).astype(jnp.float32),
    )
    attend_done = (
        lax.psum(attend_owned[0].astype(jnp.bfloat16), "ctx").astype(jnp.float32),
        lax.psum(attend_owned[1].astype(jnp.bfloat16), "ctx").astype(jnp.float32),
        lax.psum(attend_owned[2].astype(jnp.bfloat16), "ctx").astype(jnp.float32),
        lax.psum(attend_owned[3].astype(jnp.bfloat16), "ctx").astype(jnp.float32),
        lax.psum(attend_owned[4].astype(jnp.bfloat16), "ctx").astype(jnp.float32),
        lax.psum(attend_owned[5].astype(jnp.bfloat16), "ctx").astype(jnp.float32),
        lax.psum(attend_owned[6].astype(jnp.bfloat16), "ctx").astype(jnp.float32),
        lax.psum(attend_owned[7].astype(jnp.bfloat16), "ctx").astype(jnp.float32),
        lax.psum(attend_owned[8].astype(jnp.bfloat16), "ctx").astype(jnp.float32),
    )
    return (
        block_out,
        input_grad,
        attend_done[0],
        attend_done[1],
        attend_done[2],
        attend_done[3],
        attend_done[4],
        attend_done[5],
        attend_done[6],
        attend_done[7],
        attend_done[8],
        feed_done[0],
        feed_done[1],
        feed_done[2],
        feed_done[3],
        feed_done[4],
        feed_done[5],
    )


def place():
    f = lax.axis_index("fsdp"); y = lax.axis_index("ctx")
    return f // 4, (f // 2) % 2, f % 2, y

def greet(z, x, c, y, depth):
    barrier = pltpu.get_barrier_semaphore()
    def one(dz, dx, dc, dy):
        pl.semaphore_signal(barrier, inc=1, device_id=(dz * 4 + dx * 2 + dc, dy), device_id_type=MESH)
    for k in range(1, depth):
        one((z + k) % depth, x, c, y)
    one(z, 1 - x, c, y); one(z, x, 1 - c, y); one(z, x, c, 1 - y)
    pl.semaphore_wait(barrier, depth + 2)

class Gather:
    def __init__(self, depth, chunks, ins, outs, sems, where):
        self.depth, self.chunks, self.ins, self.outs = depth, chunks, ins, outs
        self.zs, self.zr, self.xs, self.xr, self.ys, self.yr, self.cs, self.cr, self.loc = sems
        self.where = where
    def src(self, ch, half):
        t, r0, h, c0, w, both = self.chunks[ch]
        if not both: return self.ins[t].at[pl.ds(r0, h), pl.ds(c0, w)]
        h2 = h // 2
        return self.ins[t].at[pl.ds(pl.multiple_of(r0 + half * h2, 16), h2), pl.ds(c0, w)]
    def dst(self, ch, dz, dx, dc, half):
        t, r0, h, c0, w, both = self.chunks[ch]
        full = self.ins[t].shape[0]
        start = (dz * 4 + dx * 2 + dc) * full + r0
        if not both: return self.outs[t].at[pl.ds(pl.multiple_of(start, 16), h), pl.ds(c0, w)]
        h2 = h // 2
        return self.outs[t].at[pl.ds(pl.multiple_of(start + half * h2, 16), h2), pl.ds(c0, w)]
    def copy(self, src, dst, s, r, dz, dx, dc, dy):
        return pltpu.make_async_remote_copy(src_ref=src, dst_ref=dst, send_sem=s, recv_sem=r,
            device_id=(dz * 4 + dx * 2 + dc, dy), device_id_type=MESH)
    def zz(self, j):
        return (self.where[0] - j + self.depth) % self.depth
    def zmove(self, ch, k, recv=False):
        z, x, c, y = self.where
        if recv:
            d = self.dst(ch, self.zz(k), x, c, y)
            return self.copy(d, d, self.zs.at[ch, k], self.zr.at[ch, k], z, x, 1 - c, y)
        return self.copy(self.src(ch, y), self.dst(ch, z, x, c, y), self.zs.at[ch, k], self.zr.at[ch, k], (z + k) % self.depth, x, c, y)
    def xmove(self, ch, j, recv=False):
        z, x, c, y = self.where
        d = self.dst(ch, self.zz(j), 1 - x if recv else x, c, y)
        s = self.src(ch, y) if (j == 0 and not recv) else d
        return self.copy(s, d, self.xs.at[ch, j], self.xr.at[ch, j], z, 1 - x, c, y)
    def ymove(self, ch, i, j, recv=False):
        z, x, c, y = self.where
        d = self.dst(ch, self.zz(j), x if i == 0 else 1 - x, c, 1 - y if recv else y)
        n = i * self.depth + j
        return self.copy(d, d, self.ys.at[ch, n], self.yr.at[ch, n], z, x, c, 1 - y)
    def cmove(self, ch, i, j, other, recv=False):
        z, x, c, y = self.where
        half = 1 - y if other else y
        d = self.dst(ch, self.zz(j), x if i == 0 else 1 - x, 1 - c if recv else c, half)
        s = self.src(ch, half) if (i == 0 and j == 0 and not recv) else d
        n = (i * self.depth + j) + (2 * self.depth if other else 0)
        return self.copy(s, d, self.cs.at[ch, n], self.cr.at[ch, n], z, x, 1 - c, y)
    def own(self, ch):
        z, x, c, y = self.where
        t, r0, h, c0, w, both = self.chunks[ch]
        full = self.ins[t].shape[0]
        return pltpu.make_async_copy(self.ins[t].at[pl.ds(r0, h), pl.ds(c0, w)],
            self.outs[t].at[pl.ds(pl.multiple_of((z * 4 + x * 2 + c) * full + r0, 16), h), pl.ds(c0, w)], self.loc.at[ch])
    def begin(self, ch):
        for k in range(1, self.depth): self.zmove(ch, k).start()
        self.xmove(ch, 0).start()
        self.cmove(ch, 0, 0, False).start()
        if self.chunks[ch][5]: self.cmove(ch, 0, 0, True).start()
        self.own(ch).start()
    def zstage(self, ch):
        for k in range(1, self.depth):
            self.zmove(ch, k, True).wait_recv()
            self.xmove(ch, k).start()
            if self.chunks[ch][5]: self.ymove(ch, 0, k).start()
            self.cmove(ch, 0, k, False).start()
    def xstage(self, ch):
        for j in range(self.depth):
            self.xmove(ch, j, True).wait_recv()
            if self.chunks[ch][5]: self.ymove(ch, 1, j).start()
            self.cmove(ch, 1, j, False).start()
    def ystage(self, ch):
        if not self.chunks[ch][5]: return
        for i in range(2):
            for j in range(1 - i, self.depth):
                self.ymove(ch, i, j, True).wait_recv()
                self.cmove(ch, i, j, True).start()
    def arrived(self, ch):
        for i in range(2):
            for j in range(self.depth):
                self.cmove(ch, i, j, False, True).wait_recv()
                if self.chunks[ch][5]: self.cmove(ch, i, j, True, True).wait_recv()
        self.own(ch).wait()
    def sent(self, ch):
        both = self.chunks[ch][5]
        for k in range(1, self.depth): self.zmove(ch, k).wait_send()
        for j in range(self.depth): self.xmove(ch, j).wait_send()
        for i in range(2):
            for j in range(self.depth):
                self.cmove(ch, i, j, False).wait_send()
                if both:
                    self.cmove(ch, i, j, True).wait_send()
                    if i or j: self.ymove(ch, i, j).wait_send()

def gather_sems(depth, n):
    S = pltpu.SemaphoreType.DMA
    return [S((n, depth)), S((n, depth)), S((n, depth)), S((n, depth)), S((n, 2 * depth)), S((n, 2 * depth)), S((n, 4 * depth)), S((n, 4 * depth)), S((n,))]

def rowwise(h, w, body):
    wide = min(w, 1024 if w % 1024 == 0 else 512)
    steps_w = w // wide
    total = (h // 16) * steps_w
    if total == 1:
        body(pl.ds(0, 16), pl.ds(0, wide)); return
    def one(i, _):
        body(pl.ds(pl.multiple_of((i // steps_w) * 16, 16), 16), pl.ds(pl.multiple_of((i % steps_w) * wide, 128), wide))
        return 0
    lax.fori_loop(0, total, one, 0)

class Scatter:
    def __init__(self, depth, chunks, grads, outs, bufs, sems, where):
        self.depth, self.chunks, self.grads, self.outs, self.bufs = depth, chunks, grads, outs, bufs
        self.ls, self.cs, self.cr, self.xs, self.xr, self.zs, self.zr, self.ys, self.yr = sems
        self.where = where
    def piece(self, ch, dz, dx, dc):
        t, k, r0, h = self.chunks[ch]
        full = self.grads[t].shape[0] // (4 * self.depth)
        return self.grads[t].at[pl.ds(pl.multiple_of((dz * 4 + dx * 2 + dc) * full + r0, 16), h)]
    def copy(self, src, dst, s, r, dz, dx, dc, dy):
        return pltpu.make_async_remote_copy(src_ref=src, dst_ref=dst, send_sem=s, recv_sem=r,
            device_id=(dz * 4 + dx * 2 + dc, dy), device_id_type=MESH)
    def zz(self, j): return (self.where[0] + j) % self.depth
    def load(self, ch, i, j):
        z, x, c, y = self.where; t, k = self.chunks[ch][:2]
        return pltpu.make_async_copy(self.piece(ch, self.zz(j), x if i == 0 else 1 - x, c), self.bufs[t][0].at[k, i, j], self.ls.at[ch, i * self.depth + j])
    def cmove(self, ch, i, j):
        z, x, c, y = self.where; t, k = self.chunks[ch][:2]; n = i * self.depth + j
        return self.copy(self.piece(ch, self.zz(j), x if i == 0 else 1 - x, 1 - c), self.bufs[t][1].at[k, i, j], self.cs.at[ch, n], self.cr.at[ch, n], z, x, 1 - c, y)
    def xmove(self, ch, j):
        z, x, c, y = self.where; t, k = self.chunks[ch][:2]
        return self.copy(self.bufs[t][0].at[k, 1, j], self.bufs[t][2].at[k, j], self.xs.at[ch, j], self.xr.at[ch, j], z, 1 - x, c, y)
    def zmove(self, ch, j):
        z, x, c, y = self.where; t, k = self.chunks[ch][:2]
        return self.copy(self.bufs[t][0].at[k, 0, j], self.bufs[t][3].at[k, j - 1], self.zs.at[ch, j], self.zr.at[ch, j], self.zz(j), x, c, y)
    def ymove(self, ch):
        z, x, c, y = self.where; t, k = self.chunks[ch][:2]
        return self.copy(self.bufs[t][4].at[k], self.bufs[t][5].at[k], self.ys.at[ch], self.yr.at[ch], z, x, c, 1 - y)
    def begin(self, ch):
        for i in (1, 0):
            for j in range(self.depth):
                self.load(ch, i, j).start()
                self.cmove(ch, i, j).start()
    def cstage(self, ch):
        t, k, r0, h = self.chunks[ch]; L, C = self.bufs[t][:2]; w = L.shape[-1]
        for i in (1, 0):
            for j in range(self.depth):
                self.load(ch, i, j).wait(); self.cmove(ch, i, j).wait_recv()
                def add(r, q):
                    L[k, i, j, r, q] = L[k, i, j, r, q] + C[k, i, j, r, q]
                rowwise(h, w, add)
                if i == 1: self.xmove(ch, j).start()
    def xstage(self, ch):
        t, k, r0, h = self.chunks[ch]; L, C, X = self.bufs[t][:3]; w = L.shape[-1]
        for j in list(range(1, self.depth)) + [0]:
            self.xmove(ch, j).wait_recv()
            def add(r, q):
                L[k, 0, j, r, q] = L[k, 0, j, r, q] + X[k, j, r, q]
            rowwise(h, w, add)
            if j: self.zmove(ch, j).start()
    def zstage(self, ch):
        t, k, r0, h = self.chunks[ch]; L, C, X, Z, F, Y = self.bufs[t]; w = L.shape[-1]
        for j in range(1, self.depth): self.zmove(ch, j).wait_recv()
        def add(r, q):
            tot = L[k, 0, 0, r, q].astype(jnp.float32)
            for j in range(1, self.depth): tot = tot + Z[k, j - 1, r, q].astype(jnp.float32)
            F[k, r, q] = tot.astype(jnp.bfloat16)
        rowwise(h, w, add)
        self.ymove(ch).start()
    def ystage(self, ch):
        t, k, r0, h = self.chunks[ch]; L, C, X, Z, F, Y = self.bufs[t]; w = L.shape[-1]
        z, x, c, y = self.where
        self.ymove(ch).wait_recv()
        out = self.outs[t]
        if out.shape[-1] == w:
            def add(r, q):
                out[pl.ds(pl.multiple_of(r0 + r.start, 16), 16), q] = F[k, r, q].astype(jnp.float32) + Y[k, r, q].astype(jnp.float32)
            rowwise(h, w, add)
        else:
            part = w // 3
            for n in range(3):
                def lay(r, q, n=n):
                    mine = F[k, r, n * part:(n + 1) * part].astype(jnp.float32)
                    other = Y[k, r, n * part:(n + 1) * part].astype(jnp.float32)
                    rr = pl.ds(pl.multiple_of(r0 + r.start, 16), 16)
                    out[rr, 2 * n * part:(2 * n + 1) * part] = jnp.where(y == 0, mine, other)
                    out[rr, (2 * n + 1) * part:(2 * n + 2) * part] = jnp.where(y == 0, other, mine)
                rowwise(h, 128, lay)
    def sent(self, ch):
        for i in range(2):
            for j in range(self.depth): self.cmove(ch, i, j).wait_send()
        for j in range(self.depth):
            self.xmove(ch, j).wait_send()
            if j: self.zmove(ch, j).wait_send()
        self.ymove(ch).wait_send()

def scatter_scratch(depth, chunks, widths):
    S = pltpu.SemaphoreType.DMA; n = len(chunks); out = []
    for t, w in enumerate(widths):
        mine = [c for c in chunks if c[0] == t]; m = len(mine); h = mine[0][3]
        B = lambda *lead: pltpu.VMEM(lead + (h, w), jnp.bfloat16)
        out += [B(m, 2, depth), B(m, 2, depth), B(m, depth), B(m, depth - 1), B(m), B(m)]
    return out + [S((n, 2 * depth)), S((n, 2 * depth)), S((n, 2 * depth)), S((n, depth)), S((n, depth)), S((n, depth)), S((n, depth)), S((n,)), S((n,))]

def rs_kernel(depth, n, chunks, lag, *refs):
    grads, outs = refs[:n], refs[n:2 * n]
    bufs = [refs[2 * n + 6 * t:2 * n + 6 * t + 6] for t in range(n)]
    sems = refs[8 * n:8 * n + 9]
    where = place()
    s = Scatter(depth, chunks, grads, outs, bufs, sems, where)
    greet(*where, depth)
    N = len(chunks)
    for ch in range(N): s.begin(ch)
    for st in range(N + 3 * lag):
        if st < N: s.cstage(st)
        if 0 <= st - lag < N: s.xstage(st - lag)
        if 0 <= st - 2 * lag < N: s.zstage(st - 2 * lag)
        if 0 <= st - 3 * lag < N: s.ystage(st - 3 * lag)
    for ch in range(N): s.sent(ch)

def scatter_all(grads, chunks, wide, depth=4, lag=1, cid=2):
    n = len(grads)
    return pl.pallas_call(
        functools.partial(rs_kernel, depth, n, chunks, lag),
        out_shape=[jax.ShapeDtypeStruct((g.shape[0] // (4 * depth), g.shape[1] * (2 if t == wide else 1)), jnp.float32) for t, g in enumerate(grads)],
        in_specs=[pl.BlockSpec(memory_space=pl.ANY)] * n,
        out_specs=[pl.BlockSpec(memory_space=pltpu.VMEM)] * n,
        scratch_shapes=scatter_scratch(depth, chunks, [g.shape[1] for g in grads]),
        compiler_params=pltpu.CompilerParams(collective_id=cid, has_side_effects=True, vmem_limit_bytes=60 * 2 ** 20),
        name="gradients_scatter")(*grads)


DEPTH, BOTH = 4, 2
f32, bf16 = jnp.float32, jnp.bfloat16
NT = (((1,), (1,)), ((), ()))
NN = (((1,), (0,)), ((), ()))
TN = (((0,), (0,)), ((), ()))
SQRT_2_PI = 0.7978845608028654


def mul(a, b, dims):
    return lax.dot_general(a, b, dims, preferred_element_type=f32)


def tall(i, size):
    return pl.ds(pl.multiple_of(i * size, 16), size)


def normalized(rows):
    centered = rows - jnp.mean(rows, axis=-1, keepdims=True)
    inverse = lax.rsqrt(jnp.mean(centered * centered, axis=-1, keepdims=True) + epsilon)
    return centered * inverse, inverse


GAIN_ONE, SHIFT_ONE, QUERY_BIAS, VALUE_BIAS, OUTPUT_BIAS, GAIN_TWO, SHIFT_TWO, DOWN_BIAS = range(8)


def forward_kernel(depth, chunks, ahead, *refs):
    (
        small, own_qkv, own_out, own_up, own_down, x_own, cot,
        all_small, all_qkv, all_out, all_up, all_down,
        normed_out, qkv_out, exact_out, inverse_out, weights_out,
        block_out, mid_grad_out, attended_grad_out, out_wgrad, up_wgrad, down_wgrad, vec_grads, up_bgrad,
        x_other, attended, vecs, up_bias, mid, normed_two,
    ) = refs[:31]
    sems = refs[31:40]
    swap_s, swap_r, att_s, att_r, loc, keep_sem = refs[40:]
    z, x, c, y = place()
    rows, width = x_own.shape
    length, half = BOTH * rows, width // BOTH
    pairs = half // 128
    wide = up_bias.shape[1]
    step = 112
    g = Gather(depth, chunks, (small, own_qkv, own_out, own_up, own_down), (all_small, all_qkv, all_out, all_up, all_down), sems, (z, x, c, y))
    greet(z, x, c, y, depth)
    total = len(chunks)
    swapping = g.copy(x_own, x_other, swap_s, swap_r, z, x, c, 1 - y)

    def service(s):
        if s < total:
            g.zstage(s)
            if s + ahead < total:
                g.begin(s + ahead)
        if 0 <= s - 1 < total:
            g.xstage(s - 1)
        if 0 <= s - 2 < total:
            g.ystage(s - 2)

    for ch in range(ahead):
        g.begin(ch)
        if ch == 1:
            swapping.start()
    service(0)
    service(1)
    g.arrived(0)

    def first_phase(small_v, normed, qkv, exact, inverse, weight, values_ones, kept):
        get = pltpu.make_async_copy(all_small, small_v, loc.at[0])
        get.start()
        get.wait()
        for chip in range(2 * depth):
            one, two = small_v[pl.ds(32 * chip, 16), :].astype(f32), small_v[pl.ds(32 * chip + 16, 16), :].astype(f32)
            vecs[0:8, 128 * chip : 128 * chip + 128] = one[0:8] + two[0:8]
            for core, part in enumerate((one, two)):
                for n in range(2):
                    at = (2 * chip + core) * 256 + 128 * n
                    up_bias[0:1, at : at + 128] = part[8 + n : 9 + n]

        def norm_one(source, first):
            gain, shift = vecs[GAIN_ONE : GAIN_ONE + 1, :], vecs[SHIFT_ONE : SHIFT_ONE + 1, :]

            def one(i, _):
                value = normalized(source[tall(i, step), :].astype(f32))[0]
                normed[pl.ds(pl.multiple_of(first + i * step, 16), step), :] = (value * gain + shift).astype(bf16)
                return 0

            lax.fori_loop(0, rows // step, one, 0)

        mine = pl.ds(pl.multiple_of(y * half, 128), half)

        def project(first):
            these = pl.ds(first, rows)
            for n, bias in enumerate((QUERY_BIAS, None, VALUE_BIAS)):
                value = mul(normed[these, :], weight[:, n * half : (n + 1) * half], NN)
                if bias is not None:
                    value = value + vecs[bias : bias + 1, mine]
                qkv[these, n * half : (n + 1) * half] = value.astype(bf16)

        norm_one(x_own, 0)
        service(2)
        g.arrived(1)
        get = pltpu.make_async_copy(all_qkv, weight, loc.at[0])
        get.start()
        get.wait()
        project(0)
        swapping.wait_recv()
        norm_one(x_other, rows)
        project(rows)
        put_normed = pltpu.make_async_copy(normed, normed_out, loc.at[1])
        put_qkv = pltpu.make_async_copy(qkv, qkv_out, loc.at[2])
        put_normed.start()
        put_qkv.start()
        service(3)

        low_lanes = lax.broadcasted_iota(jnp.int32, (rows, 128), 1) < HDIM

        def keep(pair, block, head, slot):
            return pltpu.make_async_copy(kept.at[slot, head], weights_out.at[2 * pair + head, tall(block, rows)], keep_sem.at[slot, head])

        def send(pair):
            at = pl.multiple_of(pair * 128, 128)
            there = pl.multiple_of(y * half + at, 128)
            return g.copy(
                exact_low.at[:, pl.ds(at, 128)], attended.at[:, pl.ds(there, 128)], att_s.at[pair], att_r.at[pair], z, x, c, 1 - y
            )

        exact_low = normed_two
        values_ones[:, 128:] = jnp.ones((length, 128), bf16)

        def attend(turn, _):
            pair = turn // 2
            slot = turn % 2
            block = 1 - slot
            for n, s in ((1, 4), (4, 5), (6, 6), (7, 7)):

                @pl.when(turn == n)
                def _(s=s):
                    service(s)

            @pl.when(turn > 1)
            def _():
                for head in range(2):
                    keep(0, 0, head, slot).wait()

            at = pl.multiple_of(pair * 128, 128)

            @pl.when(slot == 0)
            def _():
                values_ones[:, :128] = qkv[:, pl.ds(2 * half + at, 128)]

            these = tall(block, rows)
            queries = qkv[these, pl.ds(at, 128)] * bf16(HDIM**-0.5)
            keys = qkv[:, pl.ds(half + at, 128)]
            values = values_ones[...]
            parts = []
            for head in range(2):
                masked = jnp.where(low_lanes == (head == 0), queries, jnp.zeros_like(queries))
                scores = mul(masked, keys, NT)
                top = jnp.max(scores, axis=1, keepdims=True)
                weights = jnp.exp(scores - top).astype(bf16)
                kept[slot, head] = weights
                summed = mul(weights, values, NN)
                parts.append((summed[:, :128], 1.0 / summed[:, 128:]))
            (low, low_inverse), (high, high_inverse) = parts
            scale = jnp.where(low_lanes, low_inverse, high_inverse)
            value = jnp.where(low_lanes, low, high) * scale
            exact[these, pl.ds(at, 128)] = value
            inverse[these, pl.ds(at, 128)] = scale
            for head in range(2):
                keep(pair, block, head, slot).start()

            @pl.when(slot == 0)
            def _():
                exact_low[:, pl.ds(at, 128)] = value.astype(bf16)
                send(pair).start()

            @pl.when(slot == 1)
            def _():
                attended[:, pl.ds(pl.multiple_of(y * half + at, 128), 128)] = value.astype(bf16)

            return 0

        lax.fori_loop(0, 2 * pairs, attend, 0)
        put_exact = pltpu.make_async_copy(exact, exact_out, loc.at[3])
        put_inverse = pltpu.make_async_copy(inverse, inverse_out, loc.at[4])
        put_exact.start()
        put_inverse.start()
        for slot in range(2):
            for head in range(2):
                keep(0, 0, head, slot).wait()
        for pair in range(pairs):
            send(pair).wait()
        for put in (put_normed, put_qkv, put_exact, put_inverse):
            put.wait()

    V = pltpu.VMEM
    pl.run_scoped(
        first_phase,
        V(all_small.shape, bf16),
        V((length, width), bf16),
        V((length, 3 * half), bf16),
        V((length, half), f32),
        V((length, half), f32),
        V((width, 3 * half), bf16),
        V((length, 256), bf16),
        V((2, 2, rows, length), bf16),
    )

    def second_phase(out_w, up_w, down_w, low_t, block_sum, normed_grad, up_stage, down_stage):
        tiles = wide // width

        def get_down(j, slot):
            return pltpu.make_async_copy(all_down.at[pl.ds(pl.multiple_of(j * width, 16), width)], down_w.at[slot], loc.at[1 + slot])

        def get_up(j):
            return pltpu.make_async_copy(all_up.at[:, pl.ds(pl.multiple_of(j * width, 128), width)], up_w, loc.at[3])

        def put_up(j):
            return pltpu.make_async_copy(up_stage, up_wgrad.at[:, pl.ds(pl.multiple_of(j * width, 128), width)], loc.at[4])

        def put_down(j):
            return pltpu.make_async_copy(down_stage, down_wgrad.at[pl.ds(pl.multiple_of(j * width, 16), width)], loc.at[5])

        g.arrived(6)
        get = pltpu.make_async_copy(all_out, out_w, loc.at[0])
        get.start()
        for ch in range(2, 6):
            g.arrived(ch)
        get_down(0, 0).start()
        get.wait()
        mid[...] = mul(attended[...], out_w[...], NN)

        def norm_two(i, _):
            these = tall(i, step)
            value = mid[these, :] + vecs[OUTPUT_BIAS : OUTPUT_BIAS + 1, :] + x_own[these, :].astype(f32)
            mid[these, :] = value
            value = normalized(value)[0] * vecs[GAIN_TWO : GAIN_TWO + 1, :] + vecs[SHIFT_TWO : SHIFT_TWO + 1, :]
            normed_two[these, :] = value.astype(bf16)
            return 0

        lax.fori_loop(0, rows // step, norm_two, 0)
        low_t[...] = normed_two[...].T
        block_sum[...] = jnp.zeros_like(block_sum)
        normed_grad[...] = jnp.zeros_like(normed_grad)

        def feed(j, _):
            slot = j % 2
            for n in range(tiles):

                @pl.when(j == n)
                def _(n=n):
                    service(8 + n)
                    g.arrived(7 + n)

            get_up(j).start()
            get_down(j, slot).wait()

            @pl.when(j + 1 < tiles)
            def _():
                get_down(j + 1, 1 - slot).start()

            @pl.when(j > 0)
            def _():
                put_up(0).wait()
                put_down(0).wait()

            get_up(j).wait()
            cols = pl.ds(pl.multiple_of(j * width, 128), width)
            up, down = up_w[...], down_w[slot]
            u = mul(normed_two[...], up, NN) + up_bias[0:1, cols]
            hidden_grad = mul(cot[...], down, NT)
            inner = jnp.tanh(SQRT_2_PI * (u + 0.044715 * (u * u * u)))
            hidden = (0.5 * u * (1.0 + inner)).astype(bf16)
            slope = 0.5 * (1.0 + inner) + 0.5 * u * (1.0 - inner * inner) * (SQRT_2_PI * (1.0 + 3 * 0.044715 * (u * u)))
            grad = hidden_grad * slope
            pre_grad = grad.astype(bf16)
            block_sum[...] += mul(hidden, down, NN)
            down_stage[...] = mul(hidden, cot[...], TN).astype(bf16)
            up_stage[...] = mul(low_t[...], pre_grad, NN).astype(bf16)
            up_bgrad[0:1, cols] = jnp.sum(pre_grad.astype(f32), axis=0, keepdims=True)
            normed_grad[...] += mul(pre_grad, up, NT)
            put_up(j).start()
            put_down(j).start()
            return 0

        lax.fori_loop(0, tiles, feed, 0)

        zero = jnp.zeros((1, width), f32)

        def back_two(i, sums):
            gain_sum, shift_sum, out_sum, cot_sum = sums
            these = tall(i, step)
            rows_in = mid[these, :]
            block_sum[these, :] = block_sum[these, :] + rows_in + vecs[DOWN_BIAS : DOWN_BIAS + 1, :]
            zed, inverse = normalized(rows_in)
            grad = normed_grad[these, :]
            scaled = grad * vecs[GAIN_TWO : GAIN_TWO + 1, :]
            part = inverse * (
                scaled - jnp.mean(scaled, axis=-1, keepdims=True) - zed * jnp.mean(scaled * zed, axis=-1, keepdims=True)
            )
            above = cot[these, :].astype(f32)
            whole = above + part
            mid[these, :] = whole
            branch = whole.astype(bf16)
            normed_two[these, :] = branch
            add = lambda total, value: total + jnp.sum(value, axis=0, keepdims=True)
            return (
                add(gain_sum, grad * zed), add(shift_sum, grad), add(out_sum, branch.astype(f32)), add(cot_sum, above),
            )

        gain_sum, shift_sum, out_sum, cot_sum = lax.fori_loop(0, rows // step, back_two, (zero,) * 4)
        vec_grads[...] = jnp.zeros_like(vec_grads)
        vec_grads[GAIN_TWO : GAIN_TWO + 1, :] = gain_sum
        vec_grads[SHIFT_TWO : SHIFT_TWO + 1, :] = shift_sum
        vec_grads[OUTPUT_BIAS : OUTPUT_BIAS + 1, :] = out_sum
        vec_grads[DOWN_BIAS : DOWN_BIAS + 1, :] = cot_sum
        put_mid = pltpu.make_async_copy(mid, mid_grad_out, loc.at[0])
        put_mid.start()
        put_up(0).wait()
        put_down(0).wait()
        block_out[...] = block_sum[...].astype(bf16)
        up_stage[...] = mul(attended[...], normed_two[...], TN).astype(bf16)
        put_out = pltpu.make_async_copy(up_stage, out_wgrad, loc.at[4])
        put_out.start()
        attended_grad_out[...] = mul(normed_two[...], out_w[...], NT).astype(bf16)
        put_mid.wait()
        put_out.wait()

    pl.run_scoped(
        second_phase,
        V((width, width), bf16),
        V((width, width), bf16),
        V((2, width, width), bf16),
        V((width, rows), bf16),
        V((rows, width), f32),
        V((rows, width), f32),
        V((width, width), bf16),
        V((width, width), bf16),
    )
    swapping.wait_send()
    for ch in range(total):
        g.sent(ch)


def forward(small, own_qkv, own_out, own_up, own_down, x_own, cot, depth=DEPTH, ahead=3):
    rows, width = x_own.shape
    length, half, wide = BOTH * rows, width // BOTH, own_up.shape[1]
    chunks = gather_chunks(own_up.shape, own_down.shape)
    S, V = pltpu.SemaphoreType.DMA, pltpu.VMEM
    anywhere, fast = pl.BlockSpec(memory_space=pl.ANY), pl.BlockSpec(memory_space=pltpu.VMEM)
    shape = jax.ShapeDtypeStruct
    parts = 4 * depth
    return pl.pallas_call(
        functools.partial(forward_kernel, depth, chunks, ahead),
        out_shape=[shape((parts * s.shape[0], s.shape[1]), bf16) for s in (small, own_qkv, own_out, own_up, own_down)]
        + [
            shape((length, width), bf16),
            shape((length, 3 * half), bf16),
            shape((length, half), f32),
            shape((length, half), f32),
            shape((half // HDIM, length, length), bf16),
            shape((rows, width), bf16),
            shape((rows, width), f32),
            shape((rows, width), bf16),
            shape((width, width), bf16),
            shape((width, wide), bf16),
            shape((wide, width), bf16),
            shape((8, width), f32),
            shape((1, wide), f32),
        ],
        in_specs=[anywhere] * 5 + [fast] * 2,
        out_specs=[anywhere] * 10 + [fast, anywhere, fast] + [anywhere] * 3 + [fast] * 2,
        scratch_shapes=[
            V((rows, width), bf16), V((rows, width), bf16), V((8, width), f32), V((1, wide), f32),
            V((rows, width), f32), V((rows, width), bf16),
        ]
        + gather_sems(depth, len(chunks))
        + [S, S, S((half // 128,)), S((half // 128,)), S((6,)), S((2, 2))],
        compiler_params=pltpu.CompilerParams(collective_id=1, has_side_effects=True, vmem_limit_bytes=62 * 2**20),
        name="forward_and_feed",
    )(small, own_qkv, own_out, own_up, own_down, x_own, cot)


def gather_chunks(up_shape, down_shape):
    tall_up, wide = up_shape
    tall_down, width = down_shape
    quarter = tall_down // 4
    return (
        (0, 0, 16, 0, 128, False),
        (1, 0, tall_up, 0, 3 * width // BOTH, False),
    ) + tuple((4, quarter * i, quarter, 0, width, True) for i in range(4)) + ((2, 0, tall_up, 0, width, False),) + tuple(
        (3, 0, tall_up, width * i, width, False) for i in range(wide // width)
    )


def attend_back_kernel(block_rows, qkv, attended, inverse, grads, weights_in, out, key_sum, value_sum, kept, sem):
    length = qkv.shape[0]
    half = qkv.shape[1] // 3
    blocks, pairs = length // block_rows, half // 128
    low_lanes = lax.broadcasted_iota(jnp.int32, (block_rows, 128), 1) < HDIM

    def load(turn, head, slot):
        rows = pl.ds(pl.multiple_of((turn % blocks) * block_rows, 16), block_rows)
        return pltpu.make_async_copy(weights_in.at[2 * (turn // blocks) + head, rows], kept.at[slot, head], sem.at[slot, head])

    for head in range(2):
        load(0, head, 0).start()

    def one_pair(pair, _):
        at = pl.multiple_of(pair * 128, 128)

        def one_block(block, _):
            turn = pair * blocks + block
            slot = turn % 2
            for head in range(2):
                load(turn, head, slot).wait()

            @pl.when(turn + 1 < blocks * pairs)
            def _():
                for head in range(2):
                    load(turn + 1, head, 1 - slot).start()

            rows = pl.ds(pl.multiple_of(block * block_rows, 16), block_rows)
            queries = qkv[rows, pl.ds(at, 128)] * jnp.bfloat16(HDIM**-0.5)
            keys = qkv[:, pl.ds(half + at, 128)]
            values = qkv[:, pl.ds(2 * half + at, 128)]
            scaled = grads[rows, pl.ds(at, 128)].astype(jnp.float32) * inverse[rows, pl.ds(at, 128)]
            low = scaled.astype(jnp.bfloat16)
            product = low.astype(jnp.float32) * attended[rows, pl.ds(at, 128)]
            queries_t, low_t = queries.T, low.T
            query_parts, key_parts, value_parts = [], [], []
            for head in range(2):
                own = low_lanes == (head == 0)
                lanes = slice(HDIM * head, HDIM * head + HDIM)
                masked = jnp.where(own, low, jnp.zeros_like(low))
                prob_grad = lax.dot_general(masked, values, NT, preferred_element_type=jnp.float32)
                delta = jnp.sum(jnp.where(own, product, 0.0), axis=1, keepdims=True)
                weights = kept[slot, head]
                score_grad = (weights.astype(jnp.float32) * (prob_grad - delta)).astype(jnp.bfloat16)
                query_parts.append(lax.dot_general(score_grad, keys, NN, preferred_element_type=jnp.float32))
                key_parts.append(lax.dot_general(queries_t[lanes], score_grad, NN, preferred_element_type=jnp.float32))
                value_parts.append(lax.dot_general(low_t[lanes], weights, NN, preferred_element_type=jnp.float32))
            query_grad = jnp.where(low_lanes, query_parts[0], query_parts[1]) * HDIM**-0.5
            out[rows, pl.ds(at, 128)] = query_grad.astype(jnp.bfloat16)
            key_part = jnp.concatenate(key_parts, axis=0)
            value_part = jnp.concatenate(value_parts, axis=0)
            key_sum[...] = jnp.where(block == 0, key_part, key_sum[...] + key_part)
            value_sum[...] = jnp.where(block == 0, value_part, value_sum[...] + value_part)
            return 0

        lax.fori_loop(0, blocks, one_block, 0)
        out[:, pl.ds(half + at, 128)] = key_sum[...].T.astype(jnp.bfloat16)
        out[:, pl.ds(2 * half + at, 128)] = value_sum[...].T.astype(jnp.bfloat16)
        return 0

    lax.fori_loop(0, pairs, one_pair, 0)


def attend_back(qkv, attended, inverse, grads, weights, block_rows):
    length, wide = qkv.shape
    whole = pl.BlockSpec(memory_space=pltpu.VMEM)
    return pl.pallas_call(
        functools.partial(attend_back_kernel, block_rows),
        out_shape=jax.ShapeDtypeStruct((length, wide), jnp.bfloat16),
        in_specs=[whole] * 4 + [pl.BlockSpec(memory_space=pl.ANY)],
        out_specs=whole,
        scratch_shapes=[
            pltpu.VMEM((128, length), jnp.float32),
            pltpu.VMEM((128, length), jnp.float32),
            pltpu.VMEM((2, 2, block_rows, length), jnp.bfloat16),
            pltpu.SemaphoreType.DMA((2, 2)),
        ],
        compiler_params=pltpu.CompilerParams(vmem_limit_bytes=60 * 2**20),
        name="attend_back",
    )(qkv, attended, inverse, grads, weights)


def pack_small(vectors, up_bias, c):
    rows = jnp.stack(vectors)
    zero = jnp.zeros_like(rows)
    rows = jnp.concatenate([jnp.where(c == 0, rows, zero), jnp.where(c == 0, zero, rows)], axis=1)
    return jnp.concatenate([rows, up_bias.reshape(2, 128), jnp.zeros((6, 128), rows.dtype)], axis=0)


def unpack_small(gathered):
    blocks = gathered.astype(jnp.float32).reshape(-1, 2, 16, 128)
    vectors = (blocks[:, 0, :8] + blocks[:, 1, :8]).transpose(1, 0, 2).reshape(8, -1)
    return vectors, blocks[:, :, 8:10].reshape(-1)


def pack_small_grads(vectors, up_grad):
    parts = 4 * DEPTH
    rows = jnp.stack(vectors).reshape(8, parts, 64).transpose(1, 0, 2)
    rows = jnp.concatenate([rows, jnp.zeros_like(rows)], axis=2)
    rows = jnp.concatenate([rows, up_grad.reshape(parts, 2, 128), jnp.zeros((parts, 6, 128), jnp.float32)], axis=1)
    return rows.astype(jnp.bfloat16).reshape(parts * 16, 128)


def swap(value):
    return lax.ppermute(value, "ctx", [(0, 1), (1, 0)])


def scatter_chunks():
    return ((0, 0, 0, 16),) + tuple((4, i, 64 * i, 64) for i in range(4)) + tuple(
        (3, i, 16 * i, 16) for i in range(4)
    ) + ((2, 0, 0, 64), (1, 0, 0, 64))


def fast_device(
    activations, cotangent, query_weight, key_weight, value_weight, output_weight, first_gain, first_shift,
    query_bias, value_bias, output_bias, up_weight, down_weight, second_gain, second_shift, up_bias, down_bias,
):
    _, rows, width = activations.shape
    half = width // 2
    y = lax.axis_index("ctx")
    c = lax.axis_index("fsdp") % 2
    f32, bf16 = jnp.float32, jnp.bfloat16

    def mine(value):
        return lax.dynamic_slice_in_dim(value, y * half, half, value.ndim - 1)

    def others(value):
        return lax.dynamic_slice_in_dim(value, (1 - y) * half, half, value.ndim - 1)

    def both(own, other):
        return jnp.where(y == 0, jnp.concatenate([own, other], -1), jnp.concatenate([other, own], -1))

    small = pack_small(
        (first_gain, first_shift, query_bias, value_bias, output_bias, second_gain, second_shift, down_bias), up_bias, c
    )
    own_qkv = jnp.concatenate([mine(query_weight), mine(key_weight), mine(value_weight)], axis=1)
    x_own = activations[0]
    (
        all_small, all_qkv, _, _, _, normed_one, qkv, exact, inverse, weights, block_out, mid_grad, attended_grad,
        output_wgrad, up_wgrad, down_wgrad, vec_grads, up_bgrad,
    ) = forward(small, own_qkv, output_weight, up_weight, down_weight, x_own, cotangent[0])
    x_rows = x_own.astype(f32)
    gain_one, shift_one = unpack_small(all_small)[0][:2]
    grad_mine = jnp.concatenate([mine(attended_grad), swap(others(attended_grad))], axis=0)
    qkv_grad = attend_back(qkv, exact, inverse, grad_mine, weights, 224)
    qkv_wgrad = jnp.einsum("rd,re->de", normed_one, qkv_grad, preferred_element_type=f32).astype(bf16)
    qkv_bgrad = jnp.sum(qkv_grad.astype(f32), axis=0)
    nothing = jnp.zeros((half,), f32)
    query_bgrad = both(qkv_bgrad[:half], nothing)
    value_bgrad = both(qkv_bgrad[2 * half :], nothing)
    normed_grad = jnp.einsum("re,de->rd", qkv_grad, all_qkv, preferred_element_type=f32)
    normed_one_grad = normed_grad[:rows] + swap(normed_grad[rows:].astype(bf16)).astype(f32)
    _, norm_one_back = jax.vjp(layer_norm, x_rows, gain_one, shift_one)
    input_part, gain_one_grad, shift_one_grad = norm_one_back(normed_one_grad)
    input_grad = (mid_grad + input_part).reshape(activations.shape)
    small_grads = pack_small_grads(
        (gain_one_grad, shift_one_grad, query_bgrad, value_bgrad) + tuple(vec_grads[n] for n in range(OUTPUT_BIAS, DOWN_BIAS + 1)),
        up_bgrad[0],
    )
    own_small, own_qkv_grad, own_output, own_up, own_down = scatter_all(
        (small_grads, qkv_wgrad, output_wgrad, up_wgrad, down_wgrad), scatter_chunks(), 1
    )
    return (
        block_out.reshape(activations.shape),
        input_grad,
        own_qkv_grad[:, :width],
        own_qkv_grad[:, width : 2 * width],
        own_qkv_grad[:, 2 * width :],
        own_output,
        own_small[0, :64],
        own_small[1, :64],
        own_small[2, :64],
        own_small[3, :64],
        own_small[4, :64],
        own_up,
        own_down,
        own_small[5, :64],
        own_small[6, :64],
        own_small[8:10].reshape(-1),
        own_small[7, :64],
    )


def solution(mesh):
    fits = mesh.shape["fsdp"] == 4 * DEPTH and mesh.shape["ctx"] == BOTH
    return jax.shard_map(
        fast_device if fits else plain_device,
        mesh=mesh,
        in_specs=(
            P("fsdp", "ctx", None),
            P("fsdp", "ctx", None),
            P("fsdp", None),
            P("fsdp", None),
            P("fsdp", None),
            P("fsdp", None),
            P("fsdp"),
            P("fsdp"),
            P("fsdp"),
            P("fsdp"),
            P("fsdp"),
            P("fsdp", None),
            P("fsdp", None),
            P("fsdp"),
            P("fsdp"),
            P("fsdp"),
            P("fsdp"),
        ),
        out_specs=(
            P("fsdp", "ctx", None),
            P("fsdp", "ctx", None),
            P("fsdp", None),
            P("fsdp", None),
            P("fsdp", None),
            P("fsdp", None),
            P("fsdp"),
            P("fsdp"),
            P("fsdp"),
            P("fsdp"),
            P("fsdp"),
            P("fsdp", None),
            P("fsdp", None),
            P("fsdp"),
            P("fsdp"),
            P("fsdp"),
            P("fsdp"),
        ),
        check_vma=False,
    )
```

```python
import functools

import jax
import jax.numpy as jnp
from jax import lax
from jax.experimental import pallas as pl
from jax.experimental.pallas import tpu as pltpu
from jax.sharding import PartitionSpec as P

HEADS = 16
HDIM = 64
MESH = pl.DeviceIdType.MESH


epsilon = 1e-05


def layer_norm(token_rows, gain, shift):
    centered = token_rows - jnp.mean(token_rows, axis=-1, keepdims=True)
    variance = jnp.mean(centered * centered, axis=-1, keepdims=True)
    return centered * lax.rsqrt(variance + epsilon) * gain + shift


def gelu_act(values_in):
    return jax.nn.gelu(values_in, approximate=True)


def gather_attention(shards):
    return (
        lax.all_gather(shards[0], "fsdp", axis=0, tiled=True),
        lax.all_gather(shards[1], "fsdp", axis=0, tiled=True),
        lax.all_gather(shards[2], "fsdp", axis=0, tiled=True),
        lax.all_gather(shards[3], "fsdp", axis=0, tiled=True),
        lax.all_gather(shards[4], "fsdp", axis=0, tiled=True),
        lax.all_gather(shards[5], "fsdp", axis=0, tiled=True),
        lax.all_gather(shards[6], "fsdp", axis=0, tiled=True),
        lax.all_gather(shards[7], "fsdp", axis=0, tiled=True),
        lax.all_gather(shards[8], "fsdp", axis=0, tiled=True),
    )


def gather_feed(shards):
    return (
        lax.all_gather(shards[0], "fsdp", axis=0, tiled=True),
        lax.all_gather(shards[1], "fsdp", axis=0, tiled=True),
        lax.all_gather(shards[2], "fsdp", axis=0, tiled=True),
        lax.all_gather(shards[3], "fsdp", axis=0, tiled=True),
        lax.all_gather(shards[4], "fsdp", axis=0, tiled=True),
        lax.all_gather(shards[5], "fsdp", axis=0, tiled=True),
    )


def plain_device(
    activations,
    cotangent,
    query_weight,
    key_weight,
    value_weight,
    output_weight,
    first_gain,
    first_shift,
    query_bias,
    value_bias,
    output_bias,
    up_weight,
    down_weight,
    second_gain,
    second_shift,
    up_bias,
    down_bias,
):
    clip_count, local_len, width = activations.shape
    scaling = HDIM ** (-0.5)
    attend_shards = (
        query_weight,
        key_weight,
        value_weight,
        output_weight,
        first_gain,
        first_shift,
        query_bias,
        value_bias,
        output_bias,
    )
    feed_shards = (up_weight, down_weight, second_gain, second_shift, up_bias, down_bias)
    attend_full = gather_attention(attend_shards)
    (
        full_query,
        full_key,
        full_value,
        full_output,
        full_gain_one,
        full_shift_one,
        full_query_bias,
        full_value_bias,
        full_output_bias,
    ) = attend_full
    gain_one = full_gain_one.astype(jnp.float32)
    shift_one = full_shift_one.astype(jnp.float32)
    token_rows = activations.reshape(-1, width).astype(jnp.float32)
    normed_one = layer_norm(token_rows, gain_one, shift_one).astype(jnp.bfloat16)
    queries = (
        jnp.dot(normed_one, full_query, preferred_element_type=jnp.float32)
        + full_query_bias.astype(jnp.float32)
    ).astype(jnp.bfloat16)
    keys_local = jnp.dot(normed_one, full_key, preferred_element_type=jnp.float32).astype(
        jnp.bfloat16
    )
    values_local = (
        jnp.dot(normed_one, full_value, preferred_element_type=jnp.float32)
        + full_value_bias.astype(jnp.float32)
    ).astype(jnp.bfloat16)
    query_heads = queries.reshape(clip_count, local_len, HEADS, HDIM)
    keys_block = keys_local.reshape(clip_count, local_len, width)
    values_block = values_local.reshape(clip_count, local_len, width)
    run_max = jnp.full((clip_count, local_len, HEADS), -1e30, jnp.float32)
    key_piece = lax.all_gather(keys_block, "ctx", axis=1, tiled=True)
    value_piece = lax.all_gather(values_block, "ctx", axis=1, tiled=True)
    key_heads = key_piece.reshape(clip_count, -1, HEADS, HDIM)
    value_heads = value_piece.reshape(clip_count, -1, HEADS, HDIM)
    scores = (
        jnp.einsum("cqhd,ckhd->cqhk", query_heads, key_heads, preferred_element_type=jnp.float32)
        * scaling
    )
    new_max = jnp.maximum(run_max, jnp.max(scores, axis=-1))
    weights = jnp.exp(scores - new_max[..., None])
    run_sum = jnp.sum(weights, axis=-1)
    accum = jnp.einsum(
        "cqhk,ckhd->cqhd",
        weights.astype(jnp.bfloat16),
        value_heads,
        preferred_element_type=jnp.float32,
    )
    run_max, run_sum, accum = (new_max, run_sum, accum)
    attend_exact = accum / run_sum[..., None]
    log_total = run_max + jnp.log(run_sum)
    attended = attend_exact.reshape(-1, width).astype(jnp.bfloat16)
    mid_rows = (
        token_rows
        + jnp.dot(attended, full_output, preferred_element_type=jnp.float32)
        + full_output_bias.astype(jnp.float32)
    )
    feed_full = gather_feed(feed_shards)
    full_up, full_down, full_gain_two, full_shift_two, full_up_bias, full_down_bias = feed_full
    gain_two = full_gain_two.astype(jnp.float32)
    shift_two = full_shift_two.astype(jnp.float32)
    normed_two = layer_norm(mid_rows, gain_two, shift_two).astype(jnp.bfloat16)
    pre_act = jnp.dot(
        normed_two, full_up, preferred_element_type=jnp.float32
    ) + full_up_bias.astype(jnp.float32)
    hidden = gelu_act(pre_act).astype(jnp.bfloat16)
    block_rows = (
        mid_rows
        + jnp.dot(hidden, full_down, preferred_element_type=jnp.float32)
        + full_down_bias.astype(jnp.float32)
    )
    block_out = block_rows.astype(jnp.bfloat16).reshape(activations.shape)
    back_attend = gather_attention(attend_shards)
    back_feed = gather_feed(feed_shards)
    back_query, back_key, back_value, back_output = (
        back_attend[0],
        back_attend[1],
        back_attend[2],
        back_attend[3],
    )
    back_up, back_down = (back_feed[0], back_feed[1])
    cot_rows = cotangent.reshape(-1, width)
    outer_grad = cot_rows.astype(jnp.float32)
    down_wgrad = jnp.einsum("rf,rd->fd", hidden, cot_rows, preferred_element_type=jnp.float32)
    down_bgrad = jnp.sum(outer_grad, axis=0)
    hidden_grad = jnp.einsum("rd,fd->rf", cot_rows, back_down, preferred_element_type=jnp.float32)
    _, gelu_back = jax.vjp(gelu_act, pre_act)
    pre_grad = gelu_back(hidden_grad)[0].astype(jnp.bfloat16)
    up_wgrad = jnp.einsum("rd,rf->df", normed_two, pre_grad, preferred_element_type=jnp.float32)
    up_bgrad = jnp.sum(pre_grad.astype(jnp.float32), axis=0)
    normed_two_grad = jnp.einsum("rf,df->rd", pre_grad, back_up, preferred_element_type=jnp.float32)
    _, norm_two_back = jax.vjp(layer_norm, mid_rows, gain_two, shift_two)
    mid_part, gain_two_grad, shift_two_grad = norm_two_back(normed_two_grad)
    mid_grad = outer_grad + mid_part
    feed_owned = (
        lax.psum_scatter(
            up_wgrad.astype(jnp.bfloat16), "fsdp", scatter_dimension=0, tiled=True
        ).astype(jnp.float32),
        lax.psum_scatter(
            down_wgrad.astype(jnp.bfloat16), "fsdp", scatter_dimension=0, tiled=True
        ).astype(jnp.float32),
        lax.psum_scatter(
            gain_two_grad.astype(jnp.bfloat16), "fsdp", scatter_dimension=0, tiled=True
        ).astype(jnp.float32),
        lax.psum_scatter(
            shift_two_grad.astype(jnp.bfloat16), "fsdp", scatter_dimension=0, tiled=True
        ).astype(jnp.float32),
        lax.psum_scatter(
            up_bgrad.astype(jnp.bfloat16), "fsdp", scatter_dimension=0, tiled=True
        ).astype(jnp.float32),
        lax.psum_scatter(
            down_bgrad.astype(jnp.bfloat16), "fsdp", scatter_dimension=0, tiled=True
        ).astype(jnp.float32),
    )
    feed_done = (
        lax.psum(feed_owned[0].astype(jnp.bfloat16), "ctx").astype(jnp.float32),
        lax.psum(feed_owned[1].astype(jnp.bfloat16), "ctx").astype(jnp.float32),
        lax.psum(feed_owned[2].astype(jnp.bfloat16), "ctx").astype(jnp.float32),
        lax.psum(feed_owned[3].astype(jnp.bfloat16), "ctx").astype(jnp.float32),
        lax.psum(feed_owned[4].astype(jnp.bfloat16), "ctx").astype(jnp.float32),
        lax.psum(feed_owned[5].astype(jnp.bfloat16), "ctx").astype(jnp.float32),
    )
    branch_grad = mid_grad.astype(jnp.bfloat16)
    output_wgrad = jnp.einsum(
        "rd,re->de", attended, branch_grad, preferred_element_type=jnp.float32
    )
    output_bgrad = jnp.sum(branch_grad.astype(jnp.float32), axis=0)
    attended_grad = jnp.einsum(
        "re,de->rd", branch_grad, back_output, preferred_element_type=jnp.float32
    ).astype(jnp.bfloat16)
    grad_heads = attended_grad.reshape(clip_count, local_len, HEADS, HDIM)
    delta = jnp.sum(grad_heads.astype(jnp.float32) * attend_exact, axis=-1)
    keys_whole, values_whole = (
        lax.all_gather(keys_block, "ctx", axis=1, tiled=True),
        lax.all_gather(values_block, "ctx", axis=1, tiled=True),
    )
    key_heads_all = keys_whole.reshape(clip_count, -1, HEADS, HDIM)
    value_heads_all = values_whole.reshape(clip_count, -1, HEADS, HDIM)
    scores_all = (
        jnp.einsum(
            "cqhd,ckhd->cqhk", query_heads, key_heads_all, preferred_element_type=jnp.float32
        )
        * scaling
    )
    probs = jnp.exp(scores_all - log_total[..., None])
    prob_grad = jnp.einsum(
        "cqhd,ckhd->cqhk", grad_heads, value_heads_all, preferred_element_type=jnp.float32
    )
    score_grad = (probs * (prob_grad - delta[..., None])).astype(jnp.bfloat16)
    query_grad = (
        jnp.einsum("cqhk,ckhd->cqhd", score_grad, key_heads_all, preferred_element_type=jnp.float32)
        * scaling
    ).astype(jnp.bfloat16)
    query_grad = query_grad.reshape(-1, width)
    probs_low = probs.astype(jnp.bfloat16)
    key_part = (
        jnp.einsum("cqhk,cqhd->kchd", score_grad, query_heads, preferred_element_type=jnp.float32)
        * scaling
    )
    value_part = jnp.einsum(
        "cqhk,cqhd->kchd", probs_low, grad_heads, preferred_element_type=jnp.float32
    )
    summed = lax.psum_scatter(
        jnp.stack([key_part, value_part], axis=2)
        .reshape(lax.axis_size("ctx") * local_len, clip_count, 2, width)
        .astype(jnp.bfloat16),
        "ctx",
        scatter_dimension=0,
        tiled=True,
    ).astype(jnp.float32)
    key_grad = jnp.transpose(summed[:, :, 0], (1, 0, 2)).reshape(-1, width).astype(jnp.bfloat16)
    value_grad = jnp.transpose(summed[:, :, 1], (1, 0, 2)).reshape(-1, width).astype(jnp.bfloat16)
    query_wgrad = jnp.einsum(
        "rd,re->de", normed_one, query_grad, preferred_element_type=jnp.float32
    )
    key_wgrad = jnp.einsum("rd,re->de", normed_one, key_grad, preferred_element_type=jnp.float32)
    value_wgrad = jnp.einsum(
        "rd,re->de", normed_one, value_grad, preferred_element_type=jnp.float32
    )
    query_bgrad = jnp.sum(query_grad.astype(jnp.float32), axis=0)
    value_bgrad = jnp.sum(value_grad.astype(jnp.float32), axis=0)
    normed_one_grad = (
        jnp.einsum("re,de->rd", query_grad, back_query, preferred_element_type=jnp.float32)
        + jnp.einsum("re,de->rd", key_grad, back_key, preferred_element_type=jnp.float32)
        + jnp.einsum("re,de->rd", value_grad, back_value, preferred_element_type=jnp.float32)
    )
    _, norm_one_back = jax.vjp(layer_norm, token_rows, gain_one, shift_one)
    input_part, gain_one_grad, shift_one_grad = norm_one_back(normed_one_grad)
    input_grad = (mid_grad + input_part).reshape(activations.shape)
    attend_owned = (
        lax.psum_scatter(
            query_wgrad.astype(jnp.bfloat16), "fsdp", scatter_dimension=0, tiled=True
        ).astype(jnp.float32),
        lax.psum_scatter(
            key_wgrad.astype(jnp.bfloat16), "fsdp", scatter_dimension=0, tiled=True
        ).astype(jnp.float32),
        lax.psum_scatter(
            value_wgrad.astype(jnp.bfloat16), "fsdp", scatter_dimension=0, tiled=True
        ).astype(jnp.float32),
        lax.psum_scatter(
            output_wgrad.astype(jnp.bfloat16), "fsdp", scatter_dimension=0, tiled=True
        ).astype(jnp.float32),
        lax.psum_scatter(
            gain_one_grad.astype(jnp.bfloat16), "fsdp", scatter_dimension=0, tiled=True
        ).astype(jnp.float32),
        lax.psum_scatter(
            shift_one_grad.astype(jnp.bfloat16), "fsdp", scatter_dimension=0, tiled=True
        ).astype(jnp.float32),
        lax.psum_scatter(
            query_bgrad.astype(jnp.bfloat16), "fsdp", scatter_dimension=0, tiled=True
        ).astype(jnp.float32),
        lax.psum_scatter(
            value_bgrad.astype(jnp.bfloat16), "fsdp", scatter_dimension=0, tiled=True
        ).astype(jnp.float32),
        lax.psum_scatter(
            output_bgrad.astype(jnp.bfloat16), "fsdp", scatter_dimension=0, tiled=True
        ).astype(jnp.float32),
    )
    attend_done = (
        lax.psum(attend_owned[0].astype(jnp.bfloat16), "ctx").astype(jnp.float32),
        lax.psum(attend_owned[1].astype(jnp.bfloat16), "ctx").astype(jnp.float32),
        lax.psum(attend_owned[2].astype(jnp.bfloat16), "ctx").astype(jnp.float32),
        lax.psum(attend_owned[3].astype(jnp.bfloat16), "ctx").astype(jnp.float32),
        lax.psum(attend_owned[4].astype(jnp.bfloat16), "ctx").astype(jnp.float32),
        lax.psum(attend_owned[5].astype(jnp.bfloat16), "ctx").astype(jnp.float32),
        lax.psum(attend_owned[6].astype(jnp.bfloat16), "ctx").astype(jnp.float32),
        lax.psum(attend_owned[7].astype(jnp.bfloat16), "ctx").astype(jnp.float32),
        lax.psum(attend_owned[8].astype(jnp.bfloat16), "ctx").astype(jnp.float32),
    )
    return (
        block_out,
        input_grad,
        attend_done[0],
        attend_done[1],
        attend_done[2],
        attend_done[3],
        attend_done[4],
        attend_done[5],
        attend_done[6],
        attend_done[7],
        attend_done[8],
        feed_done[0],
        feed_done[1],
        feed_done[2],
        feed_done[3],
        feed_done[4],
        feed_done[5],
    )


def place():
    f = lax.axis_index("fsdp"); y = lax.axis_index("ctx")
    return f // 4, (f // 2) % 2, f % 2, y

def greet(z, x, c, y, depth):
    barrier = pltpu.get_barrier_semaphore()
    def one(dz, dx, dc, dy):
        pl.semaphore_signal(barrier, inc=1, device_id=(dz * 4 + dx * 2 + dc, dy), device_id_type=MESH)
    for k in range(1, depth):
        one((z + k) % depth, x, c, y)
    one(z, 1 - x, c, y); one(z, x, 1 - c, y); one(z, x, c, 1 - y)
    pl.semaphore_wait(barrier, depth + 2)

class Gather:
    def __init__(self, depth, chunks, ins, outs, sems, where):
        self.depth, self.chunks, self.ins, self.outs = depth, chunks, ins, outs
        self.zs, self.zr, self.xs, self.xr, self.ys, self.yr, self.cs, self.cr, self.loc = sems
        self.where = where
    def src(self, ch, half):
        t, r0, h, c0, w, both = self.chunks[ch]
        if not both: return self.ins[t].at[pl.ds(r0, h), pl.ds(c0, w)]
        h2 = h // 2
        return self.ins[t].at[pl.ds(pl.multiple_of(r0 + half * h2, 16), h2), pl.ds(c0, w)]
    def dst(self, ch, dz, dx, dc, half):
        t, r0, h, c0, w, both = self.chunks[ch]
        full = self.ins[t].shape[0]
        start = (dz * 4 + dx * 2 + dc) * full + r0
        if not both: return self.outs[t].at[pl.ds(pl.multiple_of(start, 16), h), pl.ds(c0, w)]
        h2 = h // 2
        return self.outs[t].at[pl.ds(pl.multiple_of(start + half * h2, 16), h2), pl.ds(c0, w)]
    def copy(self, src, dst, s, r, dz, dx, dc, dy):
        return pltpu.make_async_remote_copy(src_ref=src, dst_ref=dst, send_sem=s, recv_sem=r,
            device_id=(dz * 4 + dx * 2 + dc, dy), device_id_type=MESH)
    def zz(self, j):
        return (self.where[0] - j + self.depth) % self.depth
    def zmove(self, ch, k, recv=False):
        z, x, c, y = self.where
        if recv:
            d = self.dst(ch, self.zz(k), x, c, y)
            return self.copy(d, d, self.zs.at[ch, k], self.zr.at[ch, k], z, x, 1 - c, y)
        return self.copy(self.src(ch, y), self.dst(ch, z, x, c, y), self.zs.at[ch, k], self.zr.at[ch, k], (z + k) % self.depth, x, c, y)
    def xmove(self, ch, j, recv=False):
        z, x, c, y = self.where
        d = self.dst(ch, self.zz(j), 1 - x if recv else x, c, y)
        s = self.src(ch, y) if (j == 0 and not recv) else d
        return self.copy(s, d, self.xs.at[ch, j], self.xr.at[ch, j], z, 1 - x, c, y)
    def ymove(self, ch, i, j, recv=False):
        z, x, c, y = self.where
        d = self.dst(ch, self.zz(j), x if i == 0 else 1 - x, c, 1 - y if recv else y)
        n = i * self.depth + j
        return self.copy(d, d, self.ys.at[ch, n], self.yr.at[ch, n], z, x, c, 1 - y)
    def cmove(self, ch, i, j, other, recv=False):
        z, x, c, y = self.where
        half = 1 - y if other else y
        d = self.dst(ch, self.zz(j), x if i == 0 else 1 - x, 1 - c if recv else c, half)
        s = self.src(ch, half) if (i == 0 and j == 0 and not recv) else d
        n = (i * self.depth + j) + (2 * self.depth if other else 0)
        return self.copy(s, d, self.cs.at[ch, n], self.cr.at[ch, n], z, x, 1 - c, y)
    def own(self, ch):
        z, x, c, y = self.where
        t, r0, h, c0, w, both = self.chunks[ch]
        full = self.ins[t].shape[0]
        return pltpu.make_async_copy(self.ins[t].at[pl.ds(r0, h), pl.ds(c0, w)],
            self.outs[t].at[pl.ds(pl.multiple_of((z * 4 + x * 2 + c) * full + r0, 16), h), pl.ds(c0, w)], self.loc.at[ch])
    def begin(self, ch):
        for k in range(1, self.depth): self.zmove(ch, k).start()
        self.xmove(ch, 0).start()
        self.cmove(ch, 0, 0, False).start()
        if self.chunks[ch][5]: self.cmove(ch, 0, 0, True).start()
        self.own(ch).start()
    def zstage(self, ch):
        for k in range(1, self.depth):
            self.zmove(ch, k, True).wait_recv()
            self.xmove(ch, k).start()
            if self.chunks[ch][5]: self.ymove(ch, 0, k).start()
            self.cmove(ch, 0, k, False).start()
    def xstage(self, ch):
        for j in range(self.depth):
            self.xmove(ch, j, True).wait_recv()
            if self.chunks[ch][5]: self.ymove(ch, 1, j).start()
            self.cmove(ch, 1, j, False).start()
    def ystage(self, ch):
        if not self.chunks[ch][5]: return
        for i in range(2):
            for j in range(1 - i, self.depth):
                self.ymove(ch, i, j, True).wait_recv()
                self.cmove(ch, i, j, True).start()
    def arrived(self, ch):
        for i in range(2):
            for j in range(self.depth):
                self.cmove(ch, i, j, False, True).wait_recv()
                if self.chunks[ch][5]: self.cmove(ch, i, j, True, True).wait_recv()
        self.own(ch).wait()
    def sent(self, ch):
        both = self.chunks[ch][5]
        for k in range(1, self.depth): self.zmove(ch, k).wait_send()
        for j in range(self.depth): self.xmove(ch, j).wait_send()
        for i in range(2):
            for j in range(self.depth):
                self.cmove(ch, i, j, False).wait_send()
                if both:
                    self.cmove(ch, i, j, True).wait_send()
                    if i or j: self.ymove(ch, i, j).wait_send()

def gather_sems(depth, n):
    S = pltpu.SemaphoreType.DMA
    return [S((n, depth)), S((n, depth)), S((n, depth)), S((n, depth)), S((n, 2 * depth)), S((n, 2 * depth)), S((n, 4 * depth)), S((n, 4 * depth)), S((n,))]


DEPTH, BOTH = 4, 2
f32, bf16 = jnp.float32, jnp.bfloat16
NT = (((1,), (1,)), ((), ()))
NN = (((1,), (0,)), ((), ()))
TN = (((0,), (0,)), ((), ()))
SQRT_2_PI = 0.7978845608028654


def mul(a, b, dims):
    return lax.dot_general(a, b, dims, preferred_element_type=f32)


def tall(i, size):
    return pl.ds(pl.multiple_of(i * size, 16), size)


def normalized(rows):
    centered = rows - jnp.mean(rows, axis=-1, keepdims=True)
    inverse = lax.rsqrt(jnp.mean(centered * centered, axis=-1, keepdims=True) + epsilon)
    return centered * inverse, inverse


GAIN_ONE, SHIFT_ONE, QUERY_BIAS, VALUE_BIAS, OUTPUT_BIAS, GAIN_TWO, SHIFT_TWO, DOWN_BIAS = range(8)


def forward_kernel(depth, chunks, ahead, *refs):
    (
        small, own_qkv, own_out, own_up, own_down, x_own, cot,
        all_small, all_qkv, all_out, all_up, all_down,
        normed_out, qkv_out, exact_out, inverse_out, weights_out,
        block_out, mid_grad_out, attended_grad_out, out_wgrad, up_wgrad, down_wgrad, vec_grads, up_bgrad, vecs,
        x_other, attended, up_bias, mid, normed_two,
    ) = refs[:31]
    sems = refs[31:40]
    swap_s, swap_r, att_s, att_r, loc, keep_sem = refs[40:]
    z, x, c, y = place()
    rows, width = x_own.shape
    length, half = BOTH * rows, width // BOTH
    pairs = half // 128
    wide = up_bias.shape[1]
    step = 112
    g = Gather(depth, chunks, (small, own_qkv, own_out, own_up, own_down), (all_small, all_qkv, all_out, all_up, all_down), sems, (z, x, c, y))
    greet(z, x, c, y, depth)
    total = len(chunks)
    swapping = g.copy(x_own, x_other, swap_s, swap_r, z, x, c, 1 - y)

    def service(s):
        if s < total:
            g.zstage(s)
            if s + ahead < total:
                g.begin(s + ahead)
        if 0 <= s - 1 < total:
            g.xstage(s - 1)
        if 0 <= s - 2 < total:
            g.ystage(s - 2)

    for ch in range(ahead):
        g.begin(ch)
        if ch == 1:
            swapping.start()
    service(0)
    service(1)
    g.arrived(0)

    def first_phase(small_v, normed, qkv, exact, inverse, weight, values_ones, kept):
        get = pltpu.make_async_copy(all_small, small_v, loc.at[0])
        get.start()
        get.wait()
        for chip in range(2 * depth):
            one, two = small_v[pl.ds(32 * chip, 16), :].astype(f32), small_v[pl.ds(32 * chip + 16, 16), :].astype(f32)
            vecs[0:8, 128 * chip : 128 * chip + 128] = one[0:8] + two[0:8]
            for core, part in enumerate((one, two)):
                for n in range(2):
                    at = (2 * chip + core) * 256 + 128 * n
                    up_bias[0:1, at : at + 128] = part[8 + n : 9 + n]

        def norm_one(source, first):
            gain, shift = vecs[GAIN_ONE : GAIN_ONE + 1, :], vecs[SHIFT_ONE : SHIFT_ONE + 1, :]

            def one(i, _):
                value = normalized(source[tall(i, step), :].astype(f32))[0]
                normed[pl.ds(pl.multiple_of(first + i * step, 16), step), :] = (value * gain + shift).astype(bf16)
                return 0

            lax.fori_loop(0, rows // step, one, 0)

        mine = pl.ds(pl.multiple_of(y * half, 128), half)

        def project(first):
            these = pl.ds(first, rows)
            for n, bias in enumerate((QUERY_BIAS, None, VALUE_BIAS)):
                value = mul(normed[these, :], weight[:, n * half : (n + 1) * half], NN)
                if bias is not None:
                    value = value + vecs[bias : bias + 1, mine]
                qkv[these, n * half : (n + 1) * half] = value.astype(bf16)

        norm_one(x_own, 0)
        service(2)
        g.arrived(1)
        get = pltpu.make_async_copy(all_qkv, weight, loc.at[0])
        get.start()
        get.wait()
        project(0)
        swapping.wait_recv()
        norm_one(x_other, rows)
        project(rows)
        put_normed = pltpu.make_async_copy(normed, normed_out, loc.at[1])
        put_qkv = pltpu.make_async_copy(qkv, qkv_out, loc.at[2])
        put_normed.start()
        put_qkv.start()
        service(3)

        low_lanes = lax.broadcasted_iota(jnp.int32, (rows, 128), 1) < HDIM

        def keep(pair, block, head, slot):
            return pltpu.make_async_copy(kept.at[slot, head], weights_out.at[2 * pair + head, tall(block, rows)], keep_sem.at[slot, head])

        def send(pair):
            at = pl.multiple_of(pair * 128, 128)
            there = pl.multiple_of(y * half + at, 128)
            return g.copy(
                exact_low.at[:, pl.ds(at, 128)], attended.at[:, pl.ds(there, 128)], att_s.at[pair], att_r.at[pair], z, x, c, 1 - y
            )

        exact_low = normed_two
        values_ones[:, 128:] = jnp.ones((length, 128), bf16)

        def attend(turn, _):
            pair = turn // 2
            slot = turn % 2
            block = 1 - slot
            for n, s in ((1, 4), (4, 5), (6, 6), (7, 7)):

                @pl.when(turn == n)
                def _(s=s):
                    service(s)

            @pl.when(turn > 1)
            def _():
                for head in range(2):
                    keep(0, 0, head, slot).wait()

            at = pl.multiple_of(pair * 128, 128)

            @pl.when(slot == 0)
            def _():
                values_ones[:, :128] = qkv[:, pl.ds(2 * half + at, 128)]

            these = tall(block, rows)
            queries = qkv[these, pl.ds(at, 128)] * bf16(HDIM**-0.5)
            keys = qkv[:, pl.ds(half + at, 128)]
            values = values_ones[...]
            parts = []
            for head in range(2):
                masked = jnp.where(low_lanes == (head == 0), queries, jnp.zeros_like(queries))
                scores = mul(masked, keys, NT)
                top = jnp.max(scores, axis=1, keepdims=True)
                weights = jnp.exp(scores - top).astype(bf16)
                kept[slot, head] = weights
                summed = mul(weights, values, NN)
                parts.append((summed[:, :128], 1.0 / summed[:, 128:]))
            (low, low_inverse), (high, high_inverse) = parts
            scale = jnp.where(low_lanes, low_inverse, high_inverse)
            value = jnp.where(low_lanes, low, high) * scale
            exact[these, pl.ds(at, 128)] = value
            inverse[these, pl.ds(at, 128)] = scale
            for head in range(2):
                keep(pair, block, head, slot).start()

            @pl.when(slot == 0)
            def _():
                exact_low[:, pl.ds(at, 128)] = value.astype(bf16)
                send(pair).start()

            @pl.when(slot == 1)
            def _():
                attended[:, pl.ds(pl.multiple_of(y * half + at, 128), 128)] = value.astype(bf16)

            return 0

        lax.fori_loop(0, 2 * pairs, attend, 0)
        put_exact = pltpu.make_async_copy(exact, exact_out, loc.at[3])
        put_inverse = pltpu.make_async_copy(inverse, inverse_out, loc.at[4])
        put_exact.start()
        put_inverse.start()
        for slot in range(2):
            for head in range(2):
                keep(0, 0, head, slot).wait()
        for pair in range(pairs):
            send(pair).wait()
        for put in (put_normed, put_qkv, put_exact, put_inverse):
            put.wait()

    V = pltpu.VMEM
    pl.run_scoped(
        first_phase,
        V(all_small.shape, bf16),
        V((length, width), bf16),
        V((length, 3 * half), bf16),
        V((length, half), f32),
        V((length, half), f32),
        V((width, 3 * half), bf16),
        V((length, 256), bf16),
        V((2, 2, rows, length), bf16),
    )

    def second_phase(out_w, up_w, down_w, low_t, block_sum, normed_grad, up_stage, down_stage):
        tiles = wide // width

        def get_down(j, slot):
            return pltpu.make_async_copy(all_down.at[pl.ds(pl.multiple_of(j * width, 16), width)], down_w.at[slot], loc.at[1 + slot])

        def get_up(j):
            return pltpu.make_async_copy(all_up.at[:, pl.ds(pl.multiple_of(j * width, 128), width)], up_w, loc.at[3])

        def put_up(j):
            return pltpu.make_async_copy(up_stage, up_wgrad.at[:, pl.ds(pl.multiple_of(j * width, 128), width)], loc.at[4])

        def put_down(j):
            return pltpu.make_async_copy(down_stage, down_wgrad.at[pl.ds(pl.multiple_of(j * width, 16), width)], loc.at[5])

        g.arrived(6)
        get = pltpu.make_async_copy(all_out, out_w, loc.at[0])
        get.start()
        for ch in range(2, 6):
            g.arrived(ch)
        get_down(0, 0).start()
        get.wait()
        mid[...] = mul(attended[...], out_w[...], NN)

        def norm_two(i, _):
            these = tall(i, step)
            value = mid[these, :] + vecs[OUTPUT_BIAS : OUTPUT_BIAS + 1, :] + x_own[these, :].astype(f32)
            mid[these, :] = value
            value = normalized(value)[0] * vecs[GAIN_TWO : GAIN_TWO + 1, :] + vecs[SHIFT_TWO : SHIFT_TWO + 1, :]
            normed_two[these, :] = value.astype(bf16)
            return 0

        lax.fori_loop(0, rows // step, norm_two, 0)
        low_t[...] = normed_two[...].T
        block_sum[...] = jnp.zeros_like(block_sum)
        normed_grad[...] = jnp.zeros_like(normed_grad)

        def feed(j, _):
            slot = j % 2
            for n in range(tiles):

                @pl.when(j == n)
                def _(n=n):
                    service(8 + n)
                    g.arrived(7 + n)

            get_up(j).start()
            get_down(j, slot).wait()

            @pl.when(j + 1 < tiles)
            def _():
                get_down(j + 1, 1 - slot).start()

            @pl.when(j > 0)
            def _():
                put_up(0).wait()
                put_down(0).wait()

            get_up(j).wait()
            cols = pl.ds(pl.multiple_of(j * width, 128), width)
            up, down = up_w[...], down_w[slot]
            u = mul(normed_two[...], up, NN) + up_bias[0:1, cols]
            hidden_grad = mul(cot[...], down, NT)
            inner = jnp.tanh(SQRT_2_PI * (u + 0.044715 * (u * u * u)))
            hidden = (0.5 * u * (1.0 + inner)).astype(bf16)
            slope = 0.5 * (1.0 + inner) + 0.5 * u * (1.0 - inner * inner) * (SQRT_2_PI * (1.0 + 3 * 0.044715 * (u * u)))
            grad = hidden_grad * slope
            pre_grad = grad.astype(bf16)
            block_sum[...] += mul(hidden, down, NN)
            down_stage[...] = mul(hidden, cot[...], TN).astype(bf16)
            up_stage[...] = mul(low_t[...], pre_grad, NN).astype(bf16)
            up_bgrad[0:1, cols] = jnp.sum(pre_grad.astype(f32), axis=0, keepdims=True)
            normed_grad[...] += mul(pre_grad, up, NT)
            put_up(j).start()
            put_down(j).start()
            return 0

        lax.fori_loop(0, tiles, feed, 0)

        zero = jnp.zeros((1, width), f32)

        def back_two(i, sums):
            gain_sum, shift_sum, out_sum, cot_sum = sums
            these = tall(i, step)
            rows_in = mid[these, :]
            block_sum[these, :] = block_sum[these, :] + rows_in + vecs[DOWN_BIAS : DOWN_BIAS + 1, :]
            zed, inverse = normalized(rows_in)
            grad = normed_grad[these, :]
            scaled = grad * vecs[GAIN_TWO : GAIN_TWO + 1, :]
            part = inverse * (
                scaled - jnp.mean(scaled, axis=-1, keepdims=True) - zed * jnp.mean(scaled * zed, axis=-1, keepdims=True)
            )
            above = cot[these, :].astype(f32)
            whole = above + part
            mid[these, :] = whole
            branch = whole.astype(bf16)
            normed_two[these, :] = branch
            add = lambda total, value: total + jnp.sum(value, axis=0, keepdims=True)
            return (
                add(gain_sum, grad * zed), add(shift_sum, grad), add(out_sum, branch.astype(f32)), add(cot_sum, above),
            )

        gain_sum, shift_sum, out_sum, cot_sum = lax.fori_loop(0, rows // step, back_two, (zero,) * 4)
        vec_grads[...] = jnp.zeros_like(vec_grads)
        vec_grads[GAIN_TWO : GAIN_TWO + 1, :] = gain_sum
        vec_grads[SHIFT_TWO : SHIFT_TWO + 1, :] = shift_sum
        vec_grads[OUTPUT_BIAS : OUTPUT_BIAS + 1, :] = out_sum
        vec_grads[DOWN_BIAS : DOWN_BIAS + 1, :] = cot_sum
        put_mid = pltpu.make_async_copy(mid, mid_grad_out, loc.at[0])
        put_mid.start()
        put_up(0).wait()
        put_down(0).wait()
        block_out[...] = block_sum[...].astype(bf16)
        up_stage[...] = mul(attended[...], normed_two[...], TN).astype(bf16)
        put_out = pltpu.make_async_copy(up_stage, out_wgrad, loc.at[4])
        put_out.start()
        attended_grad_out[...] = mul(normed_two[...], out_w[...], NT).astype(bf16)
        put_mid.wait()
        put_out.wait()

    pl.run_scoped(
        second_phase,
        V((width, width), bf16),
        V((width, width), bf16),
        V((2, width, width), bf16),
        V((width, rows), bf16),
        V((rows, width), f32),
        V((rows, width), f32),
        V((width, width), bf16),
        V((width, width), bf16),
    )
    swapping.wait_send()
    for ch in range(total):
        g.sent(ch)


def forward(small, own_qkv, own_out, own_up, own_down, x_own, cot, depth=DEPTH, ahead=3):
    rows, width = x_own.shape
    length, half, wide = BOTH * rows, width // BOTH, own_up.shape[1]
    chunks = gather_chunks(own_up.shape, own_down.shape)
    S, V = pltpu.SemaphoreType.DMA, pltpu.VMEM
    anywhere, fast = pl.BlockSpec(memory_space=pl.ANY), pl.BlockSpec(memory_space=pltpu.VMEM)
    shape = jax.ShapeDtypeStruct
    parts = 4 * depth
    return pl.pallas_call(
        functools.partial(forward_kernel, depth, chunks, ahead),
        out_shape=[shape((parts * s.shape[0], s.shape[1]), bf16) for s in (small, own_qkv, own_out, own_up, own_down)]
        + [
            shape((length, width), bf16),
            shape((length, 3 * half), bf16),
            shape((length, half), f32),
            shape((length, half), f32),
            shape((half // HDIM, length, length), bf16),
            shape((rows, width), bf16),
            shape((rows, width), f32),
            shape((rows, width), bf16),
            shape((width, width), bf16),
            shape((width, wide), bf16),
            shape((wide, width), bf16),
            shape((8, width), f32),
            shape((1, wide), f32),
            shape((8, width), f32),
        ],
        in_specs=[anywhere] * 5 + [fast] * 2,
        out_specs=[anywhere] * 10 + [fast, anywhere, fast] + [anywhere] * 3 + [fast] * 3,
        scratch_shapes=[
            V((rows, width), bf16), V((rows, width), bf16), V((1, wide), f32),
            V((rows, width), f32), V((rows, width), bf16),
        ]
        + gather_sems(depth, len(chunks))
        + [S, S, S((half // 128,)), S((half // 128,)), S((6,)), S((2, 2))],
        compiler_params=pltpu.CompilerParams(collective_id=1, has_side_effects=True, vmem_limit_bytes=62 * 2**20),
        name="forward_and_feed",
    )(small, own_qkv, own_out, own_up, own_down, x_own, cot)


def gather_chunks(up_shape, down_shape):
    tall_up, wide = up_shape
    tall_down, width = down_shape
    quarter = tall_down // 4
    return (
        (0, 0, 16, 0, 128, False),
        (1, 0, tall_up, 0, 3 * width // BOTH, False),
    ) + tuple((4, quarter * i, quarter, 0, width, True) for i in range(4)) + ((2, 0, tall_up, 0, width, False),) + tuple(
        (3, 0, tall_up, width * i, width, False) for i in range(wide // width)
    )


def tiled(h, w, body):
    def one(i, _):
        body(pl.ds(pl.multiple_of(i * 16, 16), 16), pl.ds(0, w))
        return 0

    if h == 16:
        one(0, 0)
    else:
        lax.fori_loop(0, h // 16, one, 0)


class Scatter:
    def __init__(self, depth, ring, chunks, grads, outs, bufs, sems, where):
        self.depth, self.ring, self.chunks, self.grads, self.outs = depth, ring, chunks, grads, outs
        self.landed, self.sums, self.near, self.across, self.along, self.mine, self.theirs = bufs
        self.ls, self.gs, self.cs, self.cr, self.xs, self.xr, self.zs, self.zr, self.ys, self.yr = sems
        self.where = where

    def part(self, ref, ch):
        return ref.at[pl.ds(0, self.chunks[ch][2]), pl.ds(0, self.chunks[ch][4])]

    def piece(self, ch, dz, dx, dc):
        t, r0, h, c0, w = self.chunks[ch]
        full = self.grads[t].shape[0] // (4 * self.depth)
        return self.grads[t].at[pl.ds(pl.multiple_of((dz * 4 + dx * 2 + dc) * full + r0, 16), h), pl.ds(c0, w)]

    def copy(self, src, dst, s, r, dz, dx, dc, dy):
        return pltpu.make_async_remote_copy(
            src_ref=src, dst_ref=dst, send_sem=s, recv_sem=r, device_id=(dz * 4 + dx * 2 + dc, dy), device_id_type=MESH
        )

    def zz(self, j):
        return (self.where[0] + j) % self.depth

    def load(self, ch, n):
        z, x, c, y = self.where
        i, j = n // self.depth, n % self.depth
        slot = ch % self.ring
        return pltpu.make_async_copy(
            self.piece(ch, self.zz(j), x if i == 0 else 1 - x, c), self.part(self.sums.at[slot, n], ch), self.ls.at[slot, n]
        )

    def fetch(self, ch):
        t, r0, h, c0, w = self.chunks[ch]
        return pltpu.make_async_copy(
            self.landed.at[ch, :, pl.ds(0, h), pl.ds(0, w)], self.near.at[:, pl.ds(0, h), pl.ds(0, w)], self.gs
        )

    def cmove(self, ch, n):
        z, x, c, y = self.where
        i, j = n // self.depth, n % self.depth
        return self.copy(
            self.piece(ch, self.zz(j), x if i == 0 else 1 - x, 1 - c), self.part(self.landed.at[ch, n], ch),
            self.cs.at[ch, n], self.cr.at[ch, n], z, x, 1 - c, y,
        )

    def xmove(self, ch, j):
        z, x, c, y = self.where
        return self.copy(
            self.part(self.sums.at[ch % self.ring, self.depth + j], ch), self.part(self.across.at[ch, j], ch),
            self.xs.at[ch, j], self.xr.at[ch, j], z, 1 - x, c, y,
        )

    def zmove(self, ch, j):
        z, x, c, y = self.where
        return self.copy(
            self.part(self.sums.at[ch % self.ring, j], ch), self.part(self.along.at[ch, j - 1], ch),
            self.zs.at[ch, j], self.zr.at[ch, j], self.zz(j), x, c, y,
        )

    def ymove(self, ch):
        z, x, c, y = self.where
        return self.copy(
            self.part(self.mine.at[ch], ch), self.part(self.theirs.at[ch], ch), self.ys.at[ch], self.yr.at[ch], z, x, c, 1 - y
        )

    def begin(self, ch):
        for n in range(2 * self.depth):
            self.cmove(ch, n).start()

    def cstage(self, ch):
        t, r0, h, c0, w = self.chunks[ch]
        slot, count = ch % self.ring, 2 * self.depth
        if ch >= self.ring:
            for j in range(self.depth):
                self.xmove(ch - self.ring, j).wait_send()
                if j:
                    self.zmove(ch - self.ring, j).wait_send()
        for n in range(count):
            self.load(ch, n).start()
        for n in range(count):
            self.cmove(ch, n).wait_recv()
        self.fetch(ch).start()
        for n in range(count):
            self.load(ch, n).wait()
        self.fetch(ch).wait()

        def add(r, q):
            self.sums[slot, :, r, q] = self.sums[slot, :, r, q] + self.near[:, r, q]

        tiled(h, w, add)
        for j in range(self.depth):
            self.xmove(ch, j).start()

    def xstage(self, ch):
        t, r0, h, c0, w = self.chunks[ch]
        slot, count = ch % self.ring, self.depth
        for j in range(count):
            self.xmove(ch, j).wait_recv()

        def add(r, q):
            self.sums[slot, 0:count, r, q] = self.sums[slot, 0:count, r, q] + self.across[ch, :, r, q]

        tiled(h, w, add)
        for j in range(1, count):
            self.zmove(ch, j).start()

    def zstage(self, ch):
        t, r0, h, c0, w = self.chunks[ch]
        for j in range(1, self.depth):
            self.zmove(ch, j).wait_recv()

        def add(r, q):
            total = self.sums[ch % self.ring, 0, r, q].astype(f32)
            for j in range(1, self.depth):
                total = total + self.along[ch, j - 1, r, q].astype(f32)
            self.mine[ch, r, q] = total.astype(bf16)

        tiled(h, w, add)
        self.ymove(ch).start()

    def ystage(self, ch):
        t, r0, h, c0, w = self.chunks[ch]
        y = self.where[3]
        self.ymove(ch).wait_recv()
        out = self.outs[t]

        def lay(r, q):
            mine, theirs = self.mine[ch, r, q].astype(f32), self.theirs[ch, r, q].astype(f32)
            there = pl.ds(pl.multiple_of(r0 + r.start, 16), 16)
            if t == 1:
                out[there, pl.ds(2 * c0, w)] = jnp.where(y == 0, mine, theirs)
                out[there, pl.ds(2 * c0 + w, w)] = jnp.where(y == 0, theirs, mine)
            else:
                out[there, pl.ds(c0, w)] = mine + theirs

        tiled(h, w, lay)

    def sent(self, ch):
        for n in range(2 * self.depth):
            self.cmove(ch, n).wait_send()
        if ch + self.ring >= len(self.chunks):
            for j in range(self.depth):
                self.xmove(ch, j).wait_send()
                if j:
                    self.zmove(ch, j).wait_send()
        self.ymove(ch).wait_send()


def scatter_chunks(rows, width, wide):
    part = wide // (width // rows)
    return (
        tuple((3, 0, rows, width * j, width) for j in range(wide // width))
        + ((2, 0, rows, 0, width),)
        + tuple((4, rows * i, rows, 0, width) for i in range(part // rows))
        + tuple((1, 0, rows, width // BOTH * n, width // BOTH) for n in range(3))
        + ((0, 0, 16, 0, 128),)
    )


def backward_kernel(depth, ring, chunks, *refs):
    (
        qkv_in, exact_in, inverse_in, weights_in, attended_grad, normed_in, all_qkv, mid_grad, x_own, vecs,
        out_wgrad, up_wgrad, down_wgrad, vec_grads, up_bgrad,
        input_grad, own_small, own_qkv, own_out, own_up, own_down, landed,
        qkv, grads, m_other, qkv_wgrad, small_grads, sums, near, across, along, mine, theirs,
    ) = refs[:33]
    sems = refs[33:43]
    swap_s, swap_r, m_s, m_r, loc, weight_sem = refs[43:]
    z, x, c, y = place()
    rows, width = x_own.shape
    length, half = BOTH * rows, width // BOTH
    pairs = half // 128
    size = 224
    blocks = length // size
    step = 112
    total = len(chunks)
    s = Scatter(
        depth, ring, chunks, (small_grads, qkv_wgrad, out_wgrad, up_wgrad, down_wgrad), (own_small, own_qkv, own_out, own_up, own_down),
        (landed, sums, near, across, along, mine, theirs), sems, (z, x, c, y),
    )
    greet(z, x, c, y, depth)
    early = total - 4

    def service(n):
        if n + 2 < early:
            s.cstage(n + 2)
        if 0 <= n < early:
            s.xstage(n)
        if 0 <= n - 1 < early:
            s.zstage(n - 1)
        if 0 <= n - 2 < early:
            s.ystage(n - 2)

    def columns(which):
        return pl.ds(pl.multiple_of(which * half, 128), half)

    low_part, high_part = pl.ds(0, rows), pl.ds(rows, rows)
    swapping = s.copy(attended_grad.at[:, columns(1 - y)], grads.at[high_part], swap_s, swap_r, z, x, c, 1 - y)
    swapping.start()
    get_own = pltpu.make_async_copy(attended_grad.at[:, columns(y)], grads.at[low_part], loc.at[0])
    get_own.start()
    get_qkv = pltpu.make_async_copy(qkv_in, qkv, loc.at[1])
    get_qkv.start()
    for ch in range(early):
        s.begin(ch)

    def attention(exact, inverse, key_sum, value_sum, kept):
        get_exact = pltpu.make_async_copy(exact_in, exact, loc.at[2])
        get_inverse = pltpu.make_async_copy(inverse_in, inverse, loc.at[3])
        get_exact.start()
        get_inverse.start()

        def load(turn, head, slot):
            return pltpu.make_async_copy(
                weights_in.at[2 * (turn % pairs) + head, tall(turn // pairs, size)], kept.at[slot, head], weight_sem.at[slot, head]
            )

        for head in range(2):
            load(0, head, 0).start()
        s.cstage(0)
        s.cstage(1)
        for get in (get_own, get_qkv, get_exact, get_inverse):
            get.wait()
        low_lanes = lax.broadcasted_iota(jnp.int32, (size, 128), 1) < HDIM

        def attend(turn, _):
            block, pair, slot = turn // pairs, turn % pairs, turn % 2
            for n, at in enumerate((9, 16, 22)):

                @pl.when(turn == at)
                def _(n=n):
                    service(n)

            @pl.when(turn == pairs * (rows // size))
            def _():
                swapping.wait_recv()

            for head in range(2):
                load(turn, head, slot).wait()

            @pl.when(turn + 1 < blocks * pairs)
            def _():
                for head in range(2):
                    load(turn + 1, head, 1 - slot).start()

            these = tall(block, size)
            at = pl.multiple_of(pair * 128, 128)
            queries = qkv[these, pl.ds(at, 128)] * bf16(HDIM**-0.5)
            keys = qkv[:, pl.ds(half + at, 128)]
            values = qkv[:, pl.ds(2 * half + at, 128)]
            low = (grads[these, pl.ds(at, 128)].astype(f32) * inverse[these, pl.ds(at, 128)]).astype(bf16)
            product = low.astype(f32) * exact[these, pl.ds(at, 128)]
            queries_t, low_t = queries.T, low.T
            query_parts, key_parts, value_parts = [], [], []
            for head in range(2):
                own = low_lanes == (head == 0)
                lanes = slice(HDIM * head, HDIM * head + HDIM)
                masked = jnp.where(own, low, jnp.zeros_like(low))
                prob_grad = mul(masked, values, NT)
                delta = jnp.sum(jnp.where(own, product, 0.0), axis=1, keepdims=True)
                weights = kept[slot, head]
                score_grad = (weights.astype(f32) * (prob_grad - delta)).astype(bf16)
                query_parts.append(mul(score_grad, keys, NN))
                key_parts.append(mul(queries_t[lanes], score_grad, NN))
                value_parts.append(mul(low_t[lanes], weights, NN))
            query_grad = jnp.where(low_lanes, query_parts[0], query_parts[1]) * HDIM**-0.5
            qkv[these, pl.ds(at, 128)] = query_grad.astype(bf16)
            key_part = jnp.concatenate(key_parts, axis=0)
            value_part = jnp.concatenate(value_parts, axis=0)
            key_sum[pair] = jnp.where(block == 0, key_part, key_sum[pair] + key_part)
            value_sum[pair] = jnp.where(block == 0, value_part, value_sum[pair] + value_part)
            return 0

        lax.fori_loop(0, blocks * pairs, attend, 0)

        def finish(pair, _):
            at = pl.multiple_of(pair * 128, 128)
            qkv[:, pl.ds(half + at, 128)] = key_sum[pair].T.astype(bf16)
            qkv[:, pl.ds(2 * half + at, 128)] = value_sum[pair].T.astype(bf16)
            return 0

        lax.fori_loop(0, pairs, finish, 0)

    V = pltpu.VMEM
    pl.run_scoped(
        attention,
        V((length, half), f32),
        V((length, half), f32),
        V((pairs, 128, length), f32),
        V((pairs, 128, length), f32),
        V((2, 2, size, length), bf16),
    )

    def inputs(normed, weight, m_low, m_own, above, rows_in, vec_rows):
        gets = [
            pltpu.make_async_copy(src, dst, loc.at[n])
            for n, (src, dst) in enumerate(((all_qkv, weight), (normed_in, normed), (mid_grad, above), (x_own, rows_in)))
        ]
        for get in gets:
            get.start()
        gets[0].wait()
        m_low[...] = mul(qkv[high_part, :], weight[...], NT).astype(bf16)
        sending = s.copy(m_low, m_other, m_s, m_r, z, x, c, 1 - y)
        sending.start()
        service(3)
        gets[1].wait()
        for n in range(3):
            these = slice(n * half, (n + 1) * half)
            qkv_wgrad[:, these] = mul(normed[...], qkv[:, these], TN).astype(bf16)
            s.begin(early + n)
        m_own[...] = mul(qkv[low_part, :], weight[...], NT)
        service(4)
        service(5)
        ones = jnp.ones((8, length), bf16)
        vec_rows[...] = vec_grads[...]
        for row, n in ((QUERY_BIAS, 0), (VALUE_BIAS, 2)):
            value = mul(ones, qkv[:, n * half : (n + 1) * half], NN)[0:1]
            for other in range(BOTH):
                these = slice(other * half, (other + 1) * half)
                vec_rows[row : row + 1, these] = jnp.where(y == other, value, 0.0)
        service(6)
        service(7)
        gets[2].wait()
        gets[3].wait()
        sending.wait()
        zero = jnp.zeros((1, width), f32)

        def back_one(i, sums_):
            gain_sum, shift_sum = sums_
            these = tall(i, step)
            zed, inverse = normalized(rows_in[these, :].astype(f32))
            grad = m_own[these, :] + m_other[these, :].astype(f32)
            scaled = grad * vecs[GAIN_ONE : GAIN_ONE + 1, :]
            part = inverse * (
                scaled - jnp.mean(scaled, axis=-1, keepdims=True) - zed * jnp.mean(scaled * zed, axis=-1, keepdims=True)
            )
            above[these, :] = above[these, :] + part
            add = lambda so_far, value: so_far + jnp.sum(value, axis=0, keepdims=True)
            return add(gain_sum, grad * zed), add(shift_sum, grad)

        gain_sum, shift_sum = lax.fori_loop(0, rows // step, back_one, (zero, zero))
        put = pltpu.make_async_copy(above, input_grad, loc.at[0])
        put.start()
        vec_rows[GAIN_ONE : GAIN_ONE + 1, :] = gain_sum
        vec_rows[SHIFT_ONE : SHIFT_ONE + 1, :] = shift_sum
        blank = jnp.zeros((6, 128), f32)
        for chip in range(2 * depth):
            eight = vec_rows[:, 128 * chip : 128 * chip + 128]
            for core in range(2):
                at = 256 * (2 * chip + core)
                block = jnp.concatenate([eight, up_bgrad[0:1, at : at + 128], up_bgrad[0:1, at + 128 : at + 256], blank], axis=0)
                small_grads[pl.ds(32 * chip + 16 * core, 16), :] = block.astype(bf16)
        s.begin(total - 1)
        put.wait()

    pl.run_scoped(
        inputs,
        V((length, width), bf16),
        V((width, 3 * half), bf16),
        V((rows, width), bf16),
        V((rows, width), f32),
        V((rows, width), f32),
        V((rows, width), bf16),
        V((8, width), f32),
    )
    s.cstage(early)
    for n in range(early - 1, total + 2):
        if early <= n + 2 < total:
            s.cstage(n + 2)
        if n < total:
            s.xstage(n)
        if n - 1 < total:
            s.zstage(n - 1)
        s.ystage(n - 2)
    swapping.wait_send()
    for ch in range(total):
        s.sent(ch)


def backward(qkv, exact, inverse, weights, attended_grad, normed, all_qkv, mid_grad, x_own, vecs, out_wgrad, up_wgrad, down_wgrad, vec_grads, up_bgrad, depth=DEPTH, ring=4):
    rows, width = x_own.shape
    length, half, wide = BOTH * rows, width // BOTH, up_wgrad.shape[1]
    parts = 4 * depth
    high = width // parts
    chunks = scatter_chunks(high, width, wide)
    total = len(chunks)
    S, V = pltpu.SemaphoreType.DMA, pltpu.VMEM
    anywhere, fast = pl.BlockSpec(memory_space=pl.ANY), pl.BlockSpec(memory_space=pltpu.VMEM)
    shape = jax.ShapeDtypeStruct
    out = pl.pallas_call(
        functools.partial(backward_kernel, depth, ring, chunks),
        out_shape=[
            shape((rows, width), f32), shape((16, 128), f32), shape((high, 3 * width), f32), shape((high, width), f32),
            shape((high, wide), f32), shape((wide // parts, width), f32),
            shape((total, 2 * depth, high, width), bf16),
        ],
        in_specs=[anywhere] * 9 + [fast] + [anywhere] * 3 + [fast] * 2,
        out_specs=[anywhere] + [fast] * 5 + [anywhere],
        scratch_shapes=[
            V((length, 3 * half), bf16), V((length, half), bf16), V((rows, width), bf16), V((width, 3 * half), bf16), V((parts * 16, 128), bf16),
            V((ring, 2 * depth, high, width), bf16), V((2 * depth, high, width), bf16), V((total, depth, high, width), bf16),
            V((total, depth - 1, high, width), bf16), V((total, high, width), bf16), V((total, high, width), bf16),
            S((ring, 2 * depth)), S, S((total, 2 * depth)), S((total, 2 * depth)), S((total, depth)), S((total, depth)),
            S((total, depth)), S((total, depth)), S((total,)), S((total,)),
            S, S, S, S, S((4,)), S((2, 2)),
        ],
        compiler_params=pltpu.CompilerParams(collective_id=2, has_side_effects=True, vmem_limit_bytes=63 * 2**20),
        name="backward_and_sums",
    )(qkv, exact, inverse, weights, attended_grad, normed, all_qkv, mid_grad, x_own, vecs, out_wgrad, up_wgrad, down_wgrad, vec_grads, up_bgrad)
    return out[:6]


def pack_small(vectors, up_bias, c):
    rows = jnp.stack(vectors)
    zero = jnp.zeros_like(rows)
    rows = jnp.concatenate([jnp.where(c == 0, rows, zero), jnp.where(c == 0, zero, rows)], axis=1)
    return jnp.concatenate([rows, up_bias.reshape(2, 128), jnp.zeros((6, 128), rows.dtype)], axis=0)


def fast_device(
    activations, cotangent, query_weight, key_weight, value_weight, output_weight, first_gain, first_shift,
    query_bias, value_bias, output_bias, up_weight, down_weight, second_gain, second_shift, up_bias, down_bias,
):
    _, rows, width = activations.shape
    half = width // 2
    y = lax.axis_index("ctx")
    c = lax.axis_index("fsdp") % 2

    def mine(value):
        return lax.dynamic_slice_in_dim(value, y * half, half, value.ndim - 1)

    small = pack_small(
        (first_gain, first_shift, query_bias, value_bias, output_bias, second_gain, second_shift, down_bias), up_bias, c
    )
    own_qkv = jnp.concatenate([mine(query_weight), mine(key_weight), mine(value_weight)], axis=1)
    x_own = activations[0]
    (
        _, all_qkv, _, _, _, normed_one, qkv, exact, inverse, weights, block_out, mid_grad, attended_grad,
        output_wgrad, up_wgrad, down_wgrad, vec_grads, up_bgrad, vecs,
    ) = forward(small, own_qkv, output_weight, up_weight, down_weight, x_own, cotangent[0])
    input_grad, own_small, own_qkv_grad, own_output, own_up, own_down = backward(
        qkv, exact, inverse, weights, attended_grad, normed_one, all_qkv, mid_grad, x_own, vecs,
        output_wgrad, up_wgrad, down_wgrad, vec_grads, up_bgrad,
    )
    own_vecs = lax.dynamic_slice_in_dim(own_small, c * 64, 64, 1)
    return (
        block_out.reshape(activations.shape),
        input_grad.reshape(activations.shape),
        own_qkv_grad[:, :width],
        own_qkv_grad[:, width : 2 * width],
        own_qkv_grad[:, 2 * width :],
        own_output,
        own_vecs[0],
        own_vecs[1],
        own_vecs[2],
        own_vecs[3],
        own_vecs[4],
        own_up,
        own_down,
        own_vecs[5],
        own_vecs[6],
        own_small[8:10].reshape(-1),
        own_vecs[7],
    )


def solution(mesh):
    fits = mesh.shape["fsdp"] == 4 * DEPTH and mesh.shape["ctx"] == BOTH
    return jax.shard_map(
        fast_device if fits else plain_device,
        mesh=mesh,
        in_specs=(
            P("fsdp", "ctx", None),
            P("fsdp", "ctx", None),
            P("fsdp", None),
            P("fsdp", None),
            P("fsdp", None),
            P("fsdp", None),
            P("fsdp"),
            P("fsdp"),
            P("fsdp"),
            P("fsdp"),
            P("fsdp"),
            P("fsdp", None),
            P("fsdp", None),
            P("fsdp"),
            P("fsdp"),
            P("fsdp"),
            P("fsdp"),
        ),
        out_specs=(
            P("fsdp", "ctx", None),
            P("fsdp", "ctx", None),
            P("fsdp", None),
            P("fsdp", None),
            P("fsdp", None),
            P("fsdp", None),
            P("fsdp"),
            P("fsdp"),
            P("fsdp"),
            P("fsdp"),
            P("fsdp"),
            P("fsdp", None),
            P("fsdp", None),
            P("fsdp"),
            P("fsdp"),
            P("fsdp"),
            P("fsdp"),
        ),
        check_vma=False,
    )
```

```python
import functools

import jax
import jax.numpy as jnp
from jax import lax
from jax.experimental import pallas as pl
from jax.experimental.pallas import tpu as pltpu
from jax.sharding import PartitionSpec as P

HEADS = 16
HDIM = 64
MESH = pl.DeviceIdType.MESH


epsilon = 1e-05


def layer_norm(token_rows, gain, shift):
    centered = token_rows - jnp.mean(token_rows, axis=-1, keepdims=True)
    variance = jnp.mean(centered * centered, axis=-1, keepdims=True)
    return centered * lax.rsqrt(variance + epsilon) * gain + shift


def gelu_act(values_in):
    return jax.nn.gelu(values_in, approximate=True)


def gather_attention(shards):
    return (
        lax.all_gather(shards[0], "fsdp", axis=0, tiled=True),
        lax.all_gather(shards[1], "fsdp", axis=0, tiled=True),
        lax.all_gather(shards[2], "fsdp", axis=0, tiled=True),
        lax.all_gather(shards[3], "fsdp", axis=0, tiled=True),
        lax.all_gather(shards[4], "fsdp", axis=0, tiled=True),
        lax.all_gather(shards[5], "fsdp", axis=0, tiled=True),
        lax.all_gather(shards[6], "fsdp", axis=0, tiled=True),
        lax.all_gather(shards[7], "fsdp", axis=0, tiled=True),
        lax.all_gather(shards[8], "fsdp", axis=0, tiled=True),
    )


def gather_feed(shards):
    return (
        lax.all_gather(shards[0], "fsdp", axis=0, tiled=True),
        lax.all_gather(shards[1], "fsdp", axis=0, tiled=True),
        lax.all_gather(shards[2], "fsdp", axis=0, tiled=True),
        lax.all_gather(shards[3], "fsdp", axis=0, tiled=True),
        lax.all_gather(shards[4], "fsdp", axis=0, tiled=True),
        lax.all_gather(shards[5], "fsdp", axis=0, tiled=True),
    )


def plain_device(
    activations,
    cotangent,
    query_weight,
    key_weight,
    value_weight,
    output_weight,
    first_gain,
    first_shift,
    query_bias,
    value_bias,
    output_bias,
    up_weight,
    down_weight,
    second_gain,
    second_shift,
    up_bias,
    down_bias,
):
    clip_count, local_len, width = activations.shape
    scaling = HDIM ** (-0.5)
    attend_shards = (
        query_weight,
        key_weight,
        value_weight,
        output_weight,
        first_gain,
        first_shift,
        query_bias,
        value_bias,
        output_bias,
    )
    feed_shards = (up_weight, down_weight, second_gain, second_shift, up_bias, down_bias)
    attend_full = gather_attention(attend_shards)
    (
        full_query,
        full_key,
        full_value,
        full_output,
        full_gain_one,
        full_shift_one,
        full_query_bias,
        full_value_bias,
        full_output_bias,
    ) = attend_full
    gain_one = full_gain_one.astype(jnp.float32)
    shift_one = full_shift_one.astype(jnp.float32)
    token_rows = activations.reshape(-1, width).astype(jnp.float32)
    normed_one = layer_norm(token_rows, gain_one, shift_one).astype(jnp.bfloat16)
    queries = (
        jnp.dot(normed_one, full_query, preferred_element_type=jnp.float32)
        + full_query_bias.astype(jnp.float32)
    ).astype(jnp.bfloat16)
    keys_local = jnp.dot(normed_one, full_key, preferred_element_type=jnp.float32).astype(
        jnp.bfloat16
    )
    values_local = (
        jnp.dot(normed_one, full_value, preferred_element_type=jnp.float32)
        + full_value_bias.astype(jnp.float32)
    ).astype(jnp.bfloat16)
    query_heads = queries.reshape(clip_count, local_len, HEADS, HDIM)
    keys_block = keys_local.reshape(clip_count, local_len, width)
    values_block = values_local.reshape(clip_count, local_len, width)
    run_max = jnp.full((clip_count, local_len, HEADS), -1e30, jnp.float32)
    key_piece = lax.all_gather(keys_block, "ctx", axis=1, tiled=True)
    value_piece = lax.all_gather(values_block, "ctx", axis=1, tiled=True)
    key_heads = key_piece.reshape(clip_count, -1, HEADS, HDIM)
    value_heads = value_piece.reshape(clip_count, -1, HEADS, HDIM)
    scores = (
        jnp.einsum("cqhd,ckhd->cqhk", query_heads, key_heads, preferred_element_type=jnp.float32)
        * scaling
    )
    new_max = jnp.maximum(run_max, jnp.max(scores, axis=-1))
    weights = jnp.exp(scores - new_max[..., None])
    run_sum = jnp.sum(weights, axis=-1)
    accum = jnp.einsum(
        "cqhk,ckhd->cqhd",
        weights.astype(jnp.bfloat16),
        value_heads,
        preferred_element_type=jnp.float32,
    )
    run_max, run_sum, accum = (new_max, run_sum, accum)
    attend_exact = accum / run_sum[..., None]
    log_total = run_max + jnp.log(run_sum)
    attended = attend_exact.reshape(-1, width).astype(jnp.bfloat16)
    mid_rows = (
        token_rows
        + jnp.dot(attended, full_output, preferred_element_type=jnp.float32)
        + full_output_bias.astype(jnp.float32)
    )
    feed_full = gather_feed(feed_shards)
    full_up, full_down, full_gain_two, full_shift_two, full_up_bias, full_down_bias = feed_full
    gain_two = full_gain_two.astype(jnp.float32)
    shift_two = full_shift_two.astype(jnp.float32)
    normed_two = layer_norm(mid_rows, gain_two, shift_two).astype(jnp.bfloat16)
    pre_act = jnp.dot(
        normed_two, full_up, preferred_element_type=jnp.float32
    ) + full_up_bias.astype(jnp.float32)
    hidden = gelu_act(pre_act).astype(jnp.bfloat16)
    block_rows = (
        mid_rows
        + jnp.dot(hidden, full_down, preferred_element_type=jnp.float32)
        + full_down_bias.astype(jnp.float32)
    )
    block_out = block_rows.astype(jnp.bfloat16).reshape(activations.shape)
    back_attend = gather_attention(attend_shards)
    back_feed = gather_feed(feed_shards)
    back_query, back_key, back_value, back_output = (
        back_attend[0],
        back_attend[1],
        back_attend[2],
        back_attend[3],
    )
    back_up, back_down = (back_feed[0], back_feed[1])
    cot_rows = cotangent.reshape(-1, width)
    outer_grad = cot_rows.astype(jnp.float32)
    down_wgrad = jnp.einsum("rf,rd->fd", hidden, cot_rows, preferred_element_type=jnp.float32)
    down_bgrad = jnp.sum(outer_grad, axis=0)
    hidden_grad = jnp.einsum("rd,fd->rf", cot_rows, back_down, preferred_element_type=jnp.float32)
    _, gelu_back = jax.vjp(gelu_act, pre_act)
    pre_grad = gelu_back(hidden_grad)[0].astype(jnp.bfloat16)
    up_wgrad = jnp.einsum("rd,rf->df", normed_two, pre_grad, preferred_element_type=jnp.float32)
    up_bgrad = jnp.sum(pre_grad.astype(jnp.float32), axis=0)
    normed_two_grad = jnp.einsum("rf,df->rd", pre_grad, back_up, preferred_element_type=jnp.float32)
    _, norm_two_back = jax.vjp(layer_norm, mid_rows, gain_two, shift_two)
    mid_part, gain_two_grad, shift_two_grad = norm_two_back(normed_two_grad)
    mid_grad = outer_grad + mid_part
    feed_owned = (
        lax.psum_scatter(
            up_wgrad.astype(jnp.bfloat16), "fsdp", scatter_dimension=0, tiled=True
        ).astype(jnp.float32),
        lax.psum_scatter(
            down_wgrad.astype(jnp.bfloat16), "fsdp", scatter_dimension=0, tiled=True
        ).astype(jnp.float32),
        lax.psum_scatter(
            gain_two_grad.astype(jnp.bfloat16), "fsdp", scatter_dimension=0, tiled=True
        ).astype(jnp.float32),
        lax.psum_scatter(
            shift_two_grad.astype(jnp.bfloat16), "fsdp", scatter_dimension=0, tiled=True
        ).astype(jnp.float32),
        lax.psum_scatter(
            up_bgrad.astype(jnp.bfloat16), "fsdp", scatter_dimension=0, tiled=True
        ).astype(jnp.float32),
        lax.psum_scatter(
            down_bgrad.astype(jnp.bfloat16), "fsdp", scatter_dimension=0, tiled=True
        ).astype(jnp.float32),
    )
    feed_done = (
        lax.psum(feed_owned[0].astype(jnp.bfloat16), "ctx").astype(jnp.float32),
        lax.psum(feed_owned[1].astype(jnp.bfloat16), "ctx").astype(jnp.float32),
        lax.psum(feed_owned[2].astype(jnp.bfloat16), "ctx").astype(jnp.float32),
        lax.psum(feed_owned[3].astype(jnp.bfloat16), "ctx").astype(jnp.float32),
        lax.psum(feed_owned[4].astype(jnp.bfloat16), "ctx").astype(jnp.float32),
        lax.psum(feed_owned[5].astype(jnp.bfloat16), "ctx").astype(jnp.float32),
    )
    branch_grad = mid_grad.astype(jnp.bfloat16)
    output_wgrad = jnp.einsum(
        "rd,re->de", attended, branch_grad, preferred_element_type=jnp.float32
    )
    output_bgrad = jnp.sum(branch_grad.astype(jnp.float32), axis=0)
    attended_grad = jnp.einsum(
        "re,de->rd", branch_grad, back_output, preferred_element_type=jnp.float32
    ).astype(jnp.bfloat16)
    grad_heads = attended_grad.reshape(clip_count, local_len, HEADS, HDIM)
    delta = jnp.sum(grad_heads.astype(jnp.float32) * attend_exact, axis=-1)
    keys_whole, values_whole = (
        lax.all_gather(keys_block, "ctx", axis=1, tiled=True),
        lax.all_gather(values_block, "ctx", axis=1, tiled=True),
    )
    key_heads_all = keys_whole.reshape(clip_count, -1, HEADS, HDIM)
    value_heads_all = values_whole.reshape(clip_count, -1, HEADS, HDIM)
    scores_all = (
        jnp.einsum(
            "cqhd,ckhd->cqhk", query_heads, key_heads_all, preferred_element_type=jnp.float32
        )
        * scaling
    )
    probs = jnp.exp(scores_all - log_total[..., None])
    prob_grad = jnp.einsum(
        "cqhd,ckhd->cqhk", grad_heads, value_heads_all, preferred_element_type=jnp.float32
    )
    score_grad = (probs * (prob_grad - delta[..., None])).astype(jnp.bfloat16)
    query_grad = (
        jnp.einsum("cqhk,ckhd->cqhd", score_grad, key_heads_all, preferred_element_type=jnp.float32)
        * scaling
    ).astype(jnp.bfloat16)
    query_grad = query_grad.reshape(-1, width)
    probs_low = probs.astype(jnp.bfloat16)
    key_part = (
        jnp.einsum("cqhk,cqhd->kchd", score_grad, query_heads, preferred_element_type=jnp.float32)
        * scaling
    )
    value_part = jnp.einsum(
        "cqhk,cqhd->kchd", probs_low, grad_heads, preferred_element_type=jnp.float32
    )
    summed = lax.psum_scatter(
        jnp.stack([key_part, value_part], axis=2)
        .reshape(lax.axis_size("ctx") * local_len, clip_count, 2, width)
        .astype(jnp.bfloat16),
        "ctx",
        scatter_dimension=0,
        tiled=True,
    ).astype(jnp.float32)
    key_grad = jnp.transpose(summed[:, :, 0], (1, 0, 2)).reshape(-1, width).astype(jnp.bfloat16)
    value_grad = jnp.transpose(summed[:, :, 1], (1, 0, 2)).reshape(-1, width).astype(jnp.bfloat16)
    query_wgrad = jnp.einsum(
        "rd,re->de", normed_one, query_grad, preferred_element_type=jnp.float32
    )
    key_wgrad = jnp.einsum("rd,re->de", normed_one, key_grad, preferred_element_type=jnp.float32)
    value_wgrad = jnp.einsum(
        "rd,re->de", normed_one, value_grad, preferred_element_type=jnp.float32
    )
    query_bgrad = jnp.sum(query_grad.astype(jnp.float32), axis=0)
    value_bgrad = jnp.sum(value_grad.astype(jnp.float32), axis=0)
    normed_one_grad = (
        jnp.einsum("re,de->rd", query_grad, back_query, preferred_element_type=jnp.float32)
        + jnp.einsum("re,de->rd", key_grad, back_key, preferred_element_type=jnp.float32)
        + jnp.einsum("re,de->rd", value_grad, back_value, preferred_element_type=jnp.float32)
    )
    _, norm_one_back = jax.vjp(layer_norm, token_rows, gain_one, shift_one)
    input_part, gain_one_grad, shift_one_grad = norm_one_back(normed_one_grad)
    input_grad = (mid_grad + input_part).reshape(activations.shape)
    attend_owned = (
        lax.psum_scatter(
            query_wgrad.astype(jnp.bfloat16), "fsdp", scatter_dimension=0, tiled=True
        ).astype(jnp.float32),
        lax.psum_scatter(
            key_wgrad.astype(jnp.bfloat16), "fsdp", scatter_dimension=0, tiled=True
        ).astype(jnp.float32),
        lax.psum_scatter(
            value_wgrad.astype(jnp.bfloat16), "fsdp", scatter_dimension=0, tiled=True
        ).astype(jnp.float32),
        lax.psum_scatter(
            output_wgrad.astype(jnp.bfloat16), "fsdp", scatter_dimension=0, tiled=True
        ).astype(jnp.float32),
        lax.psum_scatter(
            gain_one_grad.astype(jnp.bfloat16), "fsdp", scatter_dimension=0, tiled=True
        ).astype(jnp.float32),
        lax.psum_scatter(
            shift_one_grad.astype(jnp.bfloat16), "fsdp", scatter_dimension=0, tiled=True
        ).astype(jnp.float32),
        lax.psum_scatter(
            query_bgrad.astype(jnp.bfloat16), "fsdp", scatter_dimension=0, tiled=True
        ).astype(jnp.float32),
        lax.psum_scatter(
            value_bgrad.astype(jnp.bfloat16), "fsdp", scatter_dimension=0, tiled=True
        ).astype(jnp.float32),
        lax.psum_scatter(
            output_bgrad.astype(jnp.bfloat16), "fsdp", scatter_dimension=0, tiled=True
        ).astype(jnp.float32),
    )
    attend_done = (
        lax.psum(attend_owned[0].astype(jnp.bfloat16), "ctx").astype(jnp.float32),
        lax.psum(attend_owned[1].astype(jnp.bfloat16), "ctx").astype(jnp.float32),
        lax.psum(attend_owned[2].astype(jnp.bfloat16), "ctx").astype(jnp.float32),
        lax.psum(attend_owned[3].astype(jnp.bfloat16), "ctx").astype(jnp.float32),
        lax.psum(attend_owned[4].astype(jnp.bfloat16), "ctx").astype(jnp.float32),
        lax.psum(attend_owned[5].astype(jnp.bfloat16), "ctx").astype(jnp.float32),
        lax.psum(attend_owned[6].astype(jnp.bfloat16), "ctx").astype(jnp.float32),
        lax.psum(attend_owned[7].astype(jnp.bfloat16), "ctx").astype(jnp.float32),
        lax.psum(attend_owned[8].astype(jnp.bfloat16), "ctx").astype(jnp.float32),
    )
    return (
        block_out,
        input_grad,
        attend_done[0],
        attend_done[1],
        attend_done[2],
        attend_done[3],
        attend_done[4],
        attend_done[5],
        attend_done[6],
        attend_done[7],
        attend_done[8],
        feed_done[0],
        feed_done[1],
        feed_done[2],
        feed_done[3],
        feed_done[4],
        feed_done[5],
    )


def place():
    f = lax.axis_index("fsdp"); y = lax.axis_index("ctx")
    return f // 4, (f // 2) % 2, f % 2, y

def partners(z, x, c, y, depth):
    index = lambda dz, dx, dc: dz * 4 + dx * 2 + dc
    along = [(index((z + k) % depth, x, c), y) for k in range(1, depth)]
    return along + [(index(z, 1 - x, c), y), (index(z, x, 1 - c), y), (index(z, x, c), 1 - y)]


def greet(z, x, c, y, depth):
    barrier = pltpu.get_barrier_semaphore()
    for partner in partners(z, x, c, y, depth):
        pl.semaphore_signal(barrier, inc=1, device_id=partner, device_id_type=MESH)
    pl.semaphore_wait(barrier, depth + 2)


class Gather:
    def __init__(self, depth, chunks, ins, outs, sems, where):
        self.depth, self.chunks, self.ins, self.outs = depth, chunks, ins, outs
        self.zs, self.zr, self.xs, self.xr, self.ys, self.yr, self.cs, self.cr, self.loc = sems
        self.where = where
    def source(self, ch, first, count):
        t, _, _, there, _, w, _ = self.chunks[ch]
        if there is None:
            there = pl.multiple_of(self.where[3] * w, 128)
        return self.ins[t].at[pl.ds(first, count), pl.ds(there, w)]
    def src(self, ch, half):
        _, r0, h, _, _, _, both = self.chunks[ch]
        if not both: return self.source(ch, r0, h)
        h2 = h // 2
        return self.source(ch, pl.multiple_of(r0 + half * h2, 16), h2)
    def dst(self, ch, dz, dx, dc, half):
        t, r0, h, _, c0, w, both = self.chunks[ch]
        full = self.ins[t].shape[0]
        start = (dz * 4 + dx * 2 + dc) * full + r0
        if not both: return self.outs[t].at[pl.ds(pl.multiple_of(start, 16), h), pl.ds(c0, w)]
        h2 = h // 2
        return self.outs[t].at[pl.ds(pl.multiple_of(start + half * h2, 16), h2), pl.ds(c0, w)]
    def copy(self, src, dst, s, r, dz, dx, dc, dy):
        return pltpu.make_async_remote_copy(src_ref=src, dst_ref=dst, send_sem=s, recv_sem=r,
            device_id=(dz * 4 + dx * 2 + dc, dy), device_id_type=MESH)
    def zz(self, j):
        return (self.where[0] - j + self.depth) % self.depth
    def zmove(self, ch, k, recv=False):
        z, x, c, y = self.where
        if recv:
            d = self.dst(ch, self.zz(k), x, c, y)
            return self.copy(d, d, self.zs.at[ch, k], self.zr.at[ch, k], z, x, 1 - c, y)
        return self.copy(self.src(ch, y), self.dst(ch, z, x, c, y), self.zs.at[ch, k], self.zr.at[ch, k], (z + k) % self.depth, x, c, y)
    def xmove(self, ch, j, recv=False):
        z, x, c, y = self.where
        d = self.dst(ch, self.zz(j), 1 - x if recv else x, c, y)
        s = self.src(ch, y) if (j == 0 and not recv) else d
        return self.copy(s, d, self.xs.at[ch, j], self.xr.at[ch, j], z, 1 - x, c, y)
    def ymove(self, ch, i, j, recv=False):
        z, x, c, y = self.where
        d = self.dst(ch, self.zz(j), x if i == 0 else 1 - x, c, 1 - y if recv else y)
        n = i * self.depth + j
        return self.copy(d, d, self.ys.at[ch, n], self.yr.at[ch, n], z, x, c, 1 - y)
    def cmove(self, ch, i, j, other, recv=False):
        z, x, c, y = self.where
        half = 1 - y if other else y
        d = self.dst(ch, self.zz(j), x if i == 0 else 1 - x, 1 - c if recv else c, half)
        s = self.src(ch, half) if (i == 0 and j == 0 and not recv) else d
        n = (i * self.depth + j) + (2 * self.depth if other else 0)
        return self.copy(s, d, self.cs.at[ch, n], self.cr.at[ch, n], z, x, 1 - c, y)
    def own(self, ch):
        z, x, c, y = self.where
        t, r0, h, _, c0, w, both = self.chunks[ch]
        full = self.ins[t].shape[0]
        there = self.outs[t].at[pl.ds(pl.multiple_of((z * 4 + x * 2 + c) * full + r0, 16), h), pl.ds(c0, w)]
        return pltpu.make_async_copy(self.source(ch, r0, h), there, self.loc.at[ch])
    def begin(self, ch):
        for k in range(1, self.depth): self.zmove(ch, k).start()
        self.xmove(ch, 0).start()
        self.cmove(ch, 0, 0, False).start()
        if self.chunks[ch][6]: self.cmove(ch, 0, 0, True).start()
        self.own(ch).start()
    def zstage(self, ch):
        for k in range(1, self.depth):
            self.zmove(ch, k, True).wait_recv()
            self.xmove(ch, k).start()
            if self.chunks[ch][6]: self.ymove(ch, 0, k).start()
            self.cmove(ch, 0, k, False).start()
    def xstage(self, ch):
        for j in range(self.depth):
            self.xmove(ch, j, True).wait_recv()
            if self.chunks[ch][6]: self.ymove(ch, 1, j).start()
            self.cmove(ch, 1, j, False).start()
    def ystage(self, ch):
        if not self.chunks[ch][6]: return
        for i in range(2):
            for j in range(1 - i, self.depth):
                self.ymove(ch, i, j, True).wait_recv()
                self.cmove(ch, i, j, True).start()
    def arrived(self, ch):
        for i in range(2):
            for j in range(self.depth):
                self.cmove(ch, i, j, False, True).wait_recv()
                if self.chunks[ch][6]: self.cmove(ch, i, j, True, True).wait_recv()
        self.own(ch).wait()
    def sent(self, ch):
        both = self.chunks[ch][6]
        for k in range(1, self.depth): self.zmove(ch, k).wait_send()
        for j in range(self.depth): self.xmove(ch, j).wait_send()
        for i in range(2):
            for j in range(self.depth):
                self.cmove(ch, i, j, False).wait_send()
                if both:
                    self.cmove(ch, i, j, True).wait_send()
                    if i or j: self.ymove(ch, i, j).wait_send()

def gather_sems(depth, n):
    S = pltpu.SemaphoreType.DMA
    return [S((n, depth)), S((n, depth)), S((n, depth)), S((n, depth)), S((n, 2 * depth)), S((n, 2 * depth)), S((n, 4 * depth)), S((n, 4 * depth)), S((n,))]


DEPTH, BOTH = 4, 2
f32, bf16 = jnp.float32, jnp.bfloat16
NT = (((1,), (1,)), ((), ()))
NN = (((1,), (0,)), ((), ()))
TN = (((0,), (0,)), ((), ()))
SQRT_2_PI = 0.7978845608028654


def mul(a, b, dims):
    return lax.dot_general(a, b, dims, preferred_element_type=f32)


def tall(i, size):
    return pl.ds(pl.multiple_of(i * size, 16), size)


def normalized(rows):
    centered = rows - jnp.mean(rows, axis=-1, keepdims=True)
    inverse = lax.rsqrt(jnp.mean(centered * centered, axis=-1, keepdims=True) + epsilon)
    return centered * inverse, inverse


def tiled(h, w, body):
    def one(i, _):
        body(pl.ds(pl.multiple_of(i * 16, 16), 16), pl.ds(0, w))
        return 0

    if h == 16:
        one(0, 0)
    else:
        lax.fori_loop(0, h // 16, one, 0)


class Scatter:
    def __init__(self, depth, ring, chunks, grads, outs, bufs, sems, where):
        self.depth, self.ring, self.chunks, self.grads, self.outs = depth, ring, chunks, grads, outs
        self.landed, self.sums, self.near, self.across, self.along, self.mine, self.theirs, self.stage = bufs
        self.ls, self.gs, self.cs, self.cr, self.xs, self.xr, self.zs, self.zr, self.ys, self.yr, self.ps = sems
        self.where = where

    def part(self, ref, ch):
        return ref.at[pl.ds(0, self.chunks[ch][2]), pl.ds(0, self.chunks[ch][4])]

    def piece(self, ch, dz, dx, dc):
        t, r0, h, c0, w = self.chunks[ch]
        full = self.grads[t].shape[0] // (4 * self.depth)
        return self.grads[t].at[pl.ds(pl.multiple_of((dz * 4 + dx * 2 + dc) * full + r0, 16), h), pl.ds(c0, w)]

    def copy(self, src, dst, s, r, dz, dx, dc, dy):
        return pltpu.make_async_remote_copy(
            src_ref=src, dst_ref=dst, send_sem=s, recv_sem=r, device_id=(dz * 4 + dx * 2 + dc, dy), device_id_type=MESH
        )

    def zz(self, j):
        return (self.where[0] + j) % self.depth

    def load(self, ch, n):
        z, x, c, y = self.where
        i, j = n // self.depth, n % self.depth
        slot = ch % self.ring
        return pltpu.make_async_copy(
            self.piece(ch, self.zz(j), x if i == 0 else 1 - x, c), self.part(self.sums.at[slot, n], ch), self.ls.at[slot, n]
        )

    def fetch(self, ch):
        t, r0, h, c0, w = self.chunks[ch]
        return pltpu.make_async_copy(
            self.landed.at[ch, :, pl.ds(0, h), pl.ds(0, w)], self.near.at[:, pl.ds(0, h), pl.ds(0, w)], self.gs
        )

    def cmove(self, ch, n):
        z, x, c, y = self.where
        i, j = n // self.depth, n % self.depth
        return self.copy(
            self.piece(ch, self.zz(j), x if i == 0 else 1 - x, 1 - c), self.part(self.landed.at[ch, n], ch),
            self.cs.at[ch, n], self.cr.at[ch, n], z, x, 1 - c, y,
        )

    def xmove(self, ch, j):
        z, x, c, y = self.where
        return self.copy(
            self.part(self.sums.at[ch % self.ring, self.depth + j], ch), self.part(self.across.at[ch, j], ch),
            self.xs.at[ch, j], self.xr.at[ch, j], z, 1 - x, c, y,
        )

    def zmove(self, ch, j):
        z, x, c, y = self.where
        return self.copy(
            self.part(self.sums.at[ch % self.ring, j], ch), self.part(self.along.at[ch, j - 1], ch),
            self.zs.at[ch, j], self.zr.at[ch, j], self.zz(j), x, c, y,
        )

    def ymove(self, ch):
        z, x, c, y = self.where
        return self.copy(
            self.part(self.mine.at[ch], ch), self.part(self.theirs.at[ch], ch), self.ys.at[ch], self.yr.at[ch], z, x, c, 1 - y
        )

    def begin(self, ch):
        for n in range(2 * self.depth):
            self.cmove(ch, n).start()

    def cstage(self, ch):
        t, r0, h, c0, w = self.chunks[ch]
        slot, count = ch % self.ring, 2 * self.depth
        if ch >= self.ring:
            for j in range(self.depth):
                self.xmove(ch - self.ring, j).wait_send()
                if j:
                    self.zmove(ch - self.ring, j).wait_send()
        for n in range(count):
            self.load(ch, n).start()
        for n in range(count):
            self.cmove(ch, n).wait_recv()
        self.fetch(ch).start()
        for n in range(count):
            self.load(ch, n).wait()
        self.fetch(ch).wait()

        def add(r, q):
            self.sums[slot, :, r, q] = self.sums[slot, :, r, q] + self.near[:, r, q]

        tiled(h, w, add)
        for j in range(self.depth):
            self.xmove(ch, j).start()

    def xstage(self, ch):
        t, r0, h, c0, w = self.chunks[ch]
        slot, count = ch % self.ring, self.depth
        for j in range(count):
            self.xmove(ch, j).wait_recv()

        def add(r, q):
            self.sums[slot, 0:count, r, q] = self.sums[slot, 0:count, r, q] + self.across[ch, :, r, q]

        tiled(h, w, add)
        for j in range(1, count):
            self.zmove(ch, j).start()

    def zstage(self, ch):
        t, r0, h, c0, w = self.chunks[ch]
        for j in range(1, self.depth):
            self.zmove(ch, j).wait_recv()

        def add(r, q):
            total = self.sums[ch % self.ring, 0, r, q].astype(f32)
            for j in range(1, self.depth):
                total = total + self.along[ch, j - 1, r, q].astype(f32)
            self.mine[ch, r, q] = total.astype(bf16)

        tiled(h, w, add)
        self.ymove(ch).start()

    def put(self, ch):
        t, r0, h, c0, w = self.chunks[ch]
        split = 1 <= t <= 3
        there = pl.ds(0, 2 * w) if split else pl.ds(c0, w)
        return pltpu.make_async_copy(
            self.stage.at[ch % 2, pl.ds(0, h), pl.ds(0, 2 * w if split else w)], self.outs[t].at[pl.ds(r0, h), there], self.ps.at[ch % 2]
        )

    def ystage(self, ch):
        t, r0, h, c0, w = self.chunks[ch]
        y = self.where[3]
        self.ymove(ch).wait_recv()
        if ch >= 2:
            self.put(ch - 2).wait()

        def lay(r, q):
            mine, theirs = self.mine[ch, r, q].astype(f32), self.theirs[ch, r, q].astype(f32)
            if 1 <= t <= 3:
                self.stage[ch % 2, r, 0:w] = jnp.where(y == 0, mine, theirs)
                self.stage[ch % 2, r, w : 2 * w] = jnp.where(y == 0, theirs, mine)
            else:
                self.stage[ch % 2, r, q] = mine + theirs

        tiled(h, w, lay)
        self.put(ch).start()

    def sent(self, ch):
        for n in range(2 * self.depth):
            self.cmove(ch, n).wait_send()
        if ch + self.ring >= len(self.chunks):
            for j in range(self.depth):
                self.xmove(ch, j).wait_send()
                if j:
                    self.zmove(ch, j).wait_send()
        self.ymove(ch).wait_send()
        if ch + 2 >= len(self.chunks):
            self.put(ch).wait()


GAIN_ONE, SHIFT_ONE, QUERY_BIAS, VALUE_BIAS, OUTPUT_BIAS, GAIN_TWO, SHIFT_TWO, DOWN_BIAS = range(8)
STEP = 112
SIZE = 224


def layer_kernel(depth, ring, gathers, scatters, *refs):
    (
        small, own_query, own_key, own_value, own_out, own_up, own_down, x_own, cotangent,
        block_out, input_grad, own_small, own_query_grad, own_key_grad, own_value_grad, own_out_grad, own_up_grad, own_down_grad,
        all_small, all_qkv, all_out, all_up, all_down, normed_kept, qkv_kept, exact_kept, inverse_kept, weights_kept,
        mid_grad_kept, attended_grad_kept, out_wgrad, up_wgrad, down_wgrad, landed,
        from_y, attended, grads, vecs, up_bias, vec_grads, up_bgrad, qkv_wgrad, small_grads,
    ) = refs[:43]
    gather_sems_, scatter_sems_ = refs[43:52], refs[52:63]
    entered, swap_s, swap_r, att_s, att_r, grad_s, grad_r, m_s, m_r, loc, keep_sem, pair_sem = refs[63:]
    z, x, c, y = place()
    rows, width = x_own.shape
    length, half = BOTH * rows, width // BOTH
    pairs = half // 128
    wide = up_bias.shape[1]
    tiles = wide // width
    V = pltpu.VMEM
    low_part, high_part = pl.ds(0, rows), pl.ds(rows, rows)

    def columns(which):
        return pl.ds(pl.multiple_of(which * half, 128), half)

    g = Gather(
        depth, gathers, (small, own_query, own_key, own_value, own_out, own_up, own_down),
        (all_small, all_qkv, all_qkv, all_qkv, all_out, all_up, all_down), gather_sems_, (z, x, c, y),
    )
    greet(z, x, c, y, depth)
    swapping = g.copy(x_own, from_y, swap_s, swap_r, z, x, c, 1 - y)
    count = len(gathers)
    ahead = 4

    def along(ch):
        g.zstage(ch)
        if ch + ahead < count:
            g.begin(ch + ahead)

    for ch in range(ahead):
        g.begin(ch)
        if ch == 0:
            swapping.start()
    along(0)
    g.xstage(0)
    along(1)
    along(2)
    g.xstage(1)

    def first_phase(small_v, normed, qkv, exact, inverse, weight, values_ones, kept, exact_low, x_rows):
        get_x = pltpu.make_async_copy(x_own, x_rows, loc.at[1])
        get_x.start()
        g.arrived(0)
        get = pltpu.make_async_copy(all_small, small_v, loc.at[0])
        get.start()
        get.wait()
        for chip in range(2 * depth):
            one, two = small_v[pl.ds(32 * chip, 16), :].astype(f32), small_v[pl.ds(32 * chip + 16, 16), :].astype(f32)
            vecs[0:8, 128 * chip : 128 * chip + 128] = one[0:8] + two[0:8]
            for core, part in enumerate((one, two)):
                for n in range(2):
                    at = (2 * chip + core) * 256 + 128 * n
                    up_bias[0:1, at : at + 128] = part[8 + n : 9 + n]
        get_x.wait()

        def norm_one(source, first):
            gain, shift = vecs[GAIN_ONE : GAIN_ONE + 1, :], vecs[SHIFT_ONE : SHIFT_ONE + 1, :]

            def one(i, _):
                value = normalized(source[tall(i, STEP), :].astype(f32))[0]
                normed[pl.ds(pl.multiple_of(first + i * STEP, 16), STEP), :] = (value * gain + shift).astype(bf16)
                return 0

            lax.fori_loop(0, rows // STEP, one, 0)

        def project(first):
            these = pl.ds(first, rows)
            for n, bias in enumerate((QUERY_BIAS, None, VALUE_BIAS)):
                value = mul(normed[these, :], weight[:, n * half : (n + 1) * half], NN)
                if bias is not None:
                    value = value + vecs[bias : bias + 1, columns(y)]
                qkv[these, n * half : (n + 1) * half] = value.astype(bf16)

        norm_one(x_rows, 0)
        along(3)
        g.xstage(2)
        g.xstage(3)
        for ch in (1, 2, 3):
            g.arrived(ch)
        get = pltpu.make_async_copy(all_qkv, weight, loc.at[0])
        get.start()
        get.wait()
        project(0)
        along(4)
        swapping.wait_recv()
        norm_one(from_y, rows)
        project(rows)
        put_normed = pltpu.make_async_copy(normed, normed_kept, loc.at[1])
        put_qkv = pltpu.make_async_copy(qkv, qkv_kept, loc.at[2])
        put_normed.start()
        put_qkv.start()
        low_lanes = lax.broadcasted_iota(jnp.int32, (rows, 128), 1) < HDIM

        def keep(pair, block, head, slot):
            return pltpu.make_async_copy(
                kept.at[slot, head], weights_kept.at[2 * pair + head, tall(block, rows)], keep_sem.at[slot, head]
            )

        def keep_pair(pair):
            these = pl.ds(pl.multiple_of(pair * 128, 128), 128)
            return (
                pltpu.make_async_copy(exact.at[:, these], exact_kept.at[:, these], pair_sem.at[0, pair]),
                pltpu.make_async_copy(inverse.at[:, these], inverse_kept.at[:, these], pair_sem.at[1, pair]),
            )

        def send(pair):
            at = pl.multiple_of(pair * 128, 128)
            there = pl.multiple_of(y * half + at, 128)
            return g.copy(
                exact_low.at[:, pl.ds(at, 128)], attended.at[:, pl.ds(there, 128)], att_s.at[pair], att_r.at[pair], z, x, c, 1 - y
            )

        values_ones[:, 128:] = jnp.ones((length, 128), bf16)
        services = (
            (lambda: g.xstage(4),),
            (lambda: along(5),),
            (lambda: along(6), lambda: g.xstage(5), lambda: g.ystage(4)),
            (lambda: along(7), lambda: g.xstage(6), lambda: g.ystage(5)),
            (lambda: along(8), lambda: g.xstage(7), lambda: g.ystage(6)),
            (lambda: g.ystage(7),),
            (lambda: g.xstage(8), lambda: along(9)),
            (lambda: g.xstage(9),),
        )

        def attend(turn, _):
            pair = turn // 2
            slot = turn % 2
            block = 1 - slot
            for n, todo in enumerate(services):

                @pl.when(turn == n)
                def _(todo=todo):
                    for do in todo:
                        do()

            @pl.when(turn > 1)
            def _():
                for head in range(2):
                    keep(0, 0, head, slot).wait()

            at = pl.multiple_of(pair * 128, 128)

            @pl.when(slot == 0)
            def _():
                values_ones[:, :128] = qkv[:, pl.ds(2 * half + at, 128)]

            these = tall(block, rows)
            queries = qkv[these, pl.ds(at, 128)] * bf16(HDIM**-0.5)
            keys = qkv[:, pl.ds(half + at, 128)]
            values = values_ones[...]
            parts = []
            for head in range(2):
                masked = jnp.where(low_lanes == (head == 0), queries, jnp.zeros_like(queries))
                scores = mul(masked, keys, NT)
                top = jnp.max(scores, axis=1, keepdims=True)
                weights = jnp.exp(scores - top).astype(bf16)
                kept[slot, head] = weights
                summed = mul(weights, values, NN)
                parts.append((summed[:, :128], 1.0 / summed[:, 128:]))
            (low, low_inverse), (high, high_inverse) = parts
            scale = jnp.where(low_lanes, low_inverse, high_inverse)
            value = jnp.where(low_lanes, low, high) * scale
            exact[these, pl.ds(at, 128)] = value
            inverse[these, pl.ds(at, 128)] = scale
            for head in range(2):
                keep(pair, block, head, slot).start()

            @pl.when(slot == 0)
            def _():
                exact_low[:, pl.ds(at, 128)] = value.astype(bf16)
                send(pair).start()

            @pl.when(slot == 1)
            def _():
                attended[:, pl.ds(pl.multiple_of(y * half + at, 128), 128)] = value.astype(bf16)
                for put in keep_pair(pair):
                    put.start()

            return 0

        lax.fori_loop(0, 2 * pairs, attend, 0)
        put_normed.wait()
        put_qkv.wait()
        for pair in range(pairs):
            for put in keep_pair(pair):
                put.wait()
        for slot in range(2):
            for head in range(2):
                keep(0, 0, head, slot).wait()
        for pair in range(pairs):
            send(pair).wait()
        swapping.wait_send()

    pl.run_scoped(
        first_phase,
        V(all_small.shape, bf16),
        V((length, width), bf16),
        V((length, 3 * half), bf16),
        V((length, half), f32),
        V((length, half), f32),
        V((width, 3 * half), bf16),
        V((length, 256), bf16),
        V((2, 2, rows, length), bf16),
        V((rows, half), bf16),
        V((rows, width), bf16),
    )

    def rest(sums, near, across, along_z, mine, theirs, stage):
        for partner in partners(z, x, c, y, depth):
            pl.semaphore_signal(entered, inc=1, device_id=partner, device_id_type=MESH)
        s = Scatter(
            depth, ring, scatters, (small_grads, qkv_wgrad, qkv_wgrad, qkv_wgrad, out_wgrad, up_wgrad, down_wgrad),
            (own_small, own_query_grad, own_key_grad, own_value_grad, own_out_grad, own_up_grad, own_down_grad),
            (landed, sums, near, across, along_z, mine, theirs, stage), scatter_sems_, (z, x, c, y),
        )
        total = len(scatters)
        early = total - 4

        def service(n):
            if n + 2 < early:
                s.cstage(n + 2)
            s.xstage(n)
            if n >= 1:
                s.zstage(n - 1)
            if n >= 2:
                s.ystage(n - 2)

        def feed_phase(up_w, down_w, block_sum, normed_grad, up_stage, down_stage, mid, normed_two, cot):
            def get_down(j, slot):
                return pltpu.make_async_copy(
                    all_down.at[pl.ds(pl.multiple_of(j * width, 16), width)], down_w.at[slot], loc.at[1 + slot]
                )

            def get_up(j, slot):
                return pltpu.make_async_copy(
                    all_up.at[:, pl.ds(pl.multiple_of(j * width, 128), width)], up_w.at[slot], loc.at[3 + slot]
                )

            def put_up(j):
                return pltpu.make_async_copy(up_stage, up_wgrad.at[:, pl.ds(pl.multiple_of(j * width, 128), width)], loc.at[5])

            def put_down(j):
                return pltpu.make_async_copy(down_stage, down_wgrad.at[pl.ds(pl.multiple_of(j * width, 16), width)], loc.at[6])

            get_cot = pltpu.make_async_copy(cotangent, cot, loc.at[0])
            get_x = pltpu.make_async_copy(x_own, normed_two, loc.at[7])
            get_cot.start()
            get_x.start()
            g.arrived(8)
            get_out = pltpu.make_async_copy(all_out, down_w.at[1], loc.at[2])
            get_out.start()
            for ch in range(4, 8):
                g.arrived(ch)
            get_down(0, 0).start()
            get_out.wait()
            mid[...] = mul(attended[...], down_w[1], NN)
            along(10)
            g.arrived(9)
            get_up(0, 0).start()
            get_x.wait()

            def norm_two(i, _):
                these = tall(i, STEP)
                value = mid[these, :] + vecs[OUTPUT_BIAS : OUTPUT_BIAS + 1, :] + normed_two[these, :].astype(f32)
                mid[these, :] = value
                value = normalized(value)[0] * vecs[GAIN_TWO : GAIN_TWO + 1, :] + vecs[SHIFT_TWO : SHIFT_TWO + 1, :]
                normed_two[these, :] = value.astype(bf16)
                return 0

            lax.fori_loop(0, rows // STEP, norm_two, 0)
            block_sum[...] = jnp.zeros_like(block_sum)
            normed_grad[...] = jnp.zeros_like(normed_grad)
            get_cot.wait()

            def begin_up(j):
                s.begin(j)

            at_start = (
                (lambda: None,),
                (lambda: s.begin(0),),
                (lambda: s.begin(1),),
                (lambda: s.begin(2),),
            )
            midway = (
                (lambda: g.xstage(10), lambda: along(11), lambda: g.arrived(10)),
                (
                    lambda: g.xstage(11), lambda: along(12), lambda: g.arrived(11),
                    lambda: pl.semaphore_wait(entered, depth + 2), lambda: s.cstage(0),
                ),
                (lambda: g.xstage(12), lambda: g.arrived(12), lambda: s.cstage(1), lambda: s.xstage(0)),
                (lambda: s.cstage(2), lambda: s.xstage(1), lambda: s.zstage(0)),
            )

            def feed(j, _):
                slot = j % 2

                @pl.when(j > 0)
                def _():
                    put_up(0).wait()
                    put_down(0).wait()

                for n, todo in enumerate(at_start):

                    @pl.when(j == n)
                    def _(todo=todo):
                        for do in todo:
                            do()

                get_down(j, slot).wait()

                @pl.when(j + 1 < tiles)
                def _():
                    get_down(j + 1, 1 - slot).start()

                get_up(j, slot).wait()
                cols = pl.ds(pl.multiple_of(j * width, 128), width)
                u = mul(normed_two[...], up_w[slot], NN) + up_bias[0:1, cols]
                hidden_grad = mul(cot[...], down_w[slot], NT)
                square = u * u
                gate = 0.5 + 0.5 * jnp.tanh(u * (SQRT_2_PI + (SQRT_2_PI * 0.044715) * square))
                hidden = (u * gate).astype(bf16)
                slope = gate + (u * (gate - gate * gate)) * (2 * SQRT_2_PI + (6 * SQRT_2_PI * 0.044715) * square)
                pre_grad = (hidden_grad * slope).astype(bf16)
                block_sum[...] += mul(hidden, down_w[slot], NN)
                for n, todo in enumerate(midway):

                    @pl.when(j == n)
                    def _(todo=todo):
                        for do in todo:
                            do()

                @pl.when(j + 1 < tiles)
                def _():
                    get_up(j + 1, 1 - slot).start()

                down_stage[...] = mul(hidden, cot[...], TN).astype(bf16)
                up_stage[...] = mul(normed_two[...], pre_grad, TN).astype(bf16)
                up_bgrad[0:1, cols] = jnp.sum(pre_grad.astype(f32), axis=0, keepdims=True)
                normed_grad[...] += mul(pre_grad, up_w[slot], NT)
                put_up(j).start()
                put_down(j).start()
                return 0

            lax.fori_loop(0, tiles, feed, 0)
            get_out = pltpu.make_async_copy(all_out, down_w.at[1], loc.at[2])
            get_out.start()
            zero = jnp.zeros((1, width), f32)

            def back_two(i, so_far):
                gain_sum, shift_sum, out_sum, cot_sum = so_far
                these = tall(i, STEP)
                rows_in = mid[these, :]
                block_sum[these, :] = block_sum[these, :] + rows_in + vecs[DOWN_BIAS : DOWN_BIAS + 1, :]
                zed, inverse = normalized(rows_in)
                grad = normed_grad[these, :]
                scaled = grad * vecs[GAIN_TWO : GAIN_TWO + 1, :]
                part = inverse * (
                    scaled - jnp.mean(scaled, axis=-1, keepdims=True) - zed * jnp.mean(scaled * zed, axis=-1, keepdims=True)
                )
                above = cot[these, :].astype(f32)
                whole = above + part
                mid[these, :] = whole
                branch = whole.astype(bf16)
                normed_two[these, :] = branch
                cot[these, :] = block_sum[these, :].astype(bf16)
                add = lambda total_, value: total_ + jnp.sum(value, axis=0, keepdims=True)
                return (
                    add(gain_sum, grad * zed), add(shift_sum, grad), add(out_sum, branch.astype(f32)), add(cot_sum, above),
                )

            gain_sum, shift_sum, out_sum, cot_sum = lax.fori_loop(0, rows // STEP, back_two, (zero,) * 4)
            vec_grads[...] = jnp.zeros_like(vec_grads)
            vec_grads[GAIN_TWO : GAIN_TWO + 1, :] = gain_sum
            vec_grads[SHIFT_TWO : SHIFT_TWO + 1, :] = shift_sum
            vec_grads[OUTPUT_BIAS : OUTPUT_BIAS + 1, :] = out_sum
            vec_grads[DOWN_BIAS : DOWN_BIAS + 1, :] = cot_sum
            put_mid = pltpu.make_async_copy(mid, mid_grad_kept, loc.at[0])
            put_block = pltpu.make_async_copy(cot, block_out, loc.at[7])
            put_mid.start()
            put_block.start()
            put_up(0).wait()
            put_down(0).wait()
            for ch in range(3, 3 + 1 + 4):
                s.begin(ch)
            get_out.wait()
            down_w[0, low_part, :] = mul(normed_two[...], down_w[1], NT).astype(bf16)
            put_grad = pltpu.make_async_copy(down_w.at[0, low_part], attended_grad_kept, loc.at[1])
            put_grad.start()
            put_grad.wait()
            s.copy(attended_grad_kept.at[:, columns(1 - y)], grads.at[high_part], grad_s, grad_r, z, x, c, 1 - y).start()
            get_own = pltpu.make_async_copy(attended_grad_kept.at[:, columns(y)], grads.at[low_part], loc.at[1])
            get_own.start()
            up_stage[...] = mul(attended[...], normed_two[...], TN).astype(bf16)
            put_out = pltpu.make_async_copy(up_stage, out_wgrad, loc.at[5])
            put_out.start()
            s.cstage(3)
            s.cstage(4)
            s.xstage(2)
            s.zstage(1)
            s.ystage(0)
            get_own.wait()
            put_mid.wait()
            put_block.wait()
            put_out.wait()
            s.begin(8)

        pl.run_scoped(
            feed_phase,
            V((2, width, width), bf16),
            V((2, width, width), bf16),
            V((rows, width), f32),
            V((rows, width), f32),
            V((width, width), bf16),
            V((width, width), bf16),
            V((rows, width), f32),
            V((rows, width), bf16),
            V((rows, width), bf16),
        )

        def back_phase(qkv):
            get_qkv = pltpu.make_async_copy(qkv_kept, qkv, loc.at[1])
            get_qkv.start()

            def attention(exact, inverse, key_sum, value_sum, kept):
                get_exact = pltpu.make_async_copy(exact_kept, exact, loc.at[2])
                get_inverse = pltpu.make_async_copy(inverse_kept, inverse, loc.at[3])
                get_exact.start()
                get_inverse.start()
                blocks = length // SIZE

                def load(turn, head, slot):
                    return pltpu.make_async_copy(
                        weights_kept.at[2 * (turn % pairs) + head, tall(turn // pairs, SIZE)], kept.at[slot, head],
                        keep_sem.at[slot, head],
                    )

                for head in range(2):
                    load(0, head, 0).start()
                for get in (get_qkv, get_exact, get_inverse):
                    get.wait()
                low_lanes = lax.broadcasted_iota(jnp.int32, (SIZE, 128), 1) < HDIM

                def attend(turn, _):
                    block, pair, slot = turn // pairs, turn % pairs, turn % 2
                    for n, at in ((3, 4), (4, 10), (5, 16), (6, 22)):

                        @pl.when(turn == at)
                        def _(n=n):
                            service(n)

                    @pl.when(turn == pairs * (rows // SIZE))
                    def _():
                        s.copy(attended_grad_kept.at[:, columns(1 - y)], grads.at[high_part], grad_s, grad_r, z, x, c, 1 - y).wait_recv()

                    for head in range(2):
                        load(turn, head, slot).wait()

                    @pl.when(turn + 1 < blocks * pairs)
                    def _():
                        for head in range(2):
                            load(turn + 1, head, 1 - slot).start()

                    these = tall(block, SIZE)
                    at = pl.multiple_of(pair * 128, 128)
                    queries = qkv[these, pl.ds(at, 128)] * bf16(HDIM**-0.5)
                    keys = qkv[:, pl.ds(half + at, 128)]
                    values = qkv[:, pl.ds(2 * half + at, 128)]
                    low = (grads[these, pl.ds(at, 128)].astype(f32) * inverse[these, pl.ds(at, 128)]).astype(bf16)
                    product = low.astype(f32) * exact[these, pl.ds(at, 128)]
                    queries_t, low_t = queries.T, low.T
                    query_parts, key_parts, value_parts = [], [], []
                    for head in range(2):
                        own = low_lanes == (head == 0)
                        lanes = slice(HDIM * head, HDIM * head + HDIM)
                        masked = jnp.where(own, low, jnp.zeros_like(low))
                        prob_grad = mul(masked, values, NT)
                        delta = jnp.sum(jnp.where(own, product, 0.0), axis=1, keepdims=True)
                        weights = kept[slot, head]
                        score_grad = (weights.astype(f32) * (prob_grad - delta)).astype(bf16)
                        query_parts.append(mul(score_grad, keys, NN))
                        key_parts.append(mul(queries_t[lanes], score_grad, NN))
                        value_parts.append(mul(low_t[lanes], weights, NN))
                    query_grad = jnp.where(low_lanes, query_parts[0], query_parts[1]) * HDIM**-0.5
                    qkv[these, pl.ds(at, 128)] = query_grad.astype(bf16)
                    key_part = jnp.concatenate(key_parts, axis=0)
                    value_part = jnp.concatenate(value_parts, axis=0)
                    key_sum[pair] = jnp.where(block == 0, key_part, key_sum[pair] + key_part)
                    value_sum[pair] = jnp.where(block == 0, value_part, value_sum[pair] + value_part)
                    return 0

                lax.fori_loop(0, blocks * pairs, attend, 0)

                def finish(pair, _):
                    at = pl.multiple_of(pair * 128, 128)
                    qkv[:, pl.ds(half + at, 128)] = key_sum[pair].T.astype(bf16)
                    qkv[:, pl.ds(2 * half + at, 128)] = value_sum[pair].T.astype(bf16)
                    return 0

                lax.fori_loop(0, pairs, finish, 0)

            pl.run_scoped(
                attention,
                V((length, half), f32),
                V((length, half), f32),
                V((pairs, 128, length), f32),
                V((pairs, 128, length), f32),
                V((2, 2, SIZE, length), bf16),
            )

            def inputs(normed, weight, m_low, m_own, above, rows_in):
                gets = [
                    pltpu.make_async_copy(src, dst, loc.at[n])
                    for n, (src, dst) in enumerate(((all_qkv, weight), (normed_kept, normed), (mid_grad_kept, above), (x_own, rows_in)))
                ]
                for get in gets:
                    get.start()
                gets[0].wait()
                m_low[...] = mul(qkv[high_part, :], weight[...], NT).astype(bf16)
                sending = s.copy(m_low, from_y, m_s, m_r, z, x, c, 1 - y)
                sending.start()
                gets[1].wait()
                for n in range(3):
                    these = slice(n * half, (n + 1) * half)
                    qkv_wgrad[:, these] = mul(normed[...], qkv[:, these], TN).astype(bf16)
                    s.begin(early + n)
                service(7)
                s.cstage(early)
                m_own[...] = mul(qkv[low_part, :], weight[...], NT)
                ones = jnp.ones((8, length), bf16)
                for row, n in ((QUERY_BIAS, 0), (VALUE_BIAS, 2)):
                    value = mul(ones, qkv[:, n * half : (n + 1) * half], NN)[0:1]
                    for other in range(BOTH):
                        these = slice(other * half, (other + 1) * half)
                        vec_grads[row : row + 1, these] = jnp.where(y == other, value, 0.0)
                s.xstage(8)
                s.zstage(7)
                s.ystage(6)
                s.cstage(early + 1)
                gets[2].wait()
                gets[3].wait()
                sending.wait()
                zero = jnp.zeros((1, width), f32)

                def back_one(i, so_far):
                    gain_sum, shift_sum = so_far
                    these = tall(i, STEP)
                    zed, inverse = normalized(rows_in[these, :].astype(f32))
                    grad = m_own[these, :] + from_y[these, :].astype(f32)
                    scaled = grad * vecs[GAIN_ONE : GAIN_ONE + 1, :]
                    part = inverse * (
                        scaled - jnp.mean(scaled, axis=-1, keepdims=True) - zed * jnp.mean(scaled * zed, axis=-1, keepdims=True)
                    )
                    above[these, :] = above[these, :] + part
                    add = lambda total_, value: total_ + jnp.sum(value, axis=0, keepdims=True)
                    return add(gain_sum, grad * zed), add(shift_sum, grad)

                gain_sum, shift_sum = lax.fori_loop(0, rows // STEP, back_one, (zero, zero))
                put = pltpu.make_async_copy(above, input_grad, loc.at[0])
                put.start()
                vec_grads[GAIN_ONE : GAIN_ONE + 1, :] = gain_sum
                vec_grads[SHIFT_ONE : SHIFT_ONE + 1, :] = shift_sum
                blank = jnp.zeros((6, 128), f32)
                for chip in range(2 * depth):
                    eight = vec_grads[:, 128 * chip : 128 * chip + 128]
                    for core in range(2):
                        at = 256 * (2 * chip + core)
                        block = jnp.concatenate([eight, up_bgrad[0:1, at : at + 128], up_bgrad[0:1, at + 128 : at + 256], blank], axis=0)
                        small_grads[pl.ds(32 * chip + 16 * core, 16), :] = block.astype(bf16)
                s.begin(total - 1)
                put.wait()

            pl.run_scoped(
                inputs,
                V((length, width), bf16),
                V((width, 3 * half), bf16),
                V((rows, width), bf16),
                V((rows, width), f32),
                V((rows, width), f32),
                V((rows, width), bf16),
            )

        pl.run_scoped(back_phase, V((length, 3 * half), bf16))
        for n in range(early, total + 2):
            if n + 2 < total:
                s.cstage(n + 2)
            if n < total:
                s.xstage(n)
            if n - 1 < total:
                s.zstage(n - 1)
            s.ystage(n - 2)
        s.copy(attended_grad_kept.at[:, columns(1 - y)], grads.at[high_part], grad_s, grad_r, z, x, c, 1 - y).wait_send()
        for ch in range(total):
            s.sent(ch)

    high = width // (4 * depth)
    total = len(scatters)
    pl.run_scoped(
        rest,
        V((ring, 2 * depth, high, width), bf16),
        V((2 * depth, high, width), bf16),
        V((total, depth, high, width), bf16),
        V((total, depth - 1, high, width), bf16),
        V((total, high, width), bf16),
        V((total, high, width), bf16),
        V((2, high, width), f32),
    )
    for ch in range(count):
        g.sent(ch)


def gather_chunks(high, width, wide, quarter):
    half = width // BOTH
    return (
        ((0, 0, 16, 0, 0, 128, False),)
        + tuple((1 + n, 0, high, None, n * half, half, False) for n in range(3))
        + tuple((6, quarter * i, quarter, 0, 0, width, True) for i in range(4))
        + ((4, 0, high, 0, 0, width, False),)
        + tuple((5, 0, high, width * i, width * i, width, False) for i in range(wide // width))
    )


def scatter_chunks(high, width, wide, owned):
    half = width // BOTH
    return (
        tuple((5, 0, high, width * j, width) for j in range(wide // width))
        + tuple((6, high * i, high, 0, width) for i in range(owned // high))
        + ((4, 0, high, 0, width),)
        + tuple((1 + n, 0, high, half * n, half) for n in range(3))
        + ((0, 0, 16, 0, 128),)
    )


def layer(small, own_query, own_key, own_value, own_out, own_up, own_down, x_own, cotangent, depth=DEPTH, ring=4):
    rows, width = x_own.shape
    length, half, wide = BOTH * rows, width // BOTH, own_up.shape[1]
    parts = 4 * depth
    high, owned = own_up.shape[0], own_down.shape[0]
    gathers = gather_chunks(high, width, wide, owned // 4)
    scatters = scatter_chunks(high, width, wide, owned)
    count, total = len(gathers), len(scatters)
    S, V = pltpu.SemaphoreType.DMA, pltpu.VMEM
    shape = jax.ShapeDtypeStruct
    out = [
        shape((rows, width), bf16), shape((rows, width), f32), shape((16, 128), f32),
        shape((high, width), f32), shape((high, width), f32), shape((high, width), f32), shape((high, width), f32),
        shape((high, wide), f32), shape((owned, width), f32),
        shape((parts * 16, 128), bf16), shape((width, 3 * half), bf16), shape((width, width), bf16), shape((width, wide), bf16),
        shape((wide, width), bf16), shape((length, width), bf16), shape((length, 3 * half), bf16), shape((length, half), f32),
        shape((length, half), f32), shape((half // HDIM, length, length), bf16), shape((rows, width), f32), shape((rows, width), bf16),
        shape((width, width), bf16), shape((width, wide), bf16), shape((wide, width), bf16),
        shape((total, 2 * depth, high, width), bf16),
    ]
    return pl.pallas_call(
        functools.partial(layer_kernel, depth, ring, gathers, scatters),
        out_shape=out,
        in_specs=[pl.BlockSpec(memory_space=pl.ANY)] * 9,
        out_specs=[pl.BlockSpec(memory_space=pl.ANY)] * len(out),
        scratch_shapes=[
            V((rows, width), bf16), V((rows, width), bf16), V((length, half), bf16), V((8, width), f32), V((1, wide), f32),
            V((8, width), f32), V((1, wide), f32), V((width, 3 * half), bf16), V((parts * 16, 128), bf16),
        ]
        + gather_sems(depth, count)
        + [
            S((ring, 2 * depth)), S, S((total, 2 * depth)), S((total, 2 * depth)), S((total, depth)), S((total, depth)),
            S((total, depth)), S((total, depth)), S((total,)), S((total,)), S((2,)),
            pltpu.SemaphoreType.REGULAR, S, S, S((half // 128,)), S((half // 128,)), S, S, S, S, S((8,)), S((2, 2)), S((2, half // 128)),
        ],
        compiler_params=pltpu.CompilerParams(collective_id=1, has_side_effects=True, vmem_limit_bytes=63 * 2**20),
        name="encoder_layer",
    )(small, own_query, own_key, own_value, own_out, own_up, own_down, x_own, cotangent)[:9]


def pack_small(vectors, up_bias, c):
    rows = jnp.stack(vectors)
    zero = jnp.zeros_like(rows)
    rows = jnp.concatenate([jnp.where(c == 0, rows, zero), jnp.where(c == 0, zero, rows)], axis=1)
    return jnp.concatenate([rows, up_bias.reshape(2, 128), jnp.zeros((6, 128), rows.dtype)], axis=0)


def fast_device(
    activations, cotangent, query_weight, key_weight, value_weight, output_weight, first_gain, first_shift,
    query_bias, value_bias, output_bias, up_weight, down_weight, second_gain, second_shift, up_bias, down_bias,
):
    c = lax.axis_index("fsdp") % 2
    small = pack_small(
        (first_gain, first_shift, query_bias, value_bias, output_bias, second_gain, second_shift, down_bias), up_bias, c
    )
    block_out, input_grad, own_small, own_query, own_key, own_value, own_output, own_up, own_down = layer(
        small, query_weight, key_weight, value_weight, output_weight, up_weight, down_weight, activations[0], cotangent[0]
    )
    own_vecs = lax.dynamic_slice_in_dim(own_small, c * 64, 64, 1)
    return (
        block_out.reshape(activations.shape),
        input_grad.reshape(activations.shape),
        own_query,
        own_key,
        own_value,
        own_output,
        own_vecs[0],
        own_vecs[1],
        own_vecs[2],
        own_vecs[3],
        own_vecs[4],
        own_up,
        own_down,
        own_vecs[5],
        own_vecs[6],
        own_small[8:10].reshape(-1),
        own_vecs[7],
    )


def solution(mesh):
    fits = mesh.shape["fsdp"] == 4 * DEPTH and mesh.shape["ctx"] == BOTH
    return jax.shard_map(
        fast_device if fits else plain_device,
        mesh=mesh,
        in_specs=(
            P("fsdp", "ctx", None),
            P("fsdp", "ctx", None),
            P("fsdp", None),
            P("fsdp", None),
            P("fsdp", None),
            P("fsdp", None),
            P("fsdp"),
            P("fsdp"),
            P("fsdp"),
            P("fsdp"),
            P("fsdp"),
            P("fsdp", None),
            P("fsdp", None),
            P("fsdp"),
            P("fsdp"),
            P("fsdp"),
            P("fsdp"),
        ),
        out_specs=(
            P("fsdp", "ctx", None),
            P("fsdp", "ctx", None),
            P("fsdp", None),
            P("fsdp", None),
            P("fsdp", None),
            P("fsdp", None),
            P("fsdp"),
            P("fsdp"),
            P("fsdp"),
            P("fsdp"),
            P("fsdp"),
            P("fsdp", None),
            P("fsdp", None),
            P("fsdp"),
            P("fsdp"),
            P("fsdp"),
            P("fsdp"),
        ),
        check_vma=False,
    )
```

```python
import functools

import jax
import jax.numpy as jnp
from jax import lax
from jax.experimental import pallas as pl
from jax.experimental.pallas import tpu as pltpu
from jax.sharding import PartitionSpec as P

HEADS = 16
HDIM = 64
MESH = pl.DeviceIdType.MESH


epsilon = 1e-05


def layer_norm(token_rows, gain, shift):
    centered = token_rows - jnp.mean(token_rows, axis=-1, keepdims=True)
    variance = jnp.mean(centered * centered, axis=-1, keepdims=True)
    return centered * lax.rsqrt(variance + epsilon) * gain + shift


def gelu_act(values_in):
    return jax.nn.gelu(values_in, approximate=True)


def gather_attention(shards):
    return (
        lax.all_gather(shards[0], "fsdp", axis=0, tiled=True),
        lax.all_gather(shards[1], "fsdp", axis=0, tiled=True),
        lax.all_gather(shards[2], "fsdp", axis=0, tiled=True),
        lax.all_gather(shards[3], "fsdp", axis=0, tiled=True),
        lax.all_gather(shards[4], "fsdp", axis=0, tiled=True),
        lax.all_gather(shards[5], "fsdp", axis=0, tiled=True),
        lax.all_gather(shards[6], "fsdp", axis=0, tiled=True),
        lax.all_gather(shards[7], "fsdp", axis=0, tiled=True),
        lax.all_gather(shards[8], "fsdp", axis=0, tiled=True),
    )


def gather_feed(shards):
    return (
        lax.all_gather(shards[0], "fsdp", axis=0, tiled=True),
        lax.all_gather(shards[1], "fsdp", axis=0, tiled=True),
        lax.all_gather(shards[2], "fsdp", axis=0, tiled=True),
        lax.all_gather(shards[3], "fsdp", axis=0, tiled=True),
        lax.all_gather(shards[4], "fsdp", axis=0, tiled=True),
        lax.all_gather(shards[5], "fsdp", axis=0, tiled=True),
    )


def plain_device(
    activations,
    cotangent,
    query_weight,
    key_weight,
    value_weight,
    output_weight,
    first_gain,
    first_shift,
    query_bias,
    value_bias,
    output_bias,
    up_weight,
    down_weight,
    second_gain,
    second_shift,
    up_bias,
    down_bias,
):
    clip_count, local_len, width = activations.shape
    scaling = HDIM ** (-0.5)
    attend_shards = (
        query_weight,
        key_weight,
        value_weight,
        output_weight,
        first_gain,
        first_shift,
        query_bias,
        value_bias,
        output_bias,
    )
    feed_shards = (up_weight, down_weight, second_gain, second_shift, up_bias, down_bias)
    attend_full = gather_attention(attend_shards)
    (
        full_query,
        full_key,
        full_value,
        full_output,
        full_gain_one,
        full_shift_one,
        full_query_bias,
        full_value_bias,
        full_output_bias,
    ) = attend_full
    gain_one = full_gain_one.astype(jnp.float32)
    shift_one = full_shift_one.astype(jnp.float32)
    token_rows = activations.reshape(-1, width).astype(jnp.float32)
    normed_one = layer_norm(token_rows, gain_one, shift_one).astype(jnp.bfloat16)
    queries = (
        jnp.dot(normed_one, full_query, preferred_element_type=jnp.float32)
        + full_query_bias.astype(jnp.float32)
    ).astype(jnp.bfloat16)
    keys_local = jnp.dot(normed_one, full_key, preferred_element_type=jnp.float32).astype(
        jnp.bfloat16
    )
    values_local = (
        jnp.dot(normed_one, full_value, preferred_element_type=jnp.float32)
        + full_value_bias.astype(jnp.float32)
    ).astype(jnp.bfloat16)
    query_heads = queries.reshape(clip_count, local_len, HEADS, HDIM)
    keys_block = keys_local.reshape(clip_count, local_len, width)
    values_block = values_local.reshape(clip_count, local_len, width)
    run_max = jnp.full((clip_count, local_len, HEADS), -1e30, jnp.float32)
    key_piece = lax.all_gather(keys_block, "ctx", axis=1, tiled=True)
    value_piece = lax.all_gather(values_block, "ctx", axis=1, tiled=True)
    key_heads = key_piece.reshape(clip_count, -1, HEADS, HDIM)
    value_heads = value_piece.reshape(clip_count, -1, HEADS, HDIM)
    scores = (
        jnp.einsum("cqhd,ckhd->cqhk", query_heads, key_heads, preferred_element_type=jnp.float32)
        * scaling
    )
    new_max = jnp.maximum(run_max, jnp.max(scores, axis=-1))
    weights = jnp.exp(scores - new_max[..., None])
    run_sum = jnp.sum(weights, axis=-1)
    accum = jnp.einsum(
        "cqhk,ckhd->cqhd",
        weights.astype(jnp.bfloat16),
        value_heads,
        preferred_element_type=jnp.float32,
    )
    run_max, run_sum, accum = (new_max, run_sum, accum)
    attend_exact = accum / run_sum[..., None]
    log_total = run_max + jnp.log(run_sum)
    attended = attend_exact.reshape(-1, width).astype(jnp.bfloat16)
    mid_rows = (
        token_rows
        + jnp.dot(attended, full_output, preferred_element_type=jnp.float32)
        + full_output_bias.astype(jnp.float32)
    )
    feed_full = gather_feed(feed_shards)
    full_up, full_down, full_gain_two, full_shift_two, full_up_bias, full_down_bias = feed_full
    gain_two = full_gain_two.astype(jnp.float32)
    shift_two = full_shift_two.astype(jnp.float32)
    normed_two = layer_norm(mid_rows, gain_two, shift_two).astype(jnp.bfloat16)
    pre_act = jnp.dot(
        normed_two, full_up, preferred_element_type=jnp.float32
    ) + full_up_bias.astype(jnp.float32)
    hidden = gelu_act(pre_act).astype(jnp.bfloat16)
    block_rows = (
        mid_rows
        + jnp.dot(hidden, full_down, preferred_element_type=jnp.float32)
        + full_down_bias.astype(jnp.float32)
    )
    block_out = block_rows.astype(jnp.bfloat16).reshape(activations.shape)
    back_attend = gather_attention(attend_shards)
    back_feed = gather_feed(feed_shards)
    back_query, back_key, back_value, back_output = (
        back_attend[0],
        back_attend[1],
        back_attend[2],
        back_attend[3],
    )
    back_up, back_down = (back_feed[0], back_feed[1])
    cot_rows = cotangent.reshape(-1, width)
    outer_grad = cot_rows.astype(jnp.float32)
    down_wgrad = jnp.einsum("rf,rd->fd", hidden, cot_rows, preferred_element_type=jnp.float32)
    down_bgrad = jnp.sum(outer_grad, axis=0)
    hidden_grad = jnp.einsum("rd,fd->rf", cot_rows, back_down, preferred_element_type=jnp.float32)
    _, gelu_back = jax.vjp(gelu_act, pre_act)
    pre_grad = gelu_back(hidden_grad)[0].astype(jnp.bfloat16)
    up_wgrad = jnp.einsum("rd,rf->df", normed_two, pre_grad, preferred_element_type=jnp.float32)
    up_bgrad = jnp.sum(pre_grad.astype(jnp.float32), axis=0)
    normed_two_grad = jnp.einsum("rf,df->rd", pre_grad, back_up, preferred_element_type=jnp.float32)
    _, norm_two_back = jax.vjp(layer_norm, mid_rows, gain_two, shift_two)
    mid_part, gain_two_grad, shift_two_grad = norm_two_back(normed_two_grad)
    mid_grad = outer_grad + mid_part
    feed_owned = (
        lax.psum_scatter(
            up_wgrad.astype(jnp.bfloat16), "fsdp", scatter_dimension=0, tiled=True
        ).astype(jnp.float32),
        lax.psum_scatter(
            down_wgrad.astype(jnp.bfloat16), "fsdp", scatter_dimension=0, tiled=True
        ).astype(jnp.float32),
        lax.psum_scatter(
            gain_two_grad.astype(jnp.bfloat16), "fsdp", scatter_dimension=0, tiled=True
        ).astype(jnp.float32),
        lax.psum_scatter(
            shift_two_grad.astype(jnp.bfloat16), "fsdp", scatter_dimension=0, tiled=True
        ).astype(jnp.float32),
        lax.psum_scatter(
            up_bgrad.astype(jnp.bfloat16), "fsdp", scatter_dimension=0, tiled=True
        ).astype(jnp.float32),
        lax.psum_scatter(
            down_bgrad.astype(jnp.bfloat16), "fsdp", scatter_dimension=0, tiled=True
        ).astype(jnp.float32),
    )
    feed_done = (
        lax.psum(feed_owned[0].astype(jnp.bfloat16), "ctx").astype(jnp.float32),
        lax.psum(feed_owned[1].astype(jnp.bfloat16), "ctx").astype(jnp.float32),
        lax.psum(feed_owned[2].astype(jnp.bfloat16), "ctx").astype(jnp.float32),
        lax.psum(feed_owned[3].astype(jnp.bfloat16), "ctx").astype(jnp.float32),
        lax.psum(feed_owned[4].astype(jnp.bfloat16), "ctx").astype(jnp.float32),
        lax.psum(feed_owned[5].astype(jnp.bfloat16), "ctx").astype(jnp.float32),
    )
    branch_grad = mid_grad.astype(jnp.bfloat16)
    output_wgrad = jnp.einsum(
        "rd,re->de", attended, branch_grad, preferred_element_type=jnp.float32
    )
    output_bgrad = jnp.sum(branch_grad.astype(jnp.float32), axis=0)
    attended_grad = jnp.einsum(
        "re,de->rd", branch_grad, back_output, preferred_element_type=jnp.float32
    ).astype(jnp.bfloat16)
    grad_heads = attended_grad.reshape(clip_count, local_len, HEADS, HDIM)
    delta = jnp.sum(grad_heads.astype(jnp.float32) * attend_exact, axis=-1)
    keys_whole, values_whole = (
        lax.all_gather(keys_block, "ctx", axis=1, tiled=True),
        lax.all_gather(values_block, "ctx", axis=1, tiled=True),
    )
    key_heads_all = keys_whole.reshape(clip_count, -1, HEADS, HDIM)
    value_heads_all = values_whole.reshape(clip_count, -1, HEADS, HDIM)
    scores_all = (
        jnp.einsum(
            "cqhd,ckhd->cqhk", query_heads, key_heads_all, preferred_element_type=jnp.float32
        )
        * scaling
    )
    probs = jnp.exp(scores_all - log_total[..., None])
    prob_grad = jnp.einsum(
        "cqhd,ckhd->cqhk", grad_heads, value_heads_all, preferred_element_type=jnp.float32
    )
    score_grad = (probs * (prob_grad - delta[..., None])).astype(jnp.bfloat16)
    query_grad = (
        jnp.einsum("cqhk,ckhd->cqhd", score_grad, key_heads_all, preferred_element_type=jnp.float32)
        * scaling
    ).astype(jnp.bfloat16)
    query_grad = query_grad.reshape(-1, width)
    probs_low = probs.astype(jnp.bfloat16)
    key_part = (
        jnp.einsum("cqhk,cqhd->kchd", score_grad, query_heads, preferred_element_type=jnp.float32)
        * scaling
    )
    value_part = jnp.einsum(
        "cqhk,cqhd->kchd", probs_low, grad_heads, preferred_element_type=jnp.float32
    )
    summed = lax.psum_scatter(
        jnp.stack([key_part, value_part], axis=2)
        .reshape(lax.axis_size("ctx") * local_len, clip_count, 2, width)
        .astype(jnp.bfloat16),
        "ctx",
        scatter_dimension=0,
        tiled=True,
    ).astype(jnp.float32)
    key_grad = jnp.transpose(summed[:, :, 0], (1, 0, 2)).reshape(-1, width).astype(jnp.bfloat16)
    value_grad = jnp.transpose(summed[:, :, 1], (1, 0, 2)).reshape(-1, width).astype(jnp.bfloat16)
    query_wgrad = jnp.einsum(
        "rd,re->de", normed_one, query_grad, preferred_element_type=jnp.float32
    )
    key_wgrad = jnp.einsum("rd,re->de", normed_one, key_grad, preferred_element_type=jnp.float32)
    value_wgrad = jnp.einsum(
        "rd,re->de", normed_one, value_grad, preferred_element_type=jnp.float32
    )
    query_bgrad = jnp.sum(query_grad.astype(jnp.float32), axis=0)
    value_bgrad = jnp.sum(value_grad.astype(jnp.float32), axis=0)
    normed_one_grad = (
        jnp.einsum("re,de->rd", query_grad, back_query, preferred_element_type=jnp.float32)
        + jnp.einsum("re,de->rd", key_grad, back_key, preferred_element_type=jnp.float32)
        + jnp.einsum("re,de->rd", value_grad, back_value, preferred_element_type=jnp.float32)
    )
    _, norm_one_back = jax.vjp(layer_norm, token_rows, gain_one, shift_one)
    input_part, gain_one_grad, shift_one_grad = norm_one_back(normed_one_grad)
    input_grad = (mid_grad + input_part).reshape(activations.shape)
    attend_owned = (
        lax.psum_scatter(
            query_wgrad.astype(jnp.bfloat16), "fsdp", scatter_dimension=0, tiled=True
        ).astype(jnp.float32),
        lax.psum_scatter(
            key_wgrad.astype(jnp.bfloat16), "fsdp", scatter_dimension=0, tiled=True
        ).astype(jnp.float32),
        lax.psum_scatter(
            value_wgrad.astype(jnp.bfloat16), "fsdp", scatter_dimension=0, tiled=True
        ).astype(jnp.float32),
        lax.psum_scatter(
            output_wgrad.astype(jnp.bfloat16), "fsdp", scatter_dimension=0, tiled=True
        ).astype(jnp.float32),
        lax.psum_scatter(
            gain_one_grad.astype(jnp.bfloat16), "fsdp", scatter_dimension=0, tiled=True
        ).astype(jnp.float32),
        lax.psum_scatter(
            shift_one_grad.astype(jnp.bfloat16), "fsdp", scatter_dimension=0, tiled=True
        ).astype(jnp.float32),
        lax.psum_scatter(
            query_bgrad.astype(jnp.bfloat16), "fsdp", scatter_dimension=0, tiled=True
        ).astype(jnp.float32),
        lax.psum_scatter(
            value_bgrad.astype(jnp.bfloat16), "fsdp", scatter_dimension=0, tiled=True
        ).astype(jnp.float32),
        lax.psum_scatter(
            output_bgrad.astype(jnp.bfloat16), "fsdp", scatter_dimension=0, tiled=True
        ).astype(jnp.float32),
    )
    attend_done = (
        lax.psum(attend_owned[0].astype(jnp.bfloat16), "ctx").astype(jnp.float32),
        lax.psum(attend_owned[1].astype(jnp.bfloat16), "ctx").astype(jnp.float32),
        lax.psum(attend_owned[2].astype(jnp.bfloat16), "ctx").astype(jnp.float32),
        lax.psum(attend_owned[3].astype(jnp.bfloat16), "ctx").astype(jnp.float32),
        lax.psum(attend_owned[4].astype(jnp.bfloat16), "ctx").astype(jnp.float32),
        lax.psum(attend_owned[5].astype(jnp.bfloat16), "ctx").astype(jnp.float32),
        lax.psum(attend_owned[6].astype(jnp.bfloat16), "ctx").astype(jnp.float32),
        lax.psum(attend_owned[7].astype(jnp.bfloat16), "ctx").astype(jnp.float32),
        lax.psum(attend_owned[8].astype(jnp.bfloat16), "ctx").astype(jnp.float32),
    )
    return (
        block_out,
        input_grad,
        attend_done[0],
        attend_done[1],
        attend_done[2],
        attend_done[3],
        attend_done[4],
        attend_done[5],
        attend_done[6],
        attend_done[7],
        attend_done[8],
        feed_done[0],
        feed_done[1],
        feed_done[2],
        feed_done[3],
        feed_done[4],
        feed_done[5],
    )


def place():
    f = lax.axis_index("fsdp"); y = lax.axis_index("ctx")
    return f // 4, (f // 2) % 2, f % 2, y

def partners(z, x, c, y, depth):
    index = lambda dz, dx, dc: dz * 4 + dx * 2 + dc
    along = [(index((z + k) % depth, x, c), y) for k in range(1, depth)]
    return along + [(index(z, 1 - x, c), y), (index(z, x, 1 - c), y), (index(z, x, c), 1 - y)]


def greet(z, x, c, y, depth):
    barrier = pltpu.get_barrier_semaphore()
    for partner in partners(z, x, c, y, depth):
        pl.semaphore_signal(barrier, inc=1, device_id=partner, device_id_type=MESH)
    pl.semaphore_wait(barrier, depth + 2)


class Gather:
    def __init__(self, depth, chunks, ins, outs, sems, where):
        self.depth, self.chunks, self.ins, self.outs = depth, chunks, ins, outs
        self.zs, self.zr, self.xs, self.xr, self.ys, self.yr, self.cs, self.cr, self.loc = sems
        self.where = where
    def source(self, ch, first, count):
        t, _, _, there, _, w, _ = self.chunks[ch]
        if there is None:
            there = pl.multiple_of(self.where[3] * w, 128)
        return self.ins[t].at[pl.ds(first, count), pl.ds(there, w)]
    def src(self, ch, half):
        _, r0, h, _, _, _, both = self.chunks[ch]
        if not both: return self.source(ch, r0, h)
        h2 = h // 2
        return self.source(ch, pl.multiple_of(r0 + half * h2, 16), h2)
    def dst(self, ch, dz, dx, dc, half):
        t, r0, h, _, c0, w, both = self.chunks[ch]
        full = self.ins[t].shape[0]
        start = (dz * 4 + dx * 2 + dc) * full + r0
        if not both: return self.outs[t].at[pl.ds(pl.multiple_of(start, 16), h), pl.ds(c0, w)]
        h2 = h // 2
        return self.outs[t].at[pl.ds(pl.multiple_of(start + half * h2, 16), h2), pl.ds(c0, w)]
    def copy(self, src, dst, s, r, dz, dx, dc, dy):
        return pltpu.make_async_remote_copy(src_ref=src, dst_ref=dst, send_sem=s, recv_sem=r,
            device_id=(dz * 4 + dx * 2 + dc, dy), device_id_type=MESH)
    def zz(self, j):
        return (self.where[0] - j + self.depth) % self.depth
    def zmove(self, ch, k, recv=False):
        z, x, c, y = self.where
        if recv:
            d = self.dst(ch, self.zz(k), x, c, y)
            return self.copy(d, d, self.zs.at[ch, k], self.zr.at[ch, k], z, x, 1 - c, y)
        return self.copy(self.src(ch, y), self.dst(ch, z, x, c, y), self.zs.at[ch, k], self.zr.at[ch, k], (z + k) % self.depth, x, c, y)
    def xmove(self, ch, j, recv=False):
        z, x, c, y = self.where
        d = self.dst(ch, self.zz(j), 1 - x if recv else x, c, y)
        s = self.src(ch, y) if (j == 0 and not recv) else d
        return self.copy(s, d, self.xs.at[ch, j], self.xr.at[ch, j], z, 1 - x, c, y)
    def ymove(self, ch, i, j, recv=False):
        z, x, c, y = self.where
        d = self.dst(ch, self.zz(j), x if i == 0 else 1 - x, c, 1 - y if recv else y)
        n = i * self.depth + j
        return self.copy(d, d, self.ys.at[ch, n], self.yr.at[ch, n], z, x, c, 1 - y)
    def cmove(self, ch, i, j, other, recv=False):
        z, x, c, y = self.where
        half = 1 - y if other else y
        d = self.dst(ch, self.zz(j), x if i == 0 else 1 - x, 1 - c if recv else c, half)
        s = self.src(ch, half) if (i == 0 and j == 0 and not recv) else d
        n = (i * self.depth + j) + (2 * self.depth if other else 0)
        return self.copy(s, d, self.cs.at[ch, n], self.cr.at[ch, n], z, x, 1 - c, y)
    def own(self, ch):
        z, x, c, y = self.where
        t, r0, h, _, c0, w, both = self.chunks[ch]
        full = self.ins[t].shape[0]
        there = self.outs[t].at[pl.ds(pl.multiple_of((z * 4 + x * 2 + c) * full + r0, 16), h), pl.ds(c0, w)]
        return pltpu.make_async_copy(self.source(ch, r0, h), there, self.loc.at[ch])
    def begin(self, ch):
        for k in range(1, self.depth): self.zmove(ch, k).start()
        self.xmove(ch, 0).start()
        self.cmove(ch, 0, 0, False).start()
        if self.chunks[ch][6]: self.cmove(ch, 0, 0, True).start()
        self.own(ch).start()
    def zstage(self, ch):
        for k in range(1, self.depth):
            self.zmove(ch, k, True).wait_recv()
            self.xmove(ch, k).start()
            if self.chunks[ch][6]: self.ymove(ch, 0, k).start()
            self.cmove(ch, 0, k, False).start()
    def xstage(self, ch):
        for j in range(self.depth):
            self.xmove(ch, j, True).wait_recv()
            if self.chunks[ch][6]: self.ymove(ch, 1, j).start()
            self.cmove(ch, 1, j, False).start()
    def ystage(self, ch):
        if not self.chunks[ch][6]: return
        for i in range(2):
            for j in range(1 - i, self.depth):
                self.ymove(ch, i, j, True).wait_recv()
                self.cmove(ch, i, j, True).start()
    def arrived(self, ch):
        for i in range(2):
            for j in range(self.depth):
                self.cmove(ch, i, j, False, True).wait_recv()
                if self.chunks[ch][6]: self.cmove(ch, i, j, True, True).wait_recv()
        self.own(ch).wait()
    def sent(self, ch):
        both = self.chunks[ch][6]
        for k in range(1, self.depth): self.zmove(ch, k).wait_send()
        for j in range(self.depth): self.xmove(ch, j).wait_send()
        for i in range(2):
            for j in range(self.depth):
                self.cmove(ch, i, j, False).wait_send()
                if both:
                    self.cmove(ch, i, j, True).wait_send()
                    if i or j: self.ymove(ch, i, j).wait_send()

def gather_sems(depth, n):
    S = pltpu.SemaphoreType.DMA
    return [S((n, depth)), S((n, depth)), S((n, depth)), S((n, depth)), S((n, 2 * depth)), S((n, 2 * depth)), S((n, 4 * depth)), S((n, 4 * depth)), S((n,))]


DEPTH, BOTH = 4, 2
f32, bf16 = jnp.float32, jnp.bfloat16
NT = (((1,), (1,)), ((), ()))
NN = (((1,), (0,)), ((), ()))
TN = (((0,), (0,)), ((), ()))
SQRT_2_PI = 0.7978845608028654


def mul(a, b, dims):
    return lax.dot_general(a, b, dims, preferred_element_type=f32)


def tall(i, size):
    return pl.ds(pl.multiple_of(i * size, 16), size)


def normalized(rows):
    centered = rows - jnp.mean(rows, axis=-1, keepdims=True)
    inverse = lax.rsqrt(jnp.mean(centered * centered, axis=-1, keepdims=True) + epsilon)
    return centered * inverse, inverse


def tiled(h, w, body):
    def one(i, _):
        body(pl.ds(pl.multiple_of(i * 16, 16), 16), pl.ds(0, w))
        return 0

    if h == 16:
        one(0, 0)
    else:
        lax.fori_loop(0, h // 16, one, 0)


class Scatter:
    def __init__(self, depth, ring, chunks, grads, outs, bufs, sems, where):
        self.depth, self.ring, self.chunks, self.grads, self.outs = depth, ring, chunks, grads, outs
        self.landed, self.sums, self.near, self.across, self.along, self.mine, self.theirs, self.stage = bufs
        self.ls, self.gs, self.cs, self.cr, self.xs, self.xr, self.zs, self.zr, self.ys, self.yr, self.ps = sems
        self.where = where

    def spot(self, ch):
        first = len(self.chunks) - 4
        if ch < first:
            return ch, 0
        return first + (ch - first) // 2, (ch - first) % 2 * (self.mine.shape[-1] // 2)

    def landing(self, ref, ch, *at):
        n, col = self.spot(ch)
        return ref.at[(n, *at, pl.ds(0, self.chunks[ch][2]), pl.ds(col, self.chunks[ch][4]))]

    def part(self, ref, ch):
        return ref.at[pl.ds(0, self.chunks[ch][2]), pl.ds(0, self.chunks[ch][4])]

    def piece(self, ch, dz, dx, dc):
        t, r0, h, c0, w = self.chunks[ch]
        full = self.grads[t].shape[0] // (4 * self.depth)
        if t == 5:
            return self.held.at[ch % 2, pl.ds(pl.multiple_of((dz * 4 + dx * 2 + dc) * full, 16), h), :]
        return self.grads[t].at[pl.ds(pl.multiple_of((dz * 4 + dx * 2 + dc) * full + r0, 16), h), pl.ds(c0, w)]

    def copy(self, src, dst, s, r, dz, dx, dc, dy):
        return pltpu.make_async_remote_copy(
            src_ref=src, dst_ref=dst, send_sem=s, recv_sem=r, device_id=(dz * 4 + dx * 2 + dc, dy), device_id_type=MESH
        )

    def zz(self, j):
        return (self.where[0] + j) % self.depth

    def load(self, ch, n):
        z, x, c, y = self.where
        i, j = n // self.depth, n % self.depth
        slot = ch % self.ring
        return pltpu.make_async_copy(
            self.piece(ch, self.zz(j), x if i == 0 else 1 - x, c), self.part(self.sums.at[slot, n], ch), self.ls.at[slot, n]
        )

    def fetch(self, ch):
        t, r0, h, c0, w = self.chunks[ch]
        return pltpu.make_async_copy(
            self.landed.at[ch, :, pl.ds(0, h), pl.ds(0, w)], self.near.at[ch % 2, :, pl.ds(0, h), pl.ds(0, w)], self.gs.at[ch % 2]
        )

    def cmove(self, ch, n):
        z, x, c, y = self.where
        i, j = n // self.depth, n % self.depth
        return self.copy(
            self.piece(ch, self.zz(j), x if i == 0 else 1 - x, 1 - c), self.part(self.landed.at[ch, n], ch),
            self.cs.at[ch, n], self.cr.at[ch, n], z, x, 1 - c, y,
        )

    def xmove(self, ch, j):
        z, x, c, y = self.where
        return self.copy(
            self.part(self.sums.at[ch % self.ring, self.depth + j], ch), self.landing(self.across, ch, j),
            self.xs.at[ch, j], self.xr.at[ch, j], z, 1 - x, c, y,
        )

    def zmove(self, ch, j):
        z, x, c, y = self.where
        return self.copy(
            self.part(self.sums.at[ch % self.ring, j], ch), self.landing(self.along, ch, j - 1),
            self.zs.at[ch, j], self.zr.at[ch, j], self.zz(j), x, c, y,
        )

    def ymove(self, ch):
        z, x, c, y = self.where
        return self.copy(
            self.landing(self.mine, ch), self.landing(self.theirs, ch), self.ys.at[ch], self.yr.at[ch], z, x, c, 1 - y
        )

    def begin(self, ch):
        for n in range(2 * self.depth):
            self.cmove(ch, n).start()

    def cmove_sent(self, ch):
        for n in range(2 * self.depth):
            self.cmove(ch, n).wait_send()

    def prepare(self, ch):
        if ch >= self.ring:
            for j in range(self.depth):
                self.xmove(ch - self.ring, j).wait_send()
                if j:
                    self.zmove(ch - self.ring, j).wait_send()
        for n in range(2 * self.depth):
            self.load(ch, n).start()
        for n in range(2 * self.depth):
            self.cmove(ch, n).wait_recv()
        self.fetch(ch).start()

    def cstage(self, ch):
        t, r0, h, c0, w = self.chunks[ch]
        slot = ch % self.ring
        for n in range(2 * self.depth):
            self.load(ch, n).wait()
        self.fetch(ch).wait()

        def add(r, q):
            self.sums[slot, :, r, q] = self.sums[slot, :, r, q] + self.near[ch % 2, :, r, q]

        tiled(h, w, add)
        for j in range(self.depth):
            self.xmove(ch, j).start()

    def xstage(self, ch):
        t, r0, h, c0, w = self.chunks[ch]
        slot, count = ch % self.ring, self.depth
        at, col = self.spot(ch)
        there = pl.ds(col, w)
        for j in range(count):
            self.xmove(ch, j).wait_recv()

        def add(r, q):
            self.sums[slot, 0:count, r, q] = self.sums[slot, 0:count, r, q] + self.across[at, :, r, there]

        tiled(h, w, add)
        for j in range(1, count):
            self.zmove(ch, j).start()

    def zstage(self, ch):
        t, r0, h, c0, w = self.chunks[ch]
        at, col = self.spot(ch)
        there = pl.ds(col, w)
        for j in range(1, self.depth):
            self.zmove(ch, j).wait_recv()

        def add(r, q):
            total = self.sums[ch % self.ring, 0, r, q].astype(f32)
            for j in range(1, self.depth):
                total = total + self.along[at, j - 1, r, there].astype(f32)
            self.mine[at, r, there] = total.astype(bf16)

        tiled(h, w, add)
        self.ymove(ch).start()

    def put(self, ch):
        t, r0, h, c0, w = self.chunks[ch]
        split = 1 <= t <= 3
        there = pl.ds(0, 2 * w) if split else pl.ds(c0, w)
        return pltpu.make_async_copy(
            self.stage.at[ch % 2, pl.ds(0, h), pl.ds(0, 2 * w if split else w)], self.outs[t].at[pl.ds(r0, h), there], self.ps.at[ch % 2]
        )

    def ystage(self, ch):
        t, r0, h, c0, w = self.chunks[ch]
        y = self.where[3]
        at, col = self.spot(ch)
        there = pl.ds(col, w)
        self.ymove(ch).wait_recv()
        if ch >= 2:
            self.put(ch - 2).wait()

        def lay(r, q):
            mine, theirs = self.mine[at, r, there].astype(f32), self.theirs[at, r, there].astype(f32)
            if 1 <= t <= 3:
                self.stage[ch % 2, r, 0:w] = jnp.where(y == 0, mine, theirs)
                self.stage[ch % 2, r, w : 2 * w] = jnp.where(y == 0, theirs, mine)
            else:
                self.stage[ch % 2, r, q] = mine + theirs

        tiled(h, w, lay)
        self.put(ch).start()

    def sent(self, ch):
        if self.chunks[ch][0] != 5:
            self.cmove_sent(ch)
        if ch + self.ring >= len(self.chunks):
            for j in range(self.depth):
                self.xmove(ch, j).wait_send()
                if j:
                    self.zmove(ch, j).wait_send()
        self.ymove(ch).wait_send()
        if ch + 2 >= len(self.chunks):
            self.put(ch).wait()


GAIN_ONE, SHIFT_ONE, QUERY_BIAS, VALUE_BIAS, OUTPUT_BIAS, GAIN_TWO, SHIFT_TWO, DOWN_BIAS = range(8)
STEP = 112
SIZE = 224


def layer_kernel(depth, ring, gathers, scatters, *refs):
    (
        small, own_query, own_key, own_value, own_out, own_up, own_down, x_own, cotangent,
        block_out, input_grad, own_small, own_query_grad, own_key_grad, own_value_grad, own_out_grad, own_up_grad, own_down_grad,
        all_small, all_qkv, all_out, all_up, all_down, normed_kept, qkv_kept, exact_kept, inverse_kept, weights_kept,
        mid_grad_kept, attended_grad_kept, out_wgrad, up_wgrad, down_wgrad, landed,
        from_y, attended, grads, vecs, up_bias, vec_grads, up_bgrad, qkv_wgrad, small_grads,
    ) = refs[:43]
    gather_sems_, scatter_sems_ = refs[43:52], refs[52:63]
    entered, swap_s, swap_r, att_s, att_r, grad_s, grad_r, m_s, m_r, loc, keep_sem, pair_sem = refs[63:]
    z, x, c, y = place()
    rows, width = x_own.shape
    length, half = BOTH * rows, width // BOTH
    pairs = half // 128
    wide = up_bias.shape[1]
    tiles = wide // width
    V = pltpu.VMEM
    low_part, high_part = pl.ds(0, rows), pl.ds(rows, rows)

    def columns(which):
        return pl.ds(pl.multiple_of(which * half, 128), half)

    g = Gather(
        depth, gathers, (small, own_query, own_key, own_value, own_out, own_up, own_down),
        (all_small, all_qkv, all_qkv, all_qkv, all_out, all_up, all_down), gather_sems_, (z, x, c, y),
    )
    greet(z, x, c, y, depth)
    swapping = g.copy(x_own, from_y, swap_s, swap_r, z, x, c, 1 - y)
    count = len(gathers)
    ahead = 4

    def along(ch):
        g.zstage(ch)
        if ch + ahead < count:
            g.begin(ch + ahead)

    for ch in range(ahead):
        g.begin(ch)
        if ch == 0:
            swapping.start()
    along(0)
    g.xstage(0)
    along(1)
    along(2)
    g.xstage(1)

    def first_phase(small_v, normed, qkv, exact, inverse, weight, values_ones, kept, exact_low, x_rows):
        get_x = pltpu.make_async_copy(x_own, x_rows, loc.at[1])
        get_x.start()
        g.arrived(0)
        get = pltpu.make_async_copy(all_small, small_v, loc.at[0])
        get.start()
        get.wait()
        for chip in range(2 * depth):
            one, two = small_v[pl.ds(32 * chip, 16), :].astype(f32), small_v[pl.ds(32 * chip + 16, 16), :].astype(f32)
            vecs[0:8, 128 * chip : 128 * chip + 128] = one[0:8] + two[0:8]
            for core, part in enumerate((one, two)):
                for n in range(2):
                    at = (2 * chip + core) * 256 + 128 * n
                    up_bias[0:1, at : at + 128] = part[8 + n : 9 + n]
        get_x.wait()

        def norm_one(source, first):
            gain, shift = vecs[GAIN_ONE : GAIN_ONE + 1, :], vecs[SHIFT_ONE : SHIFT_ONE + 1, :]

            def one(i, _):
                value = normalized(source[tall(i, STEP), :].astype(f32))[0]
                normed[pl.ds(pl.multiple_of(first + i * STEP, 16), STEP), :] = (value * gain + shift).astype(bf16)
                return 0

            lax.fori_loop(0, rows // STEP, one, 0)

        def project(first):
            these = pl.ds(first, rows)
            for n, bias in enumerate((QUERY_BIAS, None, VALUE_BIAS)):
                value = mul(normed[these, :], weight[:, n * half : (n + 1) * half], NN)
                if bias is not None:
                    value = value + vecs[bias : bias + 1, columns(y)]
                qkv[these, n * half : (n + 1) * half] = value.astype(bf16)

        norm_one(x_rows, 0)
        along(3)
        g.xstage(2)
        g.xstage(3)
        for ch in (1, 2, 3):
            g.arrived(ch)
        get = pltpu.make_async_copy(all_qkv, weight, loc.at[0])
        get.start()
        get.wait()
        project(0)
        along(4)
        swapping.wait_recv()
        norm_one(from_y, rows)
        project(rows)
        g.xstage(4)
        along(5)
        put_normed = pltpu.make_async_copy(normed, normed_kept, loc.at[1])
        put_qkv = pltpu.make_async_copy(qkv, qkv_kept, loc.at[2])
        put_normed.start()
        put_qkv.start()
        low_lanes = lax.broadcasted_iota(jnp.int32, (rows, 128), 1) < HDIM

        def keep(pair, block, head, slot):
            return pltpu.make_async_copy(
                kept.at[slot, head], weights_kept.at[2 * pair + head, tall(block, rows)], keep_sem.at[slot, head]
            )

        def keep_pair(pair):
            these = pl.ds(pl.multiple_of(pair * 128, 128), 128)
            return (
                pltpu.make_async_copy(exact.at[:, these], exact_kept.at[:, these], pair_sem.at[0, pair]),
                pltpu.make_async_copy(inverse.at[:, these], inverse_kept.at[:, these], pair_sem.at[1, pair]),
            )

        def send(pair):
            at = pl.multiple_of(pair * 128, 128)
            there = pl.multiple_of(y * half + at, 128)
            return g.copy(
                exact_low.at[:, pl.ds(at, 128)], attended.at[:, pl.ds(there, 128)], att_s.at[pair], att_r.at[pair], z, x, c, 1 - y
            )

        values_ones[:, 128:] = jnp.ones((length, 128), bf16)
        services = {
            0: (lambda: g.xstage(5),),
            1: (lambda: along(6),),
            2: (lambda: g.ystage(4), lambda: along(7)),
            4: (lambda: g.xstage(6), lambda: g.xstage(7)),
            5: (lambda: along(8), lambda: g.ystage(5)),
            7: (lambda: g.xstage(8),),
        }

        def attend(turn, _):
            pair = turn // 2
            slot = turn % 2
            block = 1 - slot
            for n, todo in services.items():

                @pl.when(turn == n)
                def _(todo=todo):
                    for do in todo:
                        do()

            @pl.when(turn > 1)
            def _():
                for head in range(2):
                    keep(0, 0, head, slot).wait()

            at = pl.multiple_of(pair * 128, 128)

            @pl.when(slot == 0)
            def _():
                values_ones[:, :128] = qkv[:, pl.ds(2 * half + at, 128)]

            these = tall(block, rows)
            queries = qkv[these, pl.ds(at, 128)] * bf16(HDIM**-0.5)
            keys = qkv[:, pl.ds(half + at, 128)]
            values = values_ones[...]
            parts = []
            for head in range(2):
                masked = jnp.where(low_lanes == (head == 0), queries, jnp.zeros_like(queries))
                scores = mul(masked, keys, NT)
                top = jnp.max(scores, axis=1, keepdims=True)
                weights = jnp.exp(scores - top).astype(bf16)
                kept[slot, head] = weights
                summed = mul(weights, values, NN)
                parts.append((summed[:, :128], 1.0 / summed[:, 128:]))
            (low, low_inverse), (high, high_inverse) = parts
            scale = jnp.where(low_lanes, low_inverse, high_inverse)
            value = jnp.where(low_lanes, low, high) * scale
            exact[these, pl.ds(at, 128)] = value
            inverse[these, pl.ds(at, 128)] = scale
            for head in range(2):
                keep(pair, block, head, slot).start()

            @pl.when(slot == 0)
            def _():
                exact_low[:, pl.ds(at, 128)] = value.astype(bf16)
                send(pair).start()

            @pl.when(slot == 1)
            def _():
                attended[:, pl.ds(pl.multiple_of(y * half + at, 128), 128)] = value.astype(bf16)
                for put in keep_pair(pair):
                    put.start()

            return 0

        lax.fori_loop(0, 2 * pairs, attend, 0)
        put_normed.wait()
        put_qkv.wait()
        for pair in range(pairs):
            for put in keep_pair(pair):
                put.wait()
        for slot in range(2):
            for head in range(2):
                keep(0, 0, head, slot).wait()
        for pair in range(pairs):
            send(pair).wait()
        swapping.wait_send()

    pl.run_scoped(
        first_phase,
        V(all_small.shape, bf16),
        V((length, width), bf16),
        V((length, 3 * half), bf16),
        V((length, half), f32),
        V((length, half), f32),
        V((width, 3 * half), bf16),
        V((length, 256), bf16),
        V((2, 2, rows, length), bf16),
        V((rows, half), bf16),
        V((rows, width), bf16),
    )

    def rest(sums, near, across, along_z, mine, theirs, stage):
        for partner in partners(z, x, c, y, depth):
            pl.semaphore_signal(entered, inc=1, device_id=partner, device_id_type=MESH)
        s = Scatter(
            depth, ring, scatters, (small_grads, qkv_wgrad, qkv_wgrad, qkv_wgrad, out_wgrad, up_wgrad, down_wgrad),
            (own_small, own_query_grad, own_key_grad, own_value_grad, own_out_grad, own_up_grad, own_down_grad),
            (landed, sums, near, across, along_z, mine, theirs, stage), scatter_sems_, (z, x, c, y),
        )
        total = len(scatters)
        early = total - 4

        def service(n):
            if n + 2 < early:
                s.cstage(n + 2)
            s.xstage(n)
            s.zstage(n - 1)
            if n >= 4:
                s.ystage(n - 4)
            if n + 3 < early:
                s.prepare(n + 3)

        def feed_phase(up_w, down_w, block_sum, normed_grad, up_stage, down_stage, mid, normed_two, cot):
            s.held = up_stage

            def get_down(j, slot):
                return pltpu.make_async_copy(
                    all_down.at[pl.ds(pl.multiple_of(j * width, 16), width)], down_w.at[slot], loc.at[1 + slot]
                )

            def get_up(j, slot):
                return pltpu.make_async_copy(
                    all_up.at[:, pl.ds(pl.multiple_of(j * width, 128), width)], up_w.at[slot], loc.at[3 + slot]
                )

            def put_down(j):
                return pltpu.make_async_copy(down_stage, down_wgrad.at[pl.ds(pl.multiple_of(j * width, 16), width)], loc.at[6])

            get_cot = pltpu.make_async_copy(cotangent, cot, loc.at[0])
            get_x = pltpu.make_async_copy(x_own, normed_two, loc.at[7])
            get_cot.start()
            get_x.start()
            g.arrived(6)
            get_out = pltpu.make_async_copy(all_out, down_w.at[1], loc.at[2])
            get_out.start()
            along(9)
            get_out.wait()
            mid[...] = mul(attended[...], down_w[1], NN)
            get_x.wait()

            def norm_two(i, _):
                these = tall(i, STEP)
                value = mid[these, :] + vecs[OUTPUT_BIAS : OUTPUT_BIAS + 1, :] + normed_two[these, :].astype(f32)
                mid[these, :] = value
                value = normalized(value)[0] * vecs[GAIN_TWO : GAIN_TWO + 1, :] + vecs[SHIFT_TWO : SHIFT_TWO + 1, :]
                normed_two[these, :] = value.astype(bf16)
                return 0

            lax.fori_loop(0, rows // STEP, norm_two, 0)
            block_sum[...] = jnp.zeros_like(block_sum)
            normed_grad[...] = jnp.zeros_like(normed_grad)
            get_cot.wait()
            g.ystage(7)
            g.ystage(8)
            for ch in (4, 5, 7, 8):
                g.arrived(ch)
            get_down(0, 0).start()
            along(10)
            g.xstage(9)
            g.arrived(9)
            get_up(0, 0).start()

            at_start = {
                2: (lambda: g.xstage(12), lambda: g.ystage(11), lambda: g.arrived(11), lambda: get_up(2, 0).start()),
                3: (lambda: g.ystage(12), lambda: g.arrived(12), lambda: get_up(3, 1).start()),
            }
            midway = {
                0: (lambda: along(11), lambda: g.xstage(10), lambda: g.arrived(10), lambda: get_up(1, 1).start()),
                1: (
                    lambda: s.prepare(0), lambda: along(12), lambda: g.xstage(11),
                    lambda: pl.semaphore_wait(entered, depth + 2), lambda: s.cstage(0),
                ),
                2: (lambda: s.prepare(1), lambda: s.cmove_sent(0), lambda: s.cstage(1), lambda: s.xstage(0)),
                3: (lambda: s.prepare(2), lambda: s.cmove_sent(1), lambda: s.cstage(2), lambda: s.xstage(1), lambda: s.zstage(0)),
            }

            def feed(j, _):
                slot = j % 2

                for n, todo in at_start.items():

                    @pl.when(j == n)
                    def _(todo=todo):
                        for do in todo:
                            do()

                get_down(j, slot).wait()

                @pl.when(j + 1 < tiles)
                def _():
                    get_down(j + 1, 1 - slot).start()

                get_up(j, slot).wait()
                cols = pl.ds(pl.multiple_of(j * width, 128), width)
                u = mul(normed_two[...], up_w[slot], NN) + up_bias[0:1, cols]
                hidden_grad = mul(cot[...], down_w[slot], NT)
                square = u * u
                gate = 0.5 + 0.5 * jnp.tanh(u * (SQRT_2_PI + (SQRT_2_PI * 0.044715) * square))
                hidden = (u * gate).astype(bf16)
                slope = gate + (u * (gate - gate * gate)) * (2 * SQRT_2_PI + (6 * SQRT_2_PI * 0.044715) * square)
                pre_grad = (hidden_grad * slope).astype(bf16)
                block_sum[...] += mul(hidden, down_w[slot], NN)
                for n, todo in midway.items():

                    @pl.when(j == n)
                    def _(todo=todo):
                        for do in todo:
                            do()

                @pl.when(j > 0)
                def _():
                    put_down(0).wait()

                down_stage[...] = mul(hidden, cot[...], TN).astype(bf16)
                up_stage[slot] = mul(normed_two[...], pre_grad, TN).astype(bf16)
                up_bgrad[0:1, cols] = jnp.sum(pre_grad.astype(f32), axis=0, keepdims=True)
                normed_grad[...] += mul(pre_grad, up_w[slot], NT)
                put_down(j).start()
                for n in range(tiles):

                    @pl.when(j == n)
                    def _(n=n):
                        s.begin(n)

                return 0

            lax.fori_loop(0, tiles, feed, 0)
            get_out = pltpu.make_async_copy(all_out, down_w.at[1], loc.at[2])
            get_out.start()
            zero = jnp.zeros((1, width), f32)

            def back_two(i, so_far):
                gain_sum, shift_sum, out_sum, cot_sum = so_far
                these = tall(i, STEP)
                rows_in = mid[these, :]
                block_sum[these, :] = block_sum[these, :] + rows_in + vecs[DOWN_BIAS : DOWN_BIAS + 1, :]
                zed, inverse = normalized(rows_in)
                grad = normed_grad[these, :]
                scaled = grad * vecs[GAIN_TWO : GAIN_TWO + 1, :]
                part = inverse * (
                    scaled - jnp.mean(scaled, axis=-1, keepdims=True) - zed * jnp.mean(scaled * zed, axis=-1, keepdims=True)
                )
                above = cot[these, :].astype(f32)
                whole = above + part
                mid[these, :] = whole
                branch = whole.astype(bf16)
                normed_two[these, :] = branch
                cot[these, :] = block_sum[these, :].astype(bf16)
                add = lambda total_, value: total_ + jnp.sum(value, axis=0, keepdims=True)
                return (
                    add(gain_sum, grad * zed), add(shift_sum, grad), add(out_sum, branch.astype(f32)), add(cot_sum, above),
                )

            gain_sum, shift_sum, out_sum, cot_sum = lax.fori_loop(0, rows // STEP, back_two, (zero,) * 4)
            vec_grads[...] = jnp.zeros_like(vec_grads)
            vec_grads[GAIN_TWO : GAIN_TWO + 1, :] = gain_sum
            vec_grads[SHIFT_TWO : SHIFT_TWO + 1, :] = shift_sum
            vec_grads[OUTPUT_BIAS : OUTPUT_BIAS + 1, :] = out_sum
            vec_grads[DOWN_BIAS : DOWN_BIAS + 1, :] = cot_sum
            put_mid = pltpu.make_async_copy(mid, mid_grad_kept, loc.at[0])
            put_block = pltpu.make_async_copy(cot, block_out, loc.at[7])
            put_mid.start()
            put_block.start()
            put_down(0).wait()
            for ch in range(4, 8):
                s.begin(ch)
            s.prepare(3)
            get_out.wait()
            down_w[0, low_part, :] = mul(normed_two[...], down_w[1], NT).astype(bf16)
            put_grad = pltpu.make_async_copy(down_w.at[0, low_part], attended_grad_kept, loc.at[1])
            put_grad.start()
            put_grad.wait()
            s.copy(attended_grad_kept.at[:, columns(1 - y)], grads.at[high_part], grad_s, grad_r, z, x, c, 1 - y).start()
            get_own = pltpu.make_async_copy(attended_grad_kept.at[:, columns(y)], grads.at[low_part], loc.at[1])
            get_own.start()
            s.cstage(3)
            s.prepare(4)
            down_stage[...] = mul(attended[...], normed_two[...], TN).astype(bf16)
            put_out = pltpu.make_async_copy(down_stage, out_wgrad, loc.at[5])
            put_out.start()
            s.cstage(4)
            s.xstage(2)
            s.zstage(1)
            s.prepare(5)
            s.cmove_sent(2)
            s.cmove_sent(3)
            get_own.wait()
            put_mid.wait()
            put_block.wait()
            put_out.wait()
            s.begin(8)

        pl.run_scoped(
            feed_phase,
            V((2, width, width), bf16),
            V((2, width, width), bf16),
            V((rows, width), f32),
            V((rows, width), f32),
            V((2, width, width), bf16),
            V((width, width), bf16),
            V((rows, width), f32),
            V((rows, width), bf16),
            V((rows, width), bf16),
        )

        def back_phase(qkv):
            get_qkv = pltpu.make_async_copy(qkv_kept, qkv, loc.at[1])
            get_qkv.start()

            def attention(exact, inverse, key_sum, value_sum, kept):
                get_exact = pltpu.make_async_copy(exact_kept, exact, loc.at[2])
                get_inverse = pltpu.make_async_copy(inverse_kept, inverse, loc.at[3])
                get_exact.start()
                get_inverse.start()
                blocks = length // SIZE

                def load(turn, head, slot):
                    return pltpu.make_async_copy(
                        weights_kept.at[2 * (turn % pairs) + head, tall(turn // pairs, SIZE)], kept.at[slot, head],
                        keep_sem.at[slot, head],
                    )

                for head in range(2):
                    load(0, head, 0).start()
                for get in (get_qkv, get_exact, get_inverse):
                    get.wait()
                low_lanes = lax.broadcasted_iota(jnp.int32, (SIZE, 128), 1) < HDIM

                def attend(turn, _):
                    block, pair, slot = turn // pairs, turn % pairs, turn % 2
                    for n, at in ((3, 5), (4, 12), (5, 19), (6, 26)):

                        @pl.when(turn == at)
                        def _(n=n):
                            service(n)

                    @pl.when(turn == pairs * (rows // SIZE))
                    def _():
                        s.copy(attended_grad_kept.at[:, columns(1 - y)], grads.at[high_part], grad_s, grad_r, z, x, c, 1 - y).wait_recv()

                    for head in range(2):
                        load(turn, head, slot).wait()

                    @pl.when(turn + 1 < blocks * pairs)
                    def _():
                        for head in range(2):
                            load(turn + 1, head, 1 - slot).start()

                    these = tall(block, SIZE)
                    at = pl.multiple_of(pair * 128, 128)
                    queries = qkv[these, pl.ds(at, 128)] * bf16(HDIM**-0.5)
                    keys = qkv[:, pl.ds(half + at, 128)]
                    values = qkv[:, pl.ds(2 * half + at, 128)]
                    low = (grads[these, pl.ds(at, 128)].astype(f32) * inverse[these, pl.ds(at, 128)]).astype(bf16)
                    product = low.astype(f32) * exact[these, pl.ds(at, 128)]
                    queries_t, low_t = queries.T, low.T
                    query_parts, key_parts, value_parts = [], [], []
                    for head in range(2):
                        own = low_lanes == (head == 0)
                        lanes = slice(HDIM * head, HDIM * head + HDIM)
                        masked = jnp.where(own, low, jnp.zeros_like(low))
                        prob_grad = mul(masked, values, NT)
                        delta = jnp.sum(jnp.where(own, product, 0.0), axis=1, keepdims=True)
                        weights = kept[slot, head]
                        score_grad = (weights.astype(f32) * (prob_grad - delta)).astype(bf16)
                        query_parts.append(mul(score_grad, keys, NN))
                        key_parts.append(mul(queries_t[lanes], score_grad, NN))
                        value_parts.append(mul(low_t[lanes], weights, NN))
                    query_grad = jnp.where(low_lanes, query_parts[0], query_parts[1]) * HDIM**-0.5
                    qkv[these, pl.ds(at, 128)] = query_grad.astype(bf16)
                    key_part = jnp.concatenate(key_parts, axis=0)
                    value_part = jnp.concatenate(value_parts, axis=0)
                    key_sum[pair] = jnp.where(block == 0, key_part, key_sum[pair] + key_part)
                    value_sum[pair] = jnp.where(block == 0, value_part, value_sum[pair] + value_part)
                    return 0

                lax.fori_loop(0, blocks * pairs, attend, 0)

                def finish(pair, _):
                    at = pl.multiple_of(pair * 128, 128)
                    qkv[:, pl.ds(half + at, 128)] = key_sum[pair].T.astype(bf16)
                    qkv[:, pl.ds(2 * half + at, 128)] = value_sum[pair].T.astype(bf16)
                    return 0

                lax.fori_loop(0, pairs, finish, 0)

            pl.run_scoped(
                attention,
                V((length, half), f32),
                V((length, half), f32),
                V((pairs, 128, length), f32),
                V((pairs, 128, length), f32),
                V((2, 2, SIZE, length), bf16),
            )

            def inputs(normed, weight, m_low, m_own, above, rows_in):
                gets = [
                    pltpu.make_async_copy(src, dst, loc.at[n])
                    for n, (src, dst) in enumerate(((all_qkv, weight), (normed_kept, normed), (mid_grad_kept, above), (x_own, rows_in)))
                ]
                for get in gets:
                    get.start()
                gets[0].wait()
                m_low[...] = mul(qkv[high_part, :], weight[...], NT).astype(bf16)
                sending = s.copy(m_low, from_y, m_s, m_r, z, x, c, 1 - y)
                sending.start()
                gets[1].wait()
                for n in range(3):
                    these = slice(n * half, (n + 1) * half)
                    qkv_wgrad[:, these] = mul(normed[...], qkv[:, these], TN).astype(bf16)
                    s.begin(early + n)
                s.xstage(early - 2)
                s.zstage(early - 3)
                s.prepare(early)
                m_own[...] = mul(qkv[low_part, :], weight[...], NT)
                s.cstage(early)
                s.xstage(early - 1)
                s.zstage(early - 2)
                s.prepare(early + 1)
                ones = jnp.ones((8, length), bf16)
                for row, n in ((QUERY_BIAS, 0), (VALUE_BIAS, 2)):
                    value = mul(ones, qkv[:, n * half : (n + 1) * half], NN)[0:1]
                    for other in range(BOTH):
                        these = slice(other * half, (other + 1) * half)
                        vec_grads[row : row + 1, these] = jnp.where(y == other, value, 0.0)
                s.cstage(early + 1)
                s.prepare(early + 2)
                s.xstage(early)
                s.zstage(early - 1)
                s.cstage(early + 2)
                s.xstage(early + 1)
                s.zstage(early)
                gets[2].wait()
                gets[3].wait()
                sending.wait()
                zero = jnp.zeros((1, width), f32)

                def back_one(i, so_far):
                    gain_sum, shift_sum = so_far
                    these = tall(i, STEP)
                    zed, inverse = normalized(rows_in[these, :].astype(f32))
                    grad = m_own[these, :] + from_y[these, :].astype(f32)
                    scaled = grad * vecs[GAIN_ONE : GAIN_ONE + 1, :]
                    part = inverse * (
                        scaled - jnp.mean(scaled, axis=-1, keepdims=True) - zed * jnp.mean(scaled * zed, axis=-1, keepdims=True)
                    )
                    above[these, :] = above[these, :] + part
                    add = lambda total_, value: total_ + jnp.sum(value, axis=0, keepdims=True)
                    return add(gain_sum, grad * zed), add(shift_sum, grad)

                gain_sum, shift_sum = lax.fori_loop(0, rows // STEP, back_one, (zero, zero))
                put = pltpu.make_async_copy(above, input_grad, loc.at[0])
                put.start()
                vec_grads[GAIN_ONE : GAIN_ONE + 1, :] = gain_sum
                vec_grads[SHIFT_ONE : SHIFT_ONE + 1, :] = shift_sum
                blank = jnp.zeros((6, 128), f32)
                for chip in range(2 * depth):
                    eight = vec_grads[:, 128 * chip : 128 * chip + 128]
                    for core in range(2):
                        at = 256 * (2 * chip + core)
                        block = jnp.concatenate([eight, up_bgrad[0:1, at : at + 128], up_bgrad[0:1, at + 128 : at + 256], blank], axis=0)
                        small_grads[pl.ds(32 * chip + 16 * core, 16), :] = block.astype(bf16)
                s.begin(total - 1)
                put.wait()

            pl.run_scoped(
                inputs,
                V((length, width), bf16),
                V((width, 3 * half), bf16),
                V((rows, width), bf16),
                V((rows, width), f32),
                V((rows, width), f32),
                V((rows, width), bf16),
            )

        pl.run_scoped(back_phase, V((length, 3 * half), bf16))
        s.prepare(total - 1)
        s.cstage(total - 1)
        s.xstage(total - 2)
        s.zstage(total - 3)
        s.xstage(total - 1)
        s.zstage(total - 2)
        for ch in range(3, total - 4):
            s.ystage(ch)
        s.zstage(total - 1)
        for ch in range(total - 4, total):
            s.ystage(ch)
        s.copy(attended_grad_kept.at[:, columns(1 - y)], grads.at[high_part], grad_s, grad_r, z, x, c, 1 - y).wait_send()
        for ch in range(total):
            s.sent(ch)

    high = width // (4 * depth)
    total = len(scatters)
    pl.run_scoped(
        rest,
        V((ring, 2 * depth, high, width), bf16),
        V((2, 2 * depth, high, width), bf16),
        V((total - 2, depth, high, width), bf16),
        V((total - 2, depth - 1, high, width), bf16),
        V((total - 2, high, width), bf16),
        V((total - 2, high, width), bf16),
        V((2, high, width), f32),
    )
    for ch in range(count):
        g.sent(ch)


def gather_chunks(high, width, wide, quarter):
    half = width // BOTH
    return (
        ((0, 0, 16, 0, 0, 128, False),)
        + tuple((1 + n, 0, high, None, n * half, half, False) for n in range(3))
        + tuple((6, quarter * i, quarter, 0, 0, width, True) for i in range(2))
        + ((4, 0, high, 0, 0, width, False),)
        + tuple((6, quarter * i, quarter, 0, 0, width, True) for i in range(2, 4))
        + tuple((5, 0, high, width * i, width * i, width, i > 1) for i in range(wide // width))
    )


def scatter_chunks(high, width, wide, owned):
    half = width // BOTH
    return (
        tuple((5, 0, high, width * j, width) for j in range(wide // width))
        + tuple((6, high * i, high, 0, width) for i in range(owned // high))
        + ((4, 0, high, 0, width),)
        + tuple((1 + n, 0, high, half * n, half) for n in range(3))
        + ((0, 0, 16, 0, 128),)
    )


def layer(small, own_query, own_key, own_value, own_out, own_up, own_down, x_own, cotangent, depth=DEPTH, ring=4):
    rows, width = x_own.shape
    length, half, wide = BOTH * rows, width // BOTH, own_up.shape[1]
    parts = 4 * depth
    high, owned = own_up.shape[0], own_down.shape[0]
    gathers = gather_chunks(high, width, wide, owned // 4)
    scatters = scatter_chunks(high, width, wide, owned)
    count, total = len(gathers), len(scatters)
    S, V = pltpu.SemaphoreType.DMA, pltpu.VMEM
    shape = jax.ShapeDtypeStruct
    out = [
        shape((rows, width), bf16), shape((rows, width), f32), shape((16, 128), f32),
        shape((high, width), f32), shape((high, width), f32), shape((high, width), f32), shape((high, width), f32),
        shape((high, wide), f32), shape((owned, width), f32),
        shape((parts * 16, 128), bf16), shape((width, 3 * half), bf16), shape((width, width), bf16), shape((width, wide), bf16),
        shape((wide, width), bf16), shape((length, width), bf16), shape((length, 3 * half), bf16), shape((length, half), f32),
        shape((length, half), f32), shape((half // HDIM, length, length), bf16), shape((rows, width), f32), shape((rows, width), bf16),
        shape((width, width), bf16), shape((width, wide), bf16), shape((wide, width), bf16),
        shape((total, 2 * depth, high, width), bf16),
    ]
    return pl.pallas_call(
        functools.partial(layer_kernel, depth, ring, gathers, scatters),
        out_shape=out,
        in_specs=[pl.BlockSpec(memory_space=pl.ANY)] * 9,
        out_specs=[pl.BlockSpec(memory_space=pl.ANY)] * len(out),
        scratch_shapes=[
            V((rows, width), bf16), V((rows, width), bf16), V((length, half), bf16), V((8, width), f32), V((1, wide), f32),
            V((8, width), f32), V((1, wide), f32), V((width, 3 * half), bf16), V((parts * 16, 128), bf16),
        ]
        + gather_sems(depth, count)
        + [
            S((ring, 2 * depth)), S((2,)), S((total, 2 * depth)), S((total, 2 * depth)), S((total, depth)), S((total, depth)),
            S((total, depth)), S((total, depth)), S((total,)), S((total,)), S((2,)),
            pltpu.SemaphoreType.REGULAR, S, S, S((half // 128,)), S((half // 128,)), S, S, S, S, S((8,)), S((2, 2)), S((2, half // 128)),
        ],
        compiler_params=pltpu.CompilerParams(collective_id=1, has_side_effects=True, vmem_limit_bytes=63 * 2**20),
        name="encoder_layer",
    )(small, own_query, own_key, own_value, own_out, own_up, own_down, x_own, cotangent)[:9]


def pack_small(vectors, up_bias, c):
    rows = jnp.stack(vectors)
    zero = jnp.zeros_like(rows)
    rows = jnp.concatenate([jnp.where(c == 0, rows, zero), jnp.where(c == 0, zero, rows)], axis=1)
    return jnp.concatenate([rows, up_bias.reshape(2, 128), jnp.zeros((6, 128), rows.dtype)], axis=0)


def fast_device(
    activations, cotangent, query_weight, key_weight, value_weight, output_weight, first_gain, first_shift,
    query_bias, value_bias, output_bias, up_weight, down_weight, second_gain, second_shift, up_bias, down_bias,
):
    c = lax.axis_index("fsdp") % 2
    small = pack_small(
        (first_gain, first_shift, query_bias, value_bias, output_bias, second_gain, second_shift, down_bias), up_bias, c
    )
    block_out, input_grad, own_small, own_query, own_key, own_value, own_output, own_up, own_down = layer(
        small, query_weight, key_weight, value_weight, output_weight, up_weight, down_weight, activations[0], cotangent[0]
    )
    own_vecs = lax.dynamic_slice_in_dim(own_small, c * 64, 64, 1)
    return (
        block_out.reshape(activations.shape),
        input_grad.reshape(activations.shape),
        own_query,
        own_key,
        own_value,
        own_output,
        own_vecs[0],
        own_vecs[1],
        own_vecs[2],
        own_vecs[3],
        own_vecs[4],
        own_up,
        own_down,
        own_vecs[5],
        own_vecs[6],
        own_small[8:10].reshape(-1),
        own_vecs[7],
    )


def solution(mesh):
    fits = mesh.shape["fsdp"] == 4 * DEPTH and mesh.shape["ctx"] == BOTH
    return jax.shard_map(
        fast_device if fits else plain_device,
        mesh=mesh,
        in_specs=(
            P("fsdp", "ctx", None),
            P("fsdp", "ctx", None),
            P("fsdp", None),
            P("fsdp", None),
            P("fsdp", None),
            P("fsdp", None),
            P("fsdp"),
            P("fsdp"),
            P("fsdp"),
            P("fsdp"),
            P("fsdp"),
            P("fsdp", None),
            P("fsdp", None),
            P("fsdp"),
            P("fsdp"),
            P("fsdp"),
            P("fsdp"),
        ),
        out_specs=(
            P("fsdp", "ctx", None),
            P("fsdp", "ctx", None),
            P("fsdp", None),
            P("fsdp", None),
            P("fsdp", None),
            P("fsdp", None),
            P("fsdp"),
            P("fsdp"),
            P("fsdp"),
            P("fsdp"),
            P("fsdp"),
            P("fsdp", None),
            P("fsdp", None),
            P("fsdp"),
            P("fsdp"),
            P("fsdp"),
            P("fsdp"),
        ),
        check_vma=False,
    )
```

```python
import functools

import jax
import jax.numpy as jnp
from jax import lax
from jax.experimental import pallas as pl
from jax.experimental.pallas import tpu as pltpu
from jax.sharding import PartitionSpec as P

HEADS = 16
HDIM = 64
MESH = pl.DeviceIdType.MESH


epsilon = 1e-05


def layer_norm(token_rows, gain, shift):
    centered = token_rows - jnp.mean(token_rows, axis=-1, keepdims=True)
    variance = jnp.mean(centered * centered, axis=-1, keepdims=True)
    return centered * lax.rsqrt(variance + epsilon) * gain + shift


def gelu_act(values_in):
    return jax.nn.gelu(values_in, approximate=True)


def gather_attention(shards):
    return (
        lax.all_gather(shards[0], "fsdp", axis=0, tiled=True),
        lax.all_gather(shards[1], "fsdp", axis=0, tiled=True),
        lax.all_gather(shards[2], "fsdp", axis=0, tiled=True),
        lax.all_gather(shards[3], "fsdp", axis=0, tiled=True),
        lax.all_gather(shards[4], "fsdp", axis=0, tiled=True),
        lax.all_gather(shards[5], "fsdp", axis=0, tiled=True),
        lax.all_gather(shards[6], "fsdp", axis=0, tiled=True),
        lax.all_gather(shards[7], "fsdp", axis=0, tiled=True),
        lax.all_gather(shards[8], "fsdp", axis=0, tiled=True),
    )


def gather_feed(shards):
    return (
        lax.all_gather(shards[0], "fsdp", axis=0, tiled=True),
        lax.all_gather(shards[1], "fsdp", axis=0, tiled=True),
        lax.all_gather(shards[2], "fsdp", axis=0, tiled=True),
        lax.all_gather(shards[3], "fsdp", axis=0, tiled=True),
        lax.all_gather(shards[4], "fsdp", axis=0, tiled=True),
        lax.all_gather(shards[5], "fsdp", axis=0, tiled=True),
    )


def plain_device(
    activations,
    cotangent,
    query_weight,
    key_weight,
    value_weight,
    output_weight,
    first_gain,
    first_shift,
    query_bias,
    value_bias,
    output_bias,
    up_weight,
    down_weight,
    second_gain,
    second_shift,
    up_bias,
    down_bias,
):
    clip_count, local_len, width = activations.shape
    scaling = HDIM ** (-0.5)
    attend_shards = (
        query_weight,
        key_weight,
        value_weight,
        output_weight,
        first_gain,
        first_shift,
        query_bias,
        value_bias,
        output_bias,
    )
    feed_shards = (up_weight, down_weight, second_gain, second_shift, up_bias, down_bias)
    attend_full = gather_attention(attend_shards)
    (
        full_query,
        full_key,
        full_value,
        full_output,
        full_gain_one,
        full_shift_one,
        full_query_bias,
        full_value_bias,
        full_output_bias,
    ) = attend_full
    gain_one = full_gain_one.astype(jnp.float32)
    shift_one = full_shift_one.astype(jnp.float32)
    token_rows = activations.reshape(-1, width).astype(jnp.float32)
    normed_one = layer_norm(token_rows, gain_one, shift_one).astype(jnp.bfloat16)
    queries = (
        jnp.dot(normed_one, full_query, preferred_element_type=jnp.float32)
        + full_query_bias.astype(jnp.float32)
    ).astype(jnp.bfloat16)
    keys_local = jnp.dot(normed_one, full_key, preferred_element_type=jnp.float32).astype(
        jnp.bfloat16
    )
    values_local = (
        jnp.dot(normed_one, full_value, preferred_element_type=jnp.float32)
        + full_value_bias.astype(jnp.float32)
    ).astype(jnp.bfloat16)
    query_heads = queries.reshape(clip_count, local_len, HEADS, HDIM)
    keys_block = keys_local.reshape(clip_count, local_len, width)
    values_block = values_local.reshape(clip_count, local_len, width)
    run_max = jnp.full((clip_count, local_len, HEADS), -1e30, jnp.float32)
    key_piece = lax.all_gather(keys_block, "ctx", axis=1, tiled=True)
    value_piece = lax.all_gather(values_block, "ctx", axis=1, tiled=True)
    key_heads = key_piece.reshape(clip_count, -1, HEADS, HDIM)
    value_heads = value_piece.reshape(clip_count, -1, HEADS, HDIM)
    scores = (
        jnp.einsum("cqhd,ckhd->cqhk", query_heads, key_heads, preferred_element_type=jnp.float32)
        * scaling
    )
    new_max = jnp.maximum(run_max, jnp.max(scores, axis=-1))
    weights = jnp.exp(scores - new_max[..., None])
    run_sum = jnp.sum(weights, axis=-1)
    accum = jnp.einsum(
        "cqhk,ckhd->cqhd",
        weights.astype(jnp.bfloat16),
        value_heads,
        preferred_element_type=jnp.float32,
    )
    run_max, run_sum, accum = (new_max, run_sum, accum)
    attend_exact = accum / run_sum[..., None]
    log_total = run_max + jnp.log(run_sum)
    attended = attend_exact.reshape(-1, width).astype(jnp.bfloat16)
    mid_rows = (
        token_rows
        + jnp.dot(attended, full_output, preferred_element_type=jnp.float32)
        + full_output_bias.astype(jnp.float32)
    )
    feed_full = gather_feed(feed_shards)
    full_up, full_down, full_gain_two, full_shift_two, full_up_bias, full_down_bias = feed_full
    gain_two = full_gain_two.astype(jnp.float32)
    shift_two = full_shift_two.astype(jnp.float32)
    normed_two = layer_norm(mid_rows, gain_two, shift_two).astype(jnp.bfloat16)
    pre_act = jnp.dot(
        normed_two, full_up, preferred_element_type=jnp.float32
    ) + full_up_bias.astype(jnp.float32)
    hidden = gelu_act(pre_act).astype(jnp.bfloat16)
    block_rows = (
        mid_rows
        + jnp.dot(hidden, full_down, preferred_element_type=jnp.float32)
        + full_down_bias.astype(jnp.float32)
    )
    block_out = block_rows.astype(jnp.bfloat16).reshape(activations.shape)
    back_attend = gather_attention(attend_shards)
    back_feed = gather_feed(feed_shards)
    back_query, back_key, back_value, back_output = (
        back_attend[0],
        back_attend[1],
        back_attend[2],
        back_attend[3],
    )
    back_up, back_down = (back_feed[0], back_feed[1])
    cot_rows = cotangent.reshape(-1, width)
    outer_grad = cot_rows.astype(jnp.float32)
    down_wgrad = jnp.einsum("rf,rd->fd", hidden, cot_rows, preferred_element_type=jnp.float32)
    down_bgrad = jnp.sum(outer_grad, axis=0)
    hidden_grad = jnp.einsum("rd,fd->rf", cot_rows, back_down, preferred_element_type=jnp.float32)
    _, gelu_back = jax.vjp(gelu_act, pre_act)
    pre_grad = gelu_back(hidden_grad)[0].astype(jnp.bfloat16)
    up_wgrad = jnp.einsum("rd,rf->df", normed_two, pre_grad, preferred_element_type=jnp.float32)
    up_bgrad = jnp.sum(pre_grad.astype(jnp.float32), axis=0)
    normed_two_grad = jnp.einsum("rf,df->rd", pre_grad, back_up, preferred_element_type=jnp.float32)
    _, norm_two_back = jax.vjp(layer_norm, mid_rows, gain_two, shift_two)
    mid_part, gain_two_grad, shift_two_grad = norm_two_back(normed_two_grad)
    mid_grad = outer_grad + mid_part
    feed_owned = (
        lax.psum_scatter(
            up_wgrad.astype(jnp.bfloat16), "fsdp", scatter_dimension=0, tiled=True
        ).astype(jnp.float32),
        lax.psum_scatter(
            down_wgrad.astype(jnp.bfloat16), "fsdp", scatter_dimension=0, tiled=True
        ).astype(jnp.float32),
        lax.psum_scatter(
            gain_two_grad.astype(jnp.bfloat16), "fsdp", scatter_dimension=0, tiled=True
        ).astype(jnp.float32),
        lax.psum_scatter(
            shift_two_grad.astype(jnp.bfloat16), "fsdp", scatter_dimension=0, tiled=True
        ).astype(jnp.float32),
        lax.psum_scatter(
            up_bgrad.astype(jnp.bfloat16), "fsdp", scatter_dimension=0, tiled=True
        ).astype(jnp.float32),
        lax.psum_scatter(
            down_bgrad.astype(jnp.bfloat16), "fsdp", scatter_dimension=0, tiled=True
        ).astype(jnp.float32),
    )
    feed_done = (
        lax.psum(feed_owned[0].astype(jnp.bfloat16), "ctx").astype(jnp.float32),
        lax.psum(feed_owned[1].astype(jnp.bfloat16), "ctx").astype(jnp.float32),
        lax.psum(feed_owned[2].astype(jnp.bfloat16), "ctx").astype(jnp.float32),
        lax.psum(feed_owned[3].astype(jnp.bfloat16), "ctx").astype(jnp.float32),
        lax.psum(feed_owned[4].astype(jnp.bfloat16), "ctx").astype(jnp.float32),
        lax.psum(feed_owned[5].astype(jnp.bfloat16), "ctx").astype(jnp.float32),
    )
    branch_grad = mid_grad.astype(jnp.bfloat16)
    output_wgrad = jnp.einsum(
        "rd,re->de", attended, branch_grad, preferred_element_type=jnp.float32
    )
    output_bgrad = jnp.sum(branch_grad.astype(jnp.float32), axis=0)
    attended_grad = jnp.einsum(
        "re,de->rd", branch_grad, back_output, preferred_element_type=jnp.float32
    ).astype(jnp.bfloat16)
    grad_heads = attended_grad.reshape(clip_count, local_len, HEADS, HDIM)
    delta = jnp.sum(grad_heads.astype(jnp.float32) * attend_exact, axis=-1)
    keys_whole, values_whole = (
        lax.all_gather(keys_block, "ctx", axis=1, tiled=True),
        lax.all_gather(values_block, "ctx", axis=1, tiled=True),
    )
    key_heads_all = keys_whole.reshape(clip_count, -1, HEADS, HDIM)
    value_heads_all = values_whole.reshape(clip_count, -1, HEADS, HDIM)
    scores_all = (
        jnp.einsum(
            "cqhd,ckhd->cqhk", query_heads, key_heads_all, preferred_element_type=jnp.float32
        )
        * scaling
    )
    probs = jnp.exp(scores_all - log_total[..., None])
    prob_grad = jnp.einsum(
        "cqhd,ckhd->cqhk", grad_heads, value_heads_all, preferred_element_type=jnp.float32
    )
    score_grad = (probs * (prob_grad - delta[..., None])).astype(jnp.bfloat16)
    query_grad = (
        jnp.einsum("cqhk,ckhd->cqhd", score_grad, key_heads_all, preferred_element_type=jnp.float32)
        * scaling
    ).astype(jnp.bfloat16)
    query_grad = query_grad.reshape(-1, width)
    probs_low = probs.astype(jnp.bfloat16)
    key_part = (
        jnp.einsum("cqhk,cqhd->kchd", score_grad, query_heads, preferred_element_type=jnp.float32)
        * scaling
    )
    value_part = jnp.einsum(
        "cqhk,cqhd->kchd", probs_low, grad_heads, preferred_element_type=jnp.float32
    )
    summed = lax.psum_scatter(
        jnp.stack([key_part, value_part], axis=2)
        .reshape(lax.axis_size("ctx") * local_len, clip_count, 2, width)
        .astype(jnp.bfloat16),
        "ctx",
        scatter_dimension=0,
        tiled=True,
    ).astype(jnp.float32)
    key_grad = jnp.transpose(summed[:, :, 0], (1, 0, 2)).reshape(-1, width).astype(jnp.bfloat16)
    value_grad = jnp.transpose(summed[:, :, 1], (1, 0, 2)).reshape(-1, width).astype(jnp.bfloat16)
    query_wgrad = jnp.einsum(
        "rd,re->de", normed_one, query_grad, preferred_element_type=jnp.float32
    )
    key_wgrad = jnp.einsum("rd,re->de", normed_one, key_grad, preferred_element_type=jnp.float32)
    value_wgrad = jnp.einsum(
        "rd,re->de", normed_one, value_grad, preferred_element_type=jnp.float32
    )
    query_bgrad = jnp.sum(query_grad.astype(jnp.float32), axis=0)
    value_bgrad = jnp.sum(value_grad.astype(jnp.float32), axis=0)
    normed_one_grad = (
        jnp.einsum("re,de->rd", query_grad, back_query, preferred_element_type=jnp.float32)
        + jnp.einsum("re,de->rd", key_grad, back_key, preferred_element_type=jnp.float32)
        + jnp.einsum("re,de->rd", value_grad, back_value, preferred_element_type=jnp.float32)
    )
    _, norm_one_back = jax.vjp(layer_norm, token_rows, gain_one, shift_one)
    input_part, gain_one_grad, shift_one_grad = norm_one_back(normed_one_grad)
    input_grad = (mid_grad + input_part).reshape(activations.shape)
    attend_owned = (
        lax.psum_scatter(
            query_wgrad.astype(jnp.bfloat16), "fsdp", scatter_dimension=0, tiled=True
        ).astype(jnp.float32),
        lax.psum_scatter(
            key_wgrad.astype(jnp.bfloat16), "fsdp", scatter_dimension=0, tiled=True
        ).astype(jnp.float32),
        lax.psum_scatter(
            value_wgrad.astype(jnp.bfloat16), "fsdp", scatter_dimension=0, tiled=True
        ).astype(jnp.float32),
        lax.psum_scatter(
            output_wgrad.astype(jnp.bfloat16), "fsdp", scatter_dimension=0, tiled=True
        ).astype(jnp.float32),
        lax.psum_scatter(
            gain_one_grad.astype(jnp.bfloat16), "fsdp", scatter_dimension=0, tiled=True
        ).astype(jnp.float32),
        lax.psum_scatter(
            shift_one_grad.astype(jnp.bfloat16), "fsdp", scatter_dimension=0, tiled=True
        ).astype(jnp.float32),
        lax.psum_scatter(
            query_bgrad.astype(jnp.bfloat16), "fsdp", scatter_dimension=0, tiled=True
        ).astype(jnp.float32),
        lax.psum_scatter(
            value_bgrad.astype(jnp.bfloat16), "fsdp", scatter_dimension=0, tiled=True
        ).astype(jnp.float32),
        lax.psum_scatter(
            output_bgrad.astype(jnp.bfloat16), "fsdp", scatter_dimension=0, tiled=True
        ).astype(jnp.float32),
    )
    attend_done = (
        lax.psum(attend_owned[0].astype(jnp.bfloat16), "ctx").astype(jnp.float32),
        lax.psum(attend_owned[1].astype(jnp.bfloat16), "ctx").astype(jnp.float32),
        lax.psum(attend_owned[2].astype(jnp.bfloat16), "ctx").astype(jnp.float32),
        lax.psum(attend_owned[3].astype(jnp.bfloat16), "ctx").astype(jnp.float32),
        lax.psum(attend_owned[4].astype(jnp.bfloat16), "ctx").astype(jnp.float32),
        lax.psum(attend_owned[5].astype(jnp.bfloat16), "ctx").astype(jnp.float32),
        lax.psum(attend_owned[6].astype(jnp.bfloat16), "ctx").astype(jnp.float32),
        lax.psum(attend_owned[7].astype(jnp.bfloat16), "ctx").astype(jnp.float32),
        lax.psum(attend_owned[8].astype(jnp.bfloat16), "ctx").astype(jnp.float32),
    )
    return (
        block_out,
        input_grad,
        attend_done[0],
        attend_done[1],
        attend_done[2],
        attend_done[3],
        attend_done[4],
        attend_done[5],
        attend_done[6],
        attend_done[7],
        attend_done[8],
        feed_done[0],
        feed_done[1],
        feed_done[2],
        feed_done[3],
        feed_done[4],
        feed_done[5],
    )


def place():
    f = lax.axis_index("fsdp"); y = lax.axis_index("ctx")
    return f // 4, (f // 2) % 2, f % 2, y

def partners(z, x, c, y, depth):
    index = lambda dz, dx, dc: dz * 4 + dx * 2 + dc
    along = [(index((z + k) % depth, x, c), y) for k in range(1, depth)]
    return along + [(index(z, 1 - x, c), y), (index(z, x, 1 - c), y), (index(z, x, c), 1 - y)]


def greet(z, x, c, y, depth):
    barrier = pltpu.get_barrier_semaphore()
    for partner in partners(z, x, c, y, depth):
        pl.semaphore_signal(barrier, inc=1, device_id=partner, device_id_type=MESH)
    pl.semaphore_wait(barrier, depth + 2)


class Gather:
    def __init__(self, depth, chunks, ins, outs, sems, where):
        self.depth, self.chunks, self.ins, self.outs = depth, chunks, ins, outs
        self.zs, self.zr, self.xs, self.xr, self.ys, self.yr, self.cs, self.cr, self.loc = sems
        self.where = where
    def source(self, ch, first, count):
        t, _, _, there, _, w, _ = self.chunks[ch]
        if there is None:
            there = pl.multiple_of(self.where[3] * w, 128)
        return self.ins[t].at[pl.ds(first, count), pl.ds(there, w)]
    def src(self, ch, half):
        _, r0, h, _, _, _, both = self.chunks[ch]
        if not both: return self.source(ch, r0, h)
        h2 = h // 2
        return self.source(ch, pl.multiple_of(r0 + half * h2, 16), h2)
    def dst(self, ch, dz, dx, dc, half):
        t, r0, h, _, c0, w, both = self.chunks[ch]
        full = self.ins[t].shape[0]
        start = (dz * 4 + dx * 2 + dc) * full + r0
        if not both: return self.outs[t].at[pl.ds(pl.multiple_of(start, 16), h), pl.ds(c0, w)]
        h2 = h // 2
        return self.outs[t].at[pl.ds(pl.multiple_of(start + half * h2, 16), h2), pl.ds(c0, w)]
    def copy(self, src, dst, s, r, dz, dx, dc, dy):
        return pltpu.make_async_remote_copy(src_ref=src, dst_ref=dst, send_sem=s, recv_sem=r,
            device_id=(dz * 4 + dx * 2 + dc, dy), device_id_type=MESH)
    def zz(self, j):
        return (self.where[0] - j + self.depth) % self.depth
    def zmove(self, ch, k, recv=False):
        z, x, c, y = self.where
        if recv:
            d = self.dst(ch, self.zz(k), x, c, y)
            return self.copy(d, d, self.zs.at[ch, k], self.zr.at[ch, k], z, x, 1 - c, y)
        return self.copy(self.src(ch, y), self.dst(ch, z, x, c, y), self.zs.at[ch, k], self.zr.at[ch, k], (z + k) % self.depth, x, c, y)
    def xmove(self, ch, j, recv=False):
        z, x, c, y = self.where
        d = self.dst(ch, self.zz(j), 1 - x if recv else x, c, y)
        s = self.src(ch, y) if (j == 0 and not recv) else d
        return self.copy(s, d, self.xs.at[ch, j], self.xr.at[ch, j], z, 1 - x, c, y)
    def ymove(self, ch, i, j, recv=False):
        z, x, c, y = self.where
        d = self.dst(ch, self.zz(j), x if i == 0 else 1 - x, c, 1 - y if recv else y)
        n = i * self.depth + j
        return self.copy(d, d, self.ys.at[ch, n], self.yr.at[ch, n], z, x, c, 1 - y)
    def cmove(self, ch, i, j, other, recv=False):
        z, x, c, y = self.where
        half = 1 - y if other else y
        d = self.dst(ch, self.zz(j), x if i == 0 else 1 - x, 1 - c if recv else c, half)
        s = self.src(ch, half) if (i == 0 and j == 0 and not recv) else d
        n = (i * self.depth + j) + (2 * self.depth if other else 0)
        return self.copy(s, d, self.cs.at[ch, n], self.cr.at[ch, n], z, x, 1 - c, y)
    def own(self, ch):
        z, x, c, y = self.where
        t, r0, h, _, c0, w, both = self.chunks[ch]
        full = self.ins[t].shape[0]
        there = self.outs[t].at[pl.ds(pl.multiple_of((z * 4 + x * 2 + c) * full + r0, 16), h), pl.ds(c0, w)]
        return pltpu.make_async_copy(self.source(ch, r0, h), there, self.loc.at[ch])
    def begin(self, ch):
        for k in range(1, self.depth): self.zmove(ch, k).start()
        self.xmove(ch, 0).start()
        self.cmove(ch, 0, 0, False).start()
        if self.chunks[ch][6]: self.cmove(ch, 0, 0, True).start()
        self.own(ch).start()
    def zstage(self, ch):
        for k in range(1, self.depth):
            self.zmove(ch, k, True).wait_recv()
            self.xmove(ch, k).start()
            if self.chunks[ch][6]: self.ymove(ch, 0, k).start()
            self.cmove(ch, 0, k, False).start()
    def xstage(self, ch):
        for j in range(self.depth):
            self.xmove(ch, j, True).wait_recv()
            if self.chunks[ch][6]: self.ymove(ch, 1, j).start()
            self.cmove(ch, 1, j, False).start()
    def ystage(self, ch):
        if not self.chunks[ch][6]: return
        for i in range(2):
            for j in range(1 - i, self.depth):
                self.ymove(ch, i, j, True).wait_recv()
                self.cmove(ch, i, j, True).start()
    def arrived(self, ch):
        for i in range(2):
            for j in range(self.depth):
                self.cmove(ch, i, j, False, True).wait_recv()
                if self.chunks[ch][6]: self.cmove(ch, i, j, True, True).wait_recv()
        self.own(ch).wait()
    def sent(self, ch):
        both = self.chunks[ch][6]
        for k in range(1, self.depth): self.zmove(ch, k).wait_send()
        for j in range(self.depth): self.xmove(ch, j).wait_send()
        for i in range(2):
            for j in range(self.depth):
                self.cmove(ch, i, j, False).wait_send()
                if both:
                    self.cmove(ch, i, j, True).wait_send()
                    if i or j: self.ymove(ch, i, j).wait_send()

def gather_sems(depth, n):
    S = pltpu.SemaphoreType.DMA
    return [S((n, depth)), S((n, depth)), S((n, depth)), S((n, depth)), S((n, 2 * depth)), S((n, 2 * depth)), S((n, 4 * depth)), S((n, 4 * depth)), S((n,))]


DEPTH, BOTH = 4, 2
f32, bf16 = jnp.float32, jnp.bfloat16
NT = (((1,), (1,)), ((), ()))
NN = (((1,), (0,)), ((), ()))
TN = (((0,), (0,)), ((), ()))
SQRT_2_PI = 0.7978845608028654


def mul(a, b, dims):
    return lax.dot_general(a, b, dims, preferred_element_type=f32)


def tall(i, size):
    return pl.ds(pl.multiple_of(i * size, 16), size)


def normalized(rows):
    centered = rows - jnp.mean(rows, axis=-1, keepdims=True)
    inverse = lax.rsqrt(jnp.mean(centered * centered, axis=-1, keepdims=True) + epsilon)
    return centered * inverse, inverse


def tiled(h, w, body):
    def one(i, _):
        body(pl.ds(pl.multiple_of(i * 16, 16), 16), pl.ds(0, w))
        return 0

    if h == 16:
        one(0, 0)
    else:
        lax.fori_loop(0, h // 16, one, 0)


class Scatter:
    def __init__(self, depth, ring, chunks, grads, outs, bufs, sems, where):
        self.depth, self.ring, self.chunks, self.grads, self.outs = depth, ring, chunks, grads, outs
        self.landed, self.sums, self.near, self.across, self.along, self.mine, self.theirs, self.stage = bufs
        self.ls, self.gs, self.cs, self.cr, self.xs, self.xr, self.zs, self.zr, self.ys, self.yr, self.ps = sems
        self.where = where

    def spot(self, ch):
        first = len(self.chunks) - 4
        if ch < first:
            return ch, 0
        return first + (ch - first) // 2, (ch - first) % 2 * (self.mine.shape[-1] // 2)

    def landing(self, ref, ch, *at):
        n, col = self.spot(ch)
        return ref.at[(n, *at, pl.ds(0, self.chunks[ch][2]), pl.ds(col, self.chunks[ch][4]))]

    def part(self, ref, ch):
        return ref.at[pl.ds(0, self.chunks[ch][2]), pl.ds(0, self.chunks[ch][4])]

    def piece(self, ch, dz, dx, dc):
        t, r0, h, c0, w = self.chunks[ch]
        full = self.grads[t].shape[0] // (4 * self.depth)
        if t == 5:
            return self.held.at[ch % 2, pl.ds(pl.multiple_of((dz * 4 + dx * 2 + dc) * full, 16), h), :]
        return self.grads[t].at[pl.ds(pl.multiple_of((dz * 4 + dx * 2 + dc) * full + r0, 16), h), pl.ds(c0, w)]

    def copy(self, src, dst, s, r, dz, dx, dc, dy):
        return pltpu.make_async_remote_copy(
            src_ref=src, dst_ref=dst, send_sem=s, recv_sem=r, device_id=(dz * 4 + dx * 2 + dc, dy), device_id_type=MESH
        )

    def zz(self, j):
        return (self.where[0] + j) % self.depth

    def load(self, ch, n):
        z, x, c, y = self.where
        i, j = n // self.depth, n % self.depth
        slot = ch % self.ring
        return pltpu.make_async_copy(
            self.piece(ch, self.zz(j), x if i == 0 else 1 - x, c), self.part(self.sums.at[slot, n], ch), self.ls.at[slot, n]
        )

    def fetch(self, ch):
        t, r0, h, c0, w = self.chunks[ch]
        return pltpu.make_async_copy(
            self.landed.at[ch, :, pl.ds(0, h), pl.ds(0, w)], self.near.at[ch % 2, :, pl.ds(0, h), pl.ds(0, w)], self.gs.at[ch % 2]
        )

    def cmove(self, ch, n):
        z, x, c, y = self.where
        i, j = n // self.depth, n % self.depth
        return self.copy(
            self.piece(ch, self.zz(j), x if i == 0 else 1 - x, 1 - c), self.part(self.landed.at[ch, n], ch),
            self.cs.at[ch, n], self.cr.at[ch, n], z, x, 1 - c, y,
        )

    def xmove(self, ch, j):
        z, x, c, y = self.where
        return self.copy(
            self.part(self.sums.at[ch % self.ring, self.depth + j], ch), self.landing(self.across, ch, j),
            self.xs.at[ch, j], self.xr.at[ch, j], z, 1 - x, c, y,
        )

    def zmove(self, ch, j):
        z, x, c, y = self.where
        return self.copy(
            self.part(self.sums.at[ch % self.ring, j], ch), self.landing(self.along, ch, j - 1),
            self.zs.at[ch, j], self.zr.at[ch, j], self.zz(j), x, c, y,
        )

    def ymove(self, ch):
        z, x, c, y = self.where
        return self.copy(
            self.landing(self.mine, ch), self.landing(self.theirs, ch), self.ys.at[ch], self.yr.at[ch], z, x, c, 1 - y
        )

    def begin(self, ch):
        for n in range(2 * self.depth):
            self.cmove(ch, n).start()

    def cmove_sent(self, ch):
        for n in range(2 * self.depth):
            self.cmove(ch, n).wait_send()

    def prepare(self, ch):
        if ch >= self.ring:
            for j in range(self.depth):
                self.xmove(ch - self.ring, j).wait_send()
                if j:
                    self.zmove(ch - self.ring, j).wait_send()
        for n in range(2 * self.depth):
            self.load(ch, n).start()
        for n in range(2 * self.depth):
            self.cmove(ch, n).wait_recv()
        self.fetch(ch).start()

    def cstage(self, ch):
        t, r0, h, c0, w = self.chunks[ch]
        slot = ch % self.ring
        for n in range(2 * self.depth):
            self.load(ch, n).wait()
        self.fetch(ch).wait()

        def add(r, q):
            self.sums[slot, :, r, q] = self.sums[slot, :, r, q] + self.near[ch % 2, :, r, q]

        tiled(h, w, add)
        for j in range(self.depth):
            self.xmove(ch, j).start()

    def xstage(self, ch):
        t, r0, h, c0, w = self.chunks[ch]
        slot, count = ch % self.ring, self.depth
        at, col = self.spot(ch)
        there = pl.ds(col, w)
        for j in range(count):
            self.xmove(ch, j).wait_recv()

        def add(r, q):
            self.sums[slot, 0:count, r, q] = self.sums[slot, 0:count, r, q] + self.across[at, :, r, there]

        tiled(h, w, add)
        for j in range(1, count):
            self.zmove(ch, j).start()

    def zstage(self, ch):
        t, r0, h, c0, w = self.chunks[ch]
        at, col = self.spot(ch)
        there = pl.ds(col, w)
        for j in range(1, self.depth):
            self.zmove(ch, j).wait_recv()

        def add(r, q):
            total = self.sums[ch % self.ring, 0, r, q].astype(f32)
            for j in range(1, self.depth):
                total = total + self.along[at, j - 1, r, there].astype(f32)
            self.mine[at, r, there] = total.astype(bf16)

        tiled(h, w, add)
        self.ymove(ch).start()

    def put(self, ch):
        t, r0, h, c0, w = self.chunks[ch]
        split = 1 <= t <= 3
        there = pl.ds(0, 2 * w) if split else pl.ds(c0, w)
        return pltpu.make_async_copy(
            self.stage.at[ch % 2, pl.ds(0, h), pl.ds(0, 2 * w if split else w)], self.outs[t].at[pl.ds(r0, h), there], self.ps.at[ch % 2]
        )

    def ystage(self, ch):
        t, r0, h, c0, w = self.chunks[ch]
        y = self.where[3]
        at, col = self.spot(ch)
        there = pl.ds(col, w)
        self.ymove(ch).wait_recv()
        if ch >= 2:
            self.put(ch - 2).wait()

        def lay(r, q):
            mine, theirs = self.mine[at, r, there].astype(f32), self.theirs[at, r, there].astype(f32)
            if 1 <= t <= 3:
                self.stage[ch % 2, r, 0:w] = jnp.where(y == 0, mine, theirs)
                self.stage[ch % 2, r, w : 2 * w] = jnp.where(y == 0, theirs, mine)
            else:
                self.stage[ch % 2, r, q] = mine + theirs

        tiled(h, w, lay)
        self.put(ch).start()

    def sent(self, ch):
        if self.chunks[ch][0] != 5:
            self.cmove_sent(ch)
        if ch + self.ring >= len(self.chunks):
            for j in range(self.depth):
                self.xmove(ch, j).wait_send()
                if j:
                    self.zmove(ch, j).wait_send()
        self.ymove(ch).wait_send()
        if ch + 2 >= len(self.chunks):
            self.put(ch).wait()


GAIN_ONE, SHIFT_ONE, QUERY_BIAS, VALUE_BIAS, OUTPUT_BIAS, GAIN_TWO, SHIFT_TWO, DOWN_BIAS = range(8)
STEP = 112
SIZE = 224


def layer_kernel(depth, ring, gathers, scatters, *refs):
    (
        small, own_query, own_key, own_value, own_out, own_up, own_down, x_own, cotangent,
        block_out, input_grad, own_small, own_query_grad, own_key_grad, own_value_grad, own_out_grad, own_up_grad, own_down_grad,
        all_small, all_qkv, all_out, all_up, all_down, normed_kept, qkv_kept, exact_kept, inverse_kept, weights_kept,
        mid_grad_kept, attended_grad_kept, out_wgrad, up_wgrad, down_wgrad, landed,
        from_y, attended, grads, vecs, up_bias, vec_grads, up_bgrad, qkv_wgrad, small_grads,
    ) = refs[:43]
    gather_sems_, scatter_sems_ = refs[43:52], refs[52:63]
    entered, swap_s, swap_r, att_s, att_r, grad_s, grad_r, m_s, m_r, loc, keep_sem, pair_sem = refs[63:]
    z, x, c, y = place()
    rows, width = x_own.shape
    length, half = BOTH * rows, width // BOTH
    pairs = half // 128
    wide = up_bias.shape[1]
    tiles = wide // width
    V = pltpu.VMEM
    low_part, high_part = pl.ds(0, rows), pl.ds(rows, rows)

    def columns(which):
        return pl.ds(pl.multiple_of(which * half, 128), half)

    g = Gather(
        depth, gathers, (small, own_query, own_key, own_value, own_out, own_up, own_down),
        (all_small, all_qkv, all_qkv, all_qkv, all_out, all_up, all_down), gather_sems_, (z, x, c, y),
    )
    greet(z, x, c, y, depth)
    swapping = g.copy(x_own, from_y, swap_s, swap_r, z, x, c, 1 - y)
    count = len(gathers)
    ahead = 4

    def along(ch):
        g.zstage(ch)
        if ch + ahead < count:
            g.begin(ch + ahead)

    for ch in range(ahead):
        g.begin(ch)
        if ch == 0:
            swapping.start()
    along(0)
    g.xstage(0)
    along(1)
    along(2)
    g.xstage(1)

    def first_phase(small_v, normed, qkv, exact, inverse, weight, values_ones, kept, exact_low, x_rows):
        get_x = pltpu.make_async_copy(x_own, x_rows, loc.at[1])
        get_x.start()
        g.arrived(0)
        get = pltpu.make_async_copy(all_small, small_v, loc.at[0])
        get.start()
        get.wait()
        for chip in range(2 * depth):
            one, two = small_v[pl.ds(32 * chip, 16), :].astype(f32), small_v[pl.ds(32 * chip + 16, 16), :].astype(f32)
            vecs[0:8, 128 * chip : 128 * chip + 128] = one[0:8] + two[0:8]
            for core, part in enumerate((one, two)):
                for n in range(2):
                    at = (2 * chip + core) * 256 + 128 * n
                    up_bias[0:1, at : at + 128] = part[8 + n : 9 + n]
        get_x.wait()

        def norm_one(source, first):
            gain, shift = vecs[GAIN_ONE : GAIN_ONE + 1, :], vecs[SHIFT_ONE : SHIFT_ONE + 1, :]

            def one(i, _):
                value = normalized(source[tall(i, STEP), :].astype(f32))[0]
                normed[pl.ds(pl.multiple_of(first + i * STEP, 16), STEP), :] = (value * gain + shift).astype(bf16)
                return 0

            lax.fori_loop(0, rows // STEP, one, 0)

        def project(first):
            these = pl.ds(first, rows)
            for n, bias in enumerate((QUERY_BIAS, None, VALUE_BIAS)):
                value = mul(normed[these, :], weight[:, n * half : (n + 1) * half], NN)
                if bias is not None:
                    value = value + vecs[bias : bias + 1, columns(y)]
                qkv[these, n * half : (n + 1) * half] = value.astype(bf16)

        norm_one(x_rows, 0)
        along(3)
        g.xstage(2)
        g.xstage(3)
        for ch in (1, 2, 3):
            g.arrived(ch)
        get = pltpu.make_async_copy(all_qkv, weight, loc.at[0])
        get.start()
        get.wait()
        project(0)
        along(4)
        swapping.wait_recv()
        norm_one(from_y, rows)
        project(rows)
        g.xstage(4)
        along(5)
        put_normed = pltpu.make_async_copy(normed, normed_kept, loc.at[1])
        put_qkv = pltpu.make_async_copy(qkv, qkv_kept, loc.at[2])
        put_normed.start()
        put_qkv.start()
        low_lanes = lax.broadcasted_iota(jnp.int32, (rows, 128), 1) < HDIM

        def keep(pair, block, head, slot):
            return pltpu.make_async_copy(
                kept.at[slot, head], weights_kept.at[2 * pair + head, tall(block, rows)], keep_sem.at[slot, head]
            )

        def keep_pair(pair):
            these = pl.ds(pl.multiple_of(pair * 128, 128), 128)
            return (
                pltpu.make_async_copy(exact.at[:, these], exact_kept.at[:, these], pair_sem.at[0, pair]),
                pltpu.make_async_copy(inverse.at[:, these], inverse_kept.at[:, these], pair_sem.at[1, pair]),
            )

        def send(pair):
            at = pl.multiple_of(pair * 128, 128)
            there = pl.multiple_of(y * half + at, 128)
            return g.copy(
                exact_low.at[:, pl.ds(at, 128)], attended.at[:, pl.ds(there, 128)], att_s.at[pair], att_r.at[pair], z, x, c, 1 - y
            )

        values_ones[:, 128:] = jnp.ones((length, 128), bf16)
        services = {
            0: (lambda: g.xstage(5),),
            1: (lambda: along(6),),
            2: (lambda: g.ystage(4), lambda: along(7)),
            4: (lambda: g.xstage(6), lambda: g.xstage(7)),
            5: (lambda: along(8), lambda: g.ystage(5)),
            7: (lambda: g.xstage(8),),
        }

        def attend(turn, _):
            pair = turn // 2
            slot = turn % 2
            block = 1 - slot
            for n, todo in services.items():

                @pl.when(turn == n)
                def _(todo=todo):
                    for do in todo:
                        do()

            @pl.when(turn > 1)
            def _():
                for head in range(2):
                    keep(0, 0, head, slot).wait()

            at = pl.multiple_of(pair * 128, 128)

            @pl.when(slot == 0)
            def _():
                values_ones[:, :128] = qkv[:, pl.ds(2 * half + at, 128)]

            these = tall(block, rows)
            queries = qkv[these, pl.ds(at, 128)] * bf16(HDIM**-0.5)
            keys = qkv[:, pl.ds(half + at, 128)]
            values = values_ones[...]
            parts = []
            for head in range(2):
                masked = jnp.where(low_lanes == (head == 0), queries, jnp.zeros_like(queries))
                scores = mul(masked, keys, NT)
                top = jnp.max(scores, axis=1, keepdims=True)
                weights = jnp.exp(scores - top).astype(bf16)
                kept[slot, head] = weights
                summed = mul(weights, values, NN)
                parts.append((summed[:, :128], 1.0 / summed[:, 128:]))
            (low, low_inverse), (high, high_inverse) = parts
            scale = jnp.where(low_lanes, low_inverse, high_inverse)
            value = jnp.where(low_lanes, low, high) * scale
            exact[these, pl.ds(at, 128)] = value
            inverse[these, pl.ds(at, 128)] = scale
            for head in range(2):
                keep(pair, block, head, slot).start()

            @pl.when(slot == 0)
            def _():
                exact_low[:, pl.ds(at, 128)] = value.astype(bf16)
                send(pair).start()

            @pl.when(slot == 1)
            def _():
                attended[:, pl.ds(pl.multiple_of(y * half + at, 128), 128)] = value.astype(bf16)
                for put in keep_pair(pair):
                    put.start()

            return 0

        lax.fori_loop(0, 2 * pairs, attend, 0)
        put_normed.wait()
        put_qkv.wait()
        for pair in range(pairs):
            for put in keep_pair(pair):
                put.wait()
        for slot in range(2):
            for head in range(2):
                keep(0, 0, head, slot).wait()
        for pair in range(pairs):
            send(pair).wait()
        swapping.wait_send()

    pl.run_scoped(
        first_phase,
        V(all_small.shape, bf16),
        V((length, width), bf16),
        V((length, 3 * half), bf16),
        V((length, half), f32),
        V((length, half), f32),
        V((width, 3 * half), bf16),
        V((length, 256), bf16),
        V((2, 2, rows, length), bf16),
        V((rows, half), bf16),
        V((rows, width), bf16),
    )

    def rest(sums, near, across, along_z, mine, theirs, stage):
        for partner in partners(z, x, c, y, depth):
            pl.semaphore_signal(entered, inc=1, device_id=partner, device_id_type=MESH)
        s = Scatter(
            depth, ring, scatters, (small_grads, qkv_wgrad, qkv_wgrad, qkv_wgrad, out_wgrad, up_wgrad, down_wgrad),
            (own_small, own_query_grad, own_key_grad, own_value_grad, own_out_grad, own_up_grad, own_down_grad),
            (landed, sums, near, across, along_z, mine, theirs, stage), scatter_sems_, (z, x, c, y),
        )
        total = len(scatters)
        early = total - 4

        def service(n):
            if n + 2 < early:
                s.cstage(n + 2)
            s.xstage(n)
            s.zstage(n - 1)
            if n >= 4:
                s.ystage(n - 4)
            if n + 3 < early:
                s.prepare(n + 3)

        def feed_phase(up_w, down_w, block_sum, normed_grad, up_stage, down_stage, mid, normed_two, cot):
            s.held = up_stage

            def get_down(j, slot):
                return pltpu.make_async_copy(
                    all_down.at[pl.ds(pl.multiple_of(j * width, 16), width)], down_w.at[slot], loc.at[1 + slot]
                )

            def get_up(j, slot):
                return pltpu.make_async_copy(
                    all_up.at[:, pl.ds(pl.multiple_of(j * width, 128), width)], up_w.at[slot], loc.at[3 + slot]
                )

            def put_down(j):
                return pltpu.make_async_copy(down_stage, down_wgrad.at[pl.ds(pl.multiple_of(j * width, 16), width)], loc.at[6])

            get_cot = pltpu.make_async_copy(cotangent, cot, loc.at[0])
            get_x = pltpu.make_async_copy(x_own, normed_two, loc.at[7])
            get_cot.start()
            get_x.start()
            g.arrived(6)
            get_out = pltpu.make_async_copy(all_out, down_w.at[1], loc.at[2])
            get_out.start()
            along(9)
            get_out.wait()
            mid[...] = mul(attended[...], down_w[1], NN)
            get_x.wait()

            def norm_two(i, _):
                these = tall(i, STEP)
                value = mid[these, :] + vecs[OUTPUT_BIAS : OUTPUT_BIAS + 1, :] + normed_two[these, :].astype(f32)
                mid[these, :] = value
                value = normalized(value)[0] * vecs[GAIN_TWO : GAIN_TWO + 1, :] + vecs[SHIFT_TWO : SHIFT_TWO + 1, :]
                normed_two[these, :] = value.astype(bf16)
                return 0

            lax.fori_loop(0, rows // STEP, norm_two, 0)
            block_sum[...] = jnp.zeros_like(block_sum)
            normed_grad[...] = jnp.zeros_like(normed_grad)
            get_cot.wait()
            g.ystage(7)
            g.ystage(8)
            for ch in (4, 5, 7, 8):
                g.arrived(ch)
            get_down(0, 0).start()
            along(10)
            g.xstage(9)
            g.arrived(9)
            get_up(0, 0).start()

            at_start = {
                1: (lambda: pl.semaphore_wait(entered, depth + 2), lambda: s.cstage(0)),
                2: (
                    lambda: s.cstage(1), lambda: s.cmove_sent(0),
                    lambda: g.xstage(12), lambda: g.ystage(11), lambda: g.arrived(11), lambda: get_up(2, 0).start(),
                ),
                3: (
                    lambda: s.cstage(2), lambda: s.cmove_sent(1),
                    lambda: g.ystage(12), lambda: g.arrived(12), lambda: get_up(3, 1).start(),
                ),
            }
            midway = {
                0: (lambda: along(11), lambda: g.xstage(10), lambda: g.arrived(10), lambda: get_up(1, 1).start()),
                1: (lambda: along(12), lambda: g.xstage(11)),
                2: (lambda: s.xstage(0),),
                3: (lambda: s.xstage(1), lambda: s.zstage(0)),
            }

            def feed(j, _):
                slot = j % 2

                for n, todo in at_start.items():

                    @pl.when(j == n)
                    def _(todo=todo):
                        for do in todo:
                            do()

                get_down(j, slot).wait()

                @pl.when(j + 1 < tiles)
                def _():
                    get_down(j + 1, 1 - slot).start()

                get_up(j, slot).wait()
                cols = pl.ds(pl.multiple_of(j * width, 128), width)
                u = mul(normed_two[...], up_w[slot], NN) + up_bias[0:1, cols]
                hidden_grad = mul(cot[...], down_w[slot], NT)
                square = u * u
                gate = 0.5 + 0.5 * jnp.tanh(u * (SQRT_2_PI + (SQRT_2_PI * 0.044715) * square))
                hidden = (u * gate).astype(bf16)
                slope = gate + (u * (gate - gate * gate)) * (2 * SQRT_2_PI + (6 * SQRT_2_PI * 0.044715) * square)
                pre_grad = (hidden_grad * slope).astype(bf16)
                block_sum[...] += mul(hidden, down_w[slot], NN)
                for n, todo in midway.items():

                    @pl.when(j == n)
                    def _(todo=todo):
                        for do in todo:
                            do()

                @pl.when(j > 0)
                def _():
                    put_down(0).wait()

                up_stage[slot] = mul(normed_two[...], pre_grad, TN).astype(bf16)
                for n in range(tiles):

                    @pl.when(j == n)
                    def _(n=n):
                        s.begin(n)

                down_stage[...] = mul(hidden, cot[...], TN).astype(bf16)
                put_down(j).start()
                for n in range(tiles):

                    @pl.when(j == n)
                    def _(n=n):
                        s.prepare(n)

                up_bgrad[0:1, cols] = jnp.sum(pre_grad.astype(f32), axis=0, keepdims=True)
                normed_grad[...] += mul(pre_grad, up_w[slot], NT)
                return 0

            lax.fori_loop(0, tiles, feed, 0)
            s.cstage(3)
            get_out = pltpu.make_async_copy(all_out, down_w.at[1], loc.at[2])
            get_out.start()
            zero = jnp.zeros((1, width), f32)

            def back_two(i, so_far):
                gain_sum, shift_sum, out_sum, cot_sum = so_far
                these = tall(i, STEP)
                rows_in = mid[these, :]
                block_sum[these, :] = block_sum[these, :] + rows_in + vecs[DOWN_BIAS : DOWN_BIAS + 1, :]
                zed, inverse = normalized(rows_in)
                grad = normed_grad[these, :]
                scaled = grad * vecs[GAIN_TWO : GAIN_TWO + 1, :]
                part = inverse * (
                    scaled - jnp.mean(scaled, axis=-1, keepdims=True) - zed * jnp.mean(scaled * zed, axis=-1, keepdims=True)
                )
                above = cot[these, :].astype(f32)
                whole = above + part
                mid[these, :] = whole
                branch = whole.astype(bf16)
                normed_two[these, :] = branch
                cot[these, :] = block_sum[these, :].astype(bf16)
                add = lambda total_, value: total_ + jnp.sum(value, axis=0, keepdims=True)
                return (
                    add(gain_sum, grad * zed), add(shift_sum, grad), add(out_sum, branch.astype(f32)), add(cot_sum, above),
                )

            gain_sum, shift_sum, out_sum, cot_sum = lax.fori_loop(0, rows // STEP, back_two, (zero,) * 4)
            vec_grads[...] = jnp.zeros_like(vec_grads)
            vec_grads[GAIN_TWO : GAIN_TWO + 1, :] = gain_sum
            vec_grads[SHIFT_TWO : SHIFT_TWO + 1, :] = shift_sum
            vec_grads[OUTPUT_BIAS : OUTPUT_BIAS + 1, :] = out_sum
            vec_grads[DOWN_BIAS : DOWN_BIAS + 1, :] = cot_sum
            put_mid = pltpu.make_async_copy(mid, mid_grad_kept, loc.at[0])
            put_block = pltpu.make_async_copy(cot, block_out, loc.at[7])
            put_mid.start()
            put_block.start()
            put_down(0).wait()
            for ch in range(4, 8):
                s.begin(ch)
            get_out.wait()
            down_w[0, low_part, :] = mul(normed_two[...], down_w[1], NT).astype(bf16)
            put_grad = pltpu.make_async_copy(down_w.at[0, low_part], attended_grad_kept, loc.at[1])
            put_grad.start()
            put_grad.wait()
            s.copy(attended_grad_kept.at[:, columns(1 - y)], grads.at[high_part], grad_s, grad_r, z, x, c, 1 - y).start()
            get_own = pltpu.make_async_copy(attended_grad_kept.at[:, columns(y)], grads.at[low_part], loc.at[1])
            get_own.start()
            s.prepare(4)
            down_stage[...] = mul(attended[...], normed_two[...], TN).astype(bf16)
            put_out = pltpu.make_async_copy(down_stage, out_wgrad, loc.at[5])
            put_out.start()
            s.cstage(4)
            s.xstage(2)
            s.zstage(1)
            s.prepare(5)
            s.cmove_sent(2)
            s.cmove_sent(3)
            get_own.wait()
            put_mid.wait()
            put_block.wait()
            put_out.wait()
            s.begin(8)

        pl.run_scoped(
            feed_phase,
            V((2, width, width), bf16),
            V((2, width, width), bf16),
            V((rows, width), f32),
            V((rows, width), f32),
            V((2, width, width), bf16),
            V((width, width), bf16),
            V((rows, width), f32),
            V((rows, width), bf16),
            V((rows, width), bf16),
        )

        def back_phase(qkv):
            get_qkv = pltpu.make_async_copy(qkv_kept, qkv, loc.at[1])
            get_qkv.start()

            def attention(exact, inverse, key_sum, value_sum, kept):
                get_exact = pltpu.make_async_copy(exact_kept, exact, loc.at[2])
                get_inverse = pltpu.make_async_copy(inverse_kept, inverse, loc.at[3])
                get_exact.start()
                get_inverse.start()
                blocks = length // SIZE

                def load(turn, head, slot):
                    return pltpu.make_async_copy(
                        weights_kept.at[2 * (turn % pairs) + head, tall(turn // pairs, SIZE)], kept.at[slot, head],
                        keep_sem.at[slot, head],
                    )

                for head in range(2):
                    load(0, head, 0).start()
                for get in (get_qkv, get_exact, get_inverse):
                    get.wait()
                low_lanes = lax.broadcasted_iota(jnp.int32, (SIZE, 128), 1) < HDIM

                def attend(turn, _):
                    block, pair, slot = turn // pairs, turn % pairs, turn % 2
                    for n, at in ((3, 4), (4, 11), (5, 18), (6, 25)):

                        @pl.when(turn == at)
                        def _(n=n):
                            service(n)

                    @pl.when(turn == pairs * (rows // SIZE))
                    def _():
                        s.copy(attended_grad_kept.at[:, columns(1 - y)], grads.at[high_part], grad_s, grad_r, z, x, c, 1 - y).wait_recv()

                    for head in range(2):
                        load(turn, head, slot).wait()

                    @pl.when(turn + 1 < blocks * pairs)
                    def _():
                        for head in range(2):
                            load(turn + 1, head, 1 - slot).start()

                    these = tall(block, SIZE)
                    at = pl.multiple_of(pair * 128, 128)
                    queries = qkv[these, pl.ds(at, 128)] * bf16(HDIM**-0.5)
                    keys = qkv[:, pl.ds(half + at, 128)]
                    values = qkv[:, pl.ds(2 * half + at, 128)]
                    low = (grads[these, pl.ds(at, 128)].astype(f32) * inverse[these, pl.ds(at, 128)]).astype(bf16)
                    product = low.astype(f32) * exact[these, pl.ds(at, 128)]
                    queries_t, low_t = queries.T, low.T
                    query_parts, key_parts, value_parts = [], [], []
                    for head in range(2):
                        own = low_lanes == (head == 0)
                        lanes = slice(HDIM * head, HDIM * head + HDIM)
                        masked = jnp.where(own, low, jnp.zeros_like(low))
                        prob_grad = mul(masked, values, NT)
                        delta = jnp.sum(jnp.where(own, product, 0.0), axis=1, keepdims=True)
                        weights = kept[slot, head]
                        score_grad = (weights.astype(f32) * (prob_grad - delta)).astype(bf16)
                        query_parts.append(mul(score_grad, keys, NN))
                        key_parts.append(mul(queries_t[lanes], score_grad, NN))
                        value_parts.append(mul(low_t[lanes], weights, NN))
                    query_grad = jnp.where(low_lanes, query_parts[0], query_parts[1]) * HDIM**-0.5
                    qkv[these, pl.ds(at, 128)] = query_grad.astype(bf16)
                    key_part = jnp.concatenate(key_parts, axis=0)
                    value_part = jnp.concatenate(value_parts, axis=0)
                    key_sum[pair] = jnp.where(block == 0, key_part, key_sum[pair] + key_part)
                    value_sum[pair] = jnp.where(block == 0, value_part, value_sum[pair] + value_part)
                    return 0

                lax.fori_loop(0, blocks * pairs, attend, 0)

                def finish(pair, _):
                    at = pl.multiple_of(pair * 128, 128)
                    qkv[:, pl.ds(half + at, 128)] = key_sum[pair].T.astype(bf16)
                    qkv[:, pl.ds(2 * half + at, 128)] = value_sum[pair].T.astype(bf16)
                    return 0

                lax.fori_loop(0, pairs, finish, 0)

            pl.run_scoped(
                attention,
                V((length, half), f32),
                V((length, half), f32),
                V((pairs, 128, length), f32),
                V((pairs, 128, length), f32),
                V((2, 2, SIZE, length), bf16),
            )

            def inputs(normed, weight, m_low, m_own, above, rows_in):
                gets = [
                    pltpu.make_async_copy(src, dst, loc.at[n])
                    for n, (src, dst) in enumerate(((all_qkv, weight), (normed_kept, normed), (mid_grad_kept, above), (x_own, rows_in)))
                ]
                for get in gets:
                    get.start()
                gets[0].wait()
                m_low[...] = mul(qkv[high_part, :], weight[...], NT).astype(bf16)
                sending = s.copy(m_low, from_y, m_s, m_r, z, x, c, 1 - y)
                sending.start()
                gets[1].wait()
                for n in range(3):
                    these = slice(n * half, (n + 1) * half)
                    qkv_wgrad[:, these] = mul(normed[...], qkv[:, these], TN).astype(bf16)
                    s.begin(early + n)
                s.xstage(early - 2)
                s.zstage(early - 3)
                s.prepare(early)
                m_own[...] = mul(qkv[low_part, :], weight[...], NT)
                s.cstage(early)
                s.xstage(early - 1)
                s.zstage(early - 2)
                s.prepare(early + 1)
                ones = jnp.ones((8, length), bf16)
                for row, n in ((QUERY_BIAS, 0), (VALUE_BIAS, 2)):
                    value = mul(ones, qkv[:, n * half : (n + 1) * half], NN)[0:1]
                    for other in range(BOTH):
                        these = slice(other * half, (other + 1) * half)
                        vec_grads[row : row + 1, these] = jnp.where(y == other, value, 0.0)
                s.cstage(early + 1)
                s.prepare(early + 2)
                s.xstage(early)
                s.zstage(early - 1)
                s.cstage(early + 2)
                s.xstage(early + 1)
                s.zstage(early)
                gets[2].wait()
                gets[3].wait()
                sending.wait()
                zero = jnp.zeros((1, width), f32)

                def back_one(i, so_far):
                    gain_sum, shift_sum = so_far
                    these = tall(i, STEP)
                    zed, inverse = normalized(rows_in[these, :].astype(f32))
                    grad = m_own[these, :] + from_y[these, :].astype(f32)
                    scaled = grad * vecs[GAIN_ONE : GAIN_ONE + 1, :]
                    part = inverse * (
                        scaled - jnp.mean(scaled, axis=-1, keepdims=True) - zed * jnp.mean(scaled * zed, axis=-1, keepdims=True)
                    )
                    above[these, :] = above[these, :] + part
                    add = lambda total_, value: total_ + jnp.sum(value, axis=0, keepdims=True)
                    return add(gain_sum, grad * zed), add(shift_sum, grad)

                gain_sum, shift_sum = lax.fori_loop(0, rows // STEP, back_one, (zero, zero))
                put = pltpu.make_async_copy(above, input_grad, loc.at[0])
                put.start()
                vec_grads[GAIN_ONE : GAIN_ONE + 1, :] = gain_sum
                vec_grads[SHIFT_ONE : SHIFT_ONE + 1, :] = shift_sum
                blank = jnp.zeros((6, 128), f32)
                for chip in range(2 * depth):
                    eight = vec_grads[:, 128 * chip : 128 * chip + 128]
                    for core in range(2):
                        at = 256 * (2 * chip + core)
                        block = jnp.concatenate([eight, up_bgrad[0:1, at : at + 128], up_bgrad[0:1, at + 128 : at + 256], blank], axis=0)
                        small_grads[pl.ds(32 * chip + 16 * core, 16), :] = block.astype(bf16)
                s.begin(total - 1)
                put.wait()

            pl.run_scoped(
                inputs,
                V((length, width), bf16),
                V((width, 3 * half), bf16),
                V((rows, width), bf16),
                V((rows, width), f32),
                V((rows, width), f32),
                V((rows, width), bf16),
            )

        pl.run_scoped(back_phase, V((length, 3 * half), bf16))
        s.prepare(total - 1)
        s.cstage(total - 1)
        s.xstage(total - 2)
        s.zstage(total - 3)
        s.xstage(total - 1)
        s.zstage(total - 2)
        for ch in range(3, total - 4):
            s.ystage(ch)
        s.zstage(total - 1)
        for ch in range(total - 4, total):
            s.ystage(ch)
        s.copy(attended_grad_kept.at[:, columns(1 - y)], grads.at[high_part], grad_s, grad_r, z, x, c, 1 - y).wait_send()
        for ch in range(total):
            s.sent(ch)

    high = width // (4 * depth)
    total = len(scatters)
    pl.run_scoped(
        rest,
        V((ring, 2 * depth, high, width), bf16),
        V((2, 2 * depth, high, width), bf16),
        V((total - 2, depth, high, width), bf16),
        V((total - 2, depth - 1, high, width), bf16),
        V((total - 2, high, width), bf16),
        V((total - 2, high, width), bf16),
        V((2, high, width), f32),
    )
    for ch in range(count):
        g.sent(ch)


def gather_chunks(high, width, wide, quarter):
    half = width // BOTH
    return (
        ((0, 0, 16, 0, 0, 128, False),)
        + tuple((1 + n, 0, high, None, n * half, half, False) for n in range(3))
        + tuple((6, quarter * i, quarter, 0, 0, width, True) for i in range(2))
        + ((4, 0, high, 0, 0, width, False),)
        + tuple((6, quarter * i, quarter, 0, 0, width, True) for i in range(2, 4))
        + tuple((5, 0, high, width * i, width * i, width, i > 1) for i in range(wide // width))
    )


def scatter_chunks(high, width, wide, owned):
    half = width // BOTH
    return (
        tuple((5, 0, high, width * j, width) for j in range(wide // width))
        + tuple((6, high * i, high, 0, width) for i in range(owned // high))
        + ((4, 0, high, 0, width),)
        + tuple((1 + n, 0, high, half * n, half) for n in range(3))
        + ((0, 0, 16, 0, 128),)
    )


def layer(small, own_query, own_key, own_value, own_out, own_up, own_down, x_own, cotangent, depth=DEPTH, ring=4):
    rows, width = x_own.shape
    length, half, wide = BOTH * rows, width // BOTH, own_up.shape[1]
    parts = 4 * depth
    high, owned = own_up.shape[0], own_down.shape[0]
    gathers = gather_chunks(high, width, wide, owned // 4)
    scatters = scatter_chunks(high, width, wide, owned)
    count, total = len(gathers), len(scatters)
    S, V = pltpu.SemaphoreType.DMA, pltpu.VMEM
    shape = jax.ShapeDtypeStruct
    out = [
        shape((rows, width), bf16), shape((rows, width), f32), shape((16, 128), f32),
        shape((high, width), f32), shape((high, width), f32), shape((high, width), f32), shape((high, width), f32),
        shape((high, wide), f32), shape((owned, width), f32),
        shape((parts * 16, 128), bf16), shape((width, 3 * half), bf16), shape((width, width), bf16), shape((width, wide), bf16),
        shape((wide, width), bf16), shape((length, width), bf16), shape((length, 3 * half), bf16), shape((length, half), f32),
        shape((length, half), f32), shape((half // HDIM, length, length), bf16), shape((rows, width), f32), shape((rows, width), bf16),
        shape((width, width), bf16), shape((width, wide), bf16), shape((wide, width), bf16),
        shape((total, 2 * depth, high, width), bf16),
    ]
    return pl.pallas_call(
        functools.partial(layer_kernel, depth, ring, gathers, scatters),
        out_shape=out,
        in_specs=[pl.BlockSpec(memory_space=pl.ANY)] * 9,
        out_specs=[pl.BlockSpec(memory_space=pl.ANY)] * len(out),
        scratch_shapes=[
            V((rows, width), bf16), V((rows, width), bf16), V((length, half), bf16), V((8, width), f32), V((1, wide), f32),
            V((8, width), f32), V((1, wide), f32), V((width, 3 * half), bf16), V((parts * 16, 128), bf16),
        ]
        + gather_sems(depth, count)
        + [
            S((ring, 2 * depth)), S((2,)), S((total, 2 * depth)), S((total, 2 * depth)), S((total, depth)), S((total, depth)),
            S((total, depth)), S((total, depth)), S((total,)), S((total,)), S((2,)),
            pltpu.SemaphoreType.REGULAR, S, S, S((half // 128,)), S((half // 128,)), S, S, S, S, S((8,)), S((2, 2)), S((2, half // 128)),
        ],
        compiler_params=pltpu.CompilerParams(collective_id=1, has_side_effects=True, vmem_limit_bytes=63 * 2**20),
        name="encoder_layer",
    )(small, own_query, own_key, own_value, own_out, own_up, own_down, x_own, cotangent)[:9]


def pack_small(vectors, up_bias, c):
    rows = jnp.stack(vectors)
    zero = jnp.zeros_like(rows)
    rows = jnp.concatenate([jnp.where(c == 0, rows, zero), jnp.where(c == 0, zero, rows)], axis=1)
    return jnp.concatenate([rows, up_bias.reshape(2, 128), jnp.zeros((6, 128), rows.dtype)], axis=0)


def fast_device(
    activations, cotangent, query_weight, key_weight, value_weight, output_weight, first_gain, first_shift,
    query_bias, value_bias, output_bias, up_weight, down_weight, second_gain, second_shift, up_bias, down_bias,
):
    c = lax.axis_index("fsdp") % 2
    small = pack_small(
        (first_gain, first_shift, query_bias, value_bias, output_bias, second_gain, second_shift, down_bias), up_bias, c
    )
    block_out, input_grad, own_small, own_query, own_key, own_value, own_output, own_up, own_down = layer(
        small, query_weight, key_weight, value_weight, output_weight, up_weight, down_weight, activations[0], cotangent[0]
    )
    own_vecs = lax.dynamic_slice_in_dim(own_small, c * 64, 64, 1)
    return (
        block_out.reshape(activations.shape),
        input_grad.reshape(activations.shape),
        own_query,
        own_key,
        own_value,
        own_output,
        own_vecs[0],
        own_vecs[1],
        own_vecs[2],
        own_vecs[3],
        own_vecs[4],
        own_up,
        own_down,
        own_vecs[5],
        own_vecs[6],
        own_small[8:10].reshape(-1),
        own_vecs[7],
    )


def solution(mesh):
    fits = mesh.shape["fsdp"] == 4 * DEPTH and mesh.shape["ctx"] == BOTH
    return jax.shard_map(
        fast_device if fits else plain_device,
        mesh=mesh,
        in_specs=(
            P("fsdp", "ctx", None),
            P("fsdp", "ctx", None),
            P("fsdp", None),
            P("fsdp", None),
            P("fsdp", None),
            P("fsdp", None),
            P("fsdp"),
            P("fsdp"),
            P("fsdp"),
            P("fsdp"),
            P("fsdp"),
            P("fsdp", None),
            P("fsdp", None),
            P("fsdp"),
            P("fsdp"),
            P("fsdp"),
            P("fsdp"),
        ),
        out_specs=(
            P("fsdp", "ctx", None),
            P("fsdp", "ctx", None),
            P("fsdp", None),
            P("fsdp", None),
            P("fsdp", None),
            P("fsdp", None),
            P("fsdp"),
            P("fsdp"),
            P("fsdp"),
            P("fsdp"),
            P("fsdp"),
            P("fsdp", None),
            P("fsdp", None),
            P("fsdp"),
            P("fsdp"),
            P("fsdp"),
            P("fsdp"),
        ),
        check_vma=False,
    )
```
